256 devices in a mesh: ctx: 16 (over x_hi, z), resp: 16 (over y, x_lo, core).
Axes of the slice: x: 4 (x_hi: 2, x_lo: 2; x = x_hi * 2 + x_lo), y: 4, z: 8, core: 2. Of those that a mesh axis runs over, the one named last changes fastest.
Arguments:
- q_resp: bfloat16 [16, 2048, 2048], P('resp', 'ctx'), may hold values from -8 to 8
- k_resp: bfloat16 [16, 2048, 512], P('resp', 'ctx'), may hold values from -6 to 6
- v_resp: bfloat16 [16, 2048, 512], P('resp', 'ctx'), may hold values from -6 to 6
- k_prompt: bfloat16 [1024, 512], P('ctx'), may hold values from -8 to 8
- v_prompt: bfloat16 [1024, 512], P('ctx'), may hold values from -6 to 6
- d_out: bfloat16 [16, 2048, 2048], P('resp', 'ctx'), may hold values from -4 to 4
- lengths: int32 [16], P('resp'), may hold values from 512 to 2048, as said below
- counts: int32 [16], P('resp'), may hold values from 256 to 2048, as said below
Outputs:
- attn_out: bfloat16 [16, 2048, 2048], P('resp', 'ctx')
- d_query: bfloat16 [16, 2048, 2048], P('resp', 'ctx')
- d_key_resp: bfloat16 [16, 2048, 512], P('resp', 'ctx')
- d_value_resp: bfloat16 [16, 2048, 512], P('resp', 'ctx')
- d_key_prompt: bfloat16 [1024, 512], P('ctx')
- d_value_prompt: bfloat16 [1024, 512], P('ctx')
The draws below stay inside these ranges and needn't reach their ends.
Inputs may be any that keep to these rules, and one draw needn't show every extreme that they name: Rows of response r from lengths[r] on are padding; some response has 2048 real tokens. The first counts[r] tokens of response r enter the loss; (lengths[r] + 1) // 2 <= counts[r] <= lengths[r].
All inputs are finite; a program needn't handle non-finite values.
Results may differ from the reference program's by a relative error of at most 0.035.
Values may be sent and summed in bfloat16 or wider, within the bound.
No kernel may reach another device: no remote copies, remote signals or barrier semaphores. Data moves between devices by JAX's collectives and lax.ppermute only.
A program may use at most 128 MiB of HBM per device.

```python
import jax
import jax.numpy as jnp
from jax import lax

HEADS = 16
KV_HEADS = 4
HEAD_DIM = 128
RESP_LEN = 2048
PROMPT_LEN = 1024
RESPONSES = 16


def length_pair(key):
    key = jax.random.fold_in(key, 7)
    first, second, third = jax.random.split(key, 3)
    lengths = jax.random.randint(first, (RESPONSES,), RESP_LEN // 4, RESP_LEN + 1)
    order = jax.random.permutation(second, RESPONSES)
    slots = jnp.arange(RESPONSES)
    lengths = jnp.where(slots == order[0], RESP_LEN, lengths)
    lengths = jnp.where(slots == order[1], RESP_LEN // 4, lengths)
    lower = (lengths + 1) // 2
    noise = jax.random.randint(third, (RESPONSES,), 0, 1 << 20)
    counts = lower + noise % (lengths - lower + 1)
    counts = jnp.where(slots == order[0], RESP_LEN, counts)
    counts = jnp.where(slots == order[1], lower, counts)
    return (lengths, counts)


def draw_lengths(key, part):
    return length_pair(key)[0]


def draw_counts(key, part):
    return length_pair(key)[1]


def draw_q_resp(key, part):
    key = jax.random.fold_in(key, 21)
    shape = (RESPONSES, RESP_LEN, HEADS * HEAD_DIM)
    return jax.random.truncated_normal(key, -5.0, 5.0, shape).astype(jnp.bfloat16)


def draw_k_prompt(key, part):
    key = jax.random.fold_in(key, 31)
    shape = (PROMPT_LEN, KV_HEADS * HEAD_DIM)
    return jax.random.truncated_normal(key, -5.0, 5.0, shape).astype(jnp.bfloat16)


def steps_of(rng, extent, cuts, low, top_value):
    factor_of, own = 1.0, jax.random.fold_in(rng, 6)
    for dim, parts in cuts:
        steps = jnp.exp(jax.random.uniform(jax.random.fold_in(own, dim), (parts,), jnp.float32, low / len(cuts), top_value / len(cuts)))
        factor_of = factor_of * jnp.repeat(steps, extent[dim] // parts).reshape([-1 if axis == dim else 1 for axis in range(len(extent))])
    return factor_of


def normal_values(rng, extent, deviation, most, shards=(), kind=jnp.bfloat16):
    values = jax.random.normal(rng, extent, jnp.float32) * deviation
    if len(shards) > 0:
        values = steps_of(rng, extent, shards, -0.22, 0.18) * values
    return jnp.clip(values, min=-most, max=most).astype(kind)


def setup_inputs(seed: int = 0) -> dict:
    arg_keys = jax.random.split(jax.random.key(seed), 9)
    return {
        "q_resp": draw_q_resp(jax.random.fold_in(arg_keys[8], 71), 0),
        "k_resp": normal_values(arg_keys[1], (RESPONSES, RESP_LEN, KV_HEADS * HEAD_DIM), 1.0, 6.0, ((0, 16), (1, 16))),
        "v_resp": normal_values(arg_keys[2], (RESPONSES, RESP_LEN, KV_HEADS * HEAD_DIM), 1.0, 6.0, ((0, 16), (1, 16))),
        "k_prompt": draw_k_prompt(jax.random.fold_in(arg_keys[8], 71), 0),
        "v_prompt": normal_values(arg_keys[4], (PROMPT_LEN, KV_HEADS * HEAD_DIM), 1.0, 6.0, ((0, 16),)),
        "d_out": normal_values(arg_keys[5], (RESPONSES, RESP_LEN, HEADS * HEAD_DIM), 0.5, 4.0, ((0, 16), (1, 16))),
        "lengths": draw_lengths(jax.random.fold_in(arg_keys[8], 71), 0),
        "counts": draw_counts(jax.random.fold_in(arg_keys[8], 71), 0),
    }


NEG = -1.0e30


def rounded(value):
    return lax.optimization_barrier(value.astype(jnp.bfloat16)).astype(jnp.float32)


def group_terms(query_rows, prompt_keys, prompt_values, resp_keys, resp_values, grad_rows, length, loss_count):
    key_all = jnp.concatenate([prompt_keys, resp_keys], axis=0).astype(jnp.float32)
    value_all = jnp.concatenate([prompt_values, resp_values], axis=0).astype(jnp.float32)
    query_float = query_rows.astype(jnp.float32)
    score_scale = HEAD_DIM ** -0.5
    position = jnp.arange(RESP_LEN, dtype=jnp.int32)
    key_position = jnp.arange(PROMPT_LEN + RESP_LEN, dtype=jnp.int32) - PROMPT_LEN
    allowed = key_position[None, :] <= position[:, None]
    logits = jnp.einsum("tid,jd->tij", query_float, key_all) * score_scale
    logits = jnp.where(allowed[None], logits, NEG)
    row_max = jnp.max(logits, axis=-1, keepdims=True)
    shifted = jnp.exp(logits - row_max)
    row_total = jnp.sum(shifted, axis=-1, keepdims=True)
    accumulated = jnp.einsum("tij,jd->tid", rounded(shifted), value_all)
    valid_rows = (position < length).astype(jnp.float32)
    attended = rounded(accumulated / row_total * valid_rows[None, :, None])
    log_total = row_max + jnp.log(row_total)
    weight = jnp.where(position < loss_count, RESP_LEN / loss_count.astype(jnp.float32), 0.0)
    upstream = rounded(grad_rows.astype(jnp.float32) * weight[None, :, None])
    row_delta = jnp.sum(upstream * attended, axis=-1, keepdims=True)
    probability = jnp.exp(logits - log_total)
    value_grad = jnp.einsum("tij,tid->jd", rounded(probability), upstream)
    prob_grad = jnp.einsum("tid,jd->tij", upstream, value_all)
    score_grad = rounded(probability * (prob_grad - row_delta) * score_scale)
    query_grad = jnp.einsum("tij,jd->tid", score_grad, key_all)
    key_grad = jnp.einsum("tij,tid->jd", score_grad, query_float)
    return attended, query_grad, key_grad, value_grad


def reference(q_resp, k_resp, v_resp, k_prompt, v_prompt, d_out, lengths, counts):
    group_size = HEADS // KV_HEADS
    prompt_key_heads = k_prompt.reshape(PROMPT_LEN, KV_HEADS, HEAD_DIM).transpose(1, 0, 2)
    prompt_value_heads = v_prompt.reshape(PROMPT_LEN, KV_HEADS, HEAD_DIM).transpose(1, 0, 2)

    def one_response(inputs):
        query_rows, key_rows, value_rows, grad_rows, length, loss_count = inputs
        query_heads = query_rows.reshape(RESP_LEN, KV_HEADS, group_size, HEAD_DIM).transpose(1, 2, 0, 3)
        grad_heads = grad_rows.reshape(RESP_LEN, KV_HEADS, group_size, HEAD_DIM).transpose(1, 2, 0, 3)
        key_heads = key_rows.reshape(RESP_LEN, KV_HEADS, HEAD_DIM).transpose(1, 0, 2)
        value_heads = value_rows.reshape(RESP_LEN, KV_HEADS, HEAD_DIM).transpose(1, 0, 2)

        def one_group(pieces):
            return group_terms(pieces[0], pieces[1], pieces[2], pieces[3], pieces[4], pieces[5], length, loss_count)

        attended, query_grad, key_grad, value_grad = lax.map(
            one_group, (query_heads, prompt_key_heads, prompt_value_heads, key_heads, value_heads, grad_heads))
        attended = attended.transpose(2, 0, 1, 3).reshape(RESP_LEN, HEADS * HEAD_DIM)
        query_grad = query_grad.transpose(2, 0, 1, 3).reshape(RESP_LEN, HEADS * HEAD_DIM)
        key_grad = key_grad.transpose(1, 0, 2).reshape(PROMPT_LEN + RESP_LEN, KV_HEADS * HEAD_DIM)
        value_grad = value_grad.transpose(1, 0, 2).reshape(PROMPT_LEN + RESP_LEN, KV_HEADS * HEAD_DIM)
        return (attended, query_grad, key_grad[PROMPT_LEN:], value_grad[PROMPT_LEN:],
                key_grad[:PROMPT_LEN], value_grad[:PROMPT_LEN])

    outs = lax.map(one_response, (q_resp, k_resp, v_resp, d_out, lengths, counts))
    return (outs[0].astype(jnp.bfloat16), outs[1].astype(jnp.bfloat16), outs[2].astype(jnp.bfloat16),
            outs[3].astype(jnp.bfloat16), jnp.sum(outs[4], axis=0).astype(jnp.bfloat16),
            jnp.sum(outs[5], axis=0).astype(jnp.bfloat16))
```

```python
import functools
import math

import jax
import jax.numpy as jnp
from jax import lax
from jax.experimental import pallas as pl
from jax.experimental.pallas import tpu as pltpu
from jax.sharding import Mesh
from jax.sharding import PartitionSpec as P

HEADS = 16
KV_HEADS = 4
HEAD_DIM = 128
GROUP = HEADS // KV_HEADS
RESP_LEN = 2048
PROMPT_LEN = 1024
CTX = ("xh", "zh", "zl")
QUAD = ("xh", "zl")
ROWS = 128
PROWS = 64
CHUNK = 256
KEYS = PROMPT_LEN + RESP_LEN
PROMPT_CHUNKS = PROMPT_LEN // CHUNK
CHUNKS = KEYS // CHUNK
LANES = GROUP * ROWS
SCALE = HEAD_DIM**-0.5
SCALE2 = SCALE * math.log2(math.e)
NEG = -1e30
F32 = jnp.float32
BF16 = jnp.bfloat16


def dot(a, b):
    return jnp.dot(a, b, preferred_element_type=F32)


def attn_kernel(
    info,
    weight,
    qd,
    kv,
    od,
    dkv,
    k_s,
    v_s,
    kt_s,
    vt_s,
    score_s,
    prob_s,
    dk_s,
    dv_s,
    q_s,
    qt_s,
    upt_s,
    upl_s,
    uplt_s,
    acc_s,
):
    zh, length, count = info[0], info[1], info[2]
    up_weight = weight[0]

    def load_block(i, carry):
        at_p = pl.ds(pl.multiple_of(i * PROWS, PROWS), PROWS)
        at_r = pl.ds(pl.multiple_of(PROMPT_LEN + i * ROWS, ROWS), ROWS)
        k_s[at_r, :] = kv[i, :ROWS, :HEAD_DIM]
        v_s[at_r, :] = kv[i, :ROWS, HEAD_DIM:]
        k_s[at_p, :] = kv[i, ROWS:, :HEAD_DIM]
        v_s[at_p, :] = kv[i, ROWS:, HEAD_DIM:]
        return carry

    lax.fori_loop(0, 16, load_block, 0)

    def turn_chunk(c, carry):
        at = pl.ds(pl.multiple_of(c * CHUNK, CHUNK), CHUNK)
        kt_s[c] = k_s[at, :].T
        vt_s[c] = v_s[at, :].T
        dk_s[at, :] = jnp.zeros((CHUNK, HEAD_DIM), F32)
        dv_s[at, :] = jnp.zeros((CHUNK, HEAD_DIM), F32)
        return carry

    lax.fori_loop(0, CHUNKS, turn_chunk, 0)

    def tile(s, carry):
        block = (s // 2) * 8 + zh * 2 + s % 2
        row = block * ROWS + lax.broadcasted_iota(jnp.int32, (1, ROWS), 1)
        row_weight = jnp.where(row < count, up_weight, 0.0)
        row_valid = jnp.where(row < length, 1.0, 0.0)
        for h in range(GROUP):
            cols = slice(h * HEAD_DIM, (h + 1) * HEAD_DIM)
            q_head = qd[s, :, cols]
            q_s[cols, :] = q_head
            qt_s[:, cols] = q_head.T
            grad = qd[s, :, LANES + h * HEAD_DIM : LANES + (h + 1) * HEAD_DIM]
            upt_s[:, cols] = (grad.T.astype(F32) * row_weight).astype(BF16)
        last = PROMPT_CHUNKS + block // 2

        def score_step(c, running):
            at = pl.ds(pl.multiple_of(c * CHUNK, CHUNK), CHUNK)
            score = dot(k_s[at, :], qt_s[...])
            score_s[at, :] = score
            return jnp.maximum(running, jnp.max(score.reshape(CHUNK // 8, 8, LANES), axis=0))

        running = lax.fori_loop(0, last, score_step, jnp.full((8, LANES), NEG, F32))
        last_at = pl.ds(pl.multiple_of(last * CHUNK, CHUNK), CHUNK)
        score = dot(k_s[last_at, :], qt_s[...])
        key_row = (last - PROMPT_CHUNKS) * CHUNK + lax.broadcasted_iota(
            jnp.int32, (CHUNK, LANES), 0
        )
        query_row = block * ROWS + lax.broadcasted_iota(jnp.int32, (CHUNK, LANES), 1) % ROWS
        score = jnp.where(key_row <= query_row, score, NEG)
        score_s[last_at, :] = score
        running = jnp.maximum(running, jnp.max(score.reshape(CHUNK // 8, 8, LANES), axis=0))
        shift = jnp.max(running, axis=0, keepdims=True) * SCALE2

        acc_s[...] = jnp.zeros_like(acc_s)

        def prob_step(c, total):
            at = pl.ds(pl.multiple_of(c * CHUNK, CHUNK), CHUNK)
            prob = jnp.exp2(score_s[at, :] * SCALE2 - shift)
            low = prob.astype(BF16)
            prob_s[at, :] = low
            acc_s[...] += dot(vt_s[c], low)
            return total + jnp.sum(prob.reshape(CHUNK // 8, 8, LANES), axis=0)

        total = lax.fori_loop(0, last + 1, prob_step, jnp.zeros((8, LANES), F32))
        inverse = 1.0 / jnp.sum(total, axis=0, keepdims=True)
        valid = jnp.concatenate([row_valid] * GROUP, axis=1)
        out_t = (acc_s[...] * (inverse * valid)).astype(BF16)
        up_low = (upt_s[...].astype(F32) * inverse).astype(BF16)
        uplt_s[...] = up_low
        delta = jnp.sum(up_low.astype(F32) * out_t.astype(F32), axis=0, keepdims=True)
        for h in range(GROUP):
            cols = slice(h * HEAD_DIM, (h + 1) * HEAD_DIM)
            od[s, :, cols] = out_t[:, cols].T
            upl_s[cols, :] = up_low[:, cols].T

        acc_s[...] = jnp.zeros_like(acc_s)

        def back_step(c, carry):
            at = pl.ds(pl.multiple_of(c * CHUNK, CHUNK), CHUNK)
            low = prob_s[at, :]
            prob_grad = dot(v_s[at, :], uplt_s[...])
            score_grad = (low.astype(F32) * (prob_grad - delta)).astype(BF16)
            dv_s[at, :] += dot(low, upl_s[...])
            dk_s[at, :] += dot(score_grad, q_s[...])
            acc_s[...] += dot(kt_s[c], score_grad)
            return carry

        lax.fori_loop(0, last + 1, back_step, 0)
        dq_t = (acc_s[...] * SCALE).astype(BF16)
        for h in range(GROUP):
            cols = slice(h * HEAD_DIM, (h + 1) * HEAD_DIM)
            od[s, :, LANES + h * HEAD_DIM : LANES + (h + 1) * HEAD_DIM] = dq_t[:, cols].T
        return carry

    lax.fori_loop(0, 4, tile, 0)

    def store_block(i, carry):
        at_p = pl.ds(pl.multiple_of(i * PROWS, PROWS), PROWS)
        at_r = pl.ds(pl.multiple_of(PROMPT_LEN + i * ROWS, ROWS), ROWS)
        dkv[i, :ROWS, :HEAD_DIM] = (dk_s[at_r, :] * SCALE).astype(BF16)
        dkv[i, :ROWS, HEAD_DIM:] = dv_s[at_r, :].astype(BF16)
        dkv[i, ROWS:, :HEAD_DIM] = (dk_s[at_p, :] * SCALE).astype(BF16)
        dkv[i, ROWS:, HEAD_DIM:] = dv_s[at_p, :].astype(BF16)
        return carry

    lax.fori_loop(0, 16, store_block, 0)


def attend(info, weight, qd, kv):
    vmem = pl.BlockSpec(memory_space=pltpu.VMEM)
    smem = pl.BlockSpec(memory_space=pltpu.SMEM)
    return pl.pallas_call(
        attn_kernel,
        out_shape=(
            jax.ShapeDtypeStruct(qd.shape, BF16),
            jax.ShapeDtypeStruct(kv.shape, BF16),
        ),
        in_specs=[smem, smem, vmem, vmem],
        out_specs=(vmem, vmem),
        scratch_shapes=[
            pltpu.VMEM((KEYS, HEAD_DIM), BF16),
            pltpu.VMEM((KEYS, HEAD_DIM), BF16),
            pltpu.VMEM((CHUNKS, HEAD_DIM, CHUNK), BF16),
            pltpu.VMEM((CHUNKS, HEAD_DIM, CHUNK), BF16),
            pltpu.VMEM((KEYS, LANES), F32),
            pltpu.VMEM((KEYS, LANES), BF16),
            pltpu.VMEM((KEYS, HEAD_DIM), F32),
            pltpu.VMEM((KEYS, HEAD_DIM), F32),
            pltpu.VMEM((LANES, HEAD_DIM), BF16),
            pltpu.VMEM((HEAD_DIM, LANES), BF16),
            pltpu.VMEM((HEAD_DIM, LANES), BF16),
            pltpu.VMEM((LANES, HEAD_DIM), BF16),
            pltpu.VMEM((HEAD_DIM, LANES), BF16),
            pltpu.VMEM((HEAD_DIM, LANES), F32),
        ],
        compiler_params=pltpu.CompilerParams(vmem_limit_bytes=48 * 1024 * 1024),
        cost_estimate=pl.CostEstimate(
            flops=8_000_000_000, bytes_accessed=6_000_000, transcendentals=5_000_000
        ),
    )(info, weight, qd, kv)


def heads_first(x):
    rows = x.shape[0]
    return x.reshape(rows, KV_HEADS, -1).transpose(1, 0, 2)


def body(q_resp, k_resp, v_resp, k_prompt, v_prompt, d_out, lengths, counts):
    zh = lax.axis_index("zh").astype(jnp.int32)
    qd = jnp.concatenate([heads_first(q_resp[0]), heads_first(d_out[0])], axis=2)
    keys = jnp.concatenate([k_resp[0], k_prompt], axis=0)
    values = jnp.concatenate([v_resp[0], v_prompt], axis=0)
    kv = jnp.concatenate([heads_first(keys), heads_first(values)], axis=2)
    rows = ROWS + PROWS
    kv = jnp.broadcast_to(
        kv.reshape(2, 1, 2, rows, 2 * HEAD_DIM), (2, 4, 2, rows, 2 * HEAD_DIM)
    ).reshape(16, rows, 2 * HEAD_DIM)
    kv = lax.all_to_all(kv, CTX, 0, 0, tiled=True)
    qd = lax.all_to_all(qd, QUAD, 0, 0, tiled=True)
    info = jnp.stack([zh, lengths[0], counts[0]])
    weight = (RESP_LEN / counts[0].astype(F32)).reshape(1)
    od, dkv = attend(info, weight, qd, kv)
    dkv = lax.all_to_all(dkv, CTX, 0, 0, tiled=True)
    od = lax.all_to_all(od, QUAD, 0, 0, tiled=True)

    def whole(x):
        return x.transpose(1, 0, 2).reshape(x.shape[1], -1)

    attended = whole(od[:, :, :LANES])
    query_grad = whole(od[:, :, LANES:])
    dkv = jnp.sum(dkv.reshape(2, 4, 2, rows, 2 * HEAD_DIM).astype(F32), axis=1)
    dkv = dkv.astype(BF16).reshape(KV_HEADS, rows, 2 * HEAD_DIM)
    key_grad = whole(dkv[:, :ROWS, :HEAD_DIM])
    value_grad = whole(dkv[:, :ROWS, HEAD_DIM:])
    share = dkv[:, ROWS:].reshape(KV_HEADS, 16, PROWS // 16, 2 * HEAD_DIM).transpose(1, 0, 2, 3)
    share = share.reshape(16, 4 * PROWS // 16 * 2, HEAD_DIM)
    share = lax.all_to_all(share, "resp", 0, 0, tiled=True)
    share = jnp.sum(share.astype(F32), axis=0, keepdims=True).astype(BF16)
    share = jnp.broadcast_to(share, (16,) + share.shape[1:])
    share = lax.all_to_all(share, "resp", 0, 0, tiled=True)
    share = share.reshape(16, KV_HEADS, PROWS // 16, 2, HEAD_DIM).transpose(3, 0, 2, 1, 4)
    share = share.reshape(2, PROWS, KV_HEADS * HEAD_DIM)
    return (
        attended[None],
        query_grad[None],
        key_grad[None],
        value_grad[None],
        share[0],
        share[1],
    )


def solution(mesh):
    split = Mesh(mesh.devices.reshape(2, 4, 2, 16), ("xh", "zh", "zl", "resp"))
    return jax.shard_map(
        body,
        mesh=split,
        in_specs=(
            P("resp", CTX, None),
            P("resp", CTX, None),
            P("resp", CTX, None),
            P(CTX, None),
            P(CTX, None),
            P("resp", CTX, None),
            P("resp"),
            P("resp"),
        ),
        out_specs=(
            P("resp", CTX, None),
            P("resp", CTX, None),
            P("resp", CTX, None),
            P("resp", CTX, None),
            P(CTX, None),
            P(CTX, None),
        ),
        check_vma=False,
    )
```

```python
import math

import jax
import jax.numpy as jnp
from jax import lax
from jax.experimental import pallas as pl
from jax.experimental.pallas import tpu as pltpu
from jax.sharding import Mesh
from jax.sharding import PartitionSpec as P

HEADS = 16
KV_HEADS = 4
HEAD_DIM = 128
GROUP = HEADS // KV_HEADS
RESP_LEN = 2048
PROMPT_LEN = 1024
CTX = ("xh", "zh", "zl")
QUAD = ("xh", "zl")
RESP = ("y", "xl", "core")
ROWS = 128
PROWS = 64
BOTH = ROWS + PROWS
CHUNK = 512
KEYS = PROMPT_LEN + RESP_LEN
PROMPT_CHUNKS = PROMPT_LEN // CHUNK
CHUNKS = KEYS // CHUNK
HALF = GROUP * ROWS
LANES = 2 * HALF
SCALE = HEAD_DIM**-0.5
SCALE2 = SCALE * math.log2(math.e)
NEG = -1e30
F32 = jnp.float32
BF16 = jnp.bfloat16
VMEM = pl.BlockSpec(memory_space=pltpu.VMEM)
SMEM = pl.BlockSpec(memory_space=pltpu.SMEM)


def dot(a, b):
    return jnp.dot(a, b, preferred_element_type=F32)


def head_at(h, width=HEAD_DIM):
    return slice(h * width, (h + 1) * width)


def pack_kernel(info, q, do, k, v, kp, vp, qd0, qd1, qd2, qd3, kv):
    mine = info[0]
    for d, qd in enumerate((qd0, qd1, qd2, qd3)):
        at = pl.ds(pl.multiple_of((mine ^ d) * HALF, HALF), HALF)
        qd[:, :HALF] = q[:, at]
        qd[:, HALF:] = do[:, at]
    for h in range(KV_HEADS):
        for z in range(4):
            to = (h // 2) * 8 + z * 2 + h % 2
            kv[to, :ROWS, :HEAD_DIM] = k[:, head_at(h)]
            kv[to, :ROWS, HEAD_DIM:] = v[:, head_at(h)]
            kv[to, ROWS:, :HEAD_DIM] = kp[:, head_at(h)]
            kv[to, ROWS:, HEAD_DIM:] = vp[:, head_at(h)]


def attn_kernel(
    info,
    weight,
    qd0,
    qd1,
    qd2,
    qd3,
    kv,
    od0,
    od1,
    od2,
    od3,
    dkv,
    k_s,
    v_s,
    kt_s,
    vt_s,
    score_s,
    prob_s,
    dk_s,
    dv_s,
    q_s,
    qt_s,
    upt_s,
    upl_s,
    uplt_s,
    acc_s,
):
    mine, zh, length, count = info[0], info[1], info[2], info[3]
    up_weight = weight[0]

    def load_block(i, carry):
        at_p = pl.ds(pl.multiple_of(i * PROWS, PROWS), PROWS)
        at_r = pl.ds(pl.multiple_of(PROMPT_LEN + i * ROWS, ROWS), ROWS)
        k_s[at_r, :] = kv[i, :ROWS, :HEAD_DIM]
        v_s[at_r, :] = kv[i, :ROWS, HEAD_DIM:]
        k_s[at_p, :] = kv[i, ROWS:, :HEAD_DIM]
        v_s[at_p, :] = kv[i, ROWS:, HEAD_DIM:]
        return carry

    lax.fori_loop(0, 16, load_block, 0)

    def turn_chunk(c, carry):
        at = pl.ds(pl.multiple_of(c * CHUNK, CHUNK), CHUNK)
        kt_s[c] = k_s[at, :].T
        vt_s[c] = v_s[at, :].T
        dk_s[at, :] = jnp.zeros((CHUNK, HEAD_DIM), F32)
        dv_s[at, :] = jnp.zeros((CHUNK, HEAD_DIM), F32)
        return carry

    lax.fori_loop(0, CHUNKS, turn_chunk, 0)

    def tile(half, qds, ods):
        first = half * 8 + zh * 2
        valids = []
        for j in range(2):
            start = (first + ((mine & 1) ^ j)) * ROWS
            row = start + lax.broadcasted_iota(jnp.int32, (1, ROWS), 1)
            row_weight = jnp.where(row < count, up_weight, 0.0)
            valids += [jnp.where(row < length, 1.0, 0.0)] * GROUP
            for h in range(GROUP):
                cols = slice(j * HALF + h * HEAD_DIM, j * HALF + (h + 1) * HEAD_DIM)
                q_head = qds[j][:, head_at(h)]
                q_s[cols, :] = q_head
                qt_s[:, cols] = q_head.T
                grad = qds[j][:, HALF + h * HEAD_DIM : HALF + (h + 1) * HEAD_DIM]
                upt_s[:, cols] = (grad.T.astype(F32) * row_weight).astype(BF16)
        last = PROMPT_CHUNKS + first * ROWS // CHUNK

        def score_step(c, running):
            at = pl.ds(pl.multiple_of(c * CHUNK, CHUNK), CHUNK)
            score = dot(k_s[at, :], qt_s[...])
            score_s[at, :] = score
            return jnp.maximum(running, jnp.max(score.reshape(CHUNK // 8, 8, LANES), axis=0))

        running = lax.fori_loop(0, last, score_step, jnp.full((8, LANES), NEG, F32))
        last_at = pl.ds(pl.multiple_of(last * CHUNK, CHUNK), CHUNK)
        score = dot(k_s[last_at, :], qt_s[...])
        key_row = (last - PROMPT_CHUNKS) * CHUNK + lax.broadcasted_iota(
            jnp.int32, (CHUNK, LANES), 0
        )
        lane = lax.broadcasted_iota(jnp.int32, (CHUNK, LANES), 1)
        query_row = (first + ((mine & 1) ^ (lane // HALF))) * ROWS + lane % ROWS
        score = jnp.where(key_row <= query_row, score, NEG)
        score_s[last_at, :] = score
        running = jnp.maximum(running, jnp.max(score.reshape(CHUNK // 8, 8, LANES), axis=0))
        shift = jnp.max(running, axis=0, keepdims=True) * SCALE2

        acc_s[...] = jnp.zeros_like(acc_s)

        def prob_step(c, total):
            at = pl.ds(pl.multiple_of(c * CHUNK, CHUNK), CHUNK)
            prob = jnp.exp2(score_s[at, :] * SCALE2 - shift)
            low = prob.astype(BF16)
            prob_s[at, :] = low
            acc_s[...] += dot(vt_s[c], low)
            return total + jnp.sum(prob.reshape(CHUNK // 8, 8, LANES), axis=0)

        total = lax.fori_loop(0, last + 1, prob_step, jnp.zeros((8, LANES), F32))
        inverse = 1.0 / jnp.sum(total, axis=0, keepdims=True)
        valid = jnp.concatenate(valids, axis=1)
        out_t = (acc_s[...] * (inverse * valid)).astype(BF16)
        up_low = (upt_s[...].astype(F32) * inverse).astype(BF16)
        uplt_s[...] = up_low
        delta = jnp.sum(up_low.astype(F32) * out_t.astype(F32), axis=0, keepdims=True)
        for j in range(2):
            for h in range(GROUP):
                cols = slice(j * HALF + h * HEAD_DIM, j * HALF + (h + 1) * HEAD_DIM)
                ods[j][:, head_at(h)] = out_t[:, cols].T
                upl_s[cols, :] = up_low[:, cols].T

        acc_s[...] = jnp.zeros_like(acc_s)

        def back_step(c, carry):
            at = pl.ds(pl.multiple_of(c * CHUNK, CHUNK), CHUNK)
            low = prob_s[at, :]
            prob_grad = dot(v_s[at, :], uplt_s[...])
            score_grad = (low.astype(F32) * (prob_grad - delta)).astype(BF16)
            dv_s[at, :] += dot(low, upl_s[...])
            dk_s[at, :] += dot(score_grad, q_s[...])
            acc_s[...] += dot(kt_s[c], score_grad)
            return carry

        lax.fori_loop(0, last + 1, back_step, 0)
        dq_t = (acc_s[...] * SCALE).astype(BF16)
        for j in range(2):
            for h in range(GROUP):
                cols = slice(j * HALF + h * HEAD_DIM, j * HALF + (h + 1) * HEAD_DIM)
                ods[j][:, HALF + h * HEAD_DIM : HALF + (h + 1) * HEAD_DIM] = dq_t[:, cols].T

    tile(mine // 2, (qd0, qd1), (od0, od1))
    tile(1 - mine // 2, (qd2, qd3), (od2, od3))

    def store_block(i, carry):
        at_p = pl.ds(pl.multiple_of(i * PROWS, PROWS), PROWS)
        at_r = pl.ds(pl.multiple_of(PROMPT_LEN + i * ROWS, ROWS), ROWS)
        dkv[i, :ROWS, :HEAD_DIM] = (dk_s[at_r, :] * SCALE).astype(BF16)
        dkv[i, :ROWS, HEAD_DIM:] = dv_s[at_r, :].astype(BF16)
        dkv[i, ROWS:, :HEAD_DIM] = (dk_s[at_p, :] * SCALE).astype(BF16)
        dkv[i, ROWS:, HEAD_DIM:] = dv_s[at_p, :].astype(BF16)
        return carry

    lax.fori_loop(0, 16, store_block, 0)


def unpack_kernel(info, od0, od1, od2, od3, attended, query_grad):
    mine = info[0]
    for d, od in enumerate((od0, od1, od2, od3)):
        at = pl.ds(pl.multiple_of((mine ^ d) * HALF, HALF), HALF)
        attended[:, at] = od[:, :HALF]
        query_grad[:, at] = od[:, HALF:]


def sum_kernel(dkv, key_grad, value_grad, share):
    for h in range(KV_HEADS):
        first = (h // 2) * 8 + h % 2
        both = dkv[first].astype(F32)
        for z in range(1, 4):
            both = both + dkv[first + 2 * z].astype(F32)
        both = both.astype(BF16)
        key_grad[:, head_at(h)] = both[:ROWS, :HEAD_DIM]
        value_grad[:, head_at(h)] = both[:ROWS, HEAD_DIM:]
        share[:, head_at(h)] = both[ROWS:, :HEAD_DIM]
        share[:, head_at(KV_HEADS + h)] = both[ROWS:, HEAD_DIM:]


def bf16(*shape):
    return jax.ShapeDtypeStruct(shape, BF16)


def attend(info, weight, *operands):
    return pl.pallas_call(
        attn_kernel,
        out_shape=(bf16(ROWS, LANES),) * 4 + (bf16(16, BOTH, 2 * HEAD_DIM),),
        in_specs=[SMEM, SMEM] + [VMEM] * 5,
        out_specs=(VMEM,) * 5,
        scratch_shapes=[
            pltpu.VMEM((KEYS, HEAD_DIM), BF16),
            pltpu.VMEM((KEYS, HEAD_DIM), BF16),
            pltpu.VMEM((CHUNKS, HEAD_DIM, CHUNK), BF16),
            pltpu.VMEM((CHUNKS, HEAD_DIM, CHUNK), BF16),
            pltpu.VMEM((KEYS, LANES), F32),
            pltpu.VMEM((KEYS, LANES), BF16),
            pltpu.VMEM((KEYS, HEAD_DIM), F32),
            pltpu.VMEM((KEYS, HEAD_DIM), F32),
            pltpu.VMEM((LANES, HEAD_DIM), BF16),
            pltpu.VMEM((HEAD_DIM, LANES), BF16),
            pltpu.VMEM((HEAD_DIM, LANES), BF16),
            pltpu.VMEM((LANES, HEAD_DIM), BF16),
            pltpu.VMEM((HEAD_DIM, LANES), BF16),
            pltpu.VMEM((HEAD_DIM, LANES), F32),
        ],
        compiler_params=pltpu.CompilerParams(vmem_limit_bytes=48 * 1024 * 1024),
        cost_estimate=pl.CostEstimate(
            flops=8_000_000_000, bytes_accessed=6_000_000, transcendentals=5_000_000
        ),
    )(info, weight, *operands)


def swap(x, axis):
    return lax.ppermute(x, axis, [(0, 1), (1, 0)])


def turn(x, axis, step):
    size = lax.axis_size(axis)
    return lax.ppermute(x, axis, [(i, (i + step) % size) for i in range(size)])


def partner(x, d):
    return lax.ppermute(x, QUAD, [(i, i ^ d) for i in range(4)])


def rounded(x):
    return lax.optimization_barrier(x.astype(BF16))


def body(q_resp, k_resp, v_resp, k_prompt, v_prompt, d_out, lengths, counts):
    mine = (lax.axis_index("xh") * 2 + lax.axis_index("zl")).astype(jnp.int32)
    zh = lax.axis_index("zh").astype(jnp.int32)
    info = jnp.stack([mine, zh, lengths[0], counts[0]])
    weight = (RESP_LEN / counts[0].astype(F32)).reshape(1)
    qd = pl.pallas_call(
        pack_kernel,
        out_shape=(bf16(ROWS, LANES),) * 4 + (bf16(16, BOTH, 2 * HEAD_DIM),),
        in_specs=[SMEM] + [VMEM] * 6,
        out_specs=(VMEM,) * 5,
    )(info, q_resp[0], d_out[0], k_resp[0], v_resp[0], k_prompt, v_prompt)
    qd, kv = list(qd[:4]), qd[4]
    for d in (3, 1, 2):
        qd[d] = partner(qd[d], d)
    kv = lax.all_to_all(kv, CTX, 0, 0, tiled=True)
    od = attend(info, weight, *qd, kv)
    od, dkv = list(od[:4]), od[4]
    for d in (3, 1, 2):
        od[d] = partner(od[d], d)
    dkv = lax.all_to_all(dkv, CTX, 0, 0, tiled=True)
    attended, query_grad = pl.pallas_call(
        unpack_kernel,
        out_shape=(bf16(ROWS, HEADS * HEAD_DIM),) * 2,
        in_specs=[SMEM] + [VMEM] * 4,
        out_specs=(VMEM,) * 2,
    )(info, *od)
    width = KV_HEADS * HEAD_DIM
    key_grad, value_grad, share = pl.pallas_call(
        sum_kernel,
        out_shape=(bf16(ROWS, width), bf16(ROWS, width), bf16(PROWS, 2 * width)),
        in_specs=[VMEM],
        out_specs=(VMEM,) * 3,
    )(dkv)
    for axis in ("core", "xl"):
        share = rounded(share.astype(F32) + swap(share, axis).astype(F32))
    across = share.astype(F32) + turn(share, "y", 2).astype(F32)
    beside = turn(share, "y", 1).astype(F32) + turn(share, "y", 3).astype(F32)
    share = (across + beside).astype(BF16)
    return (
        attended[None],
        query_grad[None],
        key_grad[None],
        value_grad[None],
        share[:, :width],
        share[:, width:],
    )


def solution(mesh):
    split = Mesh(mesh.devices.reshape(2, 4, 2, 4, 2, 2), CTX + RESP)
    rows = P(RESP, CTX, None)
    prompt = P(CTX, None)
    return jax.shard_map(
        body,
        mesh=split,
        in_specs=(rows, rows, rows, prompt, prompt, rows, P(RESP), P(RESP)),
        out_specs=(rows, rows, rows, rows, prompt, prompt),
        check_vma=False,
    )
```

```python
import math

import jax
import jax.numpy as jnp
from jax import lax
from jax.experimental import pallas as pl
from jax.experimental.pallas import tpu as pltpu
from jax.sharding import Mesh
from jax.sharding import PartitionSpec as P

HEADS = 16
KV_HEADS = 4
HEAD_DIM = 128
GROUP = HEADS // KV_HEADS
RESP_LEN = 2048
PROMPT_LEN = 1024
CTX = ("xh", "z")
LOCAL = ("xh", "z", "core")
RESP = ("y", "xl", "core")
ROWS = 128
PROWS = 64
BOTH = ROWS + PROWS
CHUNK = 512
KEYS = PROMPT_LEN + RESP_LEN
PROMPT_CHUNKS = PROMPT_LEN // CHUNK
CHUNKS = KEYS // CHUNK
HALF = GROUP * ROWS
LANES = 2 * HALF
SCALE = HEAD_DIM**-0.5
SCALE2 = SCALE * math.log2(math.e)
NEG = -1e30
F32 = jnp.float32
BF16 = jnp.bfloat16
VMEM = pl.BlockSpec(memory_space=pltpu.VMEM)
SMEM = pl.BlockSpec(memory_space=pltpu.SMEM)


def dot(a, b):
    return jnp.dot(a, b, preferred_element_type=F32)


def head_at(h, width=HEAD_DIM):
    return slice(h * width, (h + 1) * width)


def pack_kernel(info, q, do, k, v, kp, vp, qd0, qd1, qd2, qd3, kv0, kv1, kv2, kv3):
    mine = info[0]
    for d, (qd, kv) in enumerate(((qd0, kv0), (qd1, kv1), (qd2, kv2), (qd3, kv3))):
        at = pl.ds(pl.multiple_of((mine ^ d) * HALF, HALF), HALF)
        qd[:, :HALF] = q[:, at]
        qd[:, HALF:] = do[:, at]
        at = pl.ds(pl.multiple_of((mine ^ d) * HEAD_DIM, HEAD_DIM), HEAD_DIM)
        kv[:ROWS, :HEAD_DIM] = k[:, at]
        kv[:ROWS, HEAD_DIM:] = v[:, at]
        kv[ROWS:, :HEAD_DIM] = kp[:, at]
        kv[ROWS:, HEAD_DIM:] = vp[:, at]


def block_of(member, quad, core):
    return (member // 2) * 8 + ((quad * 2 + (member & 1) + core) & 7)


def attn_kernel(
    info,
    weight,
    qd0,
    qd1,
    qd2,
    qd3,
    kv0,
    kv1,
    kv2,
    kv3,
    kv_left,
    kv_right,
    kv_far0,
    kv_far1,
    od0,
    od1,
    od2,
    od3,
    dkv,
    k_s,
    v_s,
    kt_s,
    vt_s,
    score_s,
    prob_s,
    dk_s,
    dv_s,
    q_s,
    qt_s,
    upt_s,
    upl_s,
    uplt_s,
    acc_s,
):
    mine, quad, core, length, count = info[0], info[1], info[2], info[3], info[4]
    up_weight = weight[0]

    def load_block(kv, d, step):
        block = block_of(mine ^ d, (quad + step) & 3, core)
        at_p = pl.ds(pl.multiple_of(block * PROWS, PROWS), PROWS)
        at_r = pl.ds(pl.multiple_of(PROMPT_LEN + block * ROWS, ROWS), ROWS)
        k_s[at_r, :] = kv[:ROWS, :HEAD_DIM]
        v_s[at_r, :] = kv[:ROWS, HEAD_DIM:]
        k_s[at_p, :] = kv[ROWS:, :HEAD_DIM]
        v_s[at_p, :] = kv[ROWS:, HEAD_DIM:]

    for d, kv in enumerate((kv0, kv1, kv2, kv3)):
        load_block(kv, d, 0)
        load_block(kv_left.at[d], d, 3)
        load_block(kv_right.at[d], d, 1)
        load_block((kv_far0, kv_far1)[d // 2].at[d % 2], d, 2)

    def turn_chunk(c, carry):
        at = pl.ds(pl.multiple_of(c * CHUNK, CHUNK), CHUNK)
        kt_s[c] = k_s[at, :].T
        vt_s[c] = v_s[at, :].T
        dk_s[at, :] = jnp.zeros((CHUNK, HEAD_DIM), F32)
        dv_s[at, :] = jnp.zeros((CHUNK, HEAD_DIM), F32)
        return carry

    lax.fori_loop(0, CHUNKS, turn_chunk, 0)

    def tile(half, qds, ods):
        place0 = (quad * 2 + core) & 7
        place1 = (quad * 2 + core + 1) & 7
        lowest = half * 8 + jnp.minimum(place0, place1)
        highest = half * 8 + jnp.maximum(place0, place1)
        valids, rows = [], []
        for j in range(2):
            start = block_of(half * 2 + ((mine & 1) ^ j), quad, core) * ROWS
            row = start + lax.broadcasted_iota(jnp.int32, (1, ROWS), 1)
            row_weight = jnp.where(row < count, up_weight, 0.0)
            rows += [row] * GROUP
            valids += [jnp.where(row < length, 1.0, 0.0)] * GROUP
            for h in range(GROUP):
                cols = slice(j * HALF + h * HEAD_DIM, j * HALF + (h + 1) * HEAD_DIM)
                q_head = qds[j][:, head_at(h)]
                q_s[cols, :] = q_head
                qt_s[:, cols] = q_head.T
                grad = qds[j][:, HALF + h * HEAD_DIM : HALF + (h + 1) * HEAD_DIM]
                upt_s[:, cols] = (grad.T.astype(F32) * row_weight).astype(BF16)
        free = PROMPT_CHUNKS + lowest * ROWS // CHUNK
        steps = PROMPT_CHUNKS + highest * ROWS // CHUNK + 1

        def score_step(c, running):
            at = pl.ds(pl.multiple_of(c * CHUNK, CHUNK), CHUNK)
            score = dot(k_s[at, :], qt_s[...])
            score_s[at, :] = score
            return jnp.maximum(running, jnp.max(score.reshape(CHUNK // 8, 8, LANES), axis=0))

        def masked_step(c, running):
            at = pl.ds(pl.multiple_of(c * CHUNK, CHUNK), CHUNK)
            score = dot(k_s[at, :], qt_s[...])
            key_row = (c - PROMPT_CHUNKS) * CHUNK + lax.broadcasted_iota(
                jnp.int32, (CHUNK, LANES), 0
            )
            score = jnp.where(key_row <= query_row, score, NEG)
            score_s[at, :] = score
            return jnp.maximum(running, jnp.max(score.reshape(CHUNK // 8, 8, LANES), axis=0))

        query_row = jnp.concatenate(rows, axis=1)
        running = lax.fori_loop(0, free, score_step, jnp.full((8, LANES), NEG, F32))
        running = lax.fori_loop(free, steps, masked_step, running)
        shift = jnp.max(running, axis=0, keepdims=True) * SCALE2

        acc_s[...] = jnp.zeros_like(acc_s)

        def prob_step(c, total):
            at = pl.ds(pl.multiple_of(c * CHUNK, CHUNK), CHUNK)
            prob = jnp.exp2(score_s[at, :] * SCALE2 - shift)
            low = prob.astype(BF16)
            prob_s[at, :] = low
            acc_s[...] += dot(vt_s[c], low)
            return total + jnp.sum(prob.reshape(CHUNK // 8, 8, LANES), axis=0)

        total = lax.fori_loop(0, steps, prob_step, jnp.zeros((8, LANES), F32))
        inverse = 1.0 / jnp.sum(total, axis=0, keepdims=True)
        valid = jnp.concatenate(valids, axis=1)
        out_t = (acc_s[...] * (inverse * valid)).astype(BF16)
        up_low = (upt_s[...].astype(F32) * inverse).astype(BF16)
        uplt_s[...] = up_low
        delta = jnp.sum(up_low.astype(F32) * out_t.astype(F32), axis=0, keepdims=True)
        for j in range(2):
            for h in range(GROUP):
                cols = slice(j * HALF + h * HEAD_DIM, j * HALF + (h + 1) * HEAD_DIM)
                ods[j][:, head_at(h)] = out_t[:, cols].T
                upl_s[cols, :] = up_low[:, cols].T

        acc_s[...] = jnp.zeros_like(acc_s)

        def back_step(c, carry):
            at = pl.ds(pl.multiple_of(c * CHUNK, CHUNK), CHUNK)
            low = prob_s[at, :]
            prob_grad = dot(v_s[at, :], uplt_s[...])
            score_grad = (low.astype(F32) * (prob_grad - delta)).astype(BF16)
            dv_s[at, :] += dot(low, upl_s[...])
            dk_s[at, :] += dot(score_grad, q_s[...])
            acc_s[...] += dot(kt_s[c], score_grad)
            return carry

        lax.fori_loop(0, steps, back_step, 0)
        dq_t = (acc_s[...] * SCALE).astype(BF16)
        for j in range(2):
            for h in range(GROUP):
                cols = slice(j * HALF + h * HEAD_DIM, j * HALF + (h + 1) * HEAD_DIM)
                ods[j][:, HALF + h * HEAD_DIM : HALF + (h + 1) * HEAD_DIM] = dq_t[:, cols].T

    tile(mine // 2, (qd0, qd1), (od0, od1))
    tile(1 - mine // 2, (qd2, qd3), (od2, od3))

    def store_block(i, carry):
        at_p = pl.ds(pl.multiple_of(i * PROWS, PROWS), PROWS)
        at_r = pl.ds(pl.multiple_of(PROMPT_LEN + i * ROWS, ROWS), ROWS)
        dkv[i, :ROWS, :HEAD_DIM] = (dk_s[at_r, :] * SCALE).astype(BF16)
        dkv[i, :ROWS, HEAD_DIM:] = dv_s[at_r, :].astype(BF16)
        dkv[i, ROWS:, :HEAD_DIM] = (dk_s[at_p, :] * SCALE).astype(BF16)
        dkv[i, ROWS:, HEAD_DIM:] = dv_s[at_p, :].astype(BF16)
        return carry

    lax.fori_loop(0, 16, store_block, 0)


def unpack_kernel(info, od0, od1, od2, od3, attended, query_grad):
    mine = info[0]
    for d, od in enumerate((od0, od1, od2, od3)):
        at = pl.ds(pl.multiple_of((mine ^ d) * HALF, HALF), HALF)
        attended[:, at] = od[:, :HALF]
        query_grad[:, at] = od[:, HALF:]


def sum_kernel(info, dkv, key_grad, value_grad, share):
    core = info[2]
    for h in range(KV_HEADS):
        both = dkv[block_of(h, 0, core)].astype(F32)
        for quad in range(1, 4):
            both = both + dkv[block_of(h, quad, core)].astype(F32)
        both = both.astype(BF16)
        key_grad[:, head_at(h)] = both[:ROWS, :HEAD_DIM]
        value_grad[:, head_at(h)] = both[:ROWS, HEAD_DIM:]
        share[:, head_at(h)] = both[ROWS:, :HEAD_DIM]
        share[:, head_at(KV_HEADS + h)] = both[ROWS:, HEAD_DIM:]


def bf16(*shape):
    return jax.ShapeDtypeStruct(shape, BF16)


def attend(info, weight, *operands):
    return pl.pallas_call(
        attn_kernel,
        out_shape=(bf16(ROWS, LANES),) * 4 + (bf16(16, BOTH, 2 * HEAD_DIM),),
        in_specs=[SMEM, SMEM] + [VMEM] * len(operands),
        out_specs=(VMEM,) * 5,
        scratch_shapes=[
            pltpu.VMEM((KEYS, HEAD_DIM), BF16),
            pltpu.VMEM((KEYS, HEAD_DIM), BF16),
            pltpu.VMEM((CHUNKS, HEAD_DIM, CHUNK), BF16),
            pltpu.VMEM((CHUNKS, HEAD_DIM, CHUNK), BF16),
            pltpu.VMEM((KEYS, LANES), F32),
            pltpu.VMEM((KEYS, LANES), BF16),
            pltpu.VMEM((KEYS, HEAD_DIM), F32),
            pltpu.VMEM((KEYS, HEAD_DIM), F32),
            pltpu.VMEM((LANES, HEAD_DIM), BF16),
            pltpu.VMEM((HEAD_DIM, LANES), BF16),
            pltpu.VMEM((HEAD_DIM, LANES), BF16),
            pltpu.VMEM((LANES, HEAD_DIM), BF16),
            pltpu.VMEM((HEAD_DIM, LANES), BF16),
            pltpu.VMEM((HEAD_DIM, LANES), F32),
        ],
        compiler_params=pltpu.CompilerParams(vmem_limit_bytes=48 * 1024 * 1024),
        cost_estimate=pl.CostEstimate(
            flops=8_000_000_000, bytes_accessed=6_000_000, transcendentals=5_000_000
        ),
    )(info, weight, *operands)


def swap(x, axis):
    return lax.ppermute(x, axis, [(0, 1), (1, 0)])


def turn(x, axis, step):
    size = lax.axis_size(axis)
    return lax.ppermute(x, axis, [(i, (i + step) % size) for i in range(size)])


def local_permute(x, place):
    pairs = []
    for i in range(32):
        xh, z, core = i // 16, i // 2 % 8, i % 2
        xh, z = place(xh, (z - core) % 8)
        pairs.append((i, (xh * 8 + (z + core) % 8) * 2 + core))
    return lax.ppermute(x, LOCAL, pairs)


def partner(x, d):
    return local_permute(x, lambda xh, z: (xh ^ (d // 2), z ^ (d & 1)))


def quad_turn(x, step):
    return local_permute(x, lambda xh, z: (xh, (z + 2 * step) % 8))


def rounded(x):
    return lax.optimization_barrier(x.astype(BF16))


def body(q_resp, k_resp, v_resp, k_prompt, v_prompt, d_out, lengths, counts):
    core = lax.axis_index("core")
    z = (lax.axis_index("z") - core) & 7
    mine = lax.axis_index("xh") * 2 + (z & 1)
    info = jnp.stack([mine, z // 2, core, lengths[0], counts[0]]).astype(jnp.int32)
    weight = (RESP_LEN / counts[0].astype(F32)).reshape(1)
    packed = pl.pallas_call(
        pack_kernel,
        out_shape=(bf16(ROWS, LANES),) * 4 + (bf16(BOTH, 2 * HEAD_DIM),) * 4,
        in_specs=[SMEM] + [VMEM] * 6,
        out_specs=(VMEM,) * 8,
    )(info, q_resp[0], d_out[0], k_resp[0], v_resp[0], k_prompt, v_prompt)
    qd, kv = list(packed[:4]), list(packed[4:])
    for d in (3, 1, 2):
        kv[d] = partner(kv[d], d)
    for d in (3, 1, 2):
        qd[d] = partner(qd[d], d)
    own = jnp.stack(kv)
    left, right = quad_turn(own, 1), quad_turn(own, -1)
    far0, far1 = quad_turn(left[:2], 1), quad_turn(right[2:], -1)
    od = attend(info, weight, *qd, *kv, left, right, far0, far1)
    od, dkv = list(od[:4]), od[4]
    for d in (3, 1, 2):
        od[d] = partner(od[d], d)
    dkv = lax.all_to_all(dkv, CTX, 0, 0, tiled=True)
    dkv, *od = lax.optimization_barrier((dkv, *od))
    attended, query_grad = pl.pallas_call(
        unpack_kernel,
        out_shape=(bf16(ROWS, HEADS * HEAD_DIM),) * 2,
        in_specs=[SMEM] + [VMEM] * 4,
        out_specs=(VMEM,) * 2,
    )(info, *od)
    width = KV_HEADS * HEAD_DIM
    key_grad, value_grad, share = pl.pallas_call(
        sum_kernel,
        out_shape=(bf16(ROWS, width), bf16(ROWS, width), bf16(PROWS, 2 * width)),
        in_specs=[SMEM, VMEM],
        out_specs=(VMEM,) * 3,
    )(info, dkv)
    for axis in ("core", "xl"):
        share = rounded(share.astype(F32) + swap(share, axis).astype(F32))
    across = share.astype(F32) + turn(share, "y", 2).astype(F32)
    beside = turn(share, "y", 1).astype(F32) + turn(share, "y", 3).astype(F32)
    share = (across + beside).astype(BF16)
    return (
        attended[None],
        query_grad[None],
        key_grad[None],
        value_grad[None],
        share[:, :width],
        share[:, width:],
    )


def solution(mesh):
    split = Mesh(mesh.devices.reshape(2, 8, 4, 2, 2), CTX + RESP)
    rows = P(RESP, CTX, None)
    prompt = P(CTX, None)
    return jax.shard_map(
        body,
        mesh=split,
        in_specs=(rows, rows, rows, prompt, prompt, rows, P(RESP), P(RESP)),
        out_specs=(rows, rows, rows, rows, prompt, prompt),
        check_vma=False,
    )
```

```python
import math

import jax
import jax.numpy as jnp
from jax import lax
from jax.experimental import pallas as pl
from jax.experimental.pallas import tpu as pltpu
from jax.sharding import Mesh
from jax.sharding import PartitionSpec as P

HEADS = 16
KV_HEADS = 4
HEAD_DIM = 128
GROUP = HEADS // KV_HEADS
RESP_LEN = 2048
PROMPT_LEN = 1024
CTX = ("xh", "z")
LOCAL = ("xh", "z", "core")
RESP = ("y", "xl", "core")
ROWS = 128
PROWS = 64
BOTH = ROWS + PROWS
CHUNK = 256
SPAN = 3 * CHUNK
TILE_SPANS = (2 * CHUNK, 3 * CHUNK)
TILE_STARTS = (0, 2 * CHUNK)
PROBS = 5 * CHUNK
HALF = GROUP * ROWS
LANES = 2 * HALF
WIDE = 2 * HEAD_DIM
SCALE = HEAD_DIM**-0.5
SCALE2 = SCALE * math.log2(math.e)
NEG = -1e30
F32 = jnp.float32
BF16 = jnp.bfloat16
VMEM = pl.BlockSpec(memory_space=pltpu.VMEM)
SMEM = pl.BlockSpec(memory_space=pltpu.SMEM)


def dot(a, b):
    return jnp.dot(a, b, preferred_element_type=F32)


def head_at(h, width=HEAD_DIM):
    return slice(h * width, (h + 1) * width)


def lanes_at(j, h):
    return slice(j * HALF + h * HEAD_DIM, j * HALF + (h + 1) * HEAD_DIM)


def block_of(member, quad, core):
    return (member // 2) * 8 + ((quad * 2 + (member & 1) + core) & 7)


def pack_kernel(info, q, do, k, v, kp, vp, qd0, qd1, qd2, qd3, kv0, kv1, kv2, kv3):
    mine = info[0]
    for d, (qd, kv) in enumerate(((qd0, kv0), (qd1, kv1), (qd2, kv2), (qd3, kv3))):
        at = pl.ds(pl.multiple_of((mine ^ d) * HALF, HALF), HALF)
        qd[:, :HALF] = q[:, at]
        qd[:, HALF:] = do[:, at]
        at = pl.ds(pl.multiple_of((mine ^ d) * HEAD_DIM, HEAD_DIM), HEAD_DIM)
        kv[:ROWS, :HEAD_DIM] = k[:, at]
        kv[:ROWS, HEAD_DIM:] = v[:, at]
        kv[ROWS:, :HEAD_DIM] = kp[:, at]
        kv[ROWS:, HEAD_DIM:] = vp[:, at]


def rows_at(mine, d):
    return pl.ds(pl.multiple_of(CHUNK + (mine ^ d) // 2 * CHUNK + (d & 1) * ROWS, ROWS), ROWS)


def load_keys(mine, kvs, k_s, v_s):
    for d, kv in enumerate(kvs):
        k_s[rows_at(mine, d), :] = kv[:ROWS, :HEAD_DIM]
        v_s[rows_at(mine, d), :] = kv[:ROWS, HEAD_DIM:]
        k_s[head_at(d, PROWS), :] = kv[ROWS:, :HEAD_DIM]
        v_s[head_at(d, PROWS), :] = kv[ROWS:, HEAD_DIM:]


def query_rows(info, x):
    mine, quad, core = info[0], info[1], info[2]
    rows = []
    for j in range(2):
        start = block_of(x * 2 + ((mine & 1) ^ j), quad, core) * ROWS
        rows += [start + lax.broadcasted_iota(jnp.int32, (1, ROWS), 1)] * GROUP
    return jnp.concatenate(rows, axis=1)


def key_rows(info, x, quad):
    mine, core = info[0], info[2]
    rows = []
    for j in range(2):
        start = block_of(x * 2 + ((mine & 1) ^ j), quad, core) * ROWS
        rows.append(start + lax.broadcasted_iota(jnp.int32, (ROWS, 1), 0))
    return jnp.concatenate(rows, axis=0)


def fold(x, op):
    return op(x.reshape(x.shape[0] // 8, 8, LANES), axis=0)


def forward(info, quads, k_ss, v_ss, qt, before, score_s, probs, vt_s):
    for g in range(len(quads)):
        vt_s[:, g * SPAN : (g + 1) * SPAN] = v_ss[g][...].T
    after = []
    for x in range(2):
        place = query_rows(info, x)
        running = jnp.full((8, LANES), NEG, F32)
        for g, quad in enumerate(quads):
            for c in range(TILE_SPANS[x] // CHUNK):
                score = dot(k_ss[g][c * CHUNK : (c + 1) * CHUNK, :], qt[x])
                if c > 0:
                    score = jnp.where(key_rows(info, c - 1, quad) <= place, score, NEG)
                score_s[g * SPAN + c * CHUNK : g * SPAN + (c + 1) * CHUNK, :] = score
                running = jnp.maximum(running, fold(score, jnp.max))
        shift = jnp.max(running, axis=0, keepdims=True) * SCALE2
        if before is not None:
            shift = jnp.maximum(shift, before[0][x])
        total = jnp.zeros((8, LANES), F32)
        acc = None
        for g in range(len(quads)):
            start = TILE_STARTS[x]
            for c in range(TILE_SPANS[x] // CHUNK):
                score = score_s[g * SPAN + c * CHUNK : g * SPAN + (c + 1) * CHUNK, :]
                prob = jnp.exp2(score * SCALE2 - shift)
                total = total + fold(prob, jnp.sum)
                probs[g][start + c * CHUNK : start + (c + 1) * CHUNK, :] = prob.astype(BF16)
            part = dot(
                vt_s[:, g * SPAN : g * SPAN + TILE_SPANS[x]],
                probs[g][start : start + TILE_SPANS[x], :],
            )
            acc = part if acc is None else acc + part
        total = jnp.sum(total, axis=0, keepdims=True)
        if before is not None:
            factor = jnp.exp2(before[0][x] - shift)
            total = total + before[1][x] * factor
            acc = acc + before[2][x] * factor
        after.append((shift, total, acc))
    return after


def backward(mine, k_s, v_s, kt_s, q, uplt, upl, delta, probs, factors, grad_s, dqt, outs):
    kt_s[...] = k_s[...].T
    for c in range(3):
        at = slice(c * CHUNK, (c + 1) * CHUNK)
        dk, dv = None, None
        for x in range(2):
            if c * CHUNK >= TILE_SPANS[x]:
                continue
            here = slice(TILE_STARTS[x] + c * CHUNK, TILE_STARTS[x] + (c + 1) * CHUNK)
            low = probs[here, :]
            if factors is not None:
                low = (low.astype(F32) * factors[x]).astype(BF16)
            prob_grad = dot(v_s[at, :], uplt[x])
            grad = (low.astype(F32) * (prob_grad - delta[x])).astype(BF16)
            grad_s[here, :] = grad
            dv_part = dot(low, upl[x])
            dk_part = dot(grad, q[x])
            dv = dv_part if dv is None else dv + dv_part
            dk = dk_part if dk is None else dk + dk_part
        k_s[at, :] = (dk * SCALE).astype(BF16)
        v_s[at, :] = dv.astype(BF16)
    for x in range(2):
        part = dot(
            kt_s[:, : TILE_SPANS[x]], grad_s[TILE_STARTS[x] : TILE_STARTS[x] + TILE_SPANS[x], :]
        )
        dqt[x] = part if dqt[x] is None else dqt[x] + part
    for d, out in enumerate(outs):
        out[:ROWS, :HEAD_DIM] = k_s[rows_at(mine, d), :]
        out[:ROWS, HEAD_DIM:] = v_s[rows_at(mine, d), :]
        out[ROWS:, :HEAD_DIM] = k_s[head_at(d, PROWS), :]
        out[ROWS:, HEAD_DIM:] = v_s[head_at(d, PROWS), :]


def pieces(a, b):
    return a.at[0], a.at[1], b.at[0], b.at[1]


def first_kernel(
    info, weight, qd0, qd1, qd2, qd3, own_a, own_b,
    qt, q, upt, probs, shift, total, acc,
    k_s, v_s, vt_s, score_s,
):
    mine, quad, core, count = info[0], info[1], info[2], info[4]
    load_keys(mine, pieces(own_a, own_b), k_s, v_s)
    for d, qd in enumerate((qd0, qd1, qd2, qd3)):
        x = (mine ^ d) // 2
        row = block_of(mine ^ d, quad, core) * ROWS
        row = row + lax.broadcasted_iota(jnp.int32, (1, ROWS), 1)
        row_weight = jnp.where(row < count, weight[0], 0.0)
        for h in range(GROUP):
            cols = lanes_at(d & 1, h)
            q_head = qd[:, head_at(h)]
            q[x, cols, :] = q_head
            qt[x, :, cols] = q_head.T
            grad = qd[:, HALF + h * HEAD_DIM : HALF + (h + 1) * HEAD_DIM]
            upt[x, :, cols] = (grad.T.astype(F32) * row_weight).astype(BF16)
    after = forward(info, (quad,), (k_s,), (v_s,), qt, None, score_s, (probs,), vt_s)
    for x in range(2):
        shift[x], total[x], acc[x] = after[x]


def side_kernel(
    info, qt, left_a, left_b, right_a, right_b, shift0, total0, acc0,
    probs_l, probs_r, shift, total, acc,
    kl_s, vl_s, kr_s, vr_s, vt_s, score_s,
):
    mine, quad = info[0], info[1]
    load_keys(mine, pieces(left_a, left_b), kl_s, vl_s)
    load_keys(mine, pieces(right_a, right_b), kr_s, vr_s)
    quads = ((quad + 3) & 3, (quad + 1) & 3)
    before = (shift0, total0, acc0)
    after = forward(
        info, quads, (kl_s, kr_s), (vl_s, vr_s), qt, before, score_s, (probs_l, probs_r), vt_s
    )
    for x in range(2):
        shift[x], total[x], acc[x] = after[x]


def far_kernel(
    info, qt, q, upt, far_a, far_b, shift0, total0, acc0,
    shift, uplt, upl, delta, dqt, out_a, out_b, oa0, oa1, oa2, oa3,
    k_s, v_s, vt_s, kt_s, score_s, probs, grad_s, out_s,
):
    mine, quad, length = info[0], info[1], info[3]
    load_keys(mine, pieces(far_a, far_b), k_s, v_s)
    before = (shift0, total0, acc0)
    after = forward(
        info, ((quad + 2) & 3,), (k_s,), (v_s,), qt, before, score_s, (probs,), vt_s
    )
    for x in range(2):
        now, total, acc = after[x]
        shift[x] = now
        inverse = 1.0 / total
        valid = jnp.where(query_rows(info, x) < length, 1.0, 0.0)
        out_t = (acc * (inverse * valid)).astype(BF16)
        up_low = (upt[x].astype(F32) * inverse).astype(BF16)
        uplt[x] = up_low
        delta[x] = jnp.sum(up_low.astype(F32) * out_t.astype(F32), axis=0, keepdims=True)
        out_s[x] = out_t
        for j in range(2):
            for h in range(GROUP):
                upl[x, lanes_at(j, h), :] = up_low[:, lanes_at(j, h)].T
    for d, oa in enumerate((oa0, oa1, oa2, oa3)):
        for h in range(GROUP):
            oa[:, head_at(h)] = out_s[(mine ^ d) // 2, :, lanes_at(d & 1, h)].T
    grads = [None, None]
    backward(
        mine, k_s, v_s, kt_s, q, uplt, upl, delta, probs, None, grad_s, grads,
        pieces(out_a, out_b),
    )
    for x in range(2):
        dqt[x] = grads[x]


def back_side_kernel(
    info, q, uplt, upl, delta, shift_then, shift_last, probs_l, probs_r,
    left_a, left_b, right_a, right_b, dqt0,
    dqt, out_la, out_lb, out_ra, out_rb,
    k_s, v_s, kt_s, grad_s,
):
    mine = info[0]
    factors = [jnp.exp2(shift_then[x] - shift_last[x]) for x in range(2)]
    grads = [dqt0[0], dqt0[1]]
    for kvs, probs, outs in (
        (pieces(left_a, left_b), probs_l, pieces(out_la, out_lb)),
        (pieces(right_a, right_b), probs_r, pieces(out_ra, out_rb)),
    ):
        load_keys(mine, kvs, k_s, v_s)
        backward(
            mine, k_s, v_s, kt_s, q, uplt, upl, delta, probs, factors, grad_s, grads, outs
        )
    for x in range(2):
        dqt[x] = grads[x]


def back_own_kernel(
    info, q, uplt, upl, delta, shift_then, shift_last, probs, own_a, own_b, dqt0,
    out_a, out_b, dq0, dq1, dq2, dq3,
    k_s, v_s, kt_s, grad_s, dq_s,
):
    mine = info[0]
    factors = [jnp.exp2(shift_then[x] - shift_last[x]) for x in range(2)]
    grads = [dqt0[0], dqt0[1]]
    load_keys(mine, pieces(own_a, own_b), k_s, v_s)
    backward(
        mine, k_s, v_s, kt_s, q, uplt, upl, delta, probs, factors, grad_s, grads,
        pieces(out_a, out_b),
    )
    for x in range(2):
        dq_s[x] = (grads[x] * SCALE).astype(BF16)
    for d, dq in enumerate((dq0, dq1, dq2, dq3)):
        for h in range(GROUP):
            dq[:, head_at(h)] = dq_s[(mine ^ d) // 2, :, lanes_at(d & 1, h)].T


def place_kernel(info, o0, o1, o2, o3, whole):
    mine = info[0]
    for d, o in enumerate((o0, o1, o2, o3)):
        whole[:, pl.ds(pl.multiple_of((mine ^ d) * HALF, HALF), HALF)] = o[...]


def finish_kernel(info, g0, g1, g2, g3, key_grad, value_grad, share):
    mine = info[0]
    for d, g in enumerate((g0, g1, g2, g3)):
        at = pl.ds(pl.multiple_of((mine ^ d) * HEAD_DIM, HEAD_DIM), HEAD_DIM)
        key_grad[:, at] = g[:ROWS, :HEAD_DIM]
        value_grad[:, at] = g[:ROWS, HEAD_DIM:]
        share[:, at] = g[ROWS:, :HEAD_DIM]
        at = pl.ds(pl.multiple_of(KV_HEADS * HEAD_DIM + (mine ^ d) * HEAD_DIM, HEAD_DIM), HEAD_DIM)
        share[:, at] = g[ROWS:, HEAD_DIM:]


def sum_kernel(own, left, right, total):
    total[...] = (own[...].astype(F32) + left[...].astype(F32) + right[...].astype(F32)).astype(BF16)


def add_kernel(a, b, total):
    total[...] = (a[...].astype(F32) + b[...].astype(F32)).astype(BF16)


def bf16(*shape):
    return jax.ShapeDtypeStruct(shape, BF16)


def f32(*shape):
    return jax.ShapeDtypeStruct(shape, F32)


def call(kernel, outs, scratch, scalars, *operands, products=0):
    return pl.pallas_call(
        kernel,
        out_shape=tuple(outs),
        in_specs=[SMEM] * len(scalars) + [VMEM] * len(operands),
        out_specs=(VMEM,) * len(outs),
        scratch_shapes=[pltpu.VMEM(shape, dtype) for shape, dtype in scratch],
        compiler_params=pltpu.CompilerParams(vmem_limit_bytes=32 * 1024 * 1024),
        cost_estimate=pl.CostEstimate(
            flops=products * PROBS * LANES * HEAD_DIM * 4,
            bytes_accessed=1_000_000,
            transcendentals=0,
        ),
    )(*scalars, *operands)


def swap(x, axis):
    return lax.ppermute(x, axis, [(0, 1), (1, 0)])


def turn(x, axis, step):
    size = lax.axis_size(axis)
    return lax.ppermute(x, axis, [(i, (i + step) % size) for i in range(size)])


def local_permute(x, place):
    pairs = []
    for i in range(32):
        xh, z, core = i // 16, i // 2 % 8, i % 2
        xh, z = place(xh, (z - core) % 8)
        pairs.append((i, (xh * 8 + (z + core) % 8) * 2 + core))
    return lax.ppermute(x, LOCAL, pairs)


def partner(x, d):
    return local_permute(x, lambda xh, z: (xh ^ (d // 2), z ^ (d & 1)))


def quad_turn(x, step):
    return local_permute(x, lambda xh, z: (xh, (z + 2 * step) % 8))


def rounded(x):
    return lax.optimization_barrier(x.astype(BF16))


def body(q_resp, k_resp, v_resp, k_prompt, v_prompt, d_out, lengths, counts):
    core = lax.axis_index("core")
    z = (lax.axis_index("z") - core) & 7
    mine = lax.axis_index("xh") * 2 + (z & 1)
    info = jnp.stack([mine, z // 2, core, lengths[0], counts[0]]).astype(jnp.int32)
    weight = (RESP_LEN / counts[0].astype(F32)).reshape(1)
    packed = call(
        pack_kernel,
        (bf16(ROWS, LANES),) * 4 + (bf16(BOTH, WIDE),) * 4,
        (),
        (info,),
        q_resp[0], d_out[0], k_resp[0], v_resp[0], k_prompt, v_prompt,
    )
    qd, kv = list(packed[:4]), list(packed[4:])
    for d in (1, 2, 3):
        kv[d] = partner(kv[d], d)
    for d in (1, 2, 3):
        qd[d] = partner(qd[d], d)
    own_a, own_b = jnp.stack(kv[:2]), jnp.stack(kv[2:])
    left_a, right_b = quad_turn(own_a, 1), quad_turn(own_b, -1)
    left_b, right_a = quad_turn(own_b, 1), quad_turn(own_a, -1)
    far_a, far_b = quad_turn(left_a, 1), quad_turn(right_b, -1)

    tiles = (2, HEAD_DIM, LANES)
    line = f32(2, 1, LANES)
    keys = [((SPAN, HEAD_DIM), BF16)] * 2
    turned = ((HEAD_DIM, SPAN), BF16)
    probs_s = ((PROBS, LANES), BF16)
    piece = bf16(2, BOTH, WIDE)
    qt, q, upt, probs1, shift1, total1, acc1 = call(
        first_kernel,
        (bf16(*tiles), bf16(2, LANES, HEAD_DIM), bf16(*tiles), bf16(PROBS, LANES), line, line, f32(*tiles)),
        keys + [turned, ((SPAN, LANES), F32)],
        (info, weight),
        *qd, own_a, own_b,
        products=2,
    )
    probs_l, probs_r, shift2, total2, acc2 = call(
        side_kernel,
        (bf16(PROBS, LANES), bf16(PROBS, LANES), line, line, f32(*tiles)),
        keys + keys + [((HEAD_DIM, 2 * SPAN), BF16), ((2 * SPAN, LANES), F32)],
        (info,),
        qt, left_a, left_b, right_a, right_b, shift1, total1, acc1,
        products=4,
    )
    shift3, uplt, upl, delta, dqt, far_ga, far_gb, *attn = call(
        far_kernel,
        (line, bf16(*tiles), bf16(2, LANES, HEAD_DIM), line, f32(*tiles), piece, piece)
        + (bf16(ROWS, HALF),) * 4,
        keys + [turned, turned, ((SPAN, LANES), F32), probs_s, probs_s, (tiles, BF16)],
        (info,),
        qt, q, upt, far_a, far_b, shift2, total2, acc2,
        products=6,
    )
    far_ga, far_gb = quad_turn(far_ga, 1), quad_turn(far_gb, -1)
    for d in (1, 2, 3):
        attn[d] = partner(attn[d], d)
    dqt, left_ga, left_gb, right_ga, right_gb = call(
        back_side_kernel,
        (f32(*tiles), piece, piece, piece, piece),
        keys + [turned, probs_s],
        (info,),
        q, uplt, upl, delta, shift2, shift3, probs_l, probs_r,
        left_a, left_b, right_a, right_b, dqt,
        products=8,
    )
    (right_ga,) = call(add_kernel, (piece,), (), (), right_ga, far_ga)
    (left_gb,) = call(add_kernel, (piece,), (), (), left_gb, far_gb)
    right_gb, left_ga = quad_turn(right_gb, 1), quad_turn(left_ga, -1)
    right_ga, left_gb = quad_turn(right_ga, 1), quad_turn(left_gb, -1)
    own_ga, own_gb, *dq = call(
        back_own_kernel,
        (piece, piece) + (bf16(ROWS, HALF),) * 4,
        keys + [turned, probs_s, (tiles, BF16)],
        (info,),
        q, uplt, upl, delta, shift1, shift3, probs1, own_a, own_b, dqt,
        products=4,
    )
    for d in (1, 2, 3):
        dq[d] = partner(dq[d], d)
    left_ga, right_ga, *attn = lax.optimization_barrier((left_ga, right_ga, *attn))
    (own_ga,) = call(sum_kernel, (piece,), (), (), own_ga, left_ga, right_ga)
    (own_gb,) = call(sum_kernel, (piece,), (), (), own_gb, left_gb, right_gb)
    grads = [own_ga[0], own_ga[1], own_gb[0], own_gb[1]]
    for d in (1, 2, 3):
        grads[d] = partner(grads[d], d)
    tied = lax.optimization_barrier((*grads, *dq))
    grads, dq = tied[:4], tied[4:]
    width = KV_HEADS * HEAD_DIM
    rows = bf16(ROWS, HEADS * HEAD_DIM)
    (attended,) = call(place_kernel, (rows,), (), (info,), *attn)
    (query_grad,) = call(place_kernel, (rows,), (), (info,), *dq)
    key_grad, value_grad, share = call(
        finish_kernel,
        (bf16(ROWS, width), bf16(ROWS, width), bf16(PROWS, 2 * width)),
        (),
        (info,),
        *grads,
    )
    for axis in ("core", "xl"):
        share = rounded(share.astype(F32) + swap(share, axis).astype(F32))
    across = share.astype(F32) + turn(share, "y", 2).astype(F32)
    beside = turn(share, "y", 1).astype(F32) + turn(share, "y", 3).astype(F32)
    share = (across + beside).astype(BF16)
    return (
        attended[None],
        query_grad[None],
        key_grad[None],
        value_grad[None],
        share[:, :width],
        share[:, width:],
    )


def solution(mesh):
    split = Mesh(mesh.devices.reshape(2, 8, 4, 2, 2), CTX + RESP)
    rows = P(RESP, CTX, None)
    prompt = P(CTX, None)
    return jax.shard_map(
        body,
        mesh=split,
        in_specs=(rows, rows, rows, prompt, prompt, rows, P(RESP), P(RESP)),
        out_specs=(rows, rows, rows, rows, prompt, prompt),
        check_vma=False,
    )
```

```python
import math

import jax
import jax.numpy as jnp
from jax import lax
from jax.experimental import pallas as pl
from jax.experimental.pallas import tpu as pltpu
from jax.sharding import Mesh
from jax.sharding import PartitionSpec as P

HEADS = 16
KV_HEADS = 4
HEAD_DIM = 128
GROUP = HEADS // KV_HEADS
RESP_LEN = 2048
PROMPT_LEN = 1024
CTX = ("xh", "z")
LOCAL = ("xh", "z", "core")
RESP = ("y", "xl", "core")
ROWS = 128
PROWS = 64
BOTH = ROWS + PROWS
CHUNK = 256
SPAN = 3 * CHUNK
TILE_SPANS = (2 * CHUNK, 3 * CHUNK)
TILE_STARTS = (0, 2 * CHUNK)
PROBS = 5 * CHUNK
HALF = GROUP * ROWS
LANES = 2 * HALF
WIDE = 2 * HEAD_DIM
SCALE = HEAD_DIM**-0.5
SCALE2 = SCALE * math.log2(math.e)
NEG = -1e30
F32 = jnp.float32
BF16 = jnp.bfloat16
VMEM = pl.BlockSpec(memory_space=pltpu.VMEM)
SMEM = pl.BlockSpec(memory_space=pltpu.SMEM)


def dot(a, b):
    return jnp.dot(a, b, preferred_element_type=F32)


def head_at(h, width=HEAD_DIM):
    return slice(h * width, (h + 1) * width)


def lanes_at(j, h):
    return slice(j * HALF + h * HEAD_DIM, j * HALF + (h + 1) * HEAD_DIM)


def block_of(member, quad, core):
    return (member // 2) * 8 + ((quad * 2 + (member & 1) + core) & 7)


def pack_kv_kernel(info, k, v, kp, vp, kv0, kv1, kv2, kv3):
    mine = info[0]
    for d, kv in enumerate((kv0, kv1, kv2, kv3)):
        at = pl.ds(pl.multiple_of((mine ^ d) * HEAD_DIM, HEAD_DIM), HEAD_DIM)
        kv[:ROWS, :HEAD_DIM] = k[:, at]
        kv[:ROWS, HEAD_DIM:] = v[:, at]
        kv[ROWS:, :HEAD_DIM] = kp[:, at]
        kv[ROWS:, HEAD_DIM:] = vp[:, at]


def pack_qd_kernel(info, q, do, qd0, qd1, qd2, qd3):
    mine = info[0]
    for d, qd in enumerate((qd0, qd1, qd2, qd3)):
        at = pl.ds(pl.multiple_of((mine ^ d) * HALF, HALF), HALF)
        qd[:, :HALF] = q[:, at]
        qd[:, HALF:] = do[:, at]


def rows_at(mine, d):
    return pl.ds(pl.multiple_of(CHUNK + (mine ^ d) // 2 * CHUNK + (d & 1) * ROWS, ROWS), ROWS)


def load_keys(mine, g, kvs, k_s, v_s):
    for d, kv in enumerate(kvs):
        k_s[g, rows_at(mine, d), :] = kv[:ROWS, :HEAD_DIM]
        v_s[g, rows_at(mine, d), :] = kv[:ROWS, HEAD_DIM:]
        k_s[g, head_at(d, PROWS), :] = kv[ROWS:, :HEAD_DIM]
        v_s[g, head_at(d, PROWS), :] = kv[ROWS:, HEAD_DIM:]


def query_rows(info, x):
    mine, quad, core = info[0], info[1], info[2]
    rows = []
    for j in range(2):
        start = block_of(x * 2 + ((mine & 1) ^ j), quad, core) * ROWS
        rows += [start + lax.broadcasted_iota(jnp.int32, (1, ROWS), 1)] * GROUP
    return jnp.concatenate(rows, axis=1)


def key_rows(info, x, quad):
    mine, core = info[0], info[2]
    rows = []
    for j in range(2):
        start = block_of(x * 2 + ((mine & 1) ^ j), quad, core) * ROWS
        rows.append(start + lax.broadcasted_iota(jnp.int32, (ROWS, 1), 0))
    return jnp.concatenate(rows, axis=0)


def fold(x, op):
    return op(x.reshape(x.shape[0] // 8, 8, LANES), axis=0)


def each(count, step, carry):
    return step(0, carry) if count == 1 else lax.fori_loop(0, count, step, carry)


def forward(info, quads, count, k_s, v_s, qt, before, score_s, probs, vt_s, shift, total, acc):
    def turn_values(g, carry):
        vt_s[g] = v_s[g].T
        return carry

    each(count, turn_values, 0)
    for x in range(2):
        place = query_rows(info, x)
        start, span = TILE_STARTS[x], TILE_SPANS[x]

        def score_step(g, running):
            for c in range(span // CHUNK):
                at = slice(c * CHUNK, (c + 1) * CHUNK)
                score = dot(k_s[g, at, :], qt[x])
                if c > 0:
                    score = jnp.where(key_rows(info, c - 1, quads(g)) <= place, score, NEG)
                score_s[g, at, :] = score
                running = jnp.maximum(running, fold(score, jnp.max))
            return running

        running = each(count, score_step, jnp.full((8, LANES), NEG, F32))
        now = jnp.max(running, axis=0, keepdims=True) * SCALE2
        if before is not None:
            now = jnp.maximum(now, before[0][x])
            factor = jnp.exp2(before[0][x] - now)
            acc[x] = before[2][x] * factor

        def prob_step(g, running):
            for c in range(span // CHUNK):
                prob = jnp.exp2(score_s[g, c * CHUNK : (c + 1) * CHUNK, :] * SCALE2 - now)
                running = running + fold(prob, jnp.sum)
                probs[g, start + c * CHUNK : start + (c + 1) * CHUNK, :] = prob.astype(BF16)
            part = dot(vt_s[g, :, :span], probs[g, start : start + span, :])
            if before is None:
                acc[x] = part
            else:
                acc[x] += part
            return running

        running = each(count, prob_step, jnp.zeros((8, LANES), F32))
        sums = jnp.sum(running, axis=0, keepdims=True)
        if before is not None:
            sums = sums + before[1][x] * factor
        shift[x], total[x] = now, sums


def backward(count, k_s, v_s, kt_s, q, uplt, upl, delta, probs, factors, grad_s, before, dqt):
    for x in range(2):
        dqt[x] = jnp.zeros((HEAD_DIM, LANES), F32) if before is None else before[x]

    def step(g, carry):
        kt_s[...] = k_s[g].T
        for c in range(3):
            at = slice(c * CHUNK, (c + 1) * CHUNK)
            dk, dv = None, None
            for x in range(2):
                if c * CHUNK >= TILE_SPANS[x]:
                    continue
                here = slice(TILE_STARTS[x] + c * CHUNK, TILE_STARTS[x] + (c + 1) * CHUNK)
                low = probs[g, here, :]
                if factors is not None:
                    low = (low.astype(F32) * factors[x]).astype(BF16)
                prob_grad = dot(v_s[g, at, :], uplt[x])
                grad = (low.astype(F32) * (prob_grad - delta[x])).astype(BF16)
                grad_s[here, :] = grad
                dv_part = dot(low, upl[x])
                dk_part = dot(grad, q[x])
                dv = dv_part if dv is None else dv + dv_part
                dk = dk_part if dk is None else dk + dk_part
            k_s[g, at, :] = (dk * SCALE).astype(BF16)
            v_s[g, at, :] = dv.astype(BF16)
        for x in range(2):
            start, span = TILE_STARTS[x], TILE_SPANS[x]
            dqt[x] += dot(kt_s[:, :span], grad_s[start : start + span, :])
        return carry

    each(count, step, 0)


def store_grads(mine, g, k_s, v_s, resp, prompt):
    for d in range(4):
        resp[d][:, :HEAD_DIM] = k_s[g, rows_at(mine, d), :]
        resp[d][:, HEAD_DIM:] = v_s[g, rows_at(mine, d), :]
        prompt[d][:, :HEAD_DIM] = k_s[g, head_at(d, PROWS), :]
        prompt[d][:, HEAD_DIM:] = v_s[g, head_at(d, PROWS), :]


def pieces(*parts):
    return [part.at[d] for part in parts for d in range(part.shape[0])]


def first_kernel(
    info, weight, qd0, qd1, qd2, qd3, own,
    qt, q, upt, probs, shift, total, acc,
    k_s, v_s, vt_s, score_s,
):
    mine, quad, core, count = info[0], info[1], info[2], info[4]
    load_keys(mine, 0, pieces(own), k_s, v_s)
    for d, qd in enumerate((qd0, qd1, qd2, qd3)):
        x = (mine ^ d) // 2
        row = block_of(mine ^ d, quad, core) * ROWS
        row = row + lax.broadcasted_iota(jnp.int32, (1, ROWS), 1)
        row_weight = jnp.where(row < count, weight[0], 0.0)
        for h in range(GROUP):
            cols = lanes_at(d & 1, h)
            q_head = qd[:, head_at(h)]
            q[x, cols, :] = q_head
            qt[x, :, cols] = q_head.T
            grad = qd[:, HALF + h * HEAD_DIM : HALF + (h + 1) * HEAD_DIM]
            upt[x, :, cols] = (grad.T.astype(F32) * row_weight).astype(BF16)
    forward(
        info, lambda g: quad, 1, k_s, v_s, qt, None, score_s, probs, vt_s, shift, total, acc
    )


def side_kernel(
    info, qt, left, right, shift0, total0, acc0,
    probs, shift, total, acc,
    k_s, v_s, vt_s, score_s,
):
    mine, quad = info[0], info[1]
    load_keys(mine, 0, pieces(left), k_s, v_s)
    load_keys(mine, 1, pieces(right), k_s, v_s)
    forward(
        info, lambda g: (quad + 3 + 2 * g) & 3, 2, k_s, v_s, qt, (shift0, total0, acc0),
        score_s, probs, vt_s, shift, total, acc,
    )


def far_kernel(
    info, qt, q, upt, far_a, far_b, shift0, total0, acc0,
    shift, uplt, upl, delta, dqt, attn, out_a, out_b,
    k_s, v_s, vt_s, kt_s, score_s, probs, grad_s, acc, total,
):
    mine, quad, length = info[0], info[1], info[3]
    load_keys(mine, 0, pieces(far_a, far_b), k_s, v_s)
    forward(
        info, lambda g: (quad + 2) & 3, 1, k_s, v_s, qt, (shift0, total0, acc0),
        score_s, probs, vt_s, shift, total, acc,
    )
    for x in range(2):
        inverse = 1.0 / total[x]
        valid = jnp.where(query_rows(info, x) < length, 1.0, 0.0)
        out_t = (acc[x] * (inverse * valid)).astype(BF16)
        up_low = (upt[x].astype(F32) * inverse).astype(BF16)
        uplt[x] = up_low
        delta[x] = jnp.sum(up_low.astype(F32) * out_t.astype(F32), axis=0, keepdims=True)
        attn[x] = out_t
        for j in range(2):
            for h in range(GROUP):
                upl[x, lanes_at(j, h), :] = up_low[:, lanes_at(j, h)].T
    backward(
        1, k_s, v_s, kt_s, q, uplt, upl, delta, probs, None, grad_s, None, dqt
    )
    outs = pieces(out_a, out_b)
    store_grads(
        mine, 0, k_s, v_s, [out.at[:ROWS] for out in outs], [out.at[ROWS:] for out in outs]
    )


def back_side_kernel(
    info, q, uplt, upl, delta, shift_then, shift_last, probs,
    left, right, dqt0,
    dqt, resp_l, prompt_l, resp_r, prompt_r,
    k_s, v_s, kt_s, grad_s,
):
    mine = info[0]
    factors = [jnp.exp2(shift_then[x] - shift_last[x]) for x in range(2)]
    load_keys(mine, 0, pieces(left), k_s, v_s)
    load_keys(mine, 1, pieces(right), k_s, v_s)
    backward(
        2, k_s, v_s, kt_s, q, uplt, upl, delta, probs, factors, grad_s, dqt0, dqt
    )
    store_grads(mine, 0, k_s, v_s, pieces(resp_l), pieces(prompt_l))
    store_grads(mine, 1, k_s, v_s, pieces(resp_r), pieces(prompt_r))


def back_own_kernel(
    info, q, uplt, upl, delta, shift_then, shift_last, probs, own, dqt0, attn,
    resp, prompt, od0, od1, od2, od3,
    k_s, v_s, kt_s, grad_s, dqt, dq_s,
):
    mine = info[0]
    factors = [jnp.exp2(shift_then[x] - shift_last[x]) for x in range(2)]
    load_keys(mine, 0, pieces(own), k_s, v_s)
    backward(
        1, k_s, v_s, kt_s, q, uplt, upl, delta, probs, factors, grad_s, dqt0, dqt
    )
    store_grads(mine, 0, k_s, v_s, pieces(resp), pieces(prompt))
    for x in range(2):
        dq_s[x] = (dqt[x] * SCALE).astype(BF16)
    for d, od in enumerate((od0, od1, od2, od3)):
        x = (mine ^ d) // 2
        for h in range(GROUP):
            od[:, head_at(h)] = attn[x, :, lanes_at(d & 1, h)].T
            od[:, HALF + h * HEAD_DIM : HALF + (h + 1) * HEAD_DIM] = dq_s[
                x, :, lanes_at(d & 1, h)
            ].T


def unpack_kernel(info, od0, od1, od2, od3, attended, query_grad):
    mine = info[0]
    for d, od in enumerate((od0, od1, od2, od3)):
        at = pl.ds(pl.multiple_of((mine ^ d) * HALF, HALF), HALF)
        attended[:, at] = od[:, :HALF]
        query_grad[:, at] = od[:, HALF:]


def place_kernel(info, g0, g1, g2, g3, keys, values):
    mine = info[0]
    for d, g in enumerate((g0, g1, g2, g3)):
        at = pl.ds(pl.multiple_of((mine ^ d) * HEAD_DIM, HEAD_DIM), HEAD_DIM)
        keys[:, at] = g[:, :HEAD_DIM]
        values[:, at] = g[:, HEAD_DIM:]


def both(a, b):
    return (a.astype(F32) + b.astype(F32)).astype(BF16)


def add_kernel(
    resp_l, prompt_l, resp_r, prompt_r, far_a, far_b,
    out_pl, out_pr, out_l0, out_l1, out_r0, out_r1,
):
    out_pr[:2] = both(prompt_r[:2], far_a[:, ROWS:])
    out_pr[2:] = prompt_r[2:]
    out_pl[:2] = prompt_l[:2]
    out_pl[2:] = both(prompt_l[2:], far_b[:, ROWS:])
    out_r0[...] = both(resp_r[:2], far_a[:, :ROWS])
    out_r1[...] = resp_r[2:]
    out_l0[...] = resp_l[:2]
    out_l1[...] = both(resp_l[2:], far_b[:, :ROWS])


def sum_three(own, left, right):
    return (own.astype(F32) + left.astype(F32) + right.astype(F32)).astype(BF16)


def sum_prompt_kernel(own, left, right, *outs):
    for d, out in enumerate(outs):
        out[...] = sum_three(own[d], left[d], right[d])


def sum_resp_kernel(own, left0, left1, right0, right1, *outs):
    for d, out in enumerate(outs):
        left, right = ((left0, right0), (left1, right1))[d // 2]
        out[...] = sum_three(own[d], left[d % 2], right[d % 2])


def bf16(*shape):
    return jax.ShapeDtypeStruct(shape, BF16)


def f32(*shape):
    return jax.ShapeDtypeStruct(shape, F32)


def call(kernel, outs, scratch, scalars, *operands):
    return pl.pallas_call(
        kernel,
        out_shape=tuple(outs),
        in_specs=[SMEM] * len(scalars) + [VMEM] * len(operands),
        out_specs=(VMEM,) * len(outs),
        scratch_shapes=[pltpu.VMEM(shape, dtype) for shape, dtype in scratch],
        compiler_params=pltpu.CompilerParams(vmem_limit_bytes=32 * 1024 * 1024),
        cost_estimate=pl.CostEstimate(flops=0, bytes_accessed=0, transcendentals=0),
    )(*scalars, *operands)


def swap(x, axis):
    return lax.ppermute(x, axis, [(0, 1), (1, 0)])


def turn(x, axis, step):
    size = lax.axis_size(axis)
    return lax.ppermute(x, axis, [(i, (i + step) % size) for i in range(size)])


def local_permute(x, place):
    pairs = []
    for i in range(32):
        xh, z, core = i // 16, i // 2 % 8, i % 2
        xh, z = place(xh, (z - core) % 8)
        pairs.append((i, (xh * 8 + (z + core) % 8) * 2 + core))
    return lax.ppermute(x, LOCAL, pairs)


def partner(x, d):
    return local_permute(x, lambda xh, z: (xh ^ (d // 2), z ^ (d & 1)))


def quad_turn(x, step):
    return local_permute(x, lambda xh, z: (xh, (z + 2 * step) % 8))


def rounded(x):
    return lax.optimization_barrier(x.astype(BF16))


def body(q_resp, k_resp, v_resp, k_prompt, v_prompt, d_out, lengths, counts):
    core = lax.axis_index("core")
    z = (lax.axis_index("z") - core) & 7
    mine = lax.axis_index("xh") * 2 + (z & 1)
    info = jnp.stack([mine, z // 2, core, lengths[0], counts[0]]).astype(jnp.int32)
    weight = (RESP_LEN / counts[0].astype(F32)).reshape(1)
    kv = list(
        call(
            pack_kv_kernel,
            (bf16(BOTH, WIDE),) * 4,
            (),
            (info,),
            k_resp[0], v_resp[0], k_prompt, v_prompt,
        )
    )
    qd = list(call(pack_qd_kernel, (bf16(ROWS, LANES),) * 4, (), (info,), q_resp[0], d_out[0]))
    for d in (1, 2, 3):
        kv[d] = partner(kv[d], d)
    tied = lax.optimization_barrier((*kv, *qd))
    kv, qd = list(tied[:4]), list(tied[4:])
    own = jnp.stack(kv)
    left, right = quad_turn(own, 1), quad_turn(own, -1)
    for d in (1, 2, 3):
        qd[d] = partner(qd[d], d)
    far_a, far_b = quad_turn(left[:2], 1), quad_turn(right[2:], -1)

    tiles = (2, HEAD_DIM, LANES)
    line = f32(2, 1, LANES)

    def keys(count):
        return [((count, SPAN, HEAD_DIM), BF16)] * 2

    def forward_scratch(count):
        return keys(count) + [((count, HEAD_DIM, SPAN), BF16), ((count, SPAN, LANES), F32)]

    turned = ((HEAD_DIM, SPAN), BF16)
    grad_s = ((PROBS, LANES), BF16)
    resp, prompt = bf16(4, ROWS, WIDE), bf16(4, PROWS, WIDE)
    pair, half = bf16(2, BOTH, WIDE), bf16(2, ROWS, WIDE)
    qt, q, upt, probs1, shift1, total1, acc1 = call(
        first_kernel,
        (bf16(*tiles), bf16(2, LANES, HEAD_DIM), bf16(*tiles), bf16(1, PROBS, LANES), line, line, f32(*tiles)),
        forward_scratch(1),
        (info, weight),
        *qd, own,
    )
    probs2, shift2, total2, acc2 = call(
        side_kernel,
        (bf16(2, PROBS, LANES), line, line, f32(*tiles)),
        forward_scratch(2),
        (info,),
        qt, left, right, shift1, total1, acc1,
    )
    shift3, uplt, upl, delta, dqt, attn, far_ga, far_gb = call(
        far_kernel,
        (line, bf16(*tiles), bf16(2, LANES, HEAD_DIM), line, f32(*tiles), bf16(*tiles), pair, pair),
        keys(1) + [((1, HEAD_DIM, SPAN), BF16), turned, ((1, SPAN, LANES), F32)]
        + [((1, PROBS, LANES), BF16), grad_s, (tiles, F32), ((2, 1, LANES), F32)],
        (info,),
        qt, q, upt, far_a, far_b, shift2, total2, acc2,
    )
    far_ga, far_gb = quad_turn(far_ga, 1), quad_turn(far_gb, -1)
    dqt, *side = call(
        back_side_kernel,
        (f32(*tiles), resp, prompt, resp, prompt),
        keys(2) + [turned, grad_s],
        (info,),
        q, uplt, upl, delta, shift2, shift3, probs2,
        left, right, dqt,
    )
    prompt_l, prompt_r, left0, left1, right0, right1 = call(
        add_kernel, (prompt, prompt) + (half,) * 4, (), (), *side, far_ga, far_gb
    )
    prompt_l, prompt_r = quad_turn(prompt_l, -1), quad_turn(prompt_r, 1)
    left0, right0 = quad_turn(left0, -1), quad_turn(right0, 1)
    left1, right1 = quad_turn(left1, -1), quad_turn(right1, 1)
    resp_o, prompt_o, *od = call(
        back_own_kernel,
        (resp, prompt) + (bf16(ROWS, LANES),) * 4,
        keys(1) + [turned, grad_s, (tiles, F32), (tiles, BF16)],
        (info,),
        q, uplt, upl, delta, shift1, shift3, probs1, own, dqt, attn,
    )
    for d in (1, 2, 3):
        od[d] = partner(od[d], d)
    prompt_l, prompt_r, left0, right0 = lax.optimization_barrier(
        (prompt_l, prompt_r, left0, right0)
    )
    share = list(
        call(sum_prompt_kernel, (bf16(PROWS, WIDE),) * 4, (), (), prompt_o, prompt_l, prompt_r)
    )
    for d in (1, 2, 3):
        share[d] = partner(share[d], d)
    width = KV_HEADS * HEAD_DIM
    rows = bf16(ROWS, HEADS * HEAD_DIM)
    key_share, value_share = call(
        place_kernel, (bf16(PROWS, width),) * 2, (), (info,), *share
    )
    share = jnp.concatenate([key_share, value_share], axis=1)
    share, left1, right1 = lax.optimization_barrier((share, left1, right1))
    share = rounded(share.astype(F32) + swap(share, "core").astype(F32))
    grads = list(
        call(
            sum_resp_kernel, (bf16(ROWS, WIDE),) * 4, (), (),
            resp_o, left0, left1, right0, right1,
        )
    )
    for d in (1, 2, 3):
        grads[d] = partner(grads[d], d)
    share = rounded(share.astype(F32) + swap(share, "xl").astype(F32))
    share, *od = lax.optimization_barrier((share, *od))
    across = share.astype(F32) + turn(share, "y", 2).astype(F32)
    beside = turn(share, "y", 1).astype(F32) + turn(share, "y", 3).astype(F32)
    share = (across + beside).astype(BF16)
    attended, query_grad = call(unpack_kernel, (rows, rows), (), (info,), *od)
    key_grad, value_grad = call(
        place_kernel, (bf16(ROWS, width),) * 2, (), (info,), *grads
    )
    return (
        attended[None],
        query_grad[None],
        key_grad[None],
        value_grad[None],
        share[:, :width],
        share[:, width:],
    )


def solution(mesh):
    split = Mesh(mesh.devices.reshape(2, 8, 4, 2, 2), CTX + RESP)
    rows = P(RESP, CTX, None)
    prompt = P(CTX, None)
    return jax.shard_map(
        body,
        mesh=split,
        in_specs=(rows, rows, rows, prompt, prompt, rows, P(RESP), P(RESP)),
        out_specs=(rows, rows, rows, rows, prompt, prompt),
        check_vma=False,
    )
```

```python
import math

import jax
import jax.numpy as jnp
from jax import lax
from jax.experimental import pallas as pl
from jax.experimental.pallas import tpu as pltpu
from jax.sharding import Mesh
from jax.sharding import PartitionSpec as P

HEADS = 16
KV_HEADS = 4
HEAD_DIM = 128
GROUP = HEADS // KV_HEADS
RESP_LEN = 2048
PROMPT_LEN = 1024
CTX = ("xh", "z")
LOCAL = ("xh", "z", "core")
RESP = ("y", "xl", "core")
ROWS = 128
PROWS = 64
BOTH = ROWS + PROWS
CHUNK = 256
SPAN = 3 * CHUNK
TILE_SPANS = (2 * CHUNK, 3 * CHUNK)
TILE_STARTS = (0, 2 * CHUNK)
PROBS = 5 * CHUNK
HALF = GROUP * ROWS
LANES = 2 * HALF
WIDE = 2 * HEAD_DIM
SCALE = HEAD_DIM**-0.5
SCALE2 = SCALE * math.log2(math.e)
NEG = -1e30
F32 = jnp.float32
BF16 = jnp.bfloat16
VMEM = pl.BlockSpec(memory_space=pltpu.VMEM)
SMEM = pl.BlockSpec(memory_space=pltpu.SMEM)


def dot(a, b):
    return jnp.dot(a, b, preferred_element_type=F32)


def head_at(h, width=HEAD_DIM):
    return slice(h * width, (h + 1) * width)


def lanes_at(j, h):
    return slice(j * HALF + h * HEAD_DIM, j * HALF + (h + 1) * HEAD_DIM)


def block_of(member, quad, core):
    return (member // 2) * 8 + ((quad * 2 + (member & 1) + core) & 7)


def run_copies(pairs, sems):
    copies = [
        pltpu.make_async_copy(source, to, sems.at[i]) for i, (source, to) in enumerate(pairs)
    ]
    for copy in copies:
        copy.start()
    for copy in copies:
        copy.wait()


def pack_kv_kernel(info, k, v, kp, vp, kv0, kv1, kv2, kv3, sems):
    mine = info[0]
    pairs = []
    for d, kv in enumerate((kv0, kv1, kv2, kv3)):
        at = pl.ds(pl.multiple_of((mine ^ d) * HEAD_DIM, HEAD_DIM), HEAD_DIM)
        pairs += [
            (k.at[:, at], kv.at[:ROWS, :HEAD_DIM]),
            (v.at[:, at], kv.at[:ROWS, HEAD_DIM:]),
            (kp.at[:, at], kv.at[ROWS:, :HEAD_DIM]),
            (vp.at[:, at], kv.at[ROWS:, HEAD_DIM:]),
        ]
    run_copies(pairs, sems)


def pack_qd_kernel(info, q, do, qd0, qd1, qd2, qd3, sems):
    mine = info[0]
    pairs = []
    for d, qd in enumerate((qd0, qd1, qd2, qd3)):
        at = pl.ds(pl.multiple_of((mine ^ d) * HALF, HALF), HALF)
        pairs += [(q.at[:, at], qd.at[:, :HALF]), (do.at[:, at], qd.at[:, HALF:])]
    run_copies(pairs, sems)


def rows_at(mine, d):
    return pl.ds(pl.multiple_of(CHUNK + (mine ^ d) // 2 * CHUNK + (d & 1) * ROWS, ROWS), ROWS)


def load_keys(mine, g, kvs, k_s, v_s):
    for d, kv in enumerate(kvs):
        k_s[g, rows_at(mine, d), :] = kv[:ROWS, :HEAD_DIM]
        v_s[g, rows_at(mine, d), :] = kv[:ROWS, HEAD_DIM:]
        k_s[g, head_at(d, PROWS), :] = kv[ROWS:, :HEAD_DIM]
        v_s[g, head_at(d, PROWS), :] = kv[ROWS:, HEAD_DIM:]


def query_rows(info, x):
    mine, quad, core = info[0], info[1], info[2]
    rows = []
    for j in range(2):
        start = block_of(x * 2 + ((mine & 1) ^ j), quad, core) * ROWS
        rows += [start + lax.broadcasted_iota(jnp.int32, (1, ROWS), 1)] * GROUP
    return jnp.concatenate(rows, axis=1)


def key_rows(info, x, quad):
    mine, core = info[0], info[2]
    rows = []
    for j in range(2):
        start = block_of(x * 2 + ((mine & 1) ^ j), quad, core) * ROWS
        rows.append(start + lax.broadcasted_iota(jnp.int32, (ROWS, 1), 0))
    return jnp.concatenate(rows, axis=0)


def fold(x, op):
    return op(x.reshape(x.shape[0] // 8, 8, LANES), axis=0)


def each(count, step, carry):
    return step(0, carry) if count == 1 else lax.fori_loop(0, count, step, carry)


def forward(info, quads, count, k_s, v_s, qt, before, score_s, probs, vt_s, shift, total, acc):
    def turn_values(g, carry):
        vt_s[g] = v_s[g].T
        return carry

    each(count, turn_values, 0)
    for x in range(2):
        place = query_rows(info, x)
        start, span = TILE_STARTS[x], TILE_SPANS[x]

        def score_step(g, running):
            for c in range(span // CHUNK):
                at = slice(c * CHUNK, (c + 1) * CHUNK)
                score = dot(k_s[g, at, :], qt[x])
                if c > 0:
                    score = jnp.where(key_rows(info, c - 1, quads(g)) <= place, score, NEG)
                score_s[g, at, :] = score
                running = jnp.maximum(running, fold(score, jnp.max))
            return running

        running = each(count, score_step, jnp.full((8, LANES), NEG, F32))
        now = jnp.max(running, axis=0, keepdims=True) * SCALE2
        if before is not None:
            now = jnp.maximum(now, before[0][x])
            factor = jnp.exp2(before[0][x] - now)
            acc[x] = before[2][x] * factor

        def prob_step(g, running):
            for c in range(span // CHUNK):
                prob = jnp.exp2(score_s[g, c * CHUNK : (c + 1) * CHUNK, :] * SCALE2 - now)
                running = running + fold(prob, jnp.sum)
                probs[g, start + c * CHUNK : start + (c + 1) * CHUNK, :] = prob.astype(BF16)
            part = dot(vt_s[g, :, :span], probs[g, start : start + span, :])
            if before is None:
                acc[x] = part
            else:
                acc[x] += part
            return running

        running = each(count, prob_step, jnp.zeros((8, LANES), F32))
        sums = jnp.sum(running, axis=0, keepdims=True)
        if before is not None:
            sums = sums + before[1][x] * factor
        shift[x], total[x] = now, sums


def backward(count, k_s, v_s, kt_s, q, uplt, upl, delta, probs, factors, grad_s, before, dqt):
    for x in range(2):
        dqt[x] = jnp.zeros((HEAD_DIM, LANES), F32) if before is None else before[x]

    def chunk(g, c, tiles):
        at = pl.ds(pl.multiple_of(c * CHUNK, CHUNK), CHUNK)
        dk, dv = None, None
        for x in tiles:
            here = pl.ds(pl.multiple_of(TILE_STARTS[x] + c * CHUNK, CHUNK), CHUNK)
            low = probs[g, here, :]
            if factors is not None:
                low = (low.astype(F32) * factors[x]).astype(BF16)
            prob_grad = dot(v_s[g, at, :], uplt[x])
            grad = (low.astype(F32) * (prob_grad - delta[x])).astype(BF16)
            grad_s[here, :] = grad
            dv_part = dot(low, upl[x])
            dk_part = dot(grad, q[x])
            dv = dv_part if dv is None else dv + dv_part
            dk = dk_part if dk is None else dk + dk_part
        k_s[g, at, :] = (dk * SCALE).astype(BF16)
        v_s[g, at, :] = dv.astype(BF16)

    def step(g, carry):
        kt_s[...] = k_s[g].T

        def two_tiles(c, carry):
            chunk(g, c, (0, 1))
            return carry

        lax.fori_loop(0, 2, two_tiles, 0)
        chunk(g, 2, (1,))
        for x in range(2):
            start, span = TILE_STARTS[x], TILE_SPANS[x]
            dqt[x] += dot(kt_s[:, :span], grad_s[start : start + span, :])
        return carry

    each(count, step, 0)


def store_grads(mine, g, k_s, v_s, outs):
    for d, out in enumerate(outs):
        out[:ROWS, :HEAD_DIM] = k_s[g, rows_at(mine, d), :]
        out[:ROWS, HEAD_DIM:] = v_s[g, rows_at(mine, d), :]
        out[ROWS:, :HEAD_DIM] = k_s[g, head_at(d, PROWS), :]
        out[ROWS:, HEAD_DIM:] = v_s[g, head_at(d, PROWS), :]


def pieces(*parts):
    return [part.at[d] for part in parts for d in range(part.shape[0])]


def first_kernel(
    info, weight, qd0, qd1, qd2, qd3, own,
    qt, q, upt, probs, shift, total, acc,
    k_s, v_s, vt_s, score_s,
):
    mine, quad, core, count = info[0], info[1], info[2], info[4]
    load_keys(mine, 0, pieces(own), k_s, v_s)
    for d, qd in enumerate((qd0, qd1, qd2, qd3)):
        x = (mine ^ d) // 2
        row = block_of(mine ^ d, quad, core) * ROWS
        row = row + lax.broadcasted_iota(jnp.int32, (1, ROWS), 1)
        row_weight = jnp.where(row < count, weight[0], 0.0)
        for h in range(GROUP):
            cols = lanes_at(d & 1, h)
            q_head = qd[:, head_at(h)]
            q[x, cols, :] = q_head
            qt[x, :, cols] = q_head.T
            grad = qd[:, HALF + h * HEAD_DIM : HALF + (h + 1) * HEAD_DIM]
            upt[x, :, cols] = (grad.T.astype(F32) * row_weight).astype(BF16)
    forward(
        info, lambda g: quad, 1, k_s, v_s, qt, None, score_s, probs, vt_s, shift, total, acc
    )


def side_kernel(
    info, qt, left, right, shift0, total0, acc0,
    probs, shift, total, acc,
    k_s, v_s, vt_s, score_s,
):
    mine, quad = info[0], info[1]
    load_keys(mine, 0, pieces(left), k_s, v_s)
    load_keys(mine, 1, pieces(right), k_s, v_s)
    forward(
        info, lambda g: (quad + 3 + 2 * g) & 3, 2, k_s, v_s, qt, (shift0, total0, acc0),
        score_s, probs, vt_s, shift, total, acc,
    )


def far_kernel(
    info, qt, q, upt, far_a, far_b, shift0, total0, acc0,
    shift, uplt, upl, delta, dqt, attn, out_a, out_b,
    k_s, v_s, vt_s, kt_s, score_s, probs, grad_s, acc, total,
):
    mine, quad, length = info[0], info[1], info[3]
    load_keys(mine, 0, pieces(far_a, far_b), k_s, v_s)
    forward(
        info, lambda g: (quad + 2) & 3, 1, k_s, v_s, qt, (shift0, total0, acc0),
        score_s, probs, vt_s, shift, total, acc,
    )
    for x in range(2):
        inverse = 1.0 / total[x]
        valid = jnp.where(query_rows(info, x) < length, 1.0, 0.0)
        out_t = (acc[x] * (inverse * valid)).astype(BF16)
        up_low = (upt[x].astype(F32) * inverse).astype(BF16)
        uplt[x] = up_low
        delta[x] = jnp.sum(up_low.astype(F32) * out_t.astype(F32), axis=0, keepdims=True)
        attn[x] = out_t
        for j in range(2):
            for h in range(GROUP):
                upl[x, lanes_at(j, h), :] = up_low[:, lanes_at(j, h)].T
    backward(
        1, k_s, v_s, kt_s, q, uplt, upl, delta, probs, None, grad_s, None, dqt
    )
    store_grads(mine, 0, k_s, v_s, pieces(out_a, out_b))


def back_side_kernel(
    info, q, uplt, upl, delta, shift_then, shift_last, probs,
    left, right, dqt0,
    dqt, out_l, out_r,
    k_s, v_s, kt_s, grad_s,
):
    mine = info[0]
    factors = [jnp.exp2(shift_then[x] - shift_last[x]) for x in range(2)]
    load_keys(mine, 0, pieces(left), k_s, v_s)
    load_keys(mine, 1, pieces(right), k_s, v_s)
    backward(
        2, k_s, v_s, kt_s, q, uplt, upl, delta, probs, factors, grad_s, dqt0, dqt
    )
    store_grads(mine, 0, k_s, v_s, pieces(out_l))
    store_grads(mine, 1, k_s, v_s, pieces(out_r))


def back_own_kernel(
    info, q, uplt, upl, delta, shift_then, shift_last, probs, own, dqt0, attn,
    out, od0, od1, od2, od3,
    k_s, v_s, kt_s, grad_s, dqt, dq_s,
):
    mine = info[0]
    factors = [jnp.exp2(shift_then[x] - shift_last[x]) for x in range(2)]
    load_keys(mine, 0, pieces(own), k_s, v_s)
    backward(
        1, k_s, v_s, kt_s, q, uplt, upl, delta, probs, factors, grad_s, dqt0, dqt
    )
    store_grads(mine, 0, k_s, v_s, pieces(out))
    for x in range(2):
        dq_s[x] = (dqt[x] * SCALE).astype(BF16)
    for d, od in enumerate((od0, od1, od2, od3)):
        x = (mine ^ d) // 2
        for h in range(GROUP):
            od[:, head_at(h)] = attn[x, :, lanes_at(d & 1, h)].T
            od[:, HALF + h * HEAD_DIM : HALF + (h + 1) * HEAD_DIM] = dq_s[
                x, :, lanes_at(d & 1, h)
            ].T


def unpack_kernel(info, od0, od1, od2, od3, attended, query_grad):
    mine = info[0]
    for d, od in enumerate((od0, od1, od2, od3)):
        at = pl.ds(pl.multiple_of((mine ^ d) * HALF, HALF), HALF)
        attended[:, at] = od[:, :HALF]
        query_grad[:, at] = od[:, HALF:]


def both(a, b):
    return (a.astype(F32) + b.astype(F32)).astype(BF16)


def add_kernel(side_l, side_r, far_a, far_b, out_l, out_r):
    out_r[:2] = both(side_r[:2], far_a[...])
    out_r[2:] = side_r[2:]
    out_l[:2] = side_l[:2]
    out_l[2:] = both(side_l[2:], far_b[...])


def sum_kernel(own, left, right, *outs):
    for d, out in enumerate(outs):
        total = own[d].astype(F32) + left[d].astype(F32) + right[d].astype(F32)
        out[...] = total.astype(BF16)


def finish_kernel(info, g0, g1, g2, g3, key_grad, value_grad, share):
    mine = info[0]
    for d, g in enumerate((g0, g1, g2, g3)):
        at = pl.ds(pl.multiple_of((mine ^ d) * HEAD_DIM, HEAD_DIM), HEAD_DIM)
        key_grad[:, at] = g[:ROWS, :HEAD_DIM]
        value_grad[:, at] = g[:ROWS, HEAD_DIM:]
        share[:, at] = g[ROWS:, :HEAD_DIM]
        at = pl.ds(pl.multiple_of(KV_HEADS * HEAD_DIM + (mine ^ d) * HEAD_DIM, HEAD_DIM), HEAD_DIM)
        share[:, at] = g[ROWS:, HEAD_DIM:]


def bf16(*shape):
    return jax.ShapeDtypeStruct(shape, BF16)


def f32(*shape):
    return jax.ShapeDtypeStruct(shape, F32)


def call(kernel, outs, scratch, scalars, *operands, copies=0):
    place = pl.BlockSpec(memory_space=pl.ANY) if copies else VMEM
    scratch = [pltpu.VMEM(shape, dtype) for shape, dtype in scratch]
    if copies:
        scratch.append(pltpu.SemaphoreType.DMA((copies,)))
    return pl.pallas_call(
        kernel,
        out_shape=tuple(outs),
        in_specs=[SMEM] * len(scalars) + [place] * len(operands),
        out_specs=(VMEM,) * len(outs),
        scratch_shapes=scratch,
        compiler_params=pltpu.CompilerParams(vmem_limit_bytes=(60 if copies else 32) * 2**20),
        cost_estimate=pl.CostEstimate(flops=0, bytes_accessed=0, transcendentals=0),
    )(*scalars, *operands)


def swap(x, axis):
    return lax.ppermute(x, axis, [(0, 1), (1, 0)])


def turn(x, axis, step):
    size = lax.axis_size(axis)
    return lax.ppermute(x, axis, [(i, (i + step) % size) for i in range(size)])


def local_permute(x, place):
    pairs = []
    for i in range(32):
        xh, z, core = i // 16, i // 2 % 8, i % 2
        xh, z = place(xh, (z - core) % 8)
        pairs.append((i, (xh * 8 + (z + core) % 8) * 2 + core))
    return lax.ppermute(x, LOCAL, pairs)


def partner(x, d):
    return local_permute(x, lambda xh, z: (xh ^ (d // 2), z ^ (d & 1)))


def quad_turn(x, step):
    return local_permute(x, lambda xh, z: (xh, (z + 2 * step) % 8))


def rounded(x):
    return lax.optimization_barrier(x.astype(BF16))


def body(q_resp, k_resp, v_resp, k_prompt, v_prompt, d_out, lengths, counts):
    core = lax.axis_index("core")
    z = (lax.axis_index("z") - core) & 7
    mine = lax.axis_index("xh") * 2 + (z & 1)
    info = jnp.stack([mine, z // 2, core, lengths[0], counts[0]]).astype(jnp.int32)
    weight = (RESP_LEN / counts[0].astype(F32)).reshape(1)
    kv = list(
        call(
            pack_kv_kernel,
            (bf16(BOTH, WIDE),) * 4,
            (),
            (info,),
            k_resp[0], v_resp[0], k_prompt, v_prompt,
            copies=16,
        )
    )
    qd = list(call(pack_qd_kernel, (bf16(ROWS, LANES),) * 4, (), (info,), q_resp[0], d_out[0], copies=8))
    for d in (1, 2, 3):
        kv[d] = partner(kv[d], d)
    for d in (1, 2, 3):
        qd[d] = partner(qd[d], d)
    own = jnp.stack(kv)
    left, right = quad_turn(own, 1), quad_turn(own, -1)
    far_a, far_b = quad_turn(left[:2], 1), quad_turn(right[2:], -1)

    tiles = (2, HEAD_DIM, LANES)
    line = f32(2, 1, LANES)

    def keys(count):
        return [((count, SPAN, HEAD_DIM), BF16)] * 2

    def forward_scratch(count):
        return keys(count) + [((count, HEAD_DIM, SPAN), BF16), ((count, SPAN, LANES), F32)]

    turned = ((HEAD_DIM, SPAN), BF16)
    grad_s = ((PROBS, LANES), BF16)
    whole, pair = bf16(4, BOTH, WIDE), bf16(2, BOTH, WIDE)
    qt, q, upt, probs1, shift1, total1, acc1 = call(
        first_kernel,
        (bf16(*tiles), bf16(2, LANES, HEAD_DIM), bf16(*tiles), bf16(1, PROBS, LANES), line, line, f32(*tiles)),
        forward_scratch(1),
        (info, weight),
        *qd, own,
    )
    probs2, shift2, total2, acc2 = call(
        side_kernel,
        (bf16(2, PROBS, LANES), line, line, f32(*tiles)),
        forward_scratch(2),
        (info,),
        qt, left, right, shift1, total1, acc1,
    )
    shift3, uplt, upl, delta, dqt, attn, far_ga, far_gb = call(
        far_kernel,
        (line, bf16(*tiles), bf16(2, LANES, HEAD_DIM), line, f32(*tiles), bf16(*tiles), pair, pair),
        keys(1) + [((1, HEAD_DIM, SPAN), BF16), turned, ((1, SPAN, LANES), F32)]
        + [((1, PROBS, LANES), BF16), grad_s, (tiles, F32), ((2, 1, LANES), F32)],
        (info,),
        qt, q, upt, far_a, far_b, shift2, total2, acc2,
    )
    far_ga, far_gb = quad_turn(far_ga, 1), quad_turn(far_gb, -1)
    dqt, left_g, right_g = call(
        back_side_kernel,
        (f32(*tiles), whole, whole),
        keys(2) + [turned, grad_s],
        (info,),
        q, uplt, upl, delta, shift2, shift3, probs2,
        left, right, dqt,
    )
    left_g, right_g = call(add_kernel, (whole, whole), (), (), left_g, right_g, far_ga, far_gb)
    left_g, right_g = quad_turn(left_g, -1), quad_turn(right_g, 1)
    own_g, *od = call(
        back_own_kernel,
        (whole,) + (bf16(ROWS, LANES),) * 4,
        keys(1) + [turned, grad_s, (tiles, F32), (tiles, BF16)],
        (info,),
        q, uplt, upl, delta, shift1, shift3, probs1, own, dqt, attn,
    )
    for d in (1, 2, 3):
        od[d] = partner(od[d], d)
    grads = list(call(sum_kernel, (bf16(BOTH, WIDE),) * 4, (), (), own_g, left_g, right_g))
    for d in (1, 2, 3):
        grads[d] = partner(grads[d], d)
    tied = lax.optimization_barrier((*grads, *od))
    grads, od = tied[:4], tied[4:]
    width = KV_HEADS * HEAD_DIM
    rows = bf16(ROWS, HEADS * HEAD_DIM)
    key_grad, value_grad, share = call(
        finish_kernel,
        (bf16(ROWS, width), bf16(ROWS, width), bf16(PROWS, 2 * width)),
        (),
        (info,),
        *grads,
    )
    for axis in ("core", "xl"):
        share = rounded(share.astype(F32) + swap(share, axis).astype(F32))
    across = share.astype(F32) + turn(share, "y", 2).astype(F32)
    beside = turn(share, "y", 1).astype(F32) + turn(share, "y", 3).astype(F32)
    share = (across + beside).astype(BF16)
    attended, query_grad = call(unpack_kernel, (rows, rows), (), (info,), *od)
    return (
        attended[None],
        query_grad[None],
        key_grad[None],
        value_grad[None],
        share[:, :width],
        share[:, width:],
    )


def solution(mesh):
    split = Mesh(mesh.devices.reshape(2, 8, 4, 2, 2), CTX + RESP)
    rows = P(RESP, CTX, None)
    prompt = P(CTX, None)
    return jax.shard_map(
        body,
        mesh=split,
        in_specs=(rows, rows, rows, prompt, prompt, rows, P(RESP), P(RESP)),
        out_specs=(rows, rows, rows, rows, prompt, prompt),
        check_vma=False,
    )
```

```python
import math

import jax
import jax.numpy as jnp
from jax import lax
from jax.experimental import pallas as pl
from jax.experimental.pallas import tpu as pltpu
from jax.sharding import Mesh
from jax.sharding import PartitionSpec as P

HEADS = 16
KV_HEADS = 4
HEAD_DIM = 128
GROUP = HEADS // KV_HEADS
RESP_LEN = 2048
PROMPT_LEN = 1024
CTX = ("xh", "z")
LOCAL = ("xh", "z", "core")
RESP = ("y", "xl", "core")
ROWS = 128
PROWS = 64
BOTH = ROWS + PROWS
CHUNK = 256
SPAN = 3 * CHUNK
TILE_SPANS = (2 * CHUNK, 3 * CHUNK)
TILE_STARTS = (0, 2 * CHUNK)
PROBS = 5 * CHUNK
HALF = GROUP * ROWS
LANES = 2 * HALF
WIDE = 2 * HEAD_DIM
SCALE = HEAD_DIM**-0.5
SCALE2 = SCALE * math.log2(math.e)
NEG = -1e30
F32 = jnp.float32
BF16 = jnp.bfloat16
VMEM = pl.BlockSpec(memory_space=pltpu.VMEM)
SMEM = pl.BlockSpec(memory_space=pltpu.SMEM)


def dot(a, b):
    return jnp.dot(a, b, preferred_element_type=F32)


def head_at(h, width=HEAD_DIM):
    return slice(h * width, (h + 1) * width)


def lanes_at(j, h):
    return slice(j * HALF + h * HEAD_DIM, j * HALF + (h + 1) * HEAD_DIM)


def block_of(member, quad, core):
    return (member // 2) * 8 + ((quad * 2 + (member & 1) + core) & 7)


def run_copies(pairs, sems):
    copies = [
        pltpu.make_async_copy(source, to, sems.at[i]) for i, (source, to) in enumerate(pairs)
    ]
    for copy in copies:
        copy.start()
    for copy in copies:
        copy.wait()


def pack_kv_kernel(info, k, v, kp, vp, kv0, kv1, kv2, kv3, sems):
    mine = info[0]
    pairs = []
    for d, kv in enumerate((kv0, kv1, kv2, kv3)):
        at = pl.ds(pl.multiple_of((mine ^ d) * HEAD_DIM, HEAD_DIM), HEAD_DIM)
        pairs += [
            (k.at[:, at], kv.at[:ROWS, :HEAD_DIM]),
            (v.at[:, at], kv.at[:ROWS, HEAD_DIM:]),
            (kp.at[:, at], kv.at[ROWS:, :HEAD_DIM]),
            (vp.at[:, at], kv.at[ROWS:, HEAD_DIM:]),
        ]
    run_copies(pairs, sems)


def pack_qd_kernel(info, q, do, qd0, qd1, qd2, qd3, sems):
    mine = info[0]
    pairs = []
    for d, qd in enumerate((qd0, qd1, qd2, qd3)):
        at = pl.ds(pl.multiple_of((mine ^ d) * HALF, HALF), HALF)
        pairs += [(q.at[:, at], qd.at[:, :HALF]), (do.at[:, at], qd.at[:, HALF:])]
    run_copies(pairs, sems)


def rows_at(mine, d):
    return pl.ds(pl.multiple_of(CHUNK + (mine ^ d) // 2 * CHUNK + (d & 1) * ROWS, ROWS), ROWS)


def load_keys(mine, g, kvs, k_s, v_s):
    for d, kv in enumerate(kvs):
        k_s[g, rows_at(mine, d), :] = kv[:ROWS, :HEAD_DIM]
        v_s[g, rows_at(mine, d), :] = kv[:ROWS, HEAD_DIM:]
        k_s[g, head_at(d, PROWS), :] = kv[ROWS:, :HEAD_DIM]
        v_s[g, head_at(d, PROWS), :] = kv[ROWS:, HEAD_DIM:]


def query_rows(info, x):
    mine, quad, core = info[0], info[1], info[2]
    rows = []
    for j in range(2):
        start = block_of(x * 2 + ((mine & 1) ^ j), quad, core) * ROWS
        rows += [start + lax.broadcasted_iota(jnp.int32, (1, ROWS), 1)] * GROUP
    return jnp.concatenate(rows, axis=1)


def key_rows(info, x, quad):
    mine, core = info[0], info[2]
    rows = []
    for j in range(2):
        start = block_of(x * 2 + ((mine & 1) ^ j), quad, core) * ROWS
        rows.append(start + lax.broadcasted_iota(jnp.int32, (ROWS, 1), 0))
    return jnp.concatenate(rows, axis=0)


def fold(x, op):
    return op(x.reshape(x.shape[0] // 8, 8, LANES), axis=0)


def each(count, step, carry):
    return step(0, carry) if count == 1 else lax.fori_loop(0, count, step, carry)


def forward(info, quads, count, k_s, v_s, qt, before, score_s, probs, vt_s, shift, total, acc):
    def turn_values(g, carry):
        vt_s[g] = v_s[g].T
        return carry

    each(count, turn_values, 0)
    for x in range(2):
        place = query_rows(info, x)
        start, span = TILE_STARTS[x], TILE_SPANS[x]

        def score_step(g, running):
            for c in range(span // CHUNK):
                at = slice(c * CHUNK, (c + 1) * CHUNK)
                score = dot(k_s[g, at, :], qt[x])
                if c > 0:
                    score = jnp.where(key_rows(info, c - 1, quads(g)) <= place, score, NEG)
                score_s[g, at, :] = score
                running = jnp.maximum(running, fold(score, jnp.max))
            return running

        running = each(count, score_step, jnp.full((8, LANES), NEG, F32))
        now = jnp.max(running, axis=0, keepdims=True) * SCALE2
        if before is not None:
            now = jnp.maximum(now, before[0][x])
            factor = jnp.exp2(before[0][x] - now)
            acc[x] = before[2][x] * factor

        def prob_step(g, running):
            for c in range(span // CHUNK):
                prob = jnp.exp2(score_s[g, c * CHUNK : (c + 1) * CHUNK, :] * SCALE2 - now)
                running = running + fold(prob, jnp.sum)
                probs[g, start + c * CHUNK : start + (c + 1) * CHUNK, :] = prob.astype(BF16)
            part = dot(vt_s[g, :, :span], probs[g, start : start + span, :])
            if before is None:
                acc[x] = part
            else:
                acc[x] += part
            return running

        running = each(count, prob_step, jnp.zeros((8, LANES), F32))
        sums = jnp.sum(running, axis=0, keepdims=True)
        if before is not None:
            sums = sums + before[1][x] * factor
        shift[x], total[x] = now, sums


def backward(count, k_s, v_s, kt_s, q, uplt, upl, delta, probs, factors, grad_s, before, dqt):
    for x in range(2):
        dqt[x] = jnp.zeros((HEAD_DIM, LANES), F32) if before is None else before[x]

    def chunk(g, c, tiles):
        at = pl.ds(pl.multiple_of(c * CHUNK, CHUNK), CHUNK)
        dk, dv = None, None
        for x in tiles:
            here = pl.ds(pl.multiple_of(TILE_STARTS[x] + c * CHUNK, CHUNK), CHUNK)
            low = probs[g, here, :]
            if factors is not None:
                low = (low.astype(F32) * factors[x]).astype(BF16)
            prob_grad = dot(v_s[g, at, :], uplt[x])
            grad = (low.astype(F32) * (prob_grad - delta[x])).astype(BF16)
            grad_s[here, :] = grad
            dv_part = dot(low, upl[x])
            dk_part = dot(grad, q[x])
            dv = dv_part if dv is None else dv + dv_part
            dk = dk_part if dk is None else dk + dk_part
        k_s[g, at, :] = (dk * SCALE).astype(BF16)
        v_s[g, at, :] = dv.astype(BF16)

    def step(g, carry):
        kt_s[...] = k_s[g].T

        def two_tiles(c, carry):
            chunk(g, c, (0, 1))
            return carry

        lax.fori_loop(0, 2, two_tiles, 0)
        chunk(g, 2, (1,))
        for x in range(2):
            start, span = TILE_STARTS[x], TILE_SPANS[x]
            dqt[x] += dot(kt_s[:, :span], grad_s[start : start + span, :])
        return carry

    each(count, step, 0)


def store_grads(mine, g, k_s, v_s, outs):
    for d, out in enumerate(outs):
        out[:ROWS, :HEAD_DIM] = k_s[g, rows_at(mine, d), :]
        out[:ROWS, HEAD_DIM:] = v_s[g, rows_at(mine, d), :]
        out[ROWS:, :HEAD_DIM] = k_s[g, head_at(d, PROWS), :]
        out[ROWS:, HEAD_DIM:] = v_s[g, head_at(d, PROWS), :]


def pieces(*parts):
    return [part.at[d] for part in parts for d in range(part.shape[0])]


def first_kernel(
    info, weight, qd0, qd1, qd2, qd3, own_a, own_b,
    qt, q, upt, probs, shift, total, acc,
    k_s, v_s, vt_s, score_s,
):
    mine, quad, core, count = info[0], info[1], info[2], info[4]
    load_keys(mine, 0, pieces(own_a, own_b), k_s, v_s)
    for d, qd in enumerate((qd0, qd1, qd2, qd3)):
        x = (mine ^ d) // 2
        row = block_of(mine ^ d, quad, core) * ROWS
        row = row + lax.broadcasted_iota(jnp.int32, (1, ROWS), 1)
        row_weight = jnp.where(row < count, weight[0], 0.0)
        for h in range(GROUP):
            cols = lanes_at(d & 1, h)
            q_head = qd[:, head_at(h)]
            q[x, cols, :] = q_head
            qt[x, :, cols] = q_head.T
            grad = qd[:, HALF + h * HEAD_DIM : HALF + (h + 1) * HEAD_DIM]
            upt[x, :, cols] = (grad.T.astype(F32) * row_weight).astype(BF16)
    forward(
        info, lambda g: quad, 1, k_s, v_s, qt, None, score_s, probs, vt_s, shift, total, acc
    )


def side_kernel(
    info, qt, left_a, left_b, right_a, right_b, shift0, total0, acc0,
    probs, shift, total, acc,
    k_s, v_s, vt_s, score_s,
):
    mine, quad = info[0], info[1]
    load_keys(mine, 0, pieces(left_a, left_b), k_s, v_s)
    load_keys(mine, 1, pieces(right_a, right_b), k_s, v_s)
    forward(
        info, lambda g: (quad + 3 + 2 * g) & 3, 2, k_s, v_s, qt, (shift0, total0, acc0),
        score_s, probs, vt_s, shift, total, acc,
    )


def far_kernel(
    info, qt, q, upt, far_a, far_b, shift0, total0, acc0,
    shift, uplt, upl, delta, dqt, attn, out_a, out_b,
    k_s, v_s, vt_s, kt_s, score_s, probs, grad_s, acc, total,
):
    mine, quad, length = info[0], info[1], info[3]
    load_keys(mine, 0, pieces(far_a, far_b), k_s, v_s)
    forward(
        info, lambda g: (quad + 2) & 3, 1, k_s, v_s, qt, (shift0, total0, acc0),
        score_s, probs, vt_s, shift, total, acc,
    )
    for x in range(2):
        inverse = 1.0 / total[x]
        valid = jnp.where(query_rows(info, x) < length, 1.0, 0.0)
        out_t = (acc[x] * (inverse * valid)).astype(BF16)
        up_low = (upt[x].astype(F32) * inverse).astype(BF16)
        uplt[x] = up_low
        delta[x] = jnp.sum(up_low.astype(F32) * out_t.astype(F32), axis=0, keepdims=True)
        attn[x] = out_t
        for j in range(2):
            for h in range(GROUP):
                upl[x, lanes_at(j, h), :] = up_low[:, lanes_at(j, h)].T
    backward(
        1, k_s, v_s, kt_s, q, uplt, upl, delta, probs, None, grad_s, None, dqt
    )
    store_grads(mine, 0, k_s, v_s, pieces(out_a, out_b))


def back_side_kernel(
    info, q, uplt, upl, delta, shift_then, shift_last, probs,
    left_a, left_b, right_a, right_b, dqt0,
    dqt, out_l, out_r,
    k_s, v_s, kt_s, grad_s,
):
    mine = info[0]
    factors = [jnp.exp2(shift_then[x] - shift_last[x]) for x in range(2)]
    load_keys(mine, 0, pieces(left_a, left_b), k_s, v_s)
    load_keys(mine, 1, pieces(right_a, right_b), k_s, v_s)
    backward(
        2, k_s, v_s, kt_s, q, uplt, upl, delta, probs, factors, grad_s, dqt0, dqt
    )
    store_grads(mine, 0, k_s, v_s, pieces(out_l))
    store_grads(mine, 1, k_s, v_s, pieces(out_r))


def back_own_kernel(
    info, q, uplt, upl, delta, shift_then, shift_last, probs, own_a, own_b, dqt0, attn,
    out, od0, od1, od2, od3,
    k_s, v_s, kt_s, grad_s, dqt, dq_s,
):
    mine = info[0]
    factors = [jnp.exp2(shift_then[x] - shift_last[x]) for x in range(2)]
    load_keys(mine, 0, pieces(own_a, own_b), k_s, v_s)
    backward(
        1, k_s, v_s, kt_s, q, uplt, upl, delta, probs, factors, grad_s, dqt0, dqt
    )
    store_grads(mine, 0, k_s, v_s, pieces(out))
    for x in range(2):
        dq_s[x] = (dqt[x] * SCALE).astype(BF16)
    for d, od in enumerate((od0, od1, od2, od3)):
        x = (mine ^ d) // 2
        for h in range(GROUP):
            od[:, head_at(h)] = attn[x, :, lanes_at(d & 1, h)].T
            od[:, HALF + h * HEAD_DIM : HALF + (h + 1) * HEAD_DIM] = dq_s[
                x, :, lanes_at(d & 1, h)
            ].T


def unpack_kernel(info, od0, od1, od2, od3, attended, query_grad):
    mine = info[0]
    for d, od in enumerate((od0, od1, od2, od3)):
        at = pl.ds(pl.multiple_of((mine ^ d) * HALF, HALF), HALF)
        attended[:, at] = od[:, :HALF]
        query_grad[:, at] = od[:, HALF:]


def both(a, b):
    return (a.astype(F32) + b.astype(F32)).astype(BF16)


def add_kernel(side_l, side_r, far_a, far_b, out_l, out_r):
    out_r[:2] = both(side_r[:2], far_a[...])
    out_r[2:] = side_r[2:]
    out_l[:2] = side_l[:2]
    out_l[2:] = both(side_l[2:], far_b[...])


def sum_kernel(own, left, right, *outs):
    for d, out in enumerate(outs):
        total = own[d].astype(F32) + left[d].astype(F32) + right[d].astype(F32)
        out[...] = total.astype(BF16)


def finish_kernel(info, g0, g1, g2, g3, key_grad, value_grad, share):
    mine = info[0]
    for d, g in enumerate((g0, g1, g2, g3)):
        at = pl.ds(pl.multiple_of((mine ^ d) * HEAD_DIM, HEAD_DIM), HEAD_DIM)
        key_grad[:, at] = g[:ROWS, :HEAD_DIM]
        value_grad[:, at] = g[:ROWS, HEAD_DIM:]
        share[:, at] = g[ROWS:, :HEAD_DIM]
        at = pl.ds(pl.multiple_of(KV_HEADS * HEAD_DIM + (mine ^ d) * HEAD_DIM, HEAD_DIM), HEAD_DIM)
        share[:, at] = g[ROWS:, HEAD_DIM:]


def bf16(*shape):
    return jax.ShapeDtypeStruct(shape, BF16)


def f32(*shape):
    return jax.ShapeDtypeStruct(shape, F32)


def call(kernel, outs, scratch, scalars, *operands, copies=0, products=0):
    place = pl.BlockSpec(memory_space=pl.ANY) if copies else VMEM
    scratch = [pltpu.VMEM(shape, dtype) for shape, dtype in scratch]
    if copies:
        scratch.append(pltpu.SemaphoreType.DMA((copies,)))
    return pl.pallas_call(
        kernel,
        out_shape=tuple(outs),
        in_specs=[SMEM] * len(scalars) + [place] * len(operands),
        out_specs=(VMEM,) * len(outs),
        scratch_shapes=scratch,
        compiler_params=pltpu.CompilerParams(vmem_limit_bytes=(56 if copies == 16 else 32) * 2**20),
        cost_estimate=pl.CostEstimate(
            flops=products * PROBS * LANES * HEAD_DIM * 4,
            bytes_accessed=1_000_000,
            transcendentals=0,
        ),
    )(*scalars, *operands)


def swap(x, axis):
    return lax.ppermute(x, axis, [(0, 1), (1, 0)])


def turn(x, axis, step):
    size = lax.axis_size(axis)
    return lax.ppermute(x, axis, [(i, (i + step) % size) for i in range(size)])


def local_permute(x, place):
    pairs = []
    for i in range(32):
        xh, z, core = i // 16, i // 2 % 8, i % 2
        xh, z = place(xh, (z - core) % 8)
        pairs.append((i, (xh * 8 + (z + core) % 8) * 2 + core))
    return lax.ppermute(x, LOCAL, pairs)


def partner(x, d):
    return local_permute(x, lambda xh, z: (xh ^ (d // 2), z ^ (d & 1)))


def quad_turn(x, step):
    return local_permute(x, lambda xh, z: (xh, (z + 2 * step) % 8))


def rounded(x):
    return lax.optimization_barrier(x.astype(BF16))


def body(q_resp, k_resp, v_resp, k_prompt, v_prompt, d_out, lengths, counts):
    core = lax.axis_index("core")
    z = (lax.axis_index("z") - core) & 7
    mine = lax.axis_index("xh") * 2 + (z & 1)
    info = jnp.stack([mine, z // 2, core, lengths[0], counts[0]]).astype(jnp.int32)
    weight = (RESP_LEN / counts[0].astype(F32)).reshape(1)
    kv = list(
        call(
            pack_kv_kernel,
            (bf16(BOTH, WIDE),) * 4,
            (),
            (info,),
            k_resp[0], v_resp[0], k_prompt, v_prompt,
            copies=16,
        )
    )
    qd = list(call(pack_qd_kernel, (bf16(ROWS, LANES),) * 4, (), (info,), q_resp[0], d_out[0], copies=8))
    for d in (1, 2, 3):
        kv[d] = partner(kv[d], d)
    for d in (1, 2, 3):
        qd[d] = partner(qd[d], d)
    own_a, own_b = jnp.stack(kv[:2]), jnp.stack(kv[2:])
    left_a, right_b = quad_turn(own_a, 1), quad_turn(own_b, -1)
    left_b, right_a = quad_turn(own_b, 1), quad_turn(own_a, -1)
    far_a, far_b = quad_turn(left_a, 1), quad_turn(right_b, -1)

    tiles = (2, HEAD_DIM, LANES)
    line = f32(2, 1, LANES)

    def keys(count):
        return [((count, SPAN, HEAD_DIM), BF16)] * 2

    def forward_scratch(count):
        return keys(count) + [((count, HEAD_DIM, SPAN), BF16), ((count, SPAN, LANES), F32)]

    turned = ((HEAD_DIM, SPAN), BF16)
    grad_s = ((PROBS, LANES), BF16)
    whole, pair = bf16(4, BOTH, WIDE), bf16(2, BOTH, WIDE)
    qt, q, upt, probs1, shift1, total1, acc1 = call(
        first_kernel,
        (bf16(*tiles), bf16(2, LANES, HEAD_DIM), bf16(*tiles), bf16(1, PROBS, LANES), line, line, f32(*tiles)),
        forward_scratch(1),
        (info, weight),
        *qd, own_a, own_b,
        products=2,
    )
    probs2, shift2, total2, acc2 = call(
        side_kernel,
        (bf16(2, PROBS, LANES), line, line, f32(*tiles)),
        forward_scratch(2),
        (info,),
        qt, left_a, left_b, right_a, right_b, shift1, total1, acc1,
        products=4,
    )
    shift3, uplt, upl, delta, dqt, attn, far_ga, far_gb = call(
        far_kernel,
        (line, bf16(*tiles), bf16(2, LANES, HEAD_DIM), line, f32(*tiles), bf16(*tiles), pair, pair),
        keys(1) + [((1, HEAD_DIM, SPAN), BF16), turned, ((1, SPAN, LANES), F32)]
        + [((1, PROBS, LANES), BF16), grad_s, (tiles, F32), ((2, 1, LANES), F32)],
        (info,),
        qt, q, upt, far_a, far_b, shift2, total2, acc2,
        products=6,
    )
    far_ga, far_gb = quad_turn(far_ga, 1), quad_turn(far_gb, -1)
    dqt, left_g, right_g = call(
        back_side_kernel,
        (f32(*tiles), whole, whole),
        keys(2) + [turned, grad_s],
        (info,),
        q, uplt, upl, delta, shift2, shift3, probs2,
        left_a, left_b, right_a, right_b, dqt,
        products=8,
    )
    left_g, right_g = call(add_kernel, (whole, whole), (), (), left_g, right_g, far_ga, far_gb)
    left_g, right_g = quad_turn(left_g, -1), quad_turn(right_g, 1)
    own_g, *od = call(
        back_own_kernel,
        (whole,) + (bf16(ROWS, LANES),) * 4,
        keys(1) + [turned, grad_s, (tiles, F32), (tiles, BF16)],
        (info,),
        q, uplt, upl, delta, shift1, shift3, probs1, own_a, own_b, dqt, attn,
        products=4,
    )
    for d in (1, 2, 3):
        od[d] = partner(od[d], d)
    grads = list(call(sum_kernel, (bf16(BOTH, WIDE),) * 4, (), (), own_g, left_g, right_g))
    for d in (1, 2, 3):
        grads[d] = partner(grads[d], d)
    tied = lax.optimization_barrier((*grads, *od))
    grads, od = tied[:4], tied[4:]
    width = KV_HEADS * HEAD_DIM
    rows = bf16(ROWS, HEADS * HEAD_DIM)
    key_grad, value_grad, share = call(
        finish_kernel,
        (bf16(ROWS, width), bf16(ROWS, width), bf16(PROWS, 2 * width)),
        (),
        (info,),
        *grads,
    )
    for axis in ("core", "xl"):
        share = rounded(share.astype(F32) + swap(share, axis).astype(F32))
    across = share.astype(F32) + turn(share, "y", 2).astype(F32)
    beside = turn(share, "y", 1).astype(F32) + turn(share, "y", 3).astype(F32)
    share = (across + beside).astype(BF16)
    attended, query_grad = call(unpack_kernel, (rows, rows), (), (info,), *od)
    return (
        attended[None],
        query_grad[None],
        key_grad[None],
        value_grad[None],
        share[:, :width],
        share[:, width:],
    )


def solution(mesh):
    split = Mesh(mesh.devices.reshape(2, 8, 4, 2, 2), CTX + RESP)
    rows = P(RESP, CTX, None)
    prompt = P(CTX, None)
    return jax.shard_map(
        body,
        mesh=split,
        in_specs=(rows, rows, rows, prompt, prompt, rows, P(RESP), P(RESP)),
        out_specs=(rows, rows, rows, rows, prompt, prompt),
        check_vma=False,
    )
```

```python
import math

import jax
import jax.numpy as jnp
from jax import lax
from jax.experimental import pallas as pl
from jax.experimental.pallas import tpu as pltpu
from jax.sharding import Mesh
from jax.sharding import PartitionSpec as P

HEADS = 16
KV_HEADS = 4
HEAD_DIM = 128
GROUP = HEADS // KV_HEADS
RESP_LEN = 2048
PROMPT_LEN = 1024
CTX = ("xh", "z")
LOCAL = ("xh", "z", "core")
RESP = ("y", "xl", "core")
ROWS = 128
PROWS = 64
BOTH = ROWS + PROWS
CHUNK = 256
SPAN = 3 * CHUNK
TILE_SPANS = (2 * CHUNK, 3 * CHUNK)
TILE_STARTS = (0, 2 * CHUNK)
PROBS = 5 * CHUNK
HALF = GROUP * ROWS
LANES = 2 * HALF
WIDE = 2 * HEAD_DIM
SCALE = HEAD_DIM**-0.5
SCALE2 = SCALE * math.log2(math.e)
NEG = -1e30
F32 = jnp.float32
BF16 = jnp.bfloat16
VMEM = pl.BlockSpec(memory_space=pltpu.VMEM)
SMEM = pl.BlockSpec(memory_space=pltpu.SMEM)


def dot(a, b):
    return jnp.dot(a, b, preferred_element_type=F32)


def head_at(h, width=HEAD_DIM):
    return slice(h * width, (h + 1) * width)


def lanes_at(j, h):
    return slice(j * HALF + h * HEAD_DIM, j * HALF + (h + 1) * HEAD_DIM)


def block_of(member, quad, core):
    return (member // 2) * 8 + ((quad * 2 + (member & 1) + core) & 7)


def run_copies(pairs, sems):
    copies = [
        pltpu.make_async_copy(source, to, sems.at[i]) for i, (source, to) in enumerate(pairs)
    ]
    for copy in copies:
        copy.start()
    for copy in copies:
        copy.wait()


def pack_kv_kernel(k, v, kp, vp, kv, k_s, v_s, kp_s, vp_s, sems):
    run_copies(((k, k_s), (v, v_s), (kp, kp_s), (vp, vp_s)), sems)
    for m in range(4):
        kv[m, :ROWS, :HEAD_DIM] = k_s[:, head_at(m)]
        kv[m, :ROWS, HEAD_DIM:] = v_s[:, head_at(m)]
        kv[m, ROWS:, :HEAD_DIM] = kp_s[:, head_at(m)]
        kv[m, ROWS:, HEAD_DIM:] = vp_s[:, head_at(m)]


def pack_qd_kernel(q, do, qd, q_s, do_s, sems):
    run_copies(((q, q_s), (do, do_s)), sems)
    for m in range(4):
        qd[m, :, :HALF] = q_s[:, head_at(m, HALF)]
        qd[m, :, HALF:] = do_s[:, head_at(m, HALF)]


def rows_at(m):
    return slice(CHUNK + m * ROWS, CHUNK + (m + 1) * ROWS)


def load_keys(g, kvs, k_s, v_s):
    for m, kv in enumerate(kvs):
        k_s[g, rows_at(m), :] = kv[:ROWS, :HEAD_DIM]
        v_s[g, rows_at(m), :] = kv[:ROWS, HEAD_DIM:]
        k_s[g, head_at(m, PROWS), :] = kv[ROWS:, :HEAD_DIM]
        v_s[g, head_at(m, PROWS), :] = kv[ROWS:, HEAD_DIM:]


def query_rows(info, x):
    rows = []
    for j in range(2):
        start = block_of(x * 2 + j, info[0], info[1]) * ROWS
        rows += [start + lax.broadcasted_iota(jnp.int32, (1, ROWS), 1)] * GROUP
    return jnp.concatenate(rows, axis=1)


def key_rows(info, x, quad):
    rows = []
    for j in range(2):
        start = block_of(x * 2 + j, quad, info[1]) * ROWS
        rows.append(start + lax.broadcasted_iota(jnp.int32, (ROWS, 1), 0))
    return jnp.concatenate(rows, axis=0)


def fold(x, op):
    return op(x.reshape(x.shape[0] // 8, 8, LANES), axis=0)


def each(count, step, carry):
    return step(0, carry) if count == 1 else lax.fori_loop(0, count, step, carry)


def forward(info, quads, count, k_s, v_s, qt, before, score_s, probs, vt_s, shift, total, acc):
    def turn_values(g, carry):
        vt_s[g] = v_s[g].T
        return carry

    each(count, turn_values, 0)
    for x in range(2):
        place = query_rows(info, x)
        start, span = TILE_STARTS[x], TILE_SPANS[x]

        def score_step(g, running):
            for c in range(span // CHUNK):
                at = slice(c * CHUNK, (c + 1) * CHUNK)
                score = dot(k_s[g, at, :], qt[x])
                if c > 0:
                    score = jnp.where(key_rows(info, c - 1, quads(g)) <= place, score, NEG)
                score_s[g, at, :] = score
                running = jnp.maximum(running, fold(score, jnp.max))
            return running

        running = each(count, score_step, jnp.full((8, LANES), NEG, F32))
        now = jnp.max(running, axis=0, keepdims=True) * SCALE2
        if before is not None:
            now = jnp.maximum(now, before[0][x])
            factor = jnp.exp2(before[0][x] - now)
            acc[x] = before[2][x] * factor

        def prob_step(g, running):
            for c in range(span // CHUNK):
                prob = jnp.exp2(score_s[g, c * CHUNK : (c + 1) * CHUNK, :] * SCALE2 - now)
                running = running + fold(prob, jnp.sum)
                probs[g, start + c * CHUNK : start + (c + 1) * CHUNK, :] = prob.astype(BF16)
            part = dot(vt_s[g, :, :span], probs[g, start : start + span, :])
            if before is None:
                acc[x] = part
            else:
                acc[x] += part
            return running

        running = each(count, prob_step, jnp.zeros((8, LANES), F32))
        sums = jnp.sum(running, axis=0, keepdims=True)
        if before is not None:
            sums = sums + before[1][x] * factor
        shift[x], total[x] = now, sums


def backward(count, k_s, v_s, kt_s, q, uplt, upl, delta, probs, factors, grad_s, before, dqt):
    for x in range(2):
        dqt[x] = jnp.zeros((HEAD_DIM, LANES), F32) if before is None else before[x]

    def step(g, carry):
        kt_s[...] = k_s[g].T
        for c in range(3):
            at = slice(c * CHUNK, (c + 1) * CHUNK)
            dk, dv = None, None
            for x in range(c // 2, 2):
                here = slice(TILE_STARTS[x] + c * CHUNK, TILE_STARTS[x] + (c + 1) * CHUNK)
                low = probs[g, here, :]
                if factors is not None:
                    low = (low.astype(F32) * factors[x]).astype(BF16)
                prob_grad = dot(v_s[g, at, :], uplt[x])
                grad = (low.astype(F32) * (prob_grad - delta[x])).astype(BF16)
                grad_s[here, :] = grad
                dv_part = dot(low, upl[x])
                dk_part = dot(grad, q[x])
                dv = dv_part if dv is None else dv + dv_part
                dk = dk_part if dk is None else dk + dk_part
            k_s[g, at, :] = (dk * SCALE).astype(BF16)
            v_s[g, at, :] = dv.astype(BF16)
        for x in range(2):
            start, span = TILE_STARTS[x], TILE_SPANS[x]
            dqt[x] += dot(kt_s[:, :span], grad_s[start : start + span, :])
        return carry

    each(count, step, 0)


def store_grads(g, k_s, v_s, outs):
    for m, out in enumerate(outs):
        out[:ROWS, :HEAD_DIM] = k_s[g, rows_at(m), :]
        out[:ROWS, HEAD_DIM:] = v_s[g, rows_at(m), :]
        out[ROWS:, :HEAD_DIM] = k_s[g, head_at(m, PROWS), :]
        out[ROWS:, HEAD_DIM:] = v_s[g, head_at(m, PROWS), :]


def pieces(*parts):
    return [part.at[m] for part in parts for m in range(part.shape[0])]


def turn_rows(x, tile, out):
    for j in range(2):
        for h in range(GROUP):
            out[x * 2 + j, :, head_at(h)] = tile[:, lanes_at(j, h)].T


def first_kernel(
    info, weight, qd, own, qt, q, upt, probs, shift, total, acc, k_s, v_s, vt_s, score_s
):
    quad, core, count = info[0], info[1], info[3]
    load_keys(0, pieces(own), k_s, v_s)
    for m in range(4):
        row = block_of(m, quad, core) * ROWS
        row = row + lax.broadcasted_iota(jnp.int32, (1, ROWS), 1)
        row_weight = jnp.where(row < count, weight[0], 0.0)
        for h in range(GROUP):
            cols = lanes_at(m & 1, h)
            q_head = qd[m, :, head_at(h)]
            q[m // 2, cols, :] = q_head
            qt[m // 2, :, cols] = q_head.T
            grad = qd[m, :, HALF + h * HEAD_DIM : HALF + (h + 1) * HEAD_DIM]
            upt[m // 2, :, cols] = (grad.T.astype(F32) * row_weight).astype(BF16)
    forward(
        info, lambda g: quad, 1, k_s, v_s, qt, None, score_s, probs, vt_s, shift, total, acc
    )


def side_kernel(
    info, qt, left, right, shift0, total0, acc0,
    probs, shift, total, acc,
    k_s, v_s, vt_s, score_s,
):
    quad = info[0]
    load_keys(0, pieces(left), k_s, v_s)
    load_keys(1, pieces(right), k_s, v_s)
    forward(
        info, lambda g: (quad + 3 + 2 * g) & 3, 2, k_s, v_s, qt, (shift0, total0, acc0),
        score_s, probs, vt_s, shift, total, acc,
    )


def far_kernel(
    info, qt, q, upt, far_a, far_b, shift0, total0, acc0,
    shift, uplt, upl, delta, dqt, attn, out_a, out_b,
    k_s, v_s, vt_s, kt_s, score_s, probs, grad_s, acc, total,
):
    quad, length = info[0], info[2]
    load_keys(0, pieces(far_a, far_b), k_s, v_s)
    forward(
        info, lambda g: (quad + 2) & 3, 1, k_s, v_s, qt, (shift0, total0, acc0),
        score_s, probs, vt_s, shift, total, acc,
    )
    for x in range(2):
        inverse = 1.0 / total[x]
        valid = jnp.where(query_rows(info, x) < length, 1.0, 0.0)
        out_t = (acc[x] * (inverse * valid)).astype(BF16)
        up_low = (upt[x].astype(F32) * inverse).astype(BF16)
        uplt[x] = up_low
        delta[x] = jnp.sum(up_low.astype(F32) * out_t.astype(F32), axis=0, keepdims=True)
        turn_rows(x, out_t, attn)
        for j in range(2):
            for h in range(GROUP):
                upl[x, lanes_at(j, h), :] = up_low[:, lanes_at(j, h)].T
    backward(
        1, k_s, v_s, kt_s, q, uplt, upl, delta, probs, None, grad_s, None, dqt
    )
    store_grads(0, k_s, v_s, pieces(out_a, out_b))


def back_side_kernel(
    q, uplt, upl, delta, shift_then, shift_last, probs, left, right, dqt0,
    dqt, out_l, out_r,
    k_s, v_s, kt_s, grad_s,
):
    factors = [jnp.exp2(shift_then[x] - shift_last[x]) for x in range(2)]
    load_keys(0, pieces(left), k_s, v_s)
    load_keys(1, pieces(right), k_s, v_s)
    backward(
        2, k_s, v_s, kt_s, q, uplt, upl, delta, probs, factors, grad_s, dqt0, dqt
    )
    store_grads(0, k_s, v_s, pieces(out_l))
    store_grads(1, k_s, v_s, pieces(out_r))


def back_own_kernel(
    q, uplt, upl, delta, shift_then, shift_last, probs, own, dqt0,
    out, dq,
    k_s, v_s, kt_s, grad_s, dqt,
):
    factors = [jnp.exp2(shift_then[x] - shift_last[x]) for x in range(2)]
    load_keys(0, pieces(own), k_s, v_s)
    backward(
        1, k_s, v_s, kt_s, q, uplt, upl, delta, probs, factors, grad_s, dqt0, dqt
    )
    store_grads(0, k_s, v_s, pieces(out))
    for x in range(2):
        turn_rows(x, (dqt[x] * SCALE).astype(BF16), dq)


def unpack_kernel(attn, dq, attended, query_grad):
    for m in range(4):
        attended[:, head_at(m, HALF)] = attn[m]
        query_grad[:, head_at(m, HALF)] = dq[m]


def both(a, b):
    return (a.astype(F32) + b.astype(F32)).astype(BF16)


def add_kernel(side_l, side_r, far_a, far_b, out_l, out_r):
    out_r[:2] = both(side_r[:2], far_a[...])
    out_r[2:] = side_r[2:]
    out_l[:2] = side_l[:2]
    out_l[2:] = both(side_l[2:], far_b[...])


def sum_kernel(own, left, right, out):
    for m in range(4):
        total = own[m].astype(F32) + left[m].astype(F32) + right[m].astype(F32)
        out[m] = total.astype(BF16)


def finish_kernel(grads, key_grad, value_grad, share):
    for m in range(4):
        key_grad[:, head_at(m)] = grads[m, :ROWS, :HEAD_DIM]
        value_grad[:, head_at(m)] = grads[m, :ROWS, HEAD_DIM:]
        share[:, head_at(m)] = grads[m, ROWS:, :HEAD_DIM]
        share[:, head_at(KV_HEADS + m)] = grads[m, ROWS:, HEAD_DIM:]


def bf16(*shape):
    return jax.ShapeDtypeStruct(shape, BF16)


def f32(*shape):
    return jax.ShapeDtypeStruct(shape, F32)


def call(kernel, outs, scratch, scalars, *operands, copies=0, products=0):
    place = pl.BlockSpec(memory_space=pl.ANY) if copies else VMEM
    scratch = [pltpu.VMEM(shape, dtype) for shape, dtype in scratch]
    if copies:
        scratch.append(pltpu.SemaphoreType.DMA((copies,)))
    return pl.pallas_call(
        kernel,
        out_shape=tuple(outs),
        in_specs=[SMEM] * len(scalars) + [place] * len(operands),
        out_specs=(VMEM,) * len(outs),
        scratch_shapes=scratch,
        compiler_params=pltpu.CompilerParams(vmem_limit_bytes=(56 if copies else 32) * 2**20),
        cost_estimate=pl.CostEstimate(
            flops=products * PROBS * LANES * HEAD_DIM * 4,
            bytes_accessed=1_000_000,
            transcendentals=0,
        ),
    )(*scalars, *operands)


def swap(x, axis):
    return lax.ppermute(x, axis, [(0, 1), (1, 0)])


def turn(x, axis, step):
    size = lax.axis_size(axis)
    return lax.ppermute(x, axis, [(i, (i + step) % size) for i in range(size)])


def quad_groups():
    groups = []
    for core in range(2):
        for quad in range(4):
            groups.append([block_of(m, quad, core) * 2 + core for m in range(4)])
    return groups


def quad_exchange(x):
    return lax.all_to_all(x, LOCAL, 0, 0, axis_index_groups=quad_groups(), tiled=True)


def quad_turn(x, step):
    pairs = []
    for i in range(32):
        xh, z, core = i // 16, i // 2 % 8, i % 2
        pairs.append((i, (xh * 8 + (z + 2 * step) % 8) * 2 + core))
    return lax.ppermute(x, LOCAL, pairs)


def rounded(x):
    return lax.optimization_barrier(x.astype(BF16))


def body(q_resp, k_resp, v_resp, k_prompt, v_prompt, d_out, lengths, counts):
    core = lax.axis_index("core")
    quad = ((lax.axis_index("z") - core) & 7) // 2
    info = jnp.stack([quad, core, lengths[0], counts[0]]).astype(jnp.int32)
    weight = (RESP_LEN / counts[0].astype(F32)).reshape(1)
    width = KV_HEADS * HEAD_DIM
    (own,) = call(
        pack_kv_kernel,
        (bf16(4, BOTH, WIDE),),
        [((ROWS, width), BF16)] * 2 + [((PROWS, width), BF16)] * 2,
        (),
        k_resp[0], v_resp[0], k_prompt, v_prompt,
        copies=4,
    )
    (qd,) = call(
        pack_qd_kernel,
        (bf16(4, ROWS, LANES),),
        [((ROWS, HEADS * HEAD_DIM), BF16)] * 2,
        (),
        q_resp[0], d_out[0],
        copies=2,
    )
    own = quad_exchange(own)
    qd = quad_exchange(qd)
    left, right = quad_turn(own, 1), quad_turn(own, -1)
    far_a, far_b = quad_turn(left[:2], 1), quad_turn(right[2:], -1)

    tiles = (2, HEAD_DIM, LANES)
    line = f32(2, 1, LANES)

    def keys(count):
        return [((count, SPAN, HEAD_DIM), BF16)] * 2

    def forward_scratch(count):
        return keys(count) + [((count, HEAD_DIM, SPAN), BF16), ((count, SPAN, LANES), F32)]

    turned = ((HEAD_DIM, SPAN), BF16)
    grad_s = ((PROBS, LANES), BF16)
    whole, pair = bf16(4, BOTH, WIDE), bf16(2, BOTH, WIDE)
    quarter = bf16(4, ROWS, HALF)
    qt, q, upt, probs1, shift1, total1, acc1 = call(
        first_kernel,
        (bf16(*tiles), bf16(2, LANES, HEAD_DIM), bf16(*tiles), bf16(1, PROBS, LANES), line, line, f32(*tiles)),
        forward_scratch(1),
        (info, weight),
        qd, own,
        products=2,
    )
    probs2, shift2, total2, acc2 = call(
        side_kernel,
        (bf16(2, PROBS, LANES), line, line, f32(*tiles)),
        forward_scratch(2),
        (info,),
        qt, left, right, shift1, total1, acc1,
        products=4,
    )
    shift3, uplt, upl, delta, dqt, attn, far_ga, far_gb = call(
        far_kernel,
        (line, bf16(*tiles), bf16(2, LANES, HEAD_DIM), line, f32(*tiles), quarter, pair, pair),
        keys(1) + [((1, HEAD_DIM, SPAN), BF16), turned, ((1, SPAN, LANES), F32)]
        + [((1, PROBS, LANES), BF16), grad_s, (tiles, F32), ((2, 1, LANES), F32)],
        (info,),
        qt, q, upt, far_a, far_b, shift2, total2, acc2,
        products=6,
    )
    far_ga, far_gb = quad_turn(far_ga, 1), quad_turn(far_gb, -1)
    attn = quad_exchange(attn)
    dqt, left_g, right_g = call(
        back_side_kernel,
        (f32(*tiles), whole, whole),
        keys(2) + [turned, grad_s],
        (),
        q, uplt, upl, delta, shift2, shift3, probs2,
        left, right, dqt,
        products=8,
    )
    left_g, right_g = call(add_kernel, (whole, whole), (), (), left_g, right_g, far_ga, far_gb)
    left_g, right_g = quad_turn(left_g, -1), quad_turn(right_g, 1)
    own_g, dq = call(
        back_own_kernel,
        (whole, quarter),
        keys(1) + [turned, grad_s, (tiles, F32)],
        (),
        q, uplt, upl, delta, shift1, shift3, probs1, own, dqt,
        products=4,
    )
    dq = quad_exchange(dq)
    left_g, right_g, attn, dq = lax.optimization_barrier((left_g, right_g, attn, dq))
    (grads,) = call(sum_kernel, (whole,), (), (), own_g, left_g, right_g)
    grads = quad_exchange(grads)
    rows = bf16(ROWS, HEADS * HEAD_DIM)
    key_grad, value_grad, share = call(
        finish_kernel,
        (bf16(ROWS, width), bf16(ROWS, width), bf16(PROWS, 2 * width)),
        (),
        (),
        grads,
    )
    for axis in ("core", "xl"):
        share = rounded(share.astype(F32) + swap(share, axis).astype(F32))
    across = share.astype(F32) + turn(share, "y", 2).astype(F32)
    beside = turn(share, "y", 1).astype(F32) + turn(share, "y", 3).astype(F32)
    share = (across + beside).astype(BF16)
    attended, query_grad = call(unpack_kernel, (rows, rows), (), (), attn, dq)
    return (
        attended[None],
        query_grad[None],
        key_grad[None],
        value_grad[None],
        share[:, :width],
        share[:, width:],
    )


def solution(mesh):
    split = Mesh(mesh.devices.reshape(2, 8, 4, 2, 2), CTX + RESP)
    rows = P(RESP, CTX, None)
    prompt = P(CTX, None)
    return jax.shard_map(
        body,
        mesh=split,
        in_specs=(rows, rows, rows, prompt, prompt, rows, P(RESP), P(RESP)),
        out_specs=(rows, rows, rows, rows, prompt, prompt),
        check_vma=False,
    )
```

```python
import math

import jax
import jax.numpy as jnp
from jax import lax
from jax.experimental import pallas as pl
from jax.experimental.pallas import tpu as pltpu
from jax.sharding import Mesh
from jax.sharding import PartitionSpec as P

HEADS = 16
KV_HEADS = 4
HEAD_DIM = 128
GROUP = HEADS // KV_HEADS
RESP_LEN = 2048
PROMPT_LEN = 1024
CTX = ("xh", "z")
LOCAL = ("xh", "z", "core")
RESP = ("y", "xl", "core")
ROWS = 128
PROWS = 64
BOTH = ROWS + PROWS
CHUNK = 256
SPAN = 3 * CHUNK
TILE_SPANS = (2 * CHUNK, 3 * CHUNK)
TILE_STARTS = (0, 2 * CHUNK)
PROBS = 5 * CHUNK
HALF = GROUP * ROWS
LANES = 2 * HALF
WIDE = 2 * HEAD_DIM
SCALE = HEAD_DIM**-0.5
SCALE2 = SCALE * math.log2(math.e)
NEG = -1e30
F32 = jnp.float32
BF16 = jnp.bfloat16
VMEM = pl.BlockSpec(memory_space=pltpu.VMEM)
SMEM = pl.BlockSpec(memory_space=pltpu.SMEM)


def dot(a, b):
    return jnp.dot(a, b, preferred_element_type=F32)


def head_at(h, width=HEAD_DIM):
    return slice(h * width, (h + 1) * width)


def lanes_at(j, h):
    return slice(j * HALF + h * HEAD_DIM, j * HALF + (h + 1) * HEAD_DIM)


def block_of(member, quad, core):
    return (member // 2) * 8 + ((quad * 2 + (member & 1) + core) & 7)


def run_copies(pairs, sems):
    copies = [
        pltpu.make_async_copy(source, to, sems.at[i]) for i, (source, to) in enumerate(pairs)
    ]
    for copy in copies:
        copy.start()
    for copy in copies:
        copy.wait()


def pack_kv_kernel(info, k, v, kp, vp, kv0, kv1, kv2, kv3, k_s, v_s, kp_s, vp_s, sems):
    mine = info[0]
    run_copies(((k, k_s), (v, v_s), (kp, kp_s), (vp, vp_s)), sems)
    for d, kv in enumerate((kv0, kv1, kv2, kv3)):
        at = pl.ds(pl.multiple_of((mine ^ d) * HEAD_DIM, HEAD_DIM), HEAD_DIM)
        kv[:ROWS, :HEAD_DIM] = k_s[:, at]
        kv[:ROWS, HEAD_DIM:] = v_s[:, at]
        kv[ROWS:, :HEAD_DIM] = kp_s[:, at]
        kv[ROWS:, HEAD_DIM:] = vp_s[:, at]


def pack_qd_kernel(info, q, do, qd0, qd1, qd2, qd3, q_s, do_s, sems):
    mine = info[0]
    run_copies(((q, q_s), (do, do_s)), sems)
    for d, qd in enumerate((qd0, qd1, qd2, qd3)):
        at = pl.ds(pl.multiple_of((mine ^ d) * HALF, HALF), HALF)
        qd[:, :HALF] = q_s[:, at]
        qd[:, HALF:] = do_s[:, at]


def rows_at(mine, d):
    return pl.ds(pl.multiple_of(CHUNK + (mine ^ d) // 2 * CHUNK + (d & 1) * ROWS, ROWS), ROWS)


def load_keys(mine, g, kvs, k_s, v_s):
    for d, kv in enumerate(kvs):
        k_s[g, rows_at(mine, d), :] = kv[:ROWS, :HEAD_DIM]
        v_s[g, rows_at(mine, d), :] = kv[:ROWS, HEAD_DIM:]
        k_s[g, head_at(d, PROWS), :] = kv[ROWS:, :HEAD_DIM]
        v_s[g, head_at(d, PROWS), :] = kv[ROWS:, HEAD_DIM:]


def query_rows(info, x):
    mine, quad, core = info[0], info[1], info[2]
    rows = []
    for j in range(2):
        start = block_of(x * 2 + ((mine & 1) ^ j), quad, core) * ROWS
        rows += [start + lax.broadcasted_iota(jnp.int32, (1, ROWS), 1)] * GROUP
    return jnp.concatenate(rows, axis=1)


def key_rows(info, x, quad):
    mine, core = info[0], info[2]
    rows = []
    for j in range(2):
        start = block_of(x * 2 + ((mine & 1) ^ j), quad, core) * ROWS
        rows.append(start + lax.broadcasted_iota(jnp.int32, (ROWS, 1), 0))
    return jnp.concatenate(rows, axis=0)


def fold(x, op):
    return op(x.reshape(x.shape[0] // 8, 8, LANES), axis=0)


def each(count, step, carry):
    return step(0, carry) if count == 1 else lax.fori_loop(0, count, step, carry)


def forward(info, quads, count, k_s, v_s, qt, before, score_s, probs, vt_s, shift, total, acc):
    def turn_values(g, carry):
        vt_s[g] = v_s[g].T
        return carry

    each(count, turn_values, 0)
    for x in range(2):
        place = query_rows(info, x)
        start, span = TILE_STARTS[x], TILE_SPANS[x]

        def score_step(g, running):
            for c in range(span // CHUNK):
                at = slice(c * CHUNK, (c + 1) * CHUNK)
                score = dot(k_s[g, at, :], qt[x])
                if c > 0:
                    score = jnp.where(key_rows(info, c - 1, quads(g)) <= place, score, NEG)
                score_s[g, at, :] = score
                running = jnp.maximum(running, fold(score, jnp.max))
            return running

        running = each(count, score_step, jnp.full((8, LANES), NEG, F32))
        now = jnp.max(running, axis=0, keepdims=True) * SCALE2
        if before is not None:
            now = jnp.maximum(now, before[0][x])
            factor = jnp.exp2(before[0][x] - now)
            acc[x] = before[2][x] * factor

        def prob_step(g, running):
            for c in range(span // CHUNK):
                prob = jnp.exp2(score_s[g, c * CHUNK : (c + 1) * CHUNK, :] * SCALE2 - now)
                running = running + fold(prob, jnp.sum)
                probs[g, start + c * CHUNK : start + (c + 1) * CHUNK, :] = prob.astype(BF16)
            part = dot(vt_s[g, :, :span], probs[g, start : start + span, :])
            if before is None:
                acc[x] = part
            else:
                acc[x] += part
            return running

        running = each(count, prob_step, jnp.zeros((8, LANES), F32))
        sums = jnp.sum(running, axis=0, keepdims=True)
        if before is not None:
            sums = sums + before[1][x] * factor
        shift[x], total[x] = now, sums


def chunk_at(c, start):
    if isinstance(c, int):
        return slice(start + c * CHUNK, start + (c + 1) * CHUNK)
    return pl.ds(pl.multiple_of(start + c * CHUNK, CHUNK), CHUNK)


def backward(count, looped, k_s, v_s, kt_s, q, uplt, upl, delta, probs, factors, grad_s, before, dqt):
    for x in range(2):
        dqt[x] = jnp.zeros((HEAD_DIM, LANES), F32) if before is None else before[x]

    def chunk(g, c, tiles):
        at = chunk_at(c, 0)
        dk, dv = None, None
        for x in tiles:
            here = chunk_at(c, TILE_STARTS[x])
            low = probs[g, here, :]
            if factors is not None:
                low = (low.astype(F32) * factors[x]).astype(BF16)
            prob_grad = dot(v_s[g, at, :], uplt[x])
            grad = (low.astype(F32) * (prob_grad - delta[x])).astype(BF16)
            grad_s[here, :] = grad
            dv_part = dot(low, upl[x])
            dk_part = dot(grad, q[x])
            dv = dv_part if dv is None else dv + dv_part
            dk = dk_part if dk is None else dk + dk_part
        k_s[g, at, :] = (dk * SCALE).astype(BF16)
        v_s[g, at, :] = dv.astype(BF16)

    def step(g, carry):
        kt_s[...] = k_s[g].T

        def two_tiles(c, carry):
            chunk(g, c, (0, 1))
            return carry

        if looped:
            lax.fori_loop(0, 2, two_tiles, 0)
        else:
            two_tiles(0, 0)
            two_tiles(1, 0)
        chunk(g, 2, (1,))
        for x in range(2):
            start, span = TILE_STARTS[x], TILE_SPANS[x]
            dqt[x] += dot(kt_s[:, :span], grad_s[start : start + span, :])
        return carry

    each(count, step, 0)


def store_grads(mine, g, k_s, v_s, outs):
    for d, out in enumerate(outs):
        out[:ROWS, :HEAD_DIM] = k_s[g, rows_at(mine, d), :]
        out[:ROWS, HEAD_DIM:] = v_s[g, rows_at(mine, d), :]
        out[ROWS:, :HEAD_DIM] = k_s[g, head_at(d, PROWS), :]
        out[ROWS:, HEAD_DIM:] = v_s[g, head_at(d, PROWS), :]


def pieces(*parts):
    return [part.at[d] for part in parts for d in range(part.shape[0])]


def first_kernel(
    info, weight, qd0, qd1, qd2, qd3, own_a, own_b,
    qt, q, upt, probs, shift, total, acc,
    k_s, v_s, vt_s, score_s,
):
    mine, quad, core, count = info[0], info[1], info[2], info[4]
    load_keys(mine, 0, pieces(own_a, own_b), k_s, v_s)
    for d, qd in enumerate((qd0, qd1, qd2, qd3)):
        x = (mine ^ d) // 2
        row = block_of(mine ^ d, quad, core) * ROWS
        row = row + lax.broadcasted_iota(jnp.int32, (1, ROWS), 1)
        row_weight = jnp.where(row < count, weight[0], 0.0)
        for h in range(GROUP):
            cols = lanes_at(d & 1, h)
            q_head = qd[:, head_at(h)]
            q[x, cols, :] = q_head
            qt[x, :, cols] = q_head.T
            grad = qd[:, HALF + h * HEAD_DIM : HALF + (h + 1) * HEAD_DIM]
            upt[x, :, cols] = (grad.T.astype(F32) * row_weight).astype(BF16)
    forward(
        info, lambda g: quad, 1, k_s, v_s, qt, None, score_s, probs, vt_s, shift, total, acc
    )


def side_kernel(
    info, qt, left_a, left_b, right_a, right_b, shift0, total0, acc0,
    probs, shift, total, acc,
    k_s, v_s, vt_s, score_s,
):
    mine, quad = info[0], info[1]
    load_keys(mine, 0, pieces(left_a, left_b), k_s, v_s)
    load_keys(mine, 1, pieces(right_a, right_b), k_s, v_s)
    forward(
        info, lambda g: (quad + 3 + 2 * g) & 3, 2, k_s, v_s, qt, (shift0, total0, acc0),
        score_s, probs, vt_s, shift, total, acc,
    )


def far_kernel(
    info, qt, q, upt, far_a, far_b, shift0, total0, acc0,
    shift, uplt, upl, delta, dqt, attn, out_a, out_b,
    k_s, v_s, vt_s, kt_s, score_s, probs, grad_s, acc, total,
):
    mine, quad, length = info[0], info[1], info[3]
    load_keys(mine, 0, pieces(far_a, far_b), k_s, v_s)
    forward(
        info, lambda g: (quad + 2) & 3, 1, k_s, v_s, qt, (shift0, total0, acc0),
        score_s, probs, vt_s, shift, total, acc,
    )
    for x in range(2):
        inverse = 1.0 / total[x]
        valid = jnp.where(query_rows(info, x) < length, 1.0, 0.0)
        out_t = (acc[x] * (inverse * valid)).astype(BF16)
        up_low = (upt[x].astype(F32) * inverse).astype(BF16)
        uplt[x] = up_low
        delta[x] = jnp.sum(up_low.astype(F32) * out_t.astype(F32), axis=0, keepdims=True)
        attn[x] = out_t
        for j in range(2):
            for h in range(GROUP):
                upl[x, lanes_at(j, h), :] = up_low[:, lanes_at(j, h)].T
    backward(
        1, False, k_s, v_s, kt_s, q, uplt, upl, delta, probs, None, grad_s, None, dqt
    )
    store_grads(mine, 0, k_s, v_s, pieces(out_a, out_b))


def back_side_kernel(
    info, q, uplt, upl, delta, shift_then, shift_last, probs,
    left_a, left_b, right_a, right_b, dqt0,
    dqt, out_l, out_r,
    k_s, v_s, kt_s, grad_s,
):
    mine = info[0]
    factors = [jnp.exp2(shift_then[x] - shift_last[x]) for x in range(2)]
    load_keys(mine, 0, pieces(left_a, left_b), k_s, v_s)
    load_keys(mine, 1, pieces(right_a, right_b), k_s, v_s)
    backward(
        2, False, k_s, v_s, kt_s, q, uplt, upl, delta, probs, factors, grad_s, dqt0, dqt
    )
    store_grads(mine, 0, k_s, v_s, pieces(out_l))
    store_grads(mine, 1, k_s, v_s, pieces(out_r))


def back_own_kernel(
    info, q, uplt, upl, delta, shift_then, shift_last, probs, own_a, own_b, dqt0, attn,
    out, od0, od1, od2, od3,
    k_s, v_s, kt_s, grad_s, dqt, dq_s,
):
    mine = info[0]
    factors = [jnp.exp2(shift_then[x] - shift_last[x]) for x in range(2)]
    load_keys(mine, 0, pieces(own_a, own_b), k_s, v_s)
    backward(
        1, True, k_s, v_s, kt_s, q, uplt, upl, delta, probs, factors, grad_s, dqt0, dqt
    )
    store_grads(mine, 0, k_s, v_s, pieces(out))
    for x in range(2):
        dq_s[x] = (dqt[x] * SCALE).astype(BF16)
    for d, od in enumerate((od0, od1, od2, od3)):
        x = (mine ^ d) // 2
        for h in range(GROUP):
            od[:, head_at(h)] = attn[x, :, lanes_at(d & 1, h)].T
            od[:, HALF + h * HEAD_DIM : HALF + (h + 1) * HEAD_DIM] = dq_s[
                x, :, lanes_at(d & 1, h)
            ].T


def unpack_kernel(info, od0, od1, od2, od3, attended, query_grad):
    mine = info[0]
    for d, od in enumerate((od0, od1, od2, od3)):
        at = pl.ds(pl.multiple_of((mine ^ d) * HALF, HALF), HALF)
        attended[:, at] = od[:, :HALF]
        query_grad[:, at] = od[:, HALF:]


def both(a, b):
    return (a.astype(F32) + b.astype(F32)).astype(BF16)


def add_kernel(side_l, side_r, far_a, far_b, out_l, out_r):
    out_r[:2] = both(side_r[:2], far_a[...])
    out_r[2:] = side_r[2:]
    out_l[:2] = side_l[:2]
    out_l[2:] = both(side_l[2:], far_b[...])


def sum_kernel(own, left, right, *outs):
    for d, out in enumerate(outs):
        total = own[d].astype(F32) + left[d].astype(F32) + right[d].astype(F32)
        out[...] = total.astype(BF16)


def finish_kernel(info, g0, g1, g2, g3, key_grad, value_grad, share):
    mine = info[0]
    for d, g in enumerate((g0, g1, g2, g3)):
        at = pl.ds(pl.multiple_of((mine ^ d) * HEAD_DIM, HEAD_DIM), HEAD_DIM)
        key_grad[:, at] = g[:ROWS, :HEAD_DIM]
        value_grad[:, at] = g[:ROWS, HEAD_DIM:]
        share[:, at] = g[ROWS:, :HEAD_DIM]
        at = pl.ds(pl.multiple_of(KV_HEADS * HEAD_DIM + (mine ^ d) * HEAD_DIM, HEAD_DIM), HEAD_DIM)
        share[:, at] = g[ROWS:, HEAD_DIM:]


def bf16(*shape):
    return jax.ShapeDtypeStruct(shape, BF16)


def f32(*shape):
    return jax.ShapeDtypeStruct(shape, F32)


def call(kernel, outs, scratch, scalars, *operands, copies=0, products=0):
    place = pl.BlockSpec(memory_space=pl.ANY) if copies else VMEM
    scratch = [pltpu.VMEM(shape, dtype) for shape, dtype in scratch]
    if copies:
        scratch.append(pltpu.SemaphoreType.DMA((copies,)))
    return pl.pallas_call(
        kernel,
        out_shape=tuple(outs),
        in_specs=[SMEM] * len(scalars) + [place] * len(operands),
        out_specs=(VMEM,) * len(outs),
        scratch_shapes=scratch,
        compiler_params=pltpu.CompilerParams(vmem_limit_bytes=(56 if copies else 32) * 2**20),
        cost_estimate=pl.CostEstimate(
            flops=products * PROBS * LANES * HEAD_DIM * 4,
            bytes_accessed=1_000_000,
            transcendentals=0,
        ),
    )(*scalars, *operands)


def swap(x, axis):
    return lax.ppermute(x, axis, [(0, 1), (1, 0)])


def turn(x, axis, step):
    size = lax.axis_size(axis)
    return lax.ppermute(x, axis, [(i, (i + step) % size) for i in range(size)])


def local_permute(x, place):
    pairs = []
    for i in range(32):
        xh, z, core = i // 16, i // 2 % 8, i % 2
        xh, z = place(xh, (z - core) % 8)
        pairs.append((i, (xh * 8 + (z + core) % 8) * 2 + core))
    return lax.ppermute(x, LOCAL, pairs)


def partner(x, d):
    return local_permute(x, lambda xh, z: (xh ^ (d // 2), z ^ (d & 1)))


def quad_turn(x, step):
    return local_permute(x, lambda xh, z: (xh, (z + 2 * step) % 8))


def rounded(x):
    return lax.optimization_barrier(x.astype(BF16))


def body(q_resp, k_resp, v_resp, k_prompt, v_prompt, d_out, lengths, counts):
    core = lax.axis_index("core")
    z = (lax.axis_index("z") - core) & 7
    mine = lax.axis_index("xh") * 2 + (z & 1)
    info = jnp.stack([mine, z // 2, core, lengths[0], counts[0]]).astype(jnp.int32)
    weight = (RESP_LEN / counts[0].astype(F32)).reshape(1)
    spot = mine.reshape(1).astype(jnp.int32)
    width = KV_HEADS * HEAD_DIM
    kv = list(
        call(
            pack_kv_kernel,
            (bf16(BOTH, WIDE),) * 4,
            [((ROWS, width), BF16)] * 2 + [((PROWS, width), BF16)] * 2,
            (spot,),
            k_resp[0], v_resp[0], k_prompt, v_prompt,
            copies=4,
        )
    )
    qd = list(
        call(
            pack_qd_kernel,
            (bf16(ROWS, LANES),) * 4,
            [((ROWS, HEADS * HEAD_DIM), BF16)] * 2,
            (spot,),
            q_resp[0], d_out[0],
            copies=2,
        )
    )
    for d in (1, 2, 3):
        kv[d] = partner(kv[d], d)
    for d in (1, 2, 3):
        qd[d] = partner(qd[d], d)
    own_a, own_b = jnp.stack(kv[:2]), jnp.stack(kv[2:])
    left_a, right_b = quad_turn(own_a, 1), quad_turn(own_b, -1)
    left_b, right_a = quad_turn(own_b, 1), quad_turn(own_a, -1)
    far_a, far_b = quad_turn(left_a, 1), quad_turn(right_b, -1)

    tiles = (2, HEAD_DIM, LANES)
    line = f32(2, 1, LANES)

    def keys(count):
        return [((count, SPAN, HEAD_DIM), BF16)] * 2

    def forward_scratch(count):
        return keys(count) + [((count, HEAD_DIM, SPAN), BF16), ((count, SPAN, LANES), F32)]

    turned = ((HEAD_DIM, SPAN), BF16)
    grad_s = ((PROBS, LANES), BF16)
    whole, pair = bf16(4, BOTH, WIDE), bf16(2, BOTH, WIDE)
    qt, q, upt, probs1, shift1, total1, acc1 = call(
        first_kernel,
        (bf16(*tiles), bf16(2, LANES, HEAD_DIM), bf16(*tiles), bf16(1, PROBS, LANES), line, line, f32(*tiles)),
        forward_scratch(1),
        (info, weight),
        *qd, own_a, own_b,
        products=2,
    )
    probs2, shift2, total2, acc2 = call(
        side_kernel,
        (bf16(2, PROBS, LANES), line, line, f32(*tiles)),
        forward_scratch(2),
        (info,),
        qt, left_a, left_b, right_a, right_b, shift1, total1, acc1,
        products=4,
    )
    shift3, uplt, upl, delta, dqt, attn, far_ga, far_gb = call(
        far_kernel,
        (line, bf16(*tiles), bf16(2, LANES, HEAD_DIM), line, f32(*tiles), bf16(*tiles), pair, pair),
        keys(1) + [((1, HEAD_DIM, SPAN), BF16), turned, ((1, SPAN, LANES), F32)]
        + [((1, PROBS, LANES), BF16), grad_s, (tiles, F32), ((2, 1, LANES), F32)],
        (info,),
        qt, q, upt, far_a, far_b, shift2, total2, acc2,
        products=6,
    )
    far_ga, far_gb = quad_turn(far_ga, 1), quad_turn(far_gb, -1)
    dqt, left_g, right_g = call(
        back_side_kernel,
        (f32(*tiles), whole, whole),
        keys(2) + [turned, grad_s],
        (info,),
        q, uplt, upl, delta, shift2, shift3, probs2,
        left_a, left_b, right_a, right_b, dqt,
        products=8,
    )
    left_g, right_g = call(add_kernel, (whole, whole), (), (), left_g, right_g, far_ga, far_gb)
    left_g, right_g = quad_turn(left_g, -1), quad_turn(right_g, 1)
    own_g, *od = call(
        back_own_kernel,
        (whole,) + (bf16(ROWS, LANES),) * 4,
        keys(1) + [turned, grad_s, (tiles, F32), (tiles, BF16)],
        (info,),
        q, uplt, upl, delta, shift1, shift3, probs1, own_a, own_b, dqt, attn,
        products=4,
    )
    od[1], od[2] = partner(od[1], 1), partner(od[2], 2)
    left_g, right_g, od[3] = lax.optimization_barrier((left_g, right_g, od[3]))
    od[3] = partner(od[3], 3)
    grads = list(call(sum_kernel, (bf16(BOTH, WIDE),) * 4, (), (), own_g, left_g, right_g))
    for d in (1, 2, 3):
        grads[d] = partner(grads[d], d)
    tied = lax.optimization_barrier((*grads, od[1], od[2]))
    grads, od[1:3] = tied[:4], tied[4:]
    rows = bf16(ROWS, HEADS * HEAD_DIM)
    key_grad, value_grad, share = call(
        finish_kernel,
        (bf16(ROWS, width), bf16(ROWS, width), bf16(PROWS, 2 * width)),
        (),
        (info,),
        *grads,
    )
    for axis in ("core", "xl"):
        share = rounded(share.astype(F32) + swap(share, axis).astype(F32))
    share, od[3] = lax.optimization_barrier((share, od[3]))
    across = share.astype(F32) + turn(share, "y", 2).astype(F32)
    beside = turn(share, "y", 1).astype(F32) + turn(share, "y", 3).astype(F32)
    share = (across + beside).astype(BF16)
    attended, query_grad = call(unpack_kernel, (rows, rows), (), (info,), *od)
    return (
        attended[None],
        query_grad[None],
        key_grad[None],
        value_grad[None],
        share[:, :width],
        share[:, width:],
    )


def solution(mesh):
    split = Mesh(mesh.devices.reshape(2, 8, 4, 2, 2), CTX + RESP)
    rows = P(RESP, CTX, None)
    prompt = P(CTX, None)
    return jax.shard_map(
        body,
        mesh=split,
        in_specs=(rows, rows, rows, prompt, prompt, rows, P(RESP), P(RESP)),
        out_specs=(rows, rows, rows, rows, prompt, prompt),
        check_vma=False,
    )
```

```python
import math

import jax
import jax.numpy as jnp
from jax import lax
from jax.experimental import pallas as pl
from jax.experimental.pallas import tpu as pltpu
from jax.sharding import Mesh
from jax.sharding import PartitionSpec as P

HEADS = 16
KV_HEADS = 4
HEAD_DIM = 128
GROUP = HEADS // KV_HEADS
RESP_LEN = 2048
PROMPT_LEN = 1024
CTX = ("xh", "z")
LOCAL = ("xh", "z", "core")
RESP = ("y", "xl", "core")
ROWS = 128
PROWS = 64
BOTH = ROWS + PROWS
CHUNK = 256
SPAN = 3 * CHUNK
TILE_SPANS = (2 * CHUNK, 3 * CHUNK)
TILE_STARTS = (0, 2 * CHUNK)
PROBS = 5 * CHUNK
HALF = GROUP * ROWS
LANES = 2 * HALF
WIDE = 2 * HEAD_DIM
SCALE = HEAD_DIM**-0.5
SCALE2 = SCALE * math.log2(math.e)
NEG = -1e30
F32 = jnp.float32
BF16 = jnp.bfloat16
VMEM = pl.BlockSpec(memory_space=pltpu.VMEM)
SMEM = pl.BlockSpec(memory_space=pltpu.SMEM)


def dot(a, b):
    return jnp.dot(a, b, preferred_element_type=F32)


def head_at(h, width=HEAD_DIM):
    return slice(h * width, (h + 1) * width)


def lanes_at(j, h):
    return slice(j * HALF + h * HEAD_DIM, j * HALF + (h + 1) * HEAD_DIM)


def block_of(member, quad, core):
    return (member // 2) * 8 + ((quad * 2 + (member & 1) + core) & 7)


def run_copies(pairs, sems):
    copies = [
        pltpu.make_async_copy(source, to, sems.at[i]) for i, (source, to) in enumerate(pairs)
    ]
    for copy in copies:
        copy.start()
    for copy in copies:
        copy.wait()


def pack_kv_kernel(info, k, v, kp, vp, kv0, kv1, kv2, kv3, k_s, v_s, kp_s, vp_s, sems):
    mine = info[0]
    run_copies(((k, k_s), (v, v_s), (kp, kp_s), (vp, vp_s)), sems)
    for d, kv in enumerate((kv0, kv1, kv2, kv3)):
        at = pl.ds(pl.multiple_of((mine ^ d) * HEAD_DIM, HEAD_DIM), HEAD_DIM)
        kv[:ROWS, :HEAD_DIM] = k_s[:, at]
        kv[:ROWS, HEAD_DIM:] = v_s[:, at]
        kv[ROWS:, :HEAD_DIM] = kp_s[:, at]
        kv[ROWS:, HEAD_DIM:] = vp_s[:, at]


def pack_qd_kernel(info, q, do, qd0, qd1, qd2, qd3, q_s, do_s, sems):
    mine = info[0]
    run_copies(((q, q_s), (do, do_s)), sems)
    for d, qd in enumerate((qd0, qd1, qd2, qd3)):
        at = pl.ds(pl.multiple_of((mine ^ d) * HALF, HALF), HALF)
        qd[:, :HALF] = q_s[:, at]
        qd[:, HALF:] = do_s[:, at]


def rows_at(mine, d):
    return pl.ds(pl.multiple_of(CHUNK + (mine ^ d) // 2 * CHUNK + (d & 1) * ROWS, ROWS), ROWS)


def load_keys(mine, g, kvs, k_s, v_s):
    for d, kv in enumerate(kvs):
        k_s[g, rows_at(mine, d), :] = kv[:ROWS, :HEAD_DIM]
        v_s[g, rows_at(mine, d), :] = kv[:ROWS, HEAD_DIM:]
        k_s[g, head_at(d, PROWS), :] = kv[ROWS:, :HEAD_DIM]
        v_s[g, head_at(d, PROWS), :] = kv[ROWS:, HEAD_DIM:]


def query_rows(info, x):
    mine, quad, core = info[0], info[1], info[2]
    rows = []
    for j in range(2):
        start = block_of(x * 2 + ((mine & 1) ^ j), quad, core) * ROWS
        rows += [start + lax.broadcasted_iota(jnp.int32, (1, ROWS), 1)] * GROUP
    return jnp.concatenate(rows, axis=1)


def key_rows(info, x, quad):
    mine, core = info[0], info[2]
    rows = []
    for j in range(2):
        start = block_of(x * 2 + ((mine & 1) ^ j), quad, core) * ROWS
        rows.append(start + lax.broadcasted_iota(jnp.int32, (ROWS, 1), 0))
    return jnp.concatenate(rows, axis=0)


def fold(x, op):
    return op(x.reshape(x.shape[0] // 8, 8, LANES), axis=0)


def each(count, step, carry):
    return step(0, carry) if count == 1 else lax.fori_loop(0, count, step, carry)


def forward(info, quads, count, k_s, v_s, qt, before, score_s, probs, vt_s, shift, total, acc):
    def turn_values(g, carry):
        vt_s[g] = v_s[g].T
        return carry

    each(count, turn_values, 0)
    for x in range(2):
        place = query_rows(info, x)
        start, span = TILE_STARTS[x], TILE_SPANS[x]

        def score_step(g, running):
            for c in range(span // CHUNK):
                at = slice(c * CHUNK, (c + 1) * CHUNK)
                score = dot(k_s[g, at, :], qt[x])
                if c > 0:
                    score = jnp.where(key_rows(info, c - 1, quads(g)) <= place, score, NEG)
                score_s[g, at, :] = score
                running = jnp.maximum(running, fold(score, jnp.max))
            return running

        running = each(count, score_step, jnp.full((8, LANES), NEG, F32))
        now = jnp.max(running, axis=0, keepdims=True) * SCALE2
        if before is not None:
            now = jnp.maximum(now, before[0][x])
            factor = jnp.exp2(before[0][x] - now)
            acc[x] = before[2][x] * factor

        def prob_step(g, running):
            for c in range(span // CHUNK):
                prob = jnp.exp2(score_s[g, c * CHUNK : (c + 1) * CHUNK, :] * SCALE2 - now)
                running = running + fold(prob, jnp.sum)
                probs[g, start + c * CHUNK : start + (c + 1) * CHUNK, :] = prob.astype(BF16)
            part = dot(vt_s[g, :, :span], probs[g, start : start + span, :])
            if before is None:
                acc[x] = part
            else:
                acc[x] += part
            return running

        running = each(count, prob_step, jnp.zeros((8, LANES), F32))
        sums = jnp.sum(running, axis=0, keepdims=True)
        if before is not None:
            sums = sums + before[1][x] * factor
        shift[x], total[x] = now, sums


def chunk_at(c, start):
    if isinstance(c, int):
        return slice(start + c * CHUNK, start + (c + 1) * CHUNK)
    return pl.ds(pl.multiple_of(start + c * CHUNK, CHUNK), CHUNK)


def backward(count, looped, k_s, v_s, kt_s, q, uplt, upl, delta, probs, factors, grad_s, before, dqt):
    for x in range(2):
        dqt[x] = jnp.zeros((HEAD_DIM, LANES), F32) if before is None else before[x]

    def chunk(g, c, tiles):
        at = chunk_at(c, 0)
        dk, dv = None, None
        for x in tiles:
            here = chunk_at(c, TILE_STARTS[x])
            low = probs[g, here, :]
            if factors is not None:
                low = (low.astype(F32) * factors[x]).astype(BF16)
            prob_grad = dot(v_s[g, at, :], uplt[x])
            grad = (low.astype(F32) * (prob_grad - delta[x])).astype(BF16)
            grad_s[here, :] = grad
            dv_part = dot(low, upl[x])
            dk_part = dot(grad, q[x])
            dv = dv_part if dv is None else dv + dv_part
            dk = dk_part if dk is None else dk + dk_part
        k_s[g, at, :] = (dk * SCALE).astype(BF16)
        v_s[g, at, :] = dv.astype(BF16)

    def step(g, carry):
        kt_s[...] = k_s[g].T

        def two_tiles(c, carry):
            chunk(g, c, (0, 1))
            return carry

        if looped:
            lax.fori_loop(0, 2, two_tiles, 0)
        else:
            two_tiles(0, 0)
            two_tiles(1, 0)
        chunk(g, 2, (1,))
        for x in range(2):
            start, span = TILE_STARTS[x], TILE_SPANS[x]
            dqt[x] += dot(kt_s[:, :span], grad_s[start : start + span, :])
        return carry

    each(count, step, 0)


def store_grads(mine, g, k_s, v_s, outs):
    for d, out in enumerate(outs):
        out[:ROWS, :HEAD_DIM] = k_s[g, rows_at(mine, d), :]
        out[:ROWS, HEAD_DIM:] = v_s[g, rows_at(mine, d), :]
        out[ROWS:, :HEAD_DIM] = k_s[g, head_at(d, PROWS), :]
        out[ROWS:, HEAD_DIM:] = v_s[g, head_at(d, PROWS), :]


def pieces(*parts):
    return [part.at[d] for part in parts for d in range(part.shape[0])]


def first_kernel(
    info, weight, qd0, qd1, qd2, qd3, own_a, own_b,
    qt, q, upt, probs, shift, total, acc,
    k_s, v_s, vt_s, score_s,
):
    mine, quad, core, count = info[0], info[1], info[2], info[4]
    load_keys(mine, 0, pieces(own_a, own_b), k_s, v_s)
    for d, qd in enumerate((qd0, qd1, qd2, qd3)):
        x = (mine ^ d) // 2
        row = block_of(mine ^ d, quad, core) * ROWS
        row = row + lax.broadcasted_iota(jnp.int32, (1, ROWS), 1)
        row_weight = jnp.where(row < count, weight[0], 0.0)
        for h in range(GROUP):
            cols = lanes_at(d & 1, h)
            q_head = qd[:, head_at(h)]
            q[x, cols, :] = q_head
            qt[x, :, cols] = q_head.T
            grad = qd[:, HALF + h * HEAD_DIM : HALF + (h + 1) * HEAD_DIM]
            upt[x, :, cols] = (grad.T.astype(F32) * row_weight).astype(BF16)
    forward(
        info, lambda g: quad, 1, k_s, v_s, qt, None, score_s, probs, vt_s, shift, total, acc
    )


def side_kernel(
    info, qt, left_a, left_b, right_a, right_b, shift0, total0, acc0,
    probs, shift, total, acc,
    k_s, v_s, vt_s, score_s,
):
    mine, quad = info[0], info[1]
    load_keys(mine, 0, pieces(left_a, left_b), k_s, v_s)
    load_keys(mine, 1, pieces(right_a, right_b), k_s, v_s)
    forward(
        info, lambda g: (quad + 3 + 2 * g) & 3, 2, k_s, v_s, qt, (shift0, total0, acc0),
        score_s, probs, vt_s, shift, total, acc,
    )


def far_kernel(
    info, qt, q, upt, far_a, far_b, shift0, total0, acc0,
    shift, uplt, upl, delta, dqt, attn, out_a, out_b,
    k_s, v_s, vt_s, kt_s, score_s, probs, grad_s, acc, total,
):
    mine, quad, length = info[0], info[1], info[3]
    load_keys(mine, 0, pieces(far_a, far_b), k_s, v_s)
    forward(
        info, lambda g: (quad + 2) & 3, 1, k_s, v_s, qt, (shift0, total0, acc0),
        score_s, probs, vt_s, shift, total, acc,
    )
    for x in range(2):
        inverse = 1.0 / total[x]
        valid = jnp.where(query_rows(info, x) < length, 1.0, 0.0)
        out_t = (acc[x] * (inverse * valid)).astype(BF16)
        up_low = (upt[x].astype(F32) * inverse).astype(BF16)
        uplt[x] = up_low
        delta[x] = jnp.sum(up_low.astype(F32) * out_t.astype(F32), axis=0, keepdims=True)
        attn[x] = out_t
        for j in range(2):
            for h in range(GROUP):
                upl[x, lanes_at(j, h), :] = up_low[:, lanes_at(j, h)].T
    backward(
        1, False, k_s, v_s, kt_s, q, uplt, upl, delta, probs, None, grad_s, None, dqt
    )
    store_grads(mine, 0, k_s, v_s, pieces(out_a, out_b))


def back_side_kernel(
    info, q, uplt, upl, delta, shift_then, shift_last, probs,
    left_a, left_b, right_a, right_b, dqt0,
    dqt, out_l, out_r,
    k_s, v_s, kt_s, grad_s,
):
    mine = info[0]
    factors = [jnp.exp2(shift_then[x] - shift_last[x]) for x in range(2)]
    load_keys(mine, 0, pieces(left_a, left_b), k_s, v_s)
    load_keys(mine, 1, pieces(right_a, right_b), k_s, v_s)
    backward(
        2, False, k_s, v_s, kt_s, q, uplt, upl, delta, probs, factors, grad_s, dqt0, dqt
    )
    store_grads(mine, 0, k_s, v_s, pieces(out_l))
    store_grads(mine, 1, k_s, v_s, pieces(out_r))


def back_own_kernel(
    info, q, uplt, upl, delta, shift_then, shift_last, probs, own_a, own_b, dqt0, attn,
    out, od0, od1, od2, od3,
    k_s, v_s, kt_s, grad_s, dqt, dq_s,
):
    mine = info[0]
    factors = [jnp.exp2(shift_then[x] - shift_last[x]) for x in range(2)]
    load_keys(mine, 0, pieces(own_a, own_b), k_s, v_s)
    backward(
        1, True, k_s, v_s, kt_s, q, uplt, upl, delta, probs, factors, grad_s, dqt0, dqt
    )
    store_grads(mine, 0, k_s, v_s, pieces(out))
    for x in range(2):
        dq_s[x] = (dqt[x] * SCALE).astype(BF16)
    for d, od in enumerate((od0, od1, od2, od3)):
        x = (mine ^ d) // 2
        for h in range(GROUP):
            od[:, head_at(h)] = attn[x, :, lanes_at(d & 1, h)].T
            od[:, HALF + h * HEAD_DIM : HALF + (h + 1) * HEAD_DIM] = dq_s[
                x, :, lanes_at(d & 1, h)
            ].T


def unpack_kernel(info, od0, od1, od2, od3, attended, query_grad):
    mine = info[0]
    for d, od in enumerate((od0, od1, od2, od3)):
        at = pl.ds(pl.multiple_of((mine ^ d) * HALF, HALF), HALF)
        attended[:, at] = od[:, :HALF]
        query_grad[:, at] = od[:, HALF:]


def both(a, b):
    return (a.astype(F32) + b.astype(F32)).astype(BF16)


def add_kernel(side_l, side_r, far_a, far_b, out_l, out_r):
    out_r[:2] = both(side_r[:2], far_a[...])
    out_r[2:] = side_r[2:]
    out_l[:2] = side_l[:2]
    out_l[2:] = both(side_l[2:], far_b[...])


def sum_kernel(own, left, right, *outs):
    for d, out in enumerate(outs):
        total = own[d].astype(F32) + left[d].astype(F32) + right[d].astype(F32)
        out[...] = total.astype(BF16)


def share_kernel(info, g0, g1, g2, g3, keep, send):
    mine, first = info[0], info[2] == 0
    for d, g in enumerate((g0, g1, g2, g3)):
        at = pl.ds(pl.multiple_of((mine ^ d) * HEAD_DIM, HEAD_DIM), HEAD_DIM)
        keys, values = g[ROWS:, :HEAD_DIM], g[ROWS:, HEAD_DIM:]
        keep[:, at] = jnp.where(first, keys, values)
        send[:, at] = jnp.where(first, values, keys)


def finish_kernel(info, g0, g1, g2, g3, key_grad, value_grad):
    mine = info[0]
    for d, g in enumerate((g0, g1, g2, g3)):
        at = pl.ds(pl.multiple_of((mine ^ d) * HEAD_DIM, HEAD_DIM), HEAD_DIM)
        key_grad[:, at] = g[:ROWS, :HEAD_DIM]
        value_grad[:, at] = g[:ROWS, HEAD_DIM:]


def bf16(*shape):
    return jax.ShapeDtypeStruct(shape, BF16)


def f32(*shape):
    return jax.ShapeDtypeStruct(shape, F32)


def call(kernel, outs, scratch, scalars, *operands, copies=0, products=0):
    place = pl.BlockSpec(memory_space=pl.ANY) if copies else VMEM
    scratch = [pltpu.VMEM(shape, dtype) for shape, dtype in scratch]
    if copies:
        scratch.append(pltpu.SemaphoreType.DMA((copies,)))
    return pl.pallas_call(
        kernel,
        out_shape=tuple(outs),
        in_specs=[SMEM] * len(scalars) + [place] * len(operands),
        out_specs=(VMEM,) * len(outs),
        scratch_shapes=scratch,
        compiler_params=pltpu.CompilerParams(vmem_limit_bytes=(56 if copies else 32) * 2**20),
        cost_estimate=pl.CostEstimate(
            flops=products * PROBS * LANES * HEAD_DIM * 4,
            bytes_accessed=1_000_000,
            transcendentals=0,
        ),
    )(*scalars, *operands)


def swap(x, axis):
    return lax.ppermute(x, axis, [(0, 1), (1, 0)])


def turn(x, axis, step):
    size = lax.axis_size(axis)
    return lax.ppermute(x, axis, [(i, (i + step) % size) for i in range(size)])


def local_permute(x, place):
    pairs = []
    for i in range(32):
        xh, z, core = i // 16, i // 2 % 8, i % 2
        xh, z = place(xh, (z - core) % 8)
        pairs.append((i, (xh * 8 + (z + core) % 8) * 2 + core))
    return lax.ppermute(x, LOCAL, pairs)


def partner(x, d):
    return local_permute(x, lambda xh, z: (xh ^ (d // 2), z ^ (d & 1)))


def quad_turn(x, step):
    return local_permute(x, lambda xh, z: (xh, (z + 2 * step) % 8))


def rounded(x):
    return lax.optimization_barrier(x.astype(BF16))


def body(q_resp, k_resp, v_resp, k_prompt, v_prompt, d_out, lengths, counts):
    core = lax.axis_index("core")
    z = (lax.axis_index("z") - core) & 7
    mine = lax.axis_index("xh") * 2 + (z & 1)
    info = jnp.stack([mine, z // 2, core, lengths[0], counts[0]]).astype(jnp.int32)
    weight = (RESP_LEN / counts[0].astype(F32)).reshape(1)
    spot = mine.reshape(1).astype(jnp.int32)
    width = KV_HEADS * HEAD_DIM
    kv = list(
        call(
            pack_kv_kernel,
            (bf16(BOTH, WIDE),) * 4,
            [((ROWS, width), BF16)] * 2 + [((PROWS, width), BF16)] * 2,
            (spot,),
            k_resp[0], v_resp[0], k_prompt, v_prompt,
            copies=4,
        )
    )
    qd = list(
        call(
            pack_qd_kernel,
            (bf16(ROWS, LANES),) * 4,
            [((ROWS, HEADS * HEAD_DIM), BF16)] * 2,
            (spot,),
            q_resp[0], d_out[0],
            copies=2,
        )
    )
    for d in (1, 2, 3):
        kv[d] = partner(kv[d], d)
    for d in (1, 2, 3):
        qd[d] = partner(qd[d], d)
    own_a, own_b = jnp.stack(kv[:2]), jnp.stack(kv[2:])
    left_a, right_b = quad_turn(own_a, 1), quad_turn(own_b, -1)
    left_b, right_a = quad_turn(own_b, 1), quad_turn(own_a, -1)
    far_a, far_b = quad_turn(left_a, 1), quad_turn(right_b, -1)

    tiles = (2, HEAD_DIM, LANES)
    line = f32(2, 1, LANES)

    def keys(count):
        return [((count, SPAN, HEAD_DIM), BF16)] * 2

    def forward_scratch(count):
        return keys(count) + [((count, HEAD_DIM, SPAN), BF16), ((count, SPAN, LANES), F32)]

    turned = ((HEAD_DIM, SPAN), BF16)
    grad_s = ((PROBS, LANES), BF16)
    whole, pair = bf16(4, BOTH, WIDE), bf16(2, BOTH, WIDE)
    qt, q, upt, probs1, shift1, total1, acc1 = call(
        first_kernel,
        (bf16(*tiles), bf16(2, LANES, HEAD_DIM), bf16(*tiles), bf16(1, PROBS, LANES), line, line, f32(*tiles)),
        forward_scratch(1),
        (info, weight),
        *qd, own_a, own_b,
        products=2,
    )
    probs2, shift2, total2, acc2 = call(
        side_kernel,
        (bf16(2, PROBS, LANES), line, line, f32(*tiles)),
        forward_scratch(2),
        (info,),
        qt, left_a, left_b, right_a, right_b, shift1, total1, acc1,
        products=4,
    )
    shift3, uplt, upl, delta, dqt, attn, far_ga, far_gb = call(
        far_kernel,
        (line, bf16(*tiles), bf16(2, LANES, HEAD_DIM), line, f32(*tiles), bf16(*tiles), pair, pair),
        keys(1) + [((1, HEAD_DIM, SPAN), BF16), turned, ((1, SPAN, LANES), F32)]
        + [((1, PROBS, LANES), BF16), grad_s, (tiles, F32), ((2, 1, LANES), F32)],
        (info,),
        qt, q, upt, far_a, far_b, shift2, total2, acc2,
        products=6,
    )
    far_ga, far_gb = quad_turn(far_ga, 1), quad_turn(far_gb, -1)
    dqt, left_g, right_g = call(
        back_side_kernel,
        (f32(*tiles), whole, whole),
        keys(2) + [turned, grad_s],
        (info,),
        q, uplt, upl, delta, shift2, shift3, probs2,
        left_a, left_b, right_a, right_b, dqt,
        products=8,
    )
    left_g, right_g = call(add_kernel, (whole, whole), (), (), left_g, right_g, far_ga, far_gb)
    left_g, right_g = quad_turn(left_g, -1), quad_turn(right_g, 1)
    own_g, *od = call(
        back_own_kernel,
        (whole,) + (bf16(ROWS, LANES),) * 4,
        keys(1) + [turned, grad_s, (tiles, F32), (tiles, BF16)],
        (info,),
        q, uplt, upl, delta, shift1, shift3, probs1, own_a, own_b, dqt, attn,
        products=4,
    )
    od[3], od[2] = partner(od[3], 3), partner(od[2], 2)
    left_g, right_g, od[1] = lax.optimization_barrier((left_g, right_g, od[1]))
    od[1] = partner(od[1], 1)
    grads = list(call(sum_kernel, (bf16(BOTH, WIDE),) * 4, (), (), own_g, left_g, right_g))
    for d in (1, 2, 3):
        grads[d] = partner(grads[d], d)
    tied = lax.optimization_barrier((*grads, od[2], od[3]))
    grads, od[2:] = tied[:4], tied[4:]
    rows = bf16(ROWS, HEADS * HEAD_DIM)
    keep, send = call(share_kernel, (bf16(PROWS, width),) * 2, (), (info,), *grads)
    share = rounded(keep.astype(F32) + swap(send, "core").astype(F32))
    share = rounded(share.astype(F32) + swap(share, "xl").astype(F32))
    share, od[1] = lax.optimization_barrier((share, od[1]))
    across = share.astype(F32) + turn(share, "y", 2).astype(F32)
    beside = turn(share, "y", 1).astype(F32) + turn(share, "y", 3).astype(F32)
    share = (across + beside).astype(BF16)
    key_grad, value_grad = call(
        finish_kernel, (bf16(ROWS, width),) * 2, (), (info,), *grads
    )
    attended, query_grad = call(unpack_kernel, (rows, rows), (), (info,), *od)
    share, key_grad, value_grad, attended, query_grad = lax.optimization_barrier(
        (share, key_grad, value_grad, attended, query_grad)
    )
    other = swap(share, "core")
    key_share = jnp.where(core == 0, share, other)
    value_share = jnp.where(core == 0, other, share)
    return (
        attended[None],
        query_grad[None],
        key_grad[None],
        value_grad[None],
        key_share,
        value_share,
    )


def solution(mesh):
    split = Mesh(mesh.devices.reshape(2, 8, 4, 2, 2), CTX + RESP)
    rows = P(RESP, CTX, None)
    prompt = P(CTX, None)
    return jax.shard_map(
        body,
        mesh=split,
        in_specs=(rows, rows, rows, prompt, prompt, rows, P(RESP), P(RESP)),
        out_specs=(rows, rows, rows, rows, prompt, prompt),
        check_vma=False,
    )
```

```python
import math

import jax
import jax.numpy as jnp
from jax import lax
from jax.experimental import pallas as pl
from jax.experimental.pallas import tpu as pltpu
from jax.sharding import Mesh
from jax.sharding import PartitionSpec as P

HEADS = 16
KV_HEADS = 4
HEAD_DIM = 128
GROUP = HEADS // KV_HEADS
RESP_LEN = 2048
PROMPT_LEN = 1024
CTX = ("xh", "z")
LOCAL = ("xh", "z", "core")
RESP = ("y", "xl", "core")
ROWS = 128
PROWS = 64
BOTH = ROWS + PROWS
CHUNK = 256
SPAN = 3 * CHUNK
TILE_SPANS = (2 * CHUNK, 3 * CHUNK)
TILE_STARTS = (0, 2 * CHUNK)
PROBS = 5 * CHUNK
HALF = GROUP * ROWS
LANES = 2 * HALF
WIDE = 2 * HEAD_DIM
SCALE = HEAD_DIM**-0.5
SCALE2 = SCALE * math.log2(math.e)
NEG = -1e30
F32 = jnp.float32
BF16 = jnp.bfloat16
VMEM = pl.BlockSpec(memory_space=pltpu.VMEM)
SMEM = pl.BlockSpec(memory_space=pltpu.SMEM)


def dot(a, b):
    return jnp.dot(a, b, preferred_element_type=F32)


def head_at(h, width=HEAD_DIM):
    return slice(h * width, (h + 1) * width)


def lanes_at(j, h):
    return slice(j * HALF + h * HEAD_DIM, j * HALF + (h + 1) * HEAD_DIM)


def block_of(member, quad, core):
    return (member // 2) * 8 + ((quad * 2 + (member & 1) + core) & 7)


def run_copies(pairs, sems):
    copies = [
        pltpu.make_async_copy(source, to, sems.at[i]) for i, (source, to) in enumerate(pairs)
    ]
    for copy in copies:
        copy.start()
    for copy in copies:
        copy.wait()


def pack_kv_kernel(info, k, v, kp, vp, kv0, kv1, kv2, kv3, k_s, v_s, kp_s, vp_s, sems):
    mine = info[0]
    run_copies(((k, k_s), (v, v_s), (kp, kp_s), (vp, vp_s)), sems)
    for d, kv in enumerate((kv0, kv1, kv2, kv3)):
        at = pl.ds(pl.multiple_of((mine ^ d) * HEAD_DIM, HEAD_DIM), HEAD_DIM)
        kv[:ROWS, :HEAD_DIM] = k_s[:, at]
        kv[:ROWS, HEAD_DIM:] = v_s[:, at]
        kv[ROWS:, :HEAD_DIM] = kp_s[:, at]
        kv[ROWS:, HEAD_DIM:] = vp_s[:, at]


def pack_qd_kernel(info, q, do, qd0, qd1, qd2, qd3, q_s, do_s, sems):
    mine = info[0]
    run_copies(((q, q_s), (do, do_s)), sems)
    for d, qd in enumerate((qd0, qd1, qd2, qd3)):
        at = pl.ds(pl.multiple_of((mine ^ d) * HALF, HALF), HALF)
        qd[:, :HALF] = q_s[:, at]
        qd[:, HALF:] = do_s[:, at]


def rows_at(mine, d):
    return pl.ds(pl.multiple_of(CHUNK + (mine ^ d) // 2 * CHUNK + (d & 1) * ROWS, ROWS), ROWS)


def load_keys(mine, g, kvs, k_s, v_s):
    for d, kv in enumerate(kvs):
        k_s[g, rows_at(mine, d), :] = kv[:ROWS, :HEAD_DIM]
        v_s[g, rows_at(mine, d), :] = kv[:ROWS, HEAD_DIM:]
        k_s[g, head_at(d, PROWS), :] = kv[ROWS:, :HEAD_DIM]
        v_s[g, head_at(d, PROWS), :] = kv[ROWS:, HEAD_DIM:]


def query_rows(info, x):
    mine, quad, core = info[0], info[1], info[2]
    rows = []
    for j in range(2):
        start = block_of(x * 2 + ((mine & 1) ^ j), quad, core) * ROWS
        rows += [start + lax.broadcasted_iota(jnp.int32, (1, ROWS), 1)] * GROUP
    return jnp.concatenate(rows, axis=1)


def key_rows(info, x, quad):
    mine, core = info[0], info[2]
    rows = []
    for j in range(2):
        start = block_of(x * 2 + ((mine & 1) ^ j), quad, core) * ROWS
        rows.append(start + lax.broadcasted_iota(jnp.int32, (ROWS, 1), 0))
    return jnp.concatenate(rows, axis=0)


def fold(x, op):
    return op(x.reshape(x.shape[0] // 8, 8, LANES), axis=0)


def each(count, step, carry):
    return step(0, carry) if count == 1 else lax.fori_loop(0, count, step, carry)


def forward(info, quads, count, k_s, v_s, qt, before, score_s, probs, vt_s, shift, total, acc):
    def turn_values(g, carry):
        vt_s[g] = v_s[g].T
        return carry

    each(count, turn_values, 0)
    for x in range(2):
        place = query_rows(info, x)
        start, span = TILE_STARTS[x], TILE_SPANS[x]

        def score_step(g, running):
            for c in range(span // CHUNK):
                at = slice(c * CHUNK, (c + 1) * CHUNK)
                score = dot(k_s[g, at, :], qt[x])
                if c > 0:
                    score = jnp.where(key_rows(info, c - 1, quads(g)) <= place, score, NEG)
                score_s[g, at, :] = score
                running = jnp.maximum(running, fold(score, jnp.max))
            return running

        running = each(count, score_step, jnp.full((8, LANES), NEG, F32))
        now = jnp.max(running, axis=0, keepdims=True) * SCALE2
        if before is not None:
            now = jnp.maximum(now, before[0][x])
            factor = jnp.exp2(before[0][x] - now)
            acc[x] = before[2][x] * factor

        def prob_step(g, running):
            for c in range(span // CHUNK):
                prob = jnp.exp2(score_s[g, c * CHUNK : (c + 1) * CHUNK, :] * SCALE2 - now)
                running = running + fold(prob, jnp.sum)
                probs[g, start + c * CHUNK : start + (c + 1) * CHUNK, :] = prob.astype(BF16)
            part = dot(vt_s[g, :, :span], probs[g, start : start + span, :])
            if before is None:
                acc[x] = part
            else:
                acc[x] += part
            return running

        running = each(count, prob_step, jnp.zeros((8, LANES), F32))
        sums = jnp.sum(running, axis=0, keepdims=True)
        if before is not None:
            sums = sums + before[1][x] * factor
        shift[x], total[x] = now, sums


def chunk_at(c, start):
    if isinstance(c, int):
        return slice(start + c * CHUNK, start + (c + 1) * CHUNK)
    return pl.ds(pl.multiple_of(start + c * CHUNK, CHUNK), CHUNK)


def backward(count, looped, k_s, v_s, kt_s, q, uplt, upl, delta, probs, factors, grad_s, before, dqt):
    for x in range(2):
        dqt[x] = jnp.zeros((HEAD_DIM, LANES), F32) if before is None else before[x]

    def chunk(g, c, tiles):
        at = chunk_at(c, 0)
        dk, dv = None, None
        for x in tiles:
            here = chunk_at(c, TILE_STARTS[x])
            low = probs[g, here, :]
            if factors is not None:
                low = (low.astype(F32) * factors[x]).astype(BF16)
            prob_grad = dot(v_s[g, at, :], uplt[x])
            grad = (low.astype(F32) * (prob_grad - delta[x])).astype(BF16)
            grad_s[here, :] = grad
            dv_part = dot(low, upl[x])
            dk_part = dot(grad, q[x])
            dv = dv_part if dv is None else dv + dv_part
            dk = dk_part if dk is None else dk + dk_part
        k_s[g, at, :] = (dk * SCALE).astype(BF16)
        v_s[g, at, :] = dv.astype(BF16)

    def step(g, carry):
        kt_s[...] = k_s[g].T

        def two_tiles(c, carry):
            chunk(g, c, (0, 1))
            return carry

        if looped:
            lax.fori_loop(0, 2, two_tiles, 0)
        else:
            two_tiles(0, 0)
            two_tiles(1, 0)
        chunk(g, 2, (1,))
        for x in range(2):
            start, span = TILE_STARTS[x], TILE_SPANS[x]
            dqt[x] += dot(kt_s[:, :span], grad_s[start : start + span, :])
        return carry

    each(count, step, 0)


def store_grads(mine, g, k_s, v_s, outs):
    for d, out in enumerate(outs):
        out[:ROWS, :HEAD_DIM] = k_s[g, rows_at(mine, d), :]
        out[:ROWS, HEAD_DIM:] = v_s[g, rows_at(mine, d), :]
        out[ROWS:, :HEAD_DIM] = k_s[g, head_at(d, PROWS), :]
        out[ROWS:, HEAD_DIM:] = v_s[g, head_at(d, PROWS), :]


def pieces(*parts):
    return [part.at[d] for part in parts for d in range(part.shape[0])]


def first_kernel(
    info, weight, qd0, qd1, qd2, qd3, own_a, own_b,
    qt, q, upt, probs, shift, total, acc,
    k_s, v_s, vt_s, score_s,
):
    mine, quad, core, count = info[0], info[1], info[2], info[4]
    load_keys(mine, 0, pieces(own_a, own_b), k_s, v_s)
    for d, qd in enumerate((qd0, qd1, qd2, qd3)):
        x = (mine ^ d) // 2
        row = block_of(mine ^ d, quad, core) * ROWS
        row = row + lax.broadcasted_iota(jnp.int32, (1, ROWS), 1)
        row_weight = jnp.where(row < count, weight[0], 0.0)
        for h in range(GROUP):
            cols = lanes_at(d & 1, h)
            q_head = qd[:, head_at(h)]
            q[x, cols, :] = q_head
            qt[x, :, cols] = q_head.T
            grad = qd[:, HALF + h * HEAD_DIM : HALF + (h + 1) * HEAD_DIM]
            upt[x, :, cols] = (grad.T.astype(F32) * row_weight).astype(BF16)
    forward(
        info, lambda g: quad, 1, k_s, v_s, qt, None, score_s, probs, vt_s, shift, total, acc
    )


def side_kernel(
    info, qt, left_a, left_b, right_a, right_b, shift0, total0, acc0,
    probs, shift, total, acc,
    k_s, v_s, vt_s, score_s,
):
    mine, quad = info[0], info[1]
    load_keys(mine, 0, pieces(left_a, left_b), k_s, v_s)
    load_keys(mine, 1, pieces(right_a, right_b), k_s, v_s)
    forward(
        info, lambda g: (quad + 3 + 2 * g) & 3, 2, k_s, v_s, qt, (shift0, total0, acc0),
        score_s, probs, vt_s, shift, total, acc,
    )


def far_kernel(
    info, qt, q, upt, far_a, far_b, shift0, total0, acc0,
    shift, uplt, upl, delta, dqt, attn, out_a, out_b,
    k_s, v_s, vt_s, kt_s, score_s, probs, grad_s, acc, total,
):
    mine, quad, length = info[0], info[1], info[3]
    load_keys(mine, 0, pieces(far_a, far_b), k_s, v_s)
    forward(
        info, lambda g: (quad + 2) & 3, 1, k_s, v_s, qt, (shift0, total0, acc0),
        score_s, probs, vt_s, shift, total, acc,
    )
    for x in range(2):
        inverse = 1.0 / total[x]
        valid = jnp.where(query_rows(info, x) < length, 1.0, 0.0)
        out_t = (acc[x] * (inverse * valid)).astype(BF16)
        up_low = (upt[x].astype(F32) * inverse).astype(BF16)
        uplt[x] = up_low
        delta[x] = jnp.sum(up_low.astype(F32) * out_t.astype(F32), axis=0, keepdims=True)
        attn[x] = out_t
        for j in range(2):
            for h in range(GROUP):
                upl[x, lanes_at(j, h), :] = up_low[:, lanes_at(j, h)].T
    backward(
        1, False, k_s, v_s, kt_s, q, uplt, upl, delta, probs, None, grad_s, None, dqt
    )
    store_grads(mine, 0, k_s, v_s, pieces(out_a, out_b))


def back_side_kernel(
    info, q, uplt, upl, delta, shift_then, shift_last, probs,
    left_a, left_b, right_a, right_b, dqt0,
    dqt, out_l, out_r,
    k_s, v_s, kt_s, grad_s,
):
    mine = info[0]
    factors = [jnp.exp2(shift_then[x] - shift_last[x]) for x in range(2)]
    load_keys(mine, 0, pieces(left_a, left_b), k_s, v_s)
    load_keys(mine, 1, pieces(right_a, right_b), k_s, v_s)
    backward(
        2, False, k_s, v_s, kt_s, q, uplt, upl, delta, probs, factors, grad_s, dqt0, dqt
    )
    store_grads(mine, 0, k_s, v_s, pieces(out_l))
    store_grads(mine, 1, k_s, v_s, pieces(out_r))


def back_own_kernel(
    info, q, uplt, upl, delta, shift_then, shift_last, probs, own_a, own_b, dqt0, attn,
    out, od0, od1, od2, od3,
    k_s, v_s, kt_s, grad_s, dqt, dq_s,
):
    mine = info[0]
    factors = [jnp.exp2(shift_then[x] - shift_last[x]) for x in range(2)]
    load_keys(mine, 0, pieces(own_a, own_b), k_s, v_s)
    backward(
        1, True, k_s, v_s, kt_s, q, uplt, upl, delta, probs, factors, grad_s, dqt0, dqt
    )
    store_grads(mine, 0, k_s, v_s, pieces(out))
    for x in range(2):
        dq_s[x] = (dqt[x] * SCALE).astype(BF16)
    for d, od in enumerate((od0, od1, od2, od3)):
        x = (mine ^ d) // 2
        for h in range(GROUP):
            od[:, head_at(h)] = attn[x, :, lanes_at(d & 1, h)].T
            od[:, HALF + h * HEAD_DIM : HALF + (h + 1) * HEAD_DIM] = dq_s[
                x, :, lanes_at(d & 1, h)
            ].T


def unpack_kernel(info, od0, od1, od2, od3, attended, query_grad):
    mine = info[0]
    for d, od in enumerate((od0, od1, od2, od3)):
        at = pl.ds(pl.multiple_of((mine ^ d) * HALF, HALF), HALF)
        attended[:, at] = od[:, :HALF]
        query_grad[:, at] = od[:, HALF:]


def both(a, b):
    return (a.astype(F32) + b.astype(F32)).astype(BF16)


def add_kernel(side_l, side_r, far_a, far_b, out_l, out_r):
    out_r[:2] = both(side_r[:2], far_a[...])
    out_r[2:] = side_r[2:]
    out_l[:2] = side_l[:2]
    out_l[2:] = both(side_l[2:], far_b[...])


def sum_kernel(own, left, right, *outs):
    for d, out in enumerate(outs):
        total = own[d].astype(F32) + left[d].astype(F32) + right[d].astype(F32)
        out[...] = total.astype(BF16)


def share_kernel(info, g0, g1, g2, g3, keep, send):
    mine, first = info[0], info[2] == 0
    for d, g in enumerate((g0, g1, g2, g3)):
        at = pl.ds(pl.multiple_of((mine ^ d) * HEAD_DIM, HEAD_DIM), HEAD_DIM)
        keys, values = g[ROWS:, :HEAD_DIM], g[ROWS:, HEAD_DIM:]
        keep[:, at] = jnp.where(first, keys, values)
        send[:, at] = jnp.where(first, values, keys)


def finish_kernel(info, g0, g1, g2, g3, key_grad, value_grad):
    mine = info[0]
    for d, g in enumerate((g0, g1, g2, g3)):
        at = pl.ds(pl.multiple_of((mine ^ d) * HEAD_DIM, HEAD_DIM), HEAD_DIM)
        key_grad[:, at] = g[:ROWS, :HEAD_DIM]
        value_grad[:, at] = g[:ROWS, HEAD_DIM:]


def bf16(*shape):
    return jax.ShapeDtypeStruct(shape, BF16)


def f32(*shape):
    return jax.ShapeDtypeStruct(shape, F32)


def call(kernel, outs, scratch, scalars, *operands, copies=0, products=0):
    place = pl.BlockSpec(memory_space=pl.ANY) if copies else VMEM
    scratch = [pltpu.VMEM(shape, dtype) for shape, dtype in scratch]
    if copies:
        scratch.append(pltpu.SemaphoreType.DMA((copies,)))
    return pl.pallas_call(
        kernel,
        out_shape=tuple(outs),
        in_specs=[SMEM] * len(scalars) + [place] * len(operands),
        out_specs=(VMEM,) * len(outs),
        scratch_shapes=scratch,
        compiler_params=pltpu.CompilerParams(vmem_limit_bytes=(56 if copies else 32) * 2**20),
        cost_estimate=pl.CostEstimate(
            flops=products * PROBS * LANES * HEAD_DIM * 4,
            bytes_accessed=1_000_000,
            transcendentals=0,
        ),
    )(*scalars, *operands)


def swap(x, axis):
    return lax.ppermute(x, axis, [(0, 1), (1, 0)])


def turn(x, axis, step):
    size = lax.axis_size(axis)
    return lax.ppermute(x, axis, [(i, (i + step) % size) for i in range(size)])


def local_permute(x, place):
    pairs = []
    for i in range(32):
        xh, z, core = i // 16, i // 2 % 8, i % 2
        xh, z = place(xh, (z - core) % 8)
        pairs.append((i, (xh * 8 + (z + core) % 8) * 2 + core))
    return lax.ppermute(x, LOCAL, pairs)


def partner(x, d):
    return local_permute(x, lambda xh, z: (xh ^ (d // 2), z ^ (d & 1)))


def quad_turn(x, step):
    return local_permute(x, lambda xh, z: (xh, (z + 2 * step) % 8))


def rounded(x):
    return lax.optimization_barrier(x.astype(BF16))


def body(q_resp, k_resp, v_resp, k_prompt, v_prompt, d_out, lengths, counts):
    core = lax.axis_index("core")
    z = (lax.axis_index("z") - core) & 7
    mine = lax.axis_index("xh") * 2 + (z & 1)
    info = jnp.stack([mine, z // 2, core, lengths[0], counts[0]]).astype(jnp.int32)
    weight = (RESP_LEN / counts[0].astype(F32)).reshape(1)
    spot = mine.reshape(1).astype(jnp.int32)
    width = KV_HEADS * HEAD_DIM
    kv = list(
        call(
            pack_kv_kernel,
            (bf16(BOTH, WIDE),) * 4,
            [((ROWS, width), BF16)] * 2 + [((PROWS, width), BF16)] * 2,
            (spot,),
            k_resp[0], v_resp[0], k_prompt, v_prompt,
            copies=4,
        )
    )
    qd = list(
        call(
            pack_qd_kernel,
            (bf16(ROWS, LANES),) * 4,
            [((ROWS, HEADS * HEAD_DIM), BF16)] * 2,
            (spot,),
            q_resp[0], d_out[0],
            copies=2,
        )
    )
    for d in (1, 2, 3):
        kv[d] = partner(kv[d], d)
    for d in (1, 2, 3):
        qd[d] = partner(qd[d], d)
    own_a, own_b = jnp.stack(kv[:2]), jnp.stack(kv[2:])
    left_a, right_b = quad_turn(own_a, 1), quad_turn(own_b, -1)
    left_b, right_a = quad_turn(own_b, 1), quad_turn(own_a, -1)
    far_a, far_b = quad_turn(left_a, 1), quad_turn(right_b, -1)

    tiles = (2, HEAD_DIM, LANES)
    line = f32(2, 1, LANES)

    def keys(count):
        return [((count, SPAN, HEAD_DIM), BF16)] * 2

    def forward_scratch(count):
        return keys(count) + [((count, HEAD_DIM, SPAN), BF16), ((count, SPAN, LANES), F32)]

    turned = ((HEAD_DIM, SPAN), BF16)
    grad_s = ((PROBS, LANES), BF16)
    whole, pair = bf16(4, BOTH, WIDE), bf16(2, BOTH, WIDE)
    qt, q, upt, probs1, shift1, total1, acc1 = call(
        first_kernel,
        (bf16(*tiles), bf16(2, LANES, HEAD_DIM), bf16(*tiles), bf16(1, PROBS, LANES), line, line, f32(*tiles)),
        forward_scratch(1),
        (info, weight),
        *qd, own_a, own_b,
        products=2,
    )
    probs2, shift2, total2, acc2 = call(
        side_kernel,
        (bf16(2, PROBS, LANES), line, line, f32(*tiles)),
        forward_scratch(2),
        (info,),
        qt, left_a, left_b, right_a, right_b, shift1, total1, acc1,
        products=4,
    )
    shift3, uplt, upl, delta, dqt, attn, far_ga, far_gb = call(
        far_kernel,
        (line, bf16(*tiles), bf16(2, LANES, HEAD_DIM), line, f32(*tiles), bf16(*tiles), pair, pair),
        keys(1) + [((1, HEAD_DIM, SPAN), BF16), turned, ((1, SPAN, LANES), F32)]
        + [((1, PROBS, LANES), BF16), grad_s, (tiles, F32), ((2, 1, LANES), F32)],
        (info,),
        qt, q, upt, far_a, far_b, shift2, total2, acc2,
        products=6,
    )
    far_ga, far_gb = quad_turn(far_ga, 1), quad_turn(far_gb, -1)
    dqt, left_g, right_g = call(
        back_side_kernel,
        (f32(*tiles), whole, whole),
        keys(2) + [turned, grad_s],
        (info,),
        q, uplt, upl, delta, shift2, shift3, probs2,
        left_a, left_b, right_a, right_b, dqt,
        products=8,
    )
    left_g, right_g = call(add_kernel, (whole, whole), (), (), left_g, right_g, far_ga, far_gb)
    left_g, right_g = quad_turn(left_g, -1), quad_turn(right_g, 1)
    own_g, *od = call(
        back_own_kernel,
        (whole,) + (bf16(ROWS, LANES),) * 4,
        keys(1) + [turned, grad_s, (tiles, F32), (tiles, BF16)],
        (info,),
        q, uplt, upl, delta, shift1, shift3, probs1, own_a, own_b, dqt, attn,
        products=4,
    )
    od[3], od[2] = partner(od[3], 3), partner(od[2], 2)
    left_g, right_g, od[1] = lax.optimization_barrier((left_g, right_g, od[1]))
    od[1] = partner(od[1], 1)
    grads = list(call(sum_kernel, (bf16(BOTH, WIDE),) * 4, (), (), own_g, left_g, right_g))
    for d in (1, 2, 3):
        grads[d] = partner(grads[d], d)
    tied = lax.optimization_barrier((*grads, *od[1:]))
    grads, od[1:] = tied[:4], tied[4:]
    rows = bf16(ROWS, HEADS * HEAD_DIM)
    keep, send = call(share_kernel, (bf16(PROWS, width),) * 2, (), (info,), *grads)
    share = rounded(keep.astype(F32) + swap(send, "core").astype(F32))
    share = rounded(share.astype(F32) + swap(share, "xl").astype(F32))
    key_grad, value_grad = call(
        finish_kernel, (bf16(ROWS, width),) * 2, (), (info,), *grads
    )
    attended, query_grad = call(unpack_kernel, (rows, rows), (), (info,), *od)
    share, key_grad, value_grad, attended, query_grad = lax.optimization_barrier(
        (share, key_grad, value_grad, attended, query_grad)
    )
    across = share.astype(F32) + turn(share, "y", 2).astype(F32)
    beside = turn(share, "y", 1).astype(F32) + turn(share, "y", 3).astype(F32)
    share = rounded(across + beside)
    other = swap(share, "core")
    key_share = jnp.where(core == 0, share, other)
    value_share = jnp.where(core == 0, other, share)
    return (
        attended[None],
        query_grad[None],
        key_grad[None],
        value_grad[None],
        key_share,
        value_share,
    )


def solution(mesh):
    split = Mesh(mesh.devices.reshape(2, 8, 4, 2, 2), CTX + RESP)
    rows = P(RESP, CTX, None)
    prompt = P(CTX, None)
    return jax.shard_map(
        body,
        mesh=split,
        in_specs=(rows, rows, rows, prompt, prompt, rows, P(RESP), P(RESP)),
        out_specs=(rows, rows, rows, rows, prompt, prompt),
        check_vma=False,
    )
```

```python
import math

import jax
import jax.numpy as jnp
from jax import lax
from jax.experimental import pallas as pl
from jax.experimental.pallas import tpu as pltpu
from jax.sharding import Mesh
from jax.sharding import PartitionSpec as P

HEADS = 16
KV_HEADS = 4
HEAD_DIM = 128
GROUP = HEADS // KV_HEADS
RESP_LEN = 2048
PROMPT_LEN = 1024
CTX = ("xh", "z")
LOCAL = ("xh", "z", "core")
RESP = ("y", "xl", "core")
ROWS = 128
PROWS = 64
BOTH = ROWS + PROWS
CHUNK = 256
SPAN = 3 * CHUNK
TILE_SPANS = (2 * CHUNK, 3 * CHUNK)
TILE_STARTS = (0, 2 * CHUNK)
PROBS = 5 * CHUNK
HALF = GROUP * ROWS
LANES = 2 * HALF
WIDE = 2 * HEAD_DIM
SCALE = HEAD_DIM**-0.5
SCALE2 = SCALE * math.log2(math.e)
NEG = -1e30
F32 = jnp.float32
BF16 = jnp.bfloat16
VMEM = pl.BlockSpec(memory_space=pltpu.VMEM)
SMEM = pl.BlockSpec(memory_space=pltpu.SMEM)


def dot(a, b):
    return jnp.dot(a, b, preferred_element_type=F32)


def head_at(h, width=HEAD_DIM):
    return slice(h * width, (h + 1) * width)


def lanes_at(j, h):
    return slice(j * HALF + h * HEAD_DIM, j * HALF + (h + 1) * HEAD_DIM)


def block_of(member, quad, core):
    return (member // 2) * 8 + ((quad * 2 + (member & 1) + core) & 7)


def run_copies(pairs, sems):
    copies = [
        pltpu.make_async_copy(source, to, sems.at[i]) for i, (source, to) in enumerate(pairs)
    ]
    for copy in copies:
        copy.start()
    for copy in copies:
        copy.wait()


def pack_kv_kernel(info, k, v, kp, vp, kv0, kv1, kv2, kv3, k_s, v_s, kp_s, vp_s, sems):
    mine = info[0]
    run_copies(((k, k_s), (v, v_s), (kp, kp_s), (vp, vp_s)), sems)
    for d, kv in enumerate((kv0, kv1, kv2, kv3)):
        at = pl.ds(pl.multiple_of((mine ^ d) * HEAD_DIM, HEAD_DIM), HEAD_DIM)
        kv[:ROWS, :HEAD_DIM] = k_s[:, at]
        kv[:ROWS, HEAD_DIM:] = v_s[:, at]
        kv[ROWS:, :HEAD_DIM] = kp_s[:, at]
        kv[ROWS:, HEAD_DIM:] = vp_s[:, at]


def pack_qd_kernel(info, q, do, qd0, qd1, qd2, qd3, q_s, do_s, sems):
    mine = info[0]
    run_copies(((q, q_s), (do, do_s)), sems)
    for d, qd in enumerate((qd0, qd1, qd2, qd3)):
        at = pl.ds(pl.multiple_of((mine ^ d) * HALF, HALF), HALF)
        qd[:, :HALF] = q_s[:, at]
        qd[:, HALF:] = do_s[:, at]


def rows_at(mine, d):
    return pl.ds(pl.multiple_of(CHUNK + (mine ^ d) // 2 * CHUNK + (d & 1) * ROWS, ROWS), ROWS)


def load_keys(mine, g, kvs, k_s, v_s):
    for d, kv in enumerate(kvs):
        k_s[g, rows_at(mine, d), :] = kv[:ROWS, :HEAD_DIM]
        v_s[g, rows_at(mine, d), :] = kv[:ROWS, HEAD_DIM:]
        k_s[g, head_at(d, PROWS), :] = kv[ROWS:, :HEAD_DIM]
        v_s[g, head_at(d, PROWS), :] = kv[ROWS:, HEAD_DIM:]


def query_rows(info, x):
    mine, quad, core = info[0], info[1], info[2]
    rows = []
    for j in range(2):
        start = block_of(x * 2 + ((mine & 1) ^ j), quad, core) * ROWS
        rows += [start + lax.broadcasted_iota(jnp.int32, (1, ROWS), 1)] * GROUP
    return jnp.concatenate(rows, axis=1)


def key_rows(info, x, quad):
    mine, core = info[0], info[2]
    rows = []
    for j in range(2):
        start = block_of(x * 2 + ((mine & 1) ^ j), quad, core) * ROWS
        rows.append(start + lax.broadcasted_iota(jnp.int32, (ROWS, 1), 0))
    return jnp.concatenate(rows, axis=0)


def fold(x, op):
    return op(x.reshape(x.shape[0] // 8, 8, LANES), axis=0)


def each(count, step, carry):
    return step(0, carry) if count == 1 else lax.fori_loop(0, count, step, carry)


def forward(info, quads, count, k_s, v_s, qt, before, score_s, probs, vt_s, shift, total, acc):
    def turn_values(g, carry):
        vt_s[g] = v_s[g].T
        return carry

    each(count, turn_values, 0)
    for x in range(2):
        place = query_rows(info, x)
        start, span = TILE_STARTS[x], TILE_SPANS[x]

        def score_step(g, running):
            for c in range(span // CHUNK):
                at = slice(c * CHUNK, (c + 1) * CHUNK)
                score = dot(k_s[g, at, :], qt[x])
                if c > 0:
                    score = jnp.where(key_rows(info, c - 1, quads(g, c - 1)) <= place, score, NEG)
                score_s[g, at, :] = score
                running = jnp.maximum(running, fold(score, jnp.max))
            return running

        running = each(count, score_step, jnp.full((8, LANES), NEG, F32))
        now = jnp.max(running, axis=0, keepdims=True) * SCALE2
        if before is not None:
            now = jnp.maximum(now, before[0][x])
            factor = jnp.exp2(before[0][x] - now)
            acc[x] = before[2][x] * factor

        def prob_step(g, running):
            for c in range(span // CHUNK):
                prob = jnp.exp2(score_s[g, c * CHUNK : (c + 1) * CHUNK, :] * SCALE2 - now)
                running = running + fold(prob, jnp.sum)
                probs[g, start + c * CHUNK : start + (c + 1) * CHUNK, :] = prob.astype(BF16)
            part = dot(vt_s[g, :, :span], probs[g, start : start + span, :])
            if before is None:
                acc[x] = part
            else:
                acc[x] += part
            return running

        running = each(count, prob_step, jnp.zeros((8, LANES), F32))
        sums = jnp.sum(running, axis=0, keepdims=True)
        if before is not None:
            sums = sums + before[1][x] * factor
        shift[x], total[x] = now, sums


def chunk_at(c, start):
    if isinstance(c, int):
        return slice(start + c * CHUNK, start + (c + 1) * CHUNK)
    return pl.ds(pl.multiple_of(start + c * CHUNK, CHUNK), CHUNK)


def backward(count, looped, k_s, v_s, kt_s, q, uplt, upl, delta, probs, factors, grad_s, before, dqt):
    for x in range(2):
        dqt[x] = jnp.zeros((HEAD_DIM, LANES), F32) if before is None else before[x]

    def chunk(g, c, tiles):
        at = chunk_at(c, 0)
        dk, dv = None, None
        for x in tiles:
            here = chunk_at(c, TILE_STARTS[x])
            low = probs[g, here, :]
            if factors is not None:
                low = (low.astype(F32) * factors[x]).astype(BF16)
            prob_grad = dot(v_s[g, at, :], uplt[x])
            grad = (low.astype(F32) * (prob_grad - delta[x])).astype(BF16)
            grad_s[here, :] = grad
            dv_part = dot(low, upl[x])
            dk_part = dot(grad, q[x])
            dv = dv_part if dv is None else dv + dv_part
            dk = dk_part if dk is None else dk + dk_part
        k_s[g, at, :] = (dk * SCALE).astype(BF16)
        v_s[g, at, :] = dv.astype(BF16)

    def step(g, carry):
        kt_s[...] = k_s[g].T

        def two_tiles(c, carry):
            chunk(g, c, (0, 1))
            return carry

        if looped:
            lax.fori_loop(0, 2, two_tiles, 0)
        else:
            two_tiles(0, 0)
            two_tiles(1, 0)
        chunk(g, 2, (1,))
        for x in range(2):
            start, span = TILE_STARTS[x], TILE_SPANS[x]
            dqt[x] += dot(kt_s[:, :span], grad_s[start : start + span, :])
        return carry

    each(count, step, 0)


def store_grads(mine, g, k_s, v_s, outs):
    for d, out in enumerate(outs):
        out[:ROWS, :HEAD_DIM] = k_s[g, rows_at(mine, d), :]
        out[:ROWS, HEAD_DIM:] = v_s[g, rows_at(mine, d), :]
        out[ROWS:, :HEAD_DIM] = k_s[g, head_at(d, PROWS), :]
        out[ROWS:, HEAD_DIM:] = v_s[g, head_at(d, PROWS), :]


def pieces(*parts):
    return [part.at[d] for part in parts for d in range(part.shape[0])]


def first_kernel(
    info, weight, qd0, qd1, qd2, qd3, own_a, own_b,
    qt, q, upt, probs, shift, total, acc,
    k_s, v_s, vt_s, score_s,
):
    mine, quad, core, count = info[0], info[1], info[2], info[4]
    load_keys(mine, 0, pieces(own_a, own_b), k_s, v_s)
    for d, qd in enumerate((qd0, qd1, qd2, qd3)):
        x = (mine ^ d) // 2
        row = block_of(mine ^ d, quad, core) * ROWS
        row = row + lax.broadcasted_iota(jnp.int32, (1, ROWS), 1)
        row_weight = jnp.where(row < count, weight[0], 0.0)
        for h in range(GROUP):
            cols = lanes_at(d & 1, h)
            q_head = qd[:, head_at(h)]
            q[x, cols, :] = q_head
            qt[x, :, cols] = q_head.T
            grad = qd[:, HALF + h * HEAD_DIM : HALF + (h + 1) * HEAD_DIM]
            upt[x, :, cols] = (grad.T.astype(F32) * row_weight).astype(BF16)
    forward(
        info, lambda g, x: quad, 1, k_s, v_s, qt, None, score_s, probs, vt_s, shift, total, acc
    )


def side_kernel(
    info, qt, left_a, left_b, right_a, right_b, shift0, total0, acc0,
    probs, shift, total, acc,
    k_s, v_s, vt_s, score_s,
):
    mine, quad = info[0], info[1]
    load_keys(mine, 0, pieces(left_a, right_b), k_s, v_s)
    load_keys(mine, 1, pieces(right_a, left_b), k_s, v_s)
    forward(
        info, lambda g, x: (quad + 3 - 2 * (g ^ x ^ (mine // 2))) & 3, 2, k_s, v_s, qt, (shift0, total0, acc0),
        score_s, probs, vt_s, shift, total, acc,
    )


def far_kernel(
    info, qt, q, upt, far_a, far_b, shift0, total0, acc0,
    shift, uplt, upl, delta, dqt, attn, out_a, out_b,
    k_s, v_s, vt_s, kt_s, score_s, probs, grad_s, acc, total,
):
    mine, quad, length = info[0], info[1], info[3]
    load_keys(mine, 0, pieces(far_a, far_b), k_s, v_s)
    forward(
        info, lambda g, x: (quad + 2) & 3, 1, k_s, v_s, qt, (shift0, total0, acc0),
        score_s, probs, vt_s, shift, total, acc,
    )
    for x in range(2):
        inverse = 1.0 / total[x]
        valid = jnp.where(query_rows(info, x) < length, 1.0, 0.0)
        out_t = (acc[x] * (inverse * valid)).astype(BF16)
        up_low = (upt[x].astype(F32) * inverse).astype(BF16)
        uplt[x] = up_low
        delta[x] = jnp.sum(up_low.astype(F32) * out_t.astype(F32), axis=0, keepdims=True)
        attn[x] = out_t
        for j in range(2):
            for h in range(GROUP):
                upl[x, lanes_at(j, h), :] = up_low[:, lanes_at(j, h)].T
    backward(
        1, True, k_s, v_s, kt_s, q, uplt, upl, delta, probs, None, grad_s, None, dqt
    )
    store_grads(mine, 0, k_s, v_s, pieces(out_a, out_b))


def back_kernel(
    info, q, uplt, upl, delta, shift_then, shift_last, probs, kv_a, kv_b, dqt0,
    dqt, out_a, out_b,
    k_s, v_s, kt_s, grad_s,
):
    mine = info[0]
    factors = [jnp.exp2(shift_then[x] - shift_last[x]) for x in range(2)]
    load_keys(mine, 0, pieces(kv_a, kv_b), k_s, v_s)
    backward(
        1, True, k_s, v_s, kt_s, q, uplt, upl, delta, probs, factors, grad_s, dqt0, dqt
    )
    store_grads(mine, 0, k_s, v_s, pieces(out_a, out_b))


def back_last_kernel(
    info, q, uplt, upl, delta, shift_then, shift_last, probs, kv_a, kv_b, dqt0, attn,
    out_a, out_b, od0, od1, od2, od3,
    k_s, v_s, kt_s, grad_s, dqt, dq_s,
):
    mine = info[0]
    back_kernel(
        info, q, uplt, upl, delta, shift_then, shift_last, probs.at[pl.ds(1, 1)], kv_a, kv_b,
        dqt0, dqt, out_a, out_b, k_s, v_s, kt_s, grad_s,
    )
    for x in range(2):
        dq_s[x] = (dqt[x] * SCALE).astype(BF16)
    for d, od in enumerate((od0, od1, od2, od3)):
        x = (mine ^ d) // 2
        for h in range(GROUP):
            od[:, head_at(h)] = attn[x, :, lanes_at(d & 1, h)].T
            od[:, HALF + h * HEAD_DIM : HALF + (h + 1) * HEAD_DIM] = dq_s[
                x, :, lanes_at(d & 1, h)
            ].T


def unpack_kernel(info, od0, od1, od2, od3, attended, query_grad):
    mine = info[0]
    for d, od in enumerate((od0, od1, od2, od3)):
        at = pl.ds(pl.multiple_of((mine ^ d) * HALF, HALF), HALF)
        attended[:, at] = od[:, :HALF]
        query_grad[:, at] = od[:, HALF:]


def both(a, b):
    return (a.astype(F32) + b.astype(F32)).astype(BF16)


def add_kernel(side_a, side_b, far_a, far_b, out_a, out_b):
    out_a[...] = both(side_a[...], far_a[...])
    out_b[...] = both(side_b[...], far_b[...])


def sum_kernel(own_a, own_b, left_a, left_b, right_a, right_b, *outs):
    owns, lefts, rights = pieces(own_a, own_b), pieces(left_a, left_b), pieces(right_a, right_b)
    for own, left, right, out in zip(owns, lefts, rights, outs, strict=True):
        total = own[...].astype(F32) + left[...].astype(F32) + right[...].astype(F32)
        out[...] = total.astype(BF16)


def share_kernel(info, g0, g1, g2, g3, keep, send):
    mine, first = info[0], info[2] == 0
    for d, g in enumerate((g0, g1, g2, g3)):
        at = pl.ds(pl.multiple_of((mine ^ d) * HEAD_DIM, HEAD_DIM), HEAD_DIM)
        keys, values = g[ROWS:, :HEAD_DIM], g[ROWS:, HEAD_DIM:]
        keep[:, at] = jnp.where(first, keys, values)
        send[:, at] = jnp.where(first, values, keys)


def finish_kernel(info, g0, g1, g2, g3, key_grad, value_grad):
    mine = info[0]
    for d, g in enumerate((g0, g1, g2, g3)):
        at = pl.ds(pl.multiple_of((mine ^ d) * HEAD_DIM, HEAD_DIM), HEAD_DIM)
        key_grad[:, at] = g[:ROWS, :HEAD_DIM]
        value_grad[:, at] = g[:ROWS, HEAD_DIM:]


def bf16(*shape):
    return jax.ShapeDtypeStruct(shape, BF16)


def f32(*shape):
    return jax.ShapeDtypeStruct(shape, F32)


def call(kernel, outs, scratch, scalars, *operands, copies=0, products=0):
    place = pl.BlockSpec(memory_space=pl.ANY) if copies else VMEM
    scratch = [pltpu.VMEM(shape, dtype) for shape, dtype in scratch]
    if copies:
        scratch.append(pltpu.SemaphoreType.DMA((copies,)))
    return pl.pallas_call(
        kernel,
        out_shape=tuple(outs),
        in_specs=[SMEM] * len(scalars) + [place] * len(operands),
        out_specs=(VMEM,) * len(outs),
        scratch_shapes=scratch,
        compiler_params=pltpu.CompilerParams(vmem_limit_bytes=(56 if copies else 32) * 2**20),
        cost_estimate=pl.CostEstimate(
            flops=products * PROBS * LANES * HEAD_DIM * 4 + 1,
            bytes_accessed=1_000_000 * products + 1,
            transcendentals=0,
        ),
    )(*scalars, *operands)


def swap(x, axis):
    return lax.ppermute(x, axis, [(0, 1), (1, 0)])


def local_permute(x, place):
    pairs = []
    for i in range(32):
        xh, z, core = i // 16, i // 2 % 8, i % 2
        xh, z = place(xh, (z - core) % 8)
        pairs.append((i, (xh * 8 + (z + core) % 8) * 2 + core))
    return lax.ppermute(x, LOCAL, pairs)


def partner(x, d):
    return local_permute(x, lambda xh, z: (xh ^ (d // 2), z ^ (d & 1)))


def quad_turn(x, step):
    return local_permute(x, lambda xh, z: (xh, (z + 2 * step) % 8))


def rounded(x):
    return lax.optimization_barrier(x.astype(BF16))


def body(q_resp, k_resp, v_resp, k_prompt, v_prompt, d_out, lengths, counts):
    core = lax.axis_index("core")
    z = (lax.axis_index("z") - core) & 7
    mine = lax.axis_index("xh") * 2 + (z & 1)
    info = jnp.stack([mine, z // 2, core, lengths[0], counts[0]]).astype(jnp.int32)
    weight = (RESP_LEN / counts[0].astype(F32)).reshape(1)
    spot = mine.reshape(1).astype(jnp.int32)
    width = KV_HEADS * HEAD_DIM
    kv = list(
        call(
            pack_kv_kernel,
            (bf16(BOTH, WIDE),) * 4,
            [((ROWS, width), BF16)] * 2 + [((PROWS, width), BF16)] * 2,
            (spot,),
            k_resp[0], v_resp[0], k_prompt, v_prompt,
            copies=4,
        )
    )
    qd = list(
        call(
            pack_qd_kernel,
            (bf16(ROWS, LANES),) * 4,
            [((ROWS, HEADS * HEAD_DIM), BF16)] * 2,
            (spot,),
            q_resp[0], d_out[0],
            copies=2,
        )
    )
    for d in (1, 2, 3):
        kv[d] = partner(kv[d], d)
    for d in (1, 2, 3):
        qd[d] = partner(qd[d], d)
    own_a, own_b = jnp.stack(kv[:2]), jnp.stack(kv[2:])
    left_a, right_b = quad_turn(own_a, 1), quad_turn(own_b, -1)
    left_b, right_a = quad_turn(own_b, 1), quad_turn(own_a, -1)
    far_a, far_b = quad_turn(left_a, 1), quad_turn(right_b, -1)

    tiles = (2, HEAD_DIM, LANES)
    line = f32(2, 1, LANES)

    def keys(count):
        return [((count, SPAN, HEAD_DIM), BF16)] * 2

    def forward_scratch(count):
        return keys(count) + [((count, HEAD_DIM, SPAN), BF16), ((count, SPAN, LANES), F32)]

    turned = ((HEAD_DIM, SPAN), BF16)
    grad_s = ((PROBS, LANES), BF16)
    whole, pair = bf16(4, BOTH, WIDE), bf16(2, BOTH, WIDE)
    qt, q, upt, probs1, shift1, total1, acc1 = call(
        first_kernel,
        (bf16(*tiles), bf16(2, LANES, HEAD_DIM), bf16(*tiles), bf16(1, PROBS, LANES), line, line, f32(*tiles)),
        forward_scratch(1),
        (info, weight),
        *qd, own_a, own_b,
        products=2,
    )
    probs2, shift2, total2, acc2 = call(
        side_kernel,
        (bf16(2, PROBS, LANES), line, line, f32(*tiles)),
        forward_scratch(2),
        (info,),
        qt, left_a, left_b, right_a, right_b, shift1, total1, acc1,
        products=4,
    )
    shift3, uplt, upl, delta, dqt, attn, far_ga, far_gb = call(
        far_kernel,
        (line, bf16(*tiles), bf16(2, LANES, HEAD_DIM), line, f32(*tiles), bf16(*tiles), pair, pair),
        keys(1) + [((1, HEAD_DIM, SPAN), BF16), turned, ((1, SPAN, LANES), F32)]
        + [((1, PROBS, LANES), BF16), grad_s, (tiles, F32), ((2, 1, LANES), F32)],
        (info,),
        qt, q, upt, far_a, far_b, shift2, total2, acc2,
        products=6,
    )
    far_ga, far_gb = quad_turn(far_ga, 1), quad_turn(far_gb, -1)

    def back(shift, probs, kv_a, kv_b, dqt, products):
        return call(
            back_kernel,
            (f32(*tiles), pair, pair),
            keys(1) + [turned, grad_s],
            (info,),
            q, uplt, upl, delta, shift, shift3, probs, kv_a, kv_b, dqt,
            products=products,
        )

    dqt, left_ga, right_gb = back(shift2, probs2, left_a, right_b, dqt, 4)
    left_ga, right_gb = quad_turn(left_ga, -1), quad_turn(right_gb, 1)
    dqt, own_ga, own_gb = back(shift1, probs1, own_a, own_b, dqt, 0)
    dqt, far_ga, far_gb = lax.optimization_barrier((dqt, far_ga, far_gb))
    right_ga, left_gb, *od = call(
        back_last_kernel,
        (pair, pair) + (bf16(ROWS, LANES),) * 4,
        keys(1) + [turned, grad_s, (tiles, F32), (tiles, BF16)],
        (info,),
        q, uplt, upl, delta, shift2, shift3, probs2, right_a, left_b, dqt, attn,
    )
    far_ga, far_gb, left_ga, right_gb = lax.optimization_barrier(
        (far_ga, far_gb, left_ga, right_gb)
    )
    right_ga, left_gb = call(
        add_kernel, (pair, pair), (), (), right_ga, left_gb, far_ga, far_gb
    )
    left_gb, right_ga, od[1] = lax.optimization_barrier((left_gb, right_ga, od[1]))
    left_gb, right_ga = quad_turn(left_gb, -1), quad_turn(right_ga, 1)
    for d in (3, 2, 1):
        od[d] = partner(od[d], d)
    grads = list(call(sum_kernel, (bf16(BOTH, WIDE),) * 4, (), (), own_ga, own_gb, left_ga, left_gb, right_ga, right_gb))
    for d in (1, 2, 3):
        grads[d] = partner(grads[d], d)
    tied = lax.optimization_barrier((*grads, *od[1:]))
    grads, od[1:] = tied[:4], tied[4:]
    rows = bf16(ROWS, HEADS * HEAD_DIM)
    keep, send = call(share_kernel, (bf16(PROWS, width),) * 2, (), (info,), *grads)
    share = rounded(keep.astype(F32) + swap(send, "core").astype(F32))
    share = rounded(share.astype(F32) + swap(share, "xl").astype(F32))
    key_grad, value_grad = call(
        finish_kernel, (bf16(ROWS, width),) * 2, (), (info,), *grads
    )
    attended, query_grad = call(unpack_kernel, (rows, rows), (), (info,), *od)
    share, key_grad, value_grad, attended, query_grad = lax.optimization_barrier(
        (share, key_grad, value_grad, attended, query_grad)
    )
    for pairs in ([(0, 1), (1, 0), (2, 3), (3, 2)], [(0, 3), (3, 0), (1, 2), (2, 1)]):
        share = rounded(share.astype(F32) + lax.ppermute(share, "y", pairs).astype(F32))
    other = swap(share, "core")
    key_share = jnp.where(core == 0, share, other)
    value_share = jnp.where(core == 0, other, share)
    return (
        attended[None],
        query_grad[None],
        key_grad[None],
        value_grad[None],
        key_share,
        value_share,
    )


def solution(mesh):
    split = Mesh(mesh.devices.reshape(2, 8, 4, 2, 2), CTX + RESP)
    rows = P(RESP, CTX, None)
    prompt = P(CTX, None)
    return jax.shard_map(
        body,
        mesh=split,
        in_specs=(rows, rows, rows, prompt, prompt, rows, P(RESP), P(RESP)),
        out_specs=(rows, rows, rows, rows, prompt, prompt),
        check_vma=False,
    )
```

```python
import math

import jax
import jax.numpy as jnp
from jax import lax
from jax.experimental import pallas as pl
from jax.experimental.pallas import tpu as pltpu
from jax.sharding import Mesh
from jax.sharding import PartitionSpec as P

HEADS = 16
KV_HEADS = 4
HEAD_DIM = 128
GROUP = HEADS // KV_HEADS
RESP_LEN = 2048
PROMPT_LEN = 1024
CTX = ("xh", "z")
LOCAL = ("xh", "z", "core")
RESP = ("y", "xl", "core")
ROWS = 128
PROWS = 64
BOTH = ROWS + PROWS
CHUNK = 256
SPAN = 3 * CHUNK
TILE_SPANS = (2 * CHUNK, 3 * CHUNK)
TILE_STARTS = (0, 2 * CHUNK)
PROBS = 5 * CHUNK
HALF = GROUP * ROWS
LANES = 2 * HALF
WIDE = 2 * HEAD_DIM
SCALE = HEAD_DIM**-0.5
SCALE2 = SCALE * math.log2(math.e)
NEG = -1e30
F32 = jnp.float32
BF16 = jnp.bfloat16
VMEM = pl.BlockSpec(memory_space=pltpu.VMEM)
SMEM = pl.BlockSpec(memory_space=pltpu.SMEM)


def dot(a, b):
    return jnp.dot(a, b, preferred_element_type=F32)


def head_at(h, width=HEAD_DIM):
    return slice(h * width, (h + 1) * width)


def lanes_at(j, h):
    return slice(j * HALF + h * HEAD_DIM, j * HALF + (h + 1) * HEAD_DIM)


def block_of(member, quad, core):
    return (member // 2) * 8 + ((quad * 2 + (member & 1) + core) & 7)


def run_copies(pairs, sems):
    copies = [
        pltpu.make_async_copy(source, to, sems.at[i]) for i, (source, to) in enumerate(pairs)
    ]
    for copy in copies:
        copy.start()
    for copy in copies:
        copy.wait()


def pack_kv_kernel(info, k, v, kp, vp, kv0, kv1, kv2, kv3, k_s, v_s, kp_s, vp_s, sems):
    mine = info[0]
    run_copies(((k, k_s), (v, v_s), (kp, kp_s), (vp, vp_s)), sems)
    for d, kv in enumerate((kv0, kv1, kv2, kv3)):
        at = pl.ds(pl.multiple_of((mine ^ d) * HEAD_DIM, HEAD_DIM), HEAD_DIM)
        kv[:ROWS, :HEAD_DIM] = k_s[:, at]
        kv[:ROWS, HEAD_DIM:] = v_s[:, at]
        kv[ROWS:, :HEAD_DIM] = kp_s[:, at]
        kv[ROWS:, HEAD_DIM:] = vp_s[:, at]


def pack_qd_kernel(info, q, do, qd0, qd1, qd2, qd3, q_s, do_s, sems):
    mine = info[0]
    run_copies(((q, q_s), (do, do_s)), sems)
    for d, qd in enumerate((qd0, qd1, qd2, qd3)):
        at = pl.ds(pl.multiple_of((mine ^ d) * HALF, HALF), HALF)
        qd[:, :HALF] = q_s[:, at]
        qd[:, HALF:] = do_s[:, at]


def rows_at(mine, d):
    return pl.ds(pl.multiple_of(CHUNK + (mine ^ d) // 2 * CHUNK + (d & 1) * ROWS, ROWS), ROWS)


def load_keys(mine, g, kvs, k_s, v_s):
    for d, kv in enumerate(kvs):
        k_s[g, rows_at(mine, d), :] = kv[:ROWS, :HEAD_DIM]
        v_s[g, rows_at(mine, d), :] = kv[:ROWS, HEAD_DIM:]
        k_s[g, head_at(d, PROWS), :] = kv[ROWS:, :HEAD_DIM]
        v_s[g, head_at(d, PROWS), :] = kv[ROWS:, HEAD_DIM:]


def query_rows(info, x):
    mine, quad, core = info[0], info[1], info[2]
    rows = []
    for j in range(2):
        start = block_of(x * 2 + ((mine & 1) ^ j), quad, core) * ROWS
        rows += [start + lax.broadcasted_iota(jnp.int32, (1, ROWS), 1)] * GROUP
    return jnp.concatenate(rows, axis=1)


def key_rows(info, x, quad):
    mine, core = info[0], info[2]
    rows = []
    for j in range(2):
        start = block_of(x * 2 + ((mine & 1) ^ j), quad, core) * ROWS
        rows.append(start + lax.broadcasted_iota(jnp.int32, (ROWS, 1), 0))
    return jnp.concatenate(rows, axis=0)


def fold(x, op):
    return op(x.reshape(x.shape[0] // 8, 8, LANES), axis=0)


def each(count, step, carry):
    return step(0, carry) if count == 1 else lax.fori_loop(0, count, step, carry)


def forward(info, quads, count, k_s, v_s, qt, before, score_s, probs, vt_s, shift, total, acc):
    def turn_values(g, carry):
        vt_s[g] = v_s[g].T
        return carry

    each(count, turn_values, 0)
    for x in range(2):
        place = query_rows(info, x)
        start, span = TILE_STARTS[x], TILE_SPANS[x]

        def score_step(g, running):
            for c in range(span // CHUNK):
                at = slice(c * CHUNK, (c + 1) * CHUNK)
                score = dot(k_s[g, at, :], qt[x])
                if c > 0:
                    score = jnp.where(key_rows(info, c - 1, quads(g)) <= place, score, NEG)
                score_s[g, at, :] = score
                running = jnp.maximum(running, fold(score, jnp.max))
            return running

        running = each(count, score_step, jnp.full((8, LANES), NEG, F32))
        now = jnp.max(running, axis=0, keepdims=True) * SCALE2
        if before is not None:
            now = jnp.maximum(now, before[0][x])
            factor = jnp.exp2(before[0][x] - now)
            acc[x] = before[2][x] * factor

        def prob_step(g, running):
            for c in range(span // CHUNK):
                prob = jnp.exp2(score_s[g, c * CHUNK : (c + 1) * CHUNK, :] * SCALE2 - now)
                running = running + fold(prob, jnp.sum)
                probs[g, start + c * CHUNK : start + (c + 1) * CHUNK, :] = prob.astype(BF16)
            part = dot(vt_s[g, :, :span], probs[g, start : start + span, :])
            if before is None:
                acc[x] = part
            else:
                acc[x] += part
            return running

        running = each(count, prob_step, jnp.zeros((8, LANES), F32))
        sums = jnp.sum(running, axis=0, keepdims=True)
        if before is not None:
            sums = sums + before[1][x] * factor
        shift[x], total[x] = now, sums


def chunk_at(c, start):
    if isinstance(c, int):
        return slice(start + c * CHUNK, start + (c + 1) * CHUNK)
    return pl.ds(pl.multiple_of(start + c * CHUNK, CHUNK), CHUNK)


def backward(count, looped, k_s, v_s, kt_s, q, uplt, upl, delta, probs, factors, grad_s, before, dqt):
    for x in range(2):
        dqt[x] = jnp.zeros((HEAD_DIM, LANES), F32) if before is None else before[x]

    def chunk(g, c, tiles):
        at = chunk_at(c, 0)
        dk, dv = None, None
        for x in tiles:
            here = chunk_at(c, TILE_STARTS[x])
            low = probs[g, here, :]
            if factors is not None:
                low = (low.astype(F32) * factors[x]).astype(BF16)
            prob_grad = dot(v_s[g, at, :], uplt[x])
            grad = (low.astype(F32) * (prob_grad - delta[x])).astype(BF16)
            grad_s[here, :] = grad
            dv_part = dot(low, upl[x])
            dk_part = dot(grad, q[x])
            dv = dv_part if dv is None else dv + dv_part
            dk = dk_part if dk is None else dk + dk_part
        k_s[g, at, :] = (dk * SCALE).astype(BF16)
        v_s[g, at, :] = dv.astype(BF16)

    def step(g, carry):
        kt_s[...] = k_s[g].T

        def two_tiles(c, carry):
            chunk(g, c, (0, 1))
            return carry

        if looped:
            lax.fori_loop(0, 2, two_tiles, 0)
        else:
            two_tiles(0, 0)
            two_tiles(1, 0)
        chunk(g, 2, (1,))
        for x in range(2):
            start, span = TILE_STARTS[x], TILE_SPANS[x]
            dqt[x] += dot(kt_s[:, :span], grad_s[start : start + span, :])
        return carry

    each(count, step, 0)


def store_grads(mine, g, k_s, v_s, outs):
    for d, out in enumerate(outs):
        out[:ROWS, :HEAD_DIM] = k_s[g, rows_at(mine, d), :]
        out[:ROWS, HEAD_DIM:] = v_s[g, rows_at(mine, d), :]
        out[ROWS:, :HEAD_DIM] = k_s[g, head_at(d, PROWS), :]
        out[ROWS:, HEAD_DIM:] = v_s[g, head_at(d, PROWS), :]


def pieces(*parts):
    return [part.at[d] for part in parts for d in range(part.shape[0])]


def first_kernel(
    info, weight, qd0, qd1, qd2, qd3, own_a, own_b,
    qt, q, upt, probs, shift, total, acc,
    k_s, v_s, vt_s, score_s,
):
    mine, quad, core, count = info[0], info[1], info[2], info[4]
    load_keys(mine, 0, pieces(own_a, own_b), k_s, v_s)
    for d, qd in enumerate((qd0, qd1, qd2, qd3)):
        x = (mine ^ d) // 2
        row = block_of(mine ^ d, quad, core) * ROWS
        row = row + lax.broadcasted_iota(jnp.int32, (1, ROWS), 1)
        row_weight = jnp.where(row < count, weight[0], 0.0)
        for h in range(GROUP):
            cols = lanes_at(d & 1, h)
            q_head = qd[:, head_at(h)]
            q[x, cols, :] = q_head
            qt[x, :, cols] = q_head.T
            grad = qd[:, HALF + h * HEAD_DIM : HALF + (h + 1) * HEAD_DIM]
            upt[x, :, cols] = (grad.T.astype(F32) * row_weight).astype(BF16)
    forward(
        info, lambda g: quad, 1, k_s, v_s, qt, None, score_s, probs, vt_s, shift, total, acc
    )


def side_kernel(
    info, qt, left_a, left_b, right_a, right_b, shift0, total0, acc0,
    probs, shift, total, acc,
    k_s, v_s, vt_s, score_s,
):
    mine, quad = info[0], info[1]
    load_keys(mine, 0, pieces(left_a, left_b), k_s, v_s)
    load_keys(mine, 1, pieces(right_a, right_b), k_s, v_s)
    forward(
        info, lambda g: (quad + 3 + 2 * g) & 3, 2, k_s, v_s, qt, (shift0, total0, acc0),
        score_s, probs, vt_s, shift, total, acc,
    )


def far_kernel(
    info, qt, q, upt, far_a, far_b, shift0, total0, acc0,
    shift, uplt, upl, delta, dqt, attn, out_a, out_b,
    k_s, v_s, vt_s, kt_s, score_s, probs, grad_s, acc, total,
):
    mine, quad, length = info[0], info[1], info[3]
    load_keys(mine, 0, pieces(far_a, far_b), k_s, v_s)
    forward(
        info, lambda g: (quad + 2) & 3, 1, k_s, v_s, qt, (shift0, total0, acc0),
        score_s, probs, vt_s, shift, total, acc,
    )
    for x in range(2):
        inverse = 1.0 / total[x]
        valid = jnp.where(query_rows(info, x) < length, 1.0, 0.0)
        out_t = (acc[x] * (inverse * valid)).astype(BF16)
        up_low = (upt[x].astype(F32) * inverse).astype(BF16)
        uplt[x] = up_low
        delta[x] = jnp.sum(up_low.astype(F32) * out_t.astype(F32), axis=0, keepdims=True)
        attn[x] = out_t
        for j in range(2):
            for h in range(GROUP):
                upl[x, lanes_at(j, h), :] = up_low[:, lanes_at(j, h)].T
    backward(
        1, False, k_s, v_s, kt_s, q, uplt, upl, delta, probs, None, grad_s, None, dqt
    )
    store_grads(mine, 0, k_s, v_s, pieces(out_a, out_b))


def back_side_kernel(
    info, q, uplt, upl, delta, shift_then, shift_last, probs,
    left_a, left_b, right_a, right_b, dqt0,
    dqt, out_l, out_r,
    k_s, v_s, kt_s, grad_s,
):
    mine = info[0]
    factors = [jnp.exp2(shift_then[x] - shift_last[x]) for x in range(2)]
    load_keys(mine, 0, pieces(left_a, left_b), k_s, v_s)
    load_keys(mine, 1, pieces(right_a, right_b), k_s, v_s)
    backward(
        2, False, k_s, v_s, kt_s, q, uplt, upl, delta, probs, factors, grad_s, dqt0, dqt
    )
    store_grads(mine, 0, k_s, v_s, pieces(out_l))
    store_grads(mine, 1, k_s, v_s, pieces(out_r))


def back_own_kernel(
    info, q, uplt, upl, delta, shift_then, shift_last, probs, own_a, own_b, dqt0, attn,
    out, od0, od1, od2, od3,
    k_s, v_s, kt_s, grad_s, dqt, dq_s,
):
    mine = info[0]
    factors = [jnp.exp2(shift_then[x] - shift_last[x]) for x in range(2)]
    load_keys(mine, 0, pieces(own_a, own_b), k_s, v_s)
    backward(
        1, True, k_s, v_s, kt_s, q, uplt, upl, delta, probs, factors, grad_s, dqt0, dqt
    )
    store_grads(mine, 0, k_s, v_s, pieces(out))
    for x in range(2):
        dq_s[x] = (dqt[x] * SCALE).astype(BF16)
    for d, od in enumerate((od0, od1, od2, od3)):
        x = (mine ^ d) // 2
        for h in range(GROUP):
            od[:, head_at(h)] = attn[x, :, lanes_at(d & 1, h)].T
            od[:, HALF + h * HEAD_DIM : HALF + (h + 1) * HEAD_DIM] = dq_s[
                x, :, lanes_at(d & 1, h)
            ].T


def unpack_kernel(info, od0, od1, od2, od3, attended, query_grad):
    mine = info[0]
    for d, od in enumerate((od0, od1, od2, od3)):
        at = pl.ds(pl.multiple_of((mine ^ d) * HALF, HALF), HALF)
        attended[:, at] = od[:, :HALF]
        query_grad[:, at] = od[:, HALF:]


def both(a, b):
    return (a.astype(F32) + b.astype(F32)).astype(BF16)


def add_kernel(side_l, side_r, far_a, far_b, out_l, out_r):
    out_r[:2] = both(side_r[:2], far_a[...])
    out_r[2:] = side_r[2:]
    out_l[:2] = side_l[:2]
    out_l[2:] = both(side_l[2:], far_b[...])


def sum_kernel(own, left, right, *outs):
    for d, out in enumerate(outs):
        total = own[d].astype(F32) + left[d].astype(F32) + right[d].astype(F32)
        out[...] = total.astype(BF16)


def share_kernel(info, g0, g1, g2, g3, keep, send):
    mine, first = info[0], info[2] == 0
    for d, g in enumerate((g0, g1, g2, g3)):
        at = pl.ds(pl.multiple_of((mine ^ d) * HEAD_DIM, HEAD_DIM), HEAD_DIM)
        keys, values = g[ROWS:, :HEAD_DIM], g[ROWS:, HEAD_DIM:]
        keep[:, at] = jnp.where(first, keys, values)
        send[:, at] = jnp.where(first, values, keys)


def finish_kernel(info, g0, g1, g2, g3, key_grad, value_grad):
    mine = info[0]
    for d, g in enumerate((g0, g1, g2, g3)):
        at = pl.ds(pl.multiple_of((mine ^ d) * HEAD_DIM, HEAD_DIM), HEAD_DIM)
        key_grad[:, at] = g[:ROWS, :HEAD_DIM]
        value_grad[:, at] = g[:ROWS, HEAD_DIM:]


def bf16(*shape):
    return jax.ShapeDtypeStruct(shape, BF16)


def f32(*shape):
    return jax.ShapeDtypeStruct(shape, F32)


def call(kernel, outs, scratch, scalars, *operands, copies=0, products=0):
    place = pl.BlockSpec(memory_space=pl.ANY) if copies else VMEM
    scratch = [pltpu.VMEM(shape, dtype) for shape, dtype in scratch]
    if copies:
        scratch.append(pltpu.SemaphoreType.DMA((copies,)))
    return pl.pallas_call(
        kernel,
        out_shape=tuple(outs),
        in_specs=[SMEM] * len(scalars) + [place] * len(operands),
        out_specs=(VMEM,) * len(outs),
        scratch_shapes=scratch,
        compiler_params=pltpu.CompilerParams(vmem_limit_bytes=(56 if copies else 32) * 2**20),
        cost_estimate=pl.CostEstimate(
            flops=products * PROBS * LANES * HEAD_DIM * 4,
            bytes_accessed=1_000_000,
            transcendentals=0,
        ),
    )(*scalars, *operands)


def swap(x, axis):
    return lax.ppermute(x, axis, [(0, 1), (1, 0)])


def turn(x, axis, step):
    size = lax.axis_size(axis)
    return lax.ppermute(x, axis, [(i, (i + step) % size) for i in range(size)])


def local_permute(x, place):
    pairs = []
    for i in range(32):
        xh, z, core = i // 16, i // 2 % 8, i % 2
        xh, z = place(xh, (z - core) % 8)
        pairs.append((i, (xh * 8 + (z + core) % 8) * 2 + core))
    return lax.ppermute(x, LOCAL, pairs)


def partner(x, d):
    return local_permute(x, lambda xh, z: (xh ^ (d // 2), z ^ (d & 1)))


def quad_turn(x, step):
    return local_permute(x, lambda xh, z: (xh, (z + 2 * step) % 8))


def rounded(x):
    return lax.optimization_barrier(x.astype(BF16))


def body(q_resp, k_resp, v_resp, k_prompt, v_prompt, d_out, lengths, counts):
    core = lax.axis_index("core")
    z = (lax.axis_index("z") - core) & 7
    mine = lax.axis_index("xh") * 2 + (z & 1)
    info = jnp.stack([mine, z // 2, core, lengths[0], counts[0]]).astype(jnp.int32)
    weight = (RESP_LEN / counts[0].astype(F32)).reshape(1)
    spot = mine.reshape(1).astype(jnp.int32)
    width = KV_HEADS * HEAD_DIM
    kv = list(
        call(
            pack_kv_kernel,
            (bf16(BOTH, WIDE),) * 4,
            [((ROWS, width), BF16)] * 2 + [((PROWS, width), BF16)] * 2,
            (spot,),
            k_resp[0], v_resp[0], k_prompt, v_prompt,
            copies=4,
        )
    )
    qd = list(
        call(
            pack_qd_kernel,
            (bf16(ROWS, LANES),) * 4,
            [((ROWS, HEADS * HEAD_DIM), BF16)] * 2,
            (spot,),
            q_resp[0], d_out[0],
            copies=2,
        )
    )
    for d in (1, 2, 3):
        kv[d] = partner(kv[d], d)
    for d in (1, 2, 3):
        qd[d] = partner(qd[d], d)
    own_a, own_b = jnp.stack(kv[:2]), jnp.stack(kv[2:])
    left_a, right_b = quad_turn(own_a, 1), quad_turn(own_b, -1)
    left_b, right_a = quad_turn(own_b, 1), quad_turn(own_a, -1)
    far_a, far_b = quad_turn(left_a, 1), quad_turn(right_b, -1)

    tiles = (2, HEAD_DIM, LANES)
    line = f32(2, 1, LANES)

    def keys(count):
        return [((count, SPAN, HEAD_DIM), BF16)] * 2

    def forward_scratch(count):
        return keys(count) + [((count, HEAD_DIM, SPAN), BF16), ((count, SPAN, LANES), F32)]

    turned = ((HEAD_DIM, SPAN), BF16)
    grad_s = ((PROBS, LANES), BF16)
    whole, pair = bf16(4, BOTH, WIDE), bf16(2, BOTH, WIDE)
    qt, q, upt, probs1, shift1, total1, acc1 = call(
        first_kernel,
        (bf16(*tiles), bf16(2, LANES, HEAD_DIM), bf16(*tiles), bf16(1, PROBS, LANES), line, line, f32(*tiles)),
        forward_scratch(1),
        (info, weight),
        *qd, own_a, own_b,
        products=2,
    )
    probs2, shift2, total2, acc2 = call(
        side_kernel,
        (bf16(2, PROBS, LANES), line, line, f32(*tiles)),
        forward_scratch(2),
        (info,),
        qt, left_a, left_b, right_a, right_b, shift1, total1, acc1,
        products=4,
    )
    shift3, uplt, upl, delta, dqt, attn, far_ga, far_gb = call(
        far_kernel,
        (line, bf16(*tiles), bf16(2, LANES, HEAD_DIM), line, f32(*tiles), bf16(*tiles), pair, pair),
        keys(1) + [((1, HEAD_DIM, SPAN), BF16), turned, ((1, SPAN, LANES), F32)]
        + [((1, PROBS, LANES), BF16), grad_s, (tiles, F32), ((2, 1, LANES), F32)],
        (info,),
        qt, q, upt, far_a, far_b, shift2, total2, acc2,
        products=6,
    )
    far_ga, far_gb = quad_turn(far_ga, 1), quad_turn(far_gb, -1)
    dqt, left_g, right_g = call(
        back_side_kernel,
        (f32(*tiles), whole, whole),
        keys(2) + [turned, grad_s],
        (info,),
        q, uplt, upl, delta, shift2, shift3, probs2,
        left_a, left_b, right_a, right_b, dqt,
        products=8,
    )
    left_g, right_g = call(add_kernel, (whole, whole), (), (), left_g, right_g, far_ga, far_gb)
    left_g, right_g = quad_turn(left_g, -1), quad_turn(right_g, 1)
    own_g, *od = call(
        back_own_kernel,
        (whole,) + (bf16(ROWS, LANES),) * 4,
        keys(1) + [turned, grad_s, (tiles, F32), (tiles, BF16)],
        (info,),
        q, uplt, upl, delta, shift1, shift3, probs1, own_a, own_b, dqt, attn,
        products=4,
    )
    for d in (3, 2, 1):
        od[d] = partner(od[d], d)
    grads = list(call(sum_kernel, (bf16(BOTH, WIDE),) * 4, (), (), own_g, left_g, right_g))
    for d in (1, 2, 3):
        grads[d] = partner(grads[d], d)
    tied = lax.optimization_barrier((*grads, *od[1:]))
    grads, od[1:] = tied[:4], tied[4:]
    rows = bf16(ROWS, HEADS * HEAD_DIM)
    keep, send = call(share_kernel, (bf16(PROWS, width),) * 2, (), (info,), *grads)
    share = rounded(keep.astype(F32) + swap(send, "core").astype(F32))
    share = rounded(share.astype(F32) + swap(share, "xl").astype(F32))
    key_grad, value_grad = call(
        finish_kernel, (bf16(ROWS, width),) * 2, (), (info,), *grads
    )
    attended, query_grad = call(unpack_kernel, (rows, rows), (), (info,), *od)
    share, key_grad, value_grad, attended, query_grad = lax.optimization_barrier(
        (share, key_grad, value_grad, attended, query_grad)
    )
    across = share.astype(F32) + turn(share, "y", 2).astype(F32)
    beside = turn(share, "y", 1).astype(F32) + turn(share, "y", 3).astype(F32)
    share = rounded(across + beside)
    other = swap(share, "core")
    key_share = jnp.where(core == 0, share, other)
    value_share = jnp.where(core == 0, other, share)
    return (
        attended[None],
        query_grad[None],
        key_grad[None],
        value_grad[None],
        key_share,
        value_share,
    )


def solution(mesh):
    split = Mesh(mesh.devices.reshape(2, 8, 4, 2, 2), CTX + RESP)
    rows = P(RESP, CTX, None)
    prompt = P(CTX, None)
    return jax.shard_map(
        body,
        mesh=split,
        in_specs=(rows, rows, rows, prompt, prompt, rows, P(RESP), P(RESP)),
        out_specs=(rows, rows, rows, rows, prompt, prompt),
        check_vma=False,
    )
```

```python
import math

import jax
import jax.numpy as jnp
from jax import lax
from jax.experimental import pallas as pl
from jax.experimental.pallas import tpu as pltpu
from jax.sharding import Mesh
from jax.sharding import PartitionSpec as P

HEADS = 16
KV_HEADS = 4
HEAD_DIM = 128
GROUP = HEADS // KV_HEADS
RESP_LEN = 2048
PROMPT_LEN = 1024
CTX = ("xh", "z")
LOCAL = ("xh", "z", "core")
RESP = ("y", "xl", "core")
ROWS = 128
PROWS = 64
BOTH = ROWS + PROWS
CHUNK = 256
SPAN = 3 * CHUNK
TILE_SPANS = (2 * CHUNK, 3 * CHUNK)
TILE_STARTS = (0, 2 * CHUNK)
PROBS = 5 * CHUNK
HALF = GROUP * ROWS
LANES = 2 * HALF
WIDE = 2 * HEAD_DIM
SCALE = HEAD_DIM**-0.5
SCALE2 = SCALE * math.log2(math.e)
NEG = -1e30
F32 = jnp.float32
BF16 = jnp.bfloat16
VMEM = pl.BlockSpec(memory_space=pltpu.VMEM)
SMEM = pl.BlockSpec(memory_space=pltpu.SMEM)


def dot(a, b):
    return jnp.dot(a, b, preferred_element_type=F32)


def head_at(h, width=HEAD_DIM):
    return slice(h * width, (h + 1) * width)


def lanes_at(j, h):
    return slice(j * HALF + h * HEAD_DIM, j * HALF + (h + 1) * HEAD_DIM)


def block_of(member, quad, core):
    return (member // 2) * 8 + ((quad * 2 + (member & 1) + core) & 7)


def run_copies(pairs, sems):
    copies = [
        pltpu.make_async_copy(source, to, sems.at[i]) for i, (source, to) in enumerate(pairs)
    ]
    for copy in copies:
        copy.start()
    for copy in copies:
        copy.wait()


def pack_kv_kernel(info, k, v, kp, vp, kv0, kv1, kv2, kv3, k_s, v_s, kp_s, vp_s, sems):
    mine = info[0]
    run_copies(((k, k_s), (v, v_s), (kp, kp_s), (vp, vp_s)), sems)
    for d, kv in enumerate((kv0, kv1, kv2, kv3)):
        at = pl.ds(pl.multiple_of((mine ^ d) * HEAD_DIM, HEAD_DIM), HEAD_DIM)
        kv[:ROWS, :HEAD_DIM] = k_s[:, at]
        kv[:ROWS, HEAD_DIM:] = v_s[:, at]
        kv[ROWS:, :HEAD_DIM] = kp_s[:, at]
        kv[ROWS:, HEAD_DIM:] = vp_s[:, at]


def pack_qd_kernel(info, q, do, qd0, qd1, qd2, qd3, q_s, do_s, sems):
    mine = info[0]
    run_copies(((q, q_s), (do, do_s)), sems)
    for d, qd in enumerate((qd0, qd1, qd2, qd3)):
        at = pl.ds(pl.multiple_of((mine ^ d) * HALF, HALF), HALF)
        qd[:, :HALF] = q_s[:, at]
        qd[:, HALF:] = do_s[:, at]


def rows_at(mine, d):
    return pl.ds(pl.multiple_of(CHUNK + (mine ^ d) // 2 * CHUNK + (d & 1) * ROWS, ROWS), ROWS)


def load_keys(mine, g, kvs, k_s, v_s):
    for d, kv in enumerate(kvs):
        k_s[g, rows_at(mine, d), :] = kv[:ROWS, :HEAD_DIM]
        v_s[g, rows_at(mine, d), :] = kv[:ROWS, HEAD_DIM:]
        k_s[g, head_at(d, PROWS), :] = kv[ROWS:, :HEAD_DIM]
        v_s[g, head_at(d, PROWS), :] = kv[ROWS:, HEAD_DIM:]


def query_rows(info, x):
    mine, quad, core = info[0], info[1], info[2]
    rows = []
    for j in range(2):
        start = block_of(x * 2 + ((mine & 1) ^ j), quad, core) * ROWS
        rows += [start + lax.broadcasted_iota(jnp.int32, (1, ROWS), 1)] * GROUP
    return jnp.concatenate(rows, axis=1)


def key_rows(info, x, quad):
    mine, core = info[0], info[2]
    rows = []
    for j in range(2):
        start = block_of(x * 2 + ((mine & 1) ^ j), quad, core) * ROWS
        rows.append(start + lax.broadcasted_iota(jnp.int32, (ROWS, 1), 0))
    return jnp.concatenate(rows, axis=0)


def fold(x, op):
    return op(x.reshape(x.shape[0] // 8, 8, LANES), axis=0)


def each(count, step, carry):
    return step(0, carry) if count == 1 else lax.fori_loop(0, count, step, carry)


def forward(info, quads, count, k_s, v_s, qt, before, score_s, probs, vt_s, shift, total, acc):
    def turn_values(g, carry):
        vt_s[g] = v_s[g].T
        return carry

    each(count, turn_values, 0)
    for x in range(2):
        place = query_rows(info, x)
        start, span = TILE_STARTS[x], TILE_SPANS[x]

        def score_step(g, running):
            for c in range(span // CHUNK):
                at = slice(c * CHUNK, (c + 1) * CHUNK)
                score = dot(k_s[g, at, :], qt[x])
                if c > 0:
                    score = jnp.where(key_rows(info, c - 1, quads(g)) <= place, score, NEG)
                score_s[g, at, :] = score
                running = jnp.maximum(running, fold(score, jnp.max))
            return running

        running = each(count, score_step, jnp.full((8, LANES), NEG, F32))
        now = jnp.max(running, axis=0, keepdims=True) * SCALE2
        if before is not None:
            now = jnp.maximum(now, before[0][x])
            factor = jnp.exp2(before[0][x] - now)
            acc[x] = before[2][x] * factor

        def prob_step(g, running):
            for c in range(span // CHUNK):
                prob = jnp.exp2(score_s[g, c * CHUNK : (c + 1) * CHUNK, :] * SCALE2 - now)
                running = running + fold(prob, jnp.sum)
                probs[g, start + c * CHUNK : start + (c + 1) * CHUNK, :] = prob.astype(BF16)
            part = dot(vt_s[g, :, :span], probs[g, start : start + span, :])
            if before is None:
                acc[x] = part
            else:
                acc[x] += part
            return running

        running = each(count, prob_step, jnp.zeros((8, LANES), F32))
        sums = jnp.sum(running, axis=0, keepdims=True)
        if before is not None:
            sums = sums + before[1][x] * factor
        shift[x], total[x] = now, sums


def chunk_at(c, start):
    if isinstance(c, int):
        return slice(start + c * CHUNK, start + (c + 1) * CHUNK)
    return pl.ds(pl.multiple_of(start + c * CHUNK, CHUNK), CHUNK)


def backward(count, looped, k_s, v_s, kt_s, q, uplt, upl, delta, probs, factors, grad_s, before, dqt):
    for x in range(2):
        dqt[x] = jnp.zeros((HEAD_DIM, LANES), F32) if before is None else before[x]

    def chunk(g, c, tiles):
        at = chunk_at(c, 0)
        dk, dv = None, None
        for x in tiles:
            here = chunk_at(c, TILE_STARTS[x])
            low = probs[g, here, :]
            if factors is not None:
                low = (low.astype(F32) * factors[x]).astype(BF16)
            prob_grad = dot(v_s[g, at, :], uplt[x])
            grad = (low.astype(F32) * (prob_grad - delta[x])).astype(BF16)
            grad_s[here, :] = grad
            dv_part = dot(low, upl[x])
            dk_part = dot(grad, q[x])
            dv = dv_part if dv is None else dv + dv_part
            dk = dk_part if dk is None else dk + dk_part
        k_s[g, at, :] = (dk * SCALE).astype(BF16)
        v_s[g, at, :] = dv.astype(BF16)

    def step(g, carry):
        kt_s[...] = k_s[g].T

        def two_tiles(c, carry):
            chunk(g, c, (0, 1))
            return carry

        if looped:
            lax.fori_loop(0, 2, two_tiles, 0)
        else:
            two_tiles(0, 0)
            two_tiles(1, 0)
        chunk(g, 2, (1,))
        for x in range(2):
            start, span = TILE_STARTS[x], TILE_SPANS[x]
            dqt[x] += dot(kt_s[:, :span], grad_s[start : start + span, :])
        return carry

    each(count, step, 0)


def store_grads(mine, g, k_s, v_s, outs):
    for d, out in enumerate(outs):
        out[:ROWS, :HEAD_DIM] = k_s[g, rows_at(mine, d), :]
        out[:ROWS, HEAD_DIM:] = v_s[g, rows_at(mine, d), :]
        out[ROWS:, :HEAD_DIM] = k_s[g, head_at(d, PROWS), :]
        out[ROWS:, HEAD_DIM:] = v_s[g, head_at(d, PROWS), :]


def pieces(*parts):
    return [part.at[d] for part in parts for d in range(part.shape[0])]


def first_kernel(
    info, weight, qd0, qd1, qd2, qd3, own_a, own_b,
    qt, q, upt, probs, shift, total, acc,
    k_s, v_s, vt_s, score_s,
):
    mine, quad, core, count = info[0], info[1], info[2], info[4]
    load_keys(mine, 0, pieces(own_a, own_b), k_s, v_s)
    for d, qd in enumerate((qd0, qd1, qd2, qd3)):
        x = (mine ^ d) // 2
        row = block_of(mine ^ d, quad, core) * ROWS
        row = row + lax.broadcasted_iota(jnp.int32, (1, ROWS), 1)
        row_weight = jnp.where(row < count, weight[0], 0.0)
        for h in range(GROUP):
            cols = lanes_at(d & 1, h)
            q_head = qd[:, head_at(h)]
            q[x, cols, :] = q_head
            qt[x, :, cols] = q_head.T
            grad = qd[:, HALF + h * HEAD_DIM : HALF + (h + 1) * HEAD_DIM]
            upt[x, :, cols] = (grad.T.astype(F32) * row_weight).astype(BF16)
    forward(
        info, lambda g: quad, 1, k_s, v_s, qt, None, score_s, probs, vt_s, shift, total, acc
    )


def side_kernel(
    info, qt, left_a, left_b, right_a, right_b, shift0, total0, acc0,
    probs, shift, total, acc,
    k_s, v_s, vt_s, score_s,
):
    mine, quad = info[0], info[1]
    load_keys(mine, 0, pieces(left_a, left_b), k_s, v_s)
    load_keys(mine, 1, pieces(right_a, right_b), k_s, v_s)
    forward(
        info, lambda g: (quad + 3 + 2 * g) & 3, 2, k_s, v_s, qt, (shift0, total0, acc0),
        score_s, probs, vt_s, shift, total, acc,
    )


def far_kernel(
    info, qt, q, upt, far_a, far_b, shift0, total0, acc0,
    shift, uplt, upl, delta, dqt, attn, out_a, out_b,
    k_s, v_s, vt_s, kt_s, score_s, probs, grad_s, acc, total,
):
    mine, quad, length = info[0], info[1], info[3]
    load_keys(mine, 0, pieces(far_a, far_b), k_s, v_s)
    forward(
        info, lambda g: (quad + 2) & 3, 1, k_s, v_s, qt, (shift0, total0, acc0),
        score_s, probs, vt_s, shift, total, acc,
    )
    for x in range(2):
        inverse = 1.0 / total[x]
        valid = jnp.where(query_rows(info, x) < length, 1.0, 0.0)
        out_t = (acc[x] * (inverse * valid)).astype(BF16)
        up_low = (upt[x].astype(F32) * inverse).astype(BF16)
        uplt[x] = up_low
        delta[x] = jnp.sum(up_low.astype(F32) * out_t.astype(F32), axis=0, keepdims=True)
        attn[x] = out_t
        for j in range(2):
            for h in range(GROUP):
                upl[x, lanes_at(j, h), :] = up_low[:, lanes_at(j, h)].T
    backward(
        1, False, k_s, v_s, kt_s, q, uplt, upl, delta, probs, None, grad_s, None, dqt
    )
    store_grads(mine, 0, k_s, v_s, pieces(out_a, out_b))


def back_side_kernel(
    info, q, uplt, upl, delta, shift_then, shift_last, probs,
    left_a, left_b, right_a, right_b, dqt0,
    dqt, out_l, out_r,
    k_s, v_s, kt_s, grad_s,
):
    mine = info[0]
    factors = [jnp.exp2(shift_then[x] - shift_last[x]) for x in range(2)]
    load_keys(mine, 0, pieces(left_a, left_b), k_s, v_s)
    load_keys(mine, 1, pieces(right_a, right_b), k_s, v_s)
    backward(
        2, False, k_s, v_s, kt_s, q, uplt, upl, delta, probs, factors, grad_s, dqt0, dqt
    )
    store_grads(mine, 0, k_s, v_s, pieces(out_l))
    store_grads(mine, 1, k_s, v_s, pieces(out_r))


def back_own_kernel(
    info, q, uplt, upl, delta, shift_then, shift_last, probs, own_a, own_b, dqt0, attn,
    out, od0, od1, od2, od3,
    k_s, v_s, kt_s, grad_s, dqt, dq_s,
):
    mine = info[0]
    factors = [jnp.exp2(shift_then[x] - shift_last[x]) for x in range(2)]
    load_keys(mine, 0, pieces(own_a, own_b), k_s, v_s)
    backward(
        1, True, k_s, v_s, kt_s, q, uplt, upl, delta, probs, factors, grad_s, dqt0, dqt
    )
    store_grads(mine, 0, k_s, v_s, pieces(out))
    for x in range(2):
        dq_s[x] = (dqt[x] * SCALE).astype(BF16)
    for d, od in enumerate((od0, od1, od2, od3)):
        x = (mine ^ d) // 2
        for h in range(GROUP):
            od[:, head_at(h)] = attn[x, :, lanes_at(d & 1, h)].T
            od[:, HALF + h * HEAD_DIM : HALF + (h + 1) * HEAD_DIM] = dq_s[
                x, :, lanes_at(d & 1, h)
            ].T


def unpack_kernel(info, od0, od1, od2, od3, attended, query_grad):
    mine = info[0]
    for d, od in enumerate((od0, od1, od2, od3)):
        at = pl.ds(pl.multiple_of((mine ^ d) * HALF, HALF), HALF)
        attended[:, at] = od[:, :HALF]
        query_grad[:, at] = od[:, HALF:]


def both(a, b):
    return (a.astype(F32) + b.astype(F32)).astype(BF16)


def add_kernel(side_l, side_r, far_a, far_b, out_l, out_r):
    out_r[:2] = both(side_r[:2], far_a[...])
    out_r[2:] = side_r[2:]
    out_l[:2] = side_l[:2]
    out_l[2:] = both(side_l[2:], far_b[...])


def sum_kernel(own, left, right, *outs):
    for d, out in enumerate(outs):
        total = own[d].astype(F32) + left[d].astype(F32) + right[d].astype(F32)
        out[...] = total.astype(BF16)


def share_kernel(info, g0, g1, g2, g3, keep, send):
    mine, first = info[0], info[2] == 0
    for d, g in enumerate((g0, g1, g2, g3)):
        at = pl.ds(pl.multiple_of((mine ^ d) * HEAD_DIM, HEAD_DIM), HEAD_DIM)
        keys, values = g[ROWS:, :HEAD_DIM], g[ROWS:, HEAD_DIM:]
        keep[:, at] = jnp.where(first, keys, values)
        send[:, at] = jnp.where(first, values, keys)


def finish_kernel(info, g0, g1, g2, g3, key_grad, value_grad):
    mine = info[0]
    for d, g in enumerate((g0, g1, g2, g3)):
        at = pl.ds(pl.multiple_of((mine ^ d) * HEAD_DIM, HEAD_DIM), HEAD_DIM)
        key_grad[:, at] = g[:ROWS, :HEAD_DIM]
        value_grad[:, at] = g[:ROWS, HEAD_DIM:]


def bf16(*shape):
    return jax.ShapeDtypeStruct(shape, BF16)


def f32(*shape):
    return jax.ShapeDtypeStruct(shape, F32)


def call(kernel, outs, scratch, scalars, *operands, copies=0, products=0):
    place = pl.BlockSpec(memory_space=pl.ANY) if copies else VMEM
    scratch = [pltpu.VMEM(shape, dtype) for shape, dtype in scratch]
    if copies:
        scratch.append(pltpu.SemaphoreType.DMA((copies,)))
    return pl.pallas_call(
        kernel,
        out_shape=tuple(outs),
        in_specs=[SMEM] * len(scalars) + [place] * len(operands),
        out_specs=(VMEM,) * len(outs),
        scratch_shapes=scratch,
        compiler_params=pltpu.CompilerParams(vmem_limit_bytes=(56 if copies else 32) * 2**20),
        cost_estimate=pl.CostEstimate(
            flops=products * PROBS * LANES * HEAD_DIM * 4,
            bytes_accessed=1_000_000,
            transcendentals=0,
        ),
    )(*scalars, *operands)


def swap(x, axis):
    return lax.ppermute(x, axis, [(0, 1), (1, 0)])


def turn(x, axis, step):
    size = lax.axis_size(axis)
    return lax.ppermute(x, axis, [(i, (i + step) % size) for i in range(size)])


def local_permute(x, place):
    pairs = []
    for i in range(32):
        xh, z, core = i // 16, i // 2 % 8, i % 2
        xh, z = place(xh, (z - core) % 8)
        pairs.append((i, (xh * 8 + (z + core) % 8) * 2 + core))
    return lax.ppermute(x, LOCAL, pairs)


def partner(x, d):
    return local_permute(x, lambda xh, z: (xh ^ (d // 2), z ^ (d & 1)))


def quad_turn(x, step):
    return local_permute(x, lambda xh, z: (xh, (z + 2 * step) % 8))


def rounded(x):
    return lax.optimization_barrier(x.astype(BF16))


def body(q_resp, k_resp, v_resp, k_prompt, v_prompt, d_out, lengths, counts):
    core = lax.axis_index("core")
    z = (lax.axis_index("z") - core) & 7
    mine = lax.axis_index("xh") * 2 + (z & 1)
    info = jnp.stack([mine, z // 2, core, lengths[0], counts[0]]).astype(jnp.int32)
    weight = (RESP_LEN / counts[0].astype(F32)).reshape(1)
    spot = mine.reshape(1).astype(jnp.int32)
    width = KV_HEADS * HEAD_DIM
    kv = list(
        call(
            pack_kv_kernel,
            (bf16(BOTH, WIDE),) * 4,
            [((ROWS, width), BF16)] * 2 + [((PROWS, width), BF16)] * 2,
            (spot,),
            k_resp[0], v_resp[0], k_prompt, v_prompt,
            copies=4,
        )
    )
    qd = list(
        call(
            pack_qd_kernel,
            (bf16(ROWS, LANES),) * 4,
            [((ROWS, HEADS * HEAD_DIM), BF16)] * 2,
            (spot,),
            q_resp[0], d_out[0],
            copies=2,
        )
    )
    for d in (1, 2, 3):
        kv[d] = partner(kv[d], d)
    qd[1], qd[2] = partner(qd[1], 1), partner(qd[2], 2)
    own_a, own_b = jnp.stack(kv[:2]), jnp.stack(kv[2:])
    own_a, own_b, qd[3] = lax.optimization_barrier((own_a, own_b, qd[3]))
    qd[3] = partner(qd[3], 3)
    left_a, right_b = quad_turn(own_a, 1), quad_turn(own_b, -1)
    left_b, right_a = quad_turn(own_b, 1), quad_turn(own_a, -1)
    far_a, far_b = quad_turn(left_a, 1), quad_turn(right_b, -1)

    tiles = (2, HEAD_DIM, LANES)
    line = f32(2, 1, LANES)

    def keys(count):
        return [((count, SPAN, HEAD_DIM), BF16)] * 2

    def forward_scratch(count):
        return keys(count) + [((count, HEAD_DIM, SPAN), BF16), ((count, SPAN, LANES), F32)]

    turned = ((HEAD_DIM, SPAN), BF16)
    grad_s = ((PROBS, LANES), BF16)
    whole, pair = bf16(4, BOTH, WIDE), bf16(2, BOTH, WIDE)
    qt, q, upt, probs1, shift1, total1, acc1 = call(
        first_kernel,
        (bf16(*tiles), bf16(2, LANES, HEAD_DIM), bf16(*tiles), bf16(1, PROBS, LANES), line, line, f32(*tiles)),
        forward_scratch(1),
        (info, weight),
        *qd, own_a, own_b,
        products=2,
    )
    probs2, shift2, total2, acc2 = call(
        side_kernel,
        (bf16(2, PROBS, LANES), line, line, f32(*tiles)),
        forward_scratch(2),
        (info,),
        qt, left_a, left_b, right_a, right_b, shift1, total1, acc1,
        products=4,
    )
    shift3, uplt, upl, delta, dqt, attn, far_ga, far_gb = call(
        far_kernel,
        (line, bf16(*tiles), bf16(2, LANES, HEAD_DIM), line, f32(*tiles), bf16(*tiles), pair, pair),
        keys(1) + [((1, HEAD_DIM, SPAN), BF16), turned, ((1, SPAN, LANES), F32)]
        + [((1, PROBS, LANES), BF16), grad_s, (tiles, F32), ((2, 1, LANES), F32)],
        (info,),
        qt, q, upt, far_a, far_b, shift2, total2, acc2,
        products=6,
    )
    far_ga, far_gb = quad_turn(far_ga, 1), quad_turn(far_gb, -1)
    dqt, left_g, right_g = call(
        back_side_kernel,
        (f32(*tiles), whole, whole),
        keys(2) + [turned, grad_s],
        (info,),
        q, uplt, upl, delta, shift2, shift3, probs2,
        left_a, left_b, right_a, right_b, dqt,
        products=8,
    )
    left_g, right_g = call(add_kernel, (whole, whole), (), (), left_g, right_g, far_ga, far_gb)
    left_g, right_g = quad_turn(left_g, -1), quad_turn(right_g, 1)
    own_g, *od = call(
        back_own_kernel,
        (whole,) + (bf16(ROWS, LANES),) * 4,
        keys(1) + [turned, grad_s, (tiles, F32), (tiles, BF16)],
        (info,),
        q, uplt, upl, delta, shift1, shift3, probs1, own_a, own_b, dqt, attn,
        products=4,
    )
    od[3], od[2] = partner(od[3], 3), partner(od[2], 2)
    left_g, right_g, od[1] = lax.optimization_barrier((left_g, right_g, od[1]))
    od[1] = partner(od[1], 1)
    grads = list(call(sum_kernel, (bf16(BOTH, WIDE),) * 4, (), (), own_g, left_g, right_g))
    for d in (1, 2, 3):
        grads[d] = partner(grads[d], d)
    tied = lax.optimization_barrier((*grads, *od[1:]))
    grads, od[1:] = tied[:4], tied[4:]
    rows = bf16(ROWS, HEADS * HEAD_DIM)
    keep, send = call(share_kernel, (bf16(PROWS, width),) * 2, (), (info,), *grads)
    share = rounded(keep.astype(F32) + swap(send, "core").astype(F32))
    share = rounded(share.astype(F32) + swap(share, "xl").astype(F32))
    key_grad, value_grad = call(
        finish_kernel, (bf16(ROWS, width),) * 2, (), (info,), *grads
    )
    attended, query_grad = call(unpack_kernel, (rows, rows), (), (info,), *od)
    share, key_grad, value_grad, attended, query_grad = lax.optimization_barrier(
        (share, key_grad, value_grad, attended, query_grad)
    )
    across = share.astype(F32) + turn(share, "y", 2).astype(F32)
    beside = turn(share, "y", 1).astype(F32) + turn(share, "y", 3).astype(F32)
    share = rounded(across + beside)
    other = swap(share, "core")
    key_share = jnp.where(core == 0, share, other)
    value_share = jnp.where(core == 0, other, share)
    return (
        attended[None],
        query_grad[None],
        key_grad[None],
        value_grad[None],
        key_share,
        value_share,
    )


def solution(mesh):
    split = Mesh(mesh.devices.reshape(2, 8, 4, 2, 2), CTX + RESP)
    rows = P(RESP, CTX, None)
    prompt = P(CTX, None)
    return jax.shard_map(
        body,
        mesh=split,
        in_specs=(rows, rows, rows, prompt, prompt, rows, P(RESP), P(RESP)),
        out_specs=(rows, rows, rows, rows, prompt, prompt),
        check_vma=False,
    )
```

```python
import math

import jax
import jax.numpy as jnp
from jax import lax
from jax.experimental import pallas as pl
from jax.experimental.pallas import tpu as pltpu
from jax.sharding import Mesh
from jax.sharding import PartitionSpec as P

HEADS = 16
KV_HEADS = 4
HEAD_DIM = 128
GROUP = HEADS // KV_HEADS
RESP_LEN = 2048
PROMPT_LEN = 1024
CTX = ("xh", "z")
LOCAL = ("xh", "z", "core")
RESP = ("y", "xl", "core")
ROWS = 128
PROWS = 64
BOTH = ROWS + PROWS
CHUNK = 256
SPAN = 3 * CHUNK
TILE_SPANS = (2 * CHUNK, 3 * CHUNK)
TILE_STARTS = (0, 2 * CHUNK)
PROBS = 5 * CHUNK
HALF = GROUP * ROWS
LANES = 2 * HALF
WIDE = 2 * HEAD_DIM
SCALE = HEAD_DIM**-0.5
SCALE2 = SCALE * math.log2(math.e)
NEG = -1e30
F32 = jnp.float32
BF16 = jnp.bfloat16
VMEM = pl.BlockSpec(memory_space=pltpu.VMEM)
SMEM = pl.BlockSpec(memory_space=pltpu.SMEM)


def dot(a, b):
    return jnp.dot(a, b, preferred_element_type=F32)


def head_at(h, width=HEAD_DIM):
    return slice(h * width, (h + 1) * width)


def lanes_at(j, h):
    return slice(j * HALF + h * HEAD_DIM, j * HALF + (h + 1) * HEAD_DIM)


def block_of(member, quad, core):
    return (member // 2) * 8 + ((quad * 2 + (member & 1) + core) & 7)


def run_copies(pairs, sems):
    copies = [
        pltpu.make_async_copy(source, to, sems.at[i]) for i, (source, to) in enumerate(pairs)
    ]
    for copy in copies:
        copy.start()
    for copy in copies:
        copy.wait()


def pack_kv_kernel(info, k, v, kp, vp, kv0, kv1, kv2, kv3, k_s, v_s, kp_s, vp_s, sems):
    mine = info[0]
    run_copies(((k, k_s), (v, v_s), (kp, kp_s), (vp, vp_s)), sems)
    for d, kv in enumerate((kv0, kv1, kv2, kv3)):
        at = pl.ds(pl.multiple_of((mine ^ d) * HEAD_DIM, HEAD_DIM), HEAD_DIM)
        kv[:ROWS, :HEAD_DIM] = k_s[:, at]
        kv[:ROWS, HEAD_DIM:] = v_s[:, at]
        kv[ROWS:, :HEAD_DIM] = kp_s[:, at]
        kv[ROWS:, HEAD_DIM:] = vp_s[:, at]


def pack_qd_kernel(info, q, do, qd0, qd1, qd2, qd3, q_s, do_s, sems):
    mine = info[0]
    run_copies(((q, q_s), (do, do_s)), sems)
    for d, qd in enumerate((qd0, qd1, qd2, qd3)):
        at = pl.ds(pl.multiple_of((mine ^ d) * HALF, HALF), HALF)
        qd[:, :HALF] = q_s[:, at]
        qd[:, HALF:] = do_s[:, at]


def rows_at(mine, d):
    return pl.ds(pl.multiple_of(CHUNK + (mine ^ d) // 2 * CHUNK + (d & 1) * ROWS, ROWS), ROWS)


def load_keys(mine, g, kvs, k_s, v_s):
    for d, kv in enumerate(kvs):
        k_s[g, rows_at(mine, d), :] = kv[:ROWS, :HEAD_DIM]
        v_s[g, rows_at(mine, d), :] = kv[:ROWS, HEAD_DIM:]
        k_s[g, head_at(d, PROWS), :] = kv[ROWS:, :HEAD_DIM]
        v_s[g, head_at(d, PROWS), :] = kv[ROWS:, HEAD_DIM:]


def query_rows(info, x):
    mine, quad, core = info[0], info[1], info[2]
    rows = []
    for j in range(2):
        start = block_of(x * 2 + ((mine & 1) ^ j), quad, core) * ROWS
        rows += [start + lax.broadcasted_iota(jnp.int32, (1, ROWS), 1)] * GROUP
    return jnp.concatenate(rows, axis=1)


def key_rows(info, x, quad):
    mine, core = info[0], info[2]
    rows = []
    for j in range(2):
        start = block_of(x * 2 + ((mine & 1) ^ j), quad, core) * ROWS
        rows.append(start + lax.broadcasted_iota(jnp.int32, (ROWS, 1), 0))
    return jnp.concatenate(rows, axis=0)


def fold(x, op):
    return op(x.reshape(x.shape[0] // 8, 8, LANES), axis=0)


def each(count, step, carry):
    return step(0, carry) if count == 1 else lax.fori_loop(0, count, step, carry)


def forward(info, quads, count, k_s, v_s, qt, before, score_s, probs, vt_s, shift, total, acc):
    def turn_values(g, carry):
        vt_s[g] = v_s[g].T
        return carry

    each(count, turn_values, 0)
    for x in range(2):
        place = query_rows(info, x)
        start, span = TILE_STARTS[x], TILE_SPANS[x]

        def score_step(g, running):
            for c in range(span // CHUNK):
                at = slice(c * CHUNK, (c + 1) * CHUNK)
                score = dot(k_s[g, at, :], qt[x])
                if c > 0:
                    score = jnp.where(key_rows(info, c - 1, quads(g)) <= place, score, NEG)
                score_s[g, at, :] = score
                running = jnp.maximum(running, fold(score, jnp.max))
            return running

        running = each(count, score_step, jnp.full((8, LANES), NEG, F32))
        now = jnp.max(running, axis=0, keepdims=True) * SCALE2
        if before is not None:
            now = jnp.maximum(now, before[0][x])
            factor = jnp.exp2(before[0][x] - now)
            acc[x] = before[2][x] * factor

        def prob_step(g, running):
            for c in range(span // CHUNK):
                prob = jnp.exp2(score_s[g, c * CHUNK : (c + 1) * CHUNK, :] * SCALE2 - now)
                running = running + fold(prob, jnp.sum)
                probs[g, start + c * CHUNK : start + (c + 1) * CHUNK, :] = prob.astype(BF16)
            part = dot(vt_s[g, :, :span], probs[g, start : start + span, :])
            if before is None:
                acc[x] = part
            else:
                acc[x] += part
            return running

        running = each(count, prob_step, jnp.zeros((8, LANES), F32))
        sums = jnp.sum(running, axis=0, keepdims=True)
        if before is not None:
            sums = sums + before[1][x] * factor
        shift[x], total[x] = now, sums


def chunk_at(c, start):
    if isinstance(c, int):
        return slice(start + c * CHUNK, start + (c + 1) * CHUNK)
    return pl.ds(pl.multiple_of(start + c * CHUNK, CHUNK), CHUNK)


def backward(count, looped, k_s, v_s, kt_s, q, uplt, upl, delta, probs, factors, grad_s, before, dqt):
    for x in range(2):
        dqt[x] = jnp.zeros((HEAD_DIM, LANES), F32) if before is None else before[x]

    def chunk(g, c, tiles):
        at = chunk_at(c, 0)
        dk, dv = None, None
        for x in tiles:
            here = chunk_at(c, TILE_STARTS[x])
            low = probs[g, here, :]
            if factors is not None:
                low = (low.astype(F32) * factors[x]).astype(BF16)
            prob_grad = dot(v_s[g, at, :], uplt[x])
            grad = (low.astype(F32) * (prob_grad - delta[x])).astype(BF16)
            grad_s[here, :] = grad
            dv_part = dot(low, upl[x])
            dk_part = dot(grad, q[x])
            dv = dv_part if dv is None else dv + dv_part
            dk = dk_part if dk is None else dk + dk_part
        k_s[g, at, :] = (dk * SCALE).astype(BF16)
        v_s[g, at, :] = dv.astype(BF16)

    def step(g, carry):
        kt_s[...] = k_s[g].T

        def two_tiles(c, carry):
            chunk(g, c, (0, 1))
            return carry

        if looped:
            lax.fori_loop(0, 2, two_tiles, 0)
        else:
            two_tiles(0, 0)
            two_tiles(1, 0)
        chunk(g, 2, (1,))
        for x in range(2):
            start, span = TILE_STARTS[x], TILE_SPANS[x]
            dqt[x] += dot(kt_s[:, :span], grad_s[start : start + span, :])
        return carry

    each(count, step, 0)


def store_grads(mine, g, k_s, v_s, outs):
    for d, out in enumerate(outs):
        out[:ROWS, :HEAD_DIM] = k_s[g, rows_at(mine, d), :]
        out[:ROWS, HEAD_DIM:] = v_s[g, rows_at(mine, d), :]
        out[ROWS:, :HEAD_DIM] = k_s[g, head_at(d, PROWS), :]
        out[ROWS:, HEAD_DIM:] = v_s[g, head_at(d, PROWS), :]


def pieces(*parts):
    return [part.at[d] for part in parts for d in range(part.shape[0])]


def first_kernel(
    info, weight, qd0, qd1, qd2, qd3, own_a, own_b,
    qt, q, upt, probs, shift, total, acc,
    k_s, v_s, vt_s, score_s,
):
    mine, quad, core, count = info[0], info[1], info[2], info[4]
    load_keys(mine, 0, pieces(own_a, own_b), k_s, v_s)
    for d, qd in enumerate((qd0, qd1, qd2, qd3)):
        x = (mine ^ d) // 2
        row = block_of(mine ^ d, quad, core) * ROWS
        row = row + lax.broadcasted_iota(jnp.int32, (1, ROWS), 1)
        row_weight = jnp.where(row < count, weight[0], 0.0)
        for h in range(GROUP):
            cols = lanes_at(d & 1, h)
            q_head = qd[:, head_at(h)]
            q[x, cols, :] = q_head
            qt[x, :, cols] = q_head.T
            grad = qd[:, HALF + h * HEAD_DIM : HALF + (h + 1) * HEAD_DIM]
            upt[x, :, cols] = (grad.T.astype(F32) * row_weight).astype(BF16)
    forward(
        info, lambda g: quad, 1, k_s, v_s, qt, None, score_s, probs, vt_s, shift, total, acc
    )


def side_kernel(
    info, qt, left_a, left_b, right_a, right_b, shift0, total0, acc0,
    probs, shift, total, acc,
    k_s, v_s, vt_s, score_s,
):
    mine, quad = info[0], info[1]
    load_keys(mine, 0, pieces(left_a, left_b), k_s, v_s)
    load_keys(mine, 1, pieces(right_a, right_b), k_s, v_s)
    forward(
        info, lambda g: (quad + 3 + 2 * g) & 3, 2, k_s, v_s, qt, (shift0, total0, acc0),
        score_s, probs, vt_s, shift, total, acc,
    )


def far_kernel(
    info, qt, q, upt, far_a, far_b, shift0, total0, acc0,
    shift, uplt, upl, delta, dqt, attn, out_a, out_b,
    k_s, v_s, vt_s, kt_s, score_s, probs, grad_s, acc, total,
):
    mine, quad, length = info[0], info[1], info[3]
    load_keys(mine, 0, pieces(far_a, far_b), k_s, v_s)
    forward(
        info, lambda g: (quad + 2) & 3, 1, k_s, v_s, qt, (shift0, total0, acc0),
        score_s, probs, vt_s, shift, total, acc,
    )
    for x in range(2):
        inverse = 1.0 / total[x]
        valid = jnp.where(query_rows(info, x) < length, 1.0, 0.0)
        out_t = (acc[x] * (inverse * valid)).astype(BF16)
        up_low = (upt[x].astype(F32) * inverse).astype(BF16)
        uplt[x] = up_low
        delta[x] = jnp.sum(up_low.astype(F32) * out_t.astype(F32), axis=0, keepdims=True)
        attn[x] = out_t
        for j in range(2):
            for h in range(GROUP):
                upl[x, lanes_at(j, h), :] = up_low[:, lanes_at(j, h)].T
    backward(
        1, False, k_s, v_s, kt_s, q, uplt, upl, delta, probs, None, grad_s, None, dqt
    )
    store_grads(mine, 0, k_s, v_s, pieces(out_a, out_b))


def back_side_kernel(
    info, q, uplt, upl, delta, shift_then, shift_last, probs,
    left_a, left_b, right_a, right_b, dqt0,
    dqt, out_l, out_r,
    k_s, v_s, kt_s, grad_s,
):
    mine = info[0]
    factors = [jnp.exp2(shift_then[x] - shift_last[x]) for x in range(2)]
    load_keys(mine, 0, pieces(left_a, left_b), k_s, v_s)
    load_keys(mine, 1, pieces(right_a, right_b), k_s, v_s)
    backward(
        2, False, k_s, v_s, kt_s, q, uplt, upl, delta, probs, factors, grad_s, dqt0, dqt
    )
    store_grads(mine, 0, k_s, v_s, pieces(out_l))
    store_grads(mine, 1, k_s, v_s, pieces(out_r))


def back_own_kernel(
    info, q, uplt, upl, delta, shift_then, shift_last, probs, own_a, own_b, dqt0, attn,
    out, od0, od1, od2, od3,
    k_s, v_s, kt_s, grad_s, dqt, dq_s,
):
    mine = info[0]
    factors = [jnp.exp2(shift_then[x] - shift_last[x]) for x in range(2)]
    load_keys(mine, 0, pieces(own_a, own_b), k_s, v_s)
    backward(
        1, True, k_s, v_s, kt_s, q, uplt, upl, delta, probs, factors, grad_s, dqt0, dqt
    )
    store_grads(mine, 0, k_s, v_s, pieces(out))
    for x in range(2):
        dq_s[x] = (dqt[x] * SCALE).astype(BF16)
    for d, od in enumerate((od0, od1, od2, od3)):
        x = (mine ^ d) // 2
        for h in range(GROUP):
            od[:, head_at(h)] = attn[x, :, lanes_at(d & 1, h)].T
            od[:, HALF + h * HEAD_DIM : HALF + (h + 1) * HEAD_DIM] = dq_s[
                x, :, lanes_at(d & 1, h)
            ].T


def unpack_kernel(info, od0, od1, od2, od3, attended, query_grad):
    mine = info[0]
    for d, od in enumerate((od0, od1, od2, od3)):
        at = pl.ds(pl.multiple_of((mine ^ d) * HALF, HALF), HALF)
        attended[:, at] = od[:, :HALF]
        query_grad[:, at] = od[:, HALF:]


def both(a, b):
    return (a.astype(F32) + b.astype(F32)).astype(BF16)


def add_kernel(side_l, side_r, far_a, far_b, out_l, out_r):
    out_r[:2] = both(side_r[:2], far_a[...])
    out_r[2:] = side_r[2:]
    out_l[:2] = side_l[:2]
    out_l[2:] = both(side_l[2:], far_b[...])


def sum_kernel(own, left, right, *outs):
    for d, out in enumerate(outs):
        total = own[d].astype(F32) + left[d].astype(F32) + right[d].astype(F32)
        out[...] = total.astype(BF16)


def share_kernel(info, g0, g1, g2, g3, keep, send):
    mine, first = info[0], info[2] == 0
    for d, g in enumerate((g0, g1, g2, g3)):
        at = pl.ds(pl.multiple_of((mine ^ d) * HEAD_DIM, HEAD_DIM), HEAD_DIM)
        keys, values = g[ROWS:, :HEAD_DIM], g[ROWS:, HEAD_DIM:]
        keep[:, at] = jnp.where(first, keys, values)
        send[:, at] = jnp.where(first, values, keys)


def finish_kernel(info, g0, g1, g2, g3, key_grad, value_grad):
    mine = info[0]
    for d, g in enumerate((g0, g1, g2, g3)):
        at = pl.ds(pl.multiple_of((mine ^ d) * HEAD_DIM, HEAD_DIM), HEAD_DIM)
        key_grad[:, at] = g[:ROWS, :HEAD_DIM]
        value_grad[:, at] = g[:ROWS, HEAD_DIM:]


def bf16(*shape):
    return jax.ShapeDtypeStruct(shape, BF16)


def f32(*shape):
    return jax.ShapeDtypeStruct(shape, F32)


def call(kernel, outs, scratch, scalars, *operands, copies=0, products=0):
    place = pl.BlockSpec(memory_space=pl.ANY) if copies else VMEM
    scratch = [pltpu.VMEM(shape, dtype) for shape, dtype in scratch]
    if copies:
        scratch.append(pltpu.SemaphoreType.DMA((copies,)))
    return pl.pallas_call(
        kernel,
        out_shape=tuple(outs),
        in_specs=[SMEM] * len(scalars) + [place] * len(operands),
        out_specs=(VMEM,) * len(outs),
        scratch_shapes=scratch,
        compiler_params=pltpu.CompilerParams(vmem_limit_bytes=(56 if copies else 32) * 2**20),
        cost_estimate=pl.CostEstimate(
            flops=products * PROBS * LANES * HEAD_DIM * 4,
            bytes_accessed=1_000_000,
            transcendentals=0,
        ),
    )(*scalars, *operands)


def swap(x, axis):
    return lax.ppermute(x, axis, [(0, 1), (1, 0)])


def turn(x, axis, step):
    size = lax.axis_size(axis)
    return lax.ppermute(x, axis, [(i, (i + step) % size) for i in range(size)])


def local_permute(x, place):
    pairs = []
    for i in range(32):
        xh, z, core = i // 16, i // 2 % 8, i % 2
        xh, z = place(xh, (z - core) % 8)
        pairs.append((i, (xh * 8 + (z + core) % 8) * 2 + core))
    return lax.ppermute(x, LOCAL, pairs)


def partner(x, d):
    return local_permute(x, lambda xh, z: (xh ^ (d // 2), z ^ (d & 1)))


def quad_turn(x, step):
    return local_permute(x, lambda xh, z: (xh, (z + 2 * step) % 8))


def rounded(x):
    return lax.optimization_barrier(x.astype(BF16))


def body(q_resp, k_resp, v_resp, k_prompt, v_prompt, d_out, lengths, counts):
    core = lax.axis_index("core")
    z = (lax.axis_index("z") - core) & 7
    mine = lax.axis_index("xh") * 2 + (z & 1)
    info = jnp.stack([mine, z // 2, core, lengths[0], counts[0]]).astype(jnp.int32)
    weight = (RESP_LEN / counts[0].astype(F32)).reshape(1)
    spot = mine.reshape(1).astype(jnp.int32)
    width = KV_HEADS * HEAD_DIM
    kv = list(
        call(
            pack_kv_kernel,
            (bf16(BOTH, WIDE),) * 4,
            [((ROWS, width), BF16)] * 2 + [((PROWS, width), BF16)] * 2,
            (spot,),
            k_resp[0], v_resp[0], k_prompt, v_prompt,
            copies=4,
        )
    )
    qd = list(
        call(
            pack_qd_kernel,
            (bf16(ROWS, LANES),) * 4,
            [((ROWS, HEADS * HEAD_DIM), BF16)] * 2,
            (spot,),
            q_resp[0], d_out[0],
            copies=2,
        )
    )
    for d in (1, 2, 3):
        kv[d] = partner(kv[d], d)
    for d in (1, 2, 3):
        qd[d] = partner(qd[d], d)
    own_a, own_b = jnp.stack(kv[:2]), jnp.stack(kv[2:])
    left_a, right_b = quad_turn(own_a, 1), quad_turn(own_b, -1)
    left_b, right_a = quad_turn(own_b, 1), quad_turn(own_a, -1)
    far_a, far_b = quad_turn(left_a, 1), quad_turn(right_b, -1)

    tiles = (2, HEAD_DIM, LANES)
    line = f32(2, 1, LANES)

    def keys(count):
        return [((count, SPAN, HEAD_DIM), BF16)] * 2

    def forward_scratch(count):
        return keys(count) + [((count, HEAD_DIM, SPAN), BF16), ((count, SPAN, LANES), F32)]

    turned = ((HEAD_DIM, SPAN), BF16)
    grad_s = ((PROBS, LANES), BF16)
    whole, pair = bf16(4, BOTH, WIDE), bf16(2, BOTH, WIDE)
    qt, q, upt, probs1, shift1, total1, acc1 = call(
        first_kernel,
        (bf16(*tiles), bf16(2, LANES, HEAD_DIM), bf16(*tiles), bf16(1, PROBS, LANES), line, line, f32(*tiles)),
        forward_scratch(1),
        (info, weight),
        *qd, own_a, own_b,
        products=2,
    )
    probs2, shift2, total2, acc2 = call(
        side_kernel,
        (bf16(2, PROBS, LANES), line, line, f32(*tiles)),
        forward_scratch(2),
        (info,),
        qt, left_a, left_b, right_a, right_b, shift1, total1, acc1,
        products=4,
    )
    shift3, uplt, upl, delta, dqt, attn, far_ga, far_gb = call(
        far_kernel,
        (line, bf16(*tiles), bf16(2, LANES, HEAD_DIM), line, f32(*tiles), bf16(*tiles), pair, pair),
        keys(1) + [((1, HEAD_DIM, SPAN), BF16), turned, ((1, SPAN, LANES), F32)]
        + [((1, PROBS, LANES), BF16), grad_s, (tiles, F32), ((2, 1, LANES), F32)],
        (info,),
        qt, q, upt, far_a, far_b, shift2, total2, acc2,
        products=6,
    )
    far_ga, far_gb = quad_turn(far_ga, 1), quad_turn(far_gb, -1)
    dqt, left_g, right_g = call(
        back_side_kernel,
        (f32(*tiles), whole, whole),
        keys(2) + [turned, grad_s],
        (info,),
        q, uplt, upl, delta, shift2, shift3, probs2,
        left_a, left_b, right_a, right_b, dqt,
        products=8,
    )
    left_g, right_g = call(add_kernel, (whole, whole), (), (), left_g, right_g, far_ga, far_gb)
    left_g, right_g = quad_turn(left_g, -1), quad_turn(right_g, 1)
    own_g, *od = call(
        back_own_kernel,
        (whole,) + (bf16(ROWS, LANES),) * 4,
        keys(1) + [turned, grad_s, (tiles, F32), (tiles, BF16)],
        (info,),
        q, uplt, upl, delta, shift1, shift3, probs1, own_a, own_b, dqt, attn,
        products=4,
    )
    od[3], od[2] = partner(od[3], 3), partner(od[2], 2)
    left_g, right_g, od[1] = lax.optimization_barrier((left_g, right_g, od[1]))
    od[1] = partner(od[1], 1)
    grads = list(call(sum_kernel, (bf16(BOTH, WIDE),) * 4, (), (), own_g, left_g, right_g))
    for d in (3, 2, 1):
        grads[d] = partner(grads[d], d)
    tied = lax.optimization_barrier((*grads[::-1], *od[:0:-1]))
    grads, od[1:] = tied[3::-1], tied[:3:-1]
    rows = bf16(ROWS, HEADS * HEAD_DIM)
    keep, send = call(share_kernel, (bf16(PROWS, width),) * 2, (), (info,), *grads)
    share = rounded(keep.astype(F32) + swap(send, "core").astype(F32))
    share = rounded(share.astype(F32) + swap(share, "xl").astype(F32))
    key_grad, value_grad = call(
        finish_kernel, (bf16(ROWS, width),) * 2, (), (info,), *grads
    )
    attended, query_grad = call(unpack_kernel, (rows, rows), (), (info,), *od)
    share, key_grad, value_grad, attended, query_grad = lax.optimization_barrier(
        (share, key_grad, value_grad, attended, query_grad)
    )
    across = share.astype(F32) + turn(share, "y", 2).astype(F32)
    beside = turn(share, "y", 1).astype(F32) + turn(share, "y", 3).astype(F32)
    share = rounded(across + beside)
    other = swap(share, "core")
    key_share = jnp.where(core == 0, share, other)
    value_share = jnp.where(core == 0, other, share)
    return (
        attended[None],
        query_grad[None],
        key_grad[None],
        value_grad[None],
        key_share,
        value_share,
    )


def solution(mesh):
    split = Mesh(mesh.devices.reshape(2, 8, 4, 2, 2), CTX + RESP)
    rows = P(RESP, CTX, None)
    prompt = P(CTX, None)
    return jax.shard_map(
        body,
        mesh=split,
        in_specs=(rows, rows, rows, prompt, prompt, rows, P(RESP), P(RESP)),
        out_specs=(rows, rows, rows, rows, prompt, prompt),
        check_vma=False,
    )
```

```python
import math

import jax
import jax.numpy as jnp
from jax import lax
from jax.experimental import pallas as pl
from jax.experimental.pallas import tpu as pltpu
from jax.sharding import Mesh
from jax.sharding import PartitionSpec as P

HEADS = 16
KV_HEADS = 4
HEAD_DIM = 128
GROUP = HEADS // KV_HEADS
RESP_LEN = 2048
PROMPT_LEN = 1024
CTX = ("xh", "z")
LOCAL = ("xh", "z", "core")
RESP = ("y", "xl", "core")
ROWS = 128
PROWS = 64
BOTH = ROWS + PROWS
CHUNK = 256
SPAN = 3 * CHUNK
TILE_SPANS = (2 * CHUNK, 3 * CHUNK)
TILE_STARTS = (0, 2 * CHUNK)
PROBS = 5 * CHUNK
HALF = GROUP * ROWS
LANES = 2 * HALF
WIDE = 2 * HEAD_DIM
SCALE = HEAD_DIM**-0.5
SCALE2 = SCALE * math.log2(math.e)
NEG = -1e30
F32 = jnp.float32
BF16 = jnp.bfloat16
VMEM = pl.BlockSpec(memory_space=pltpu.VMEM)
SMEM = pl.BlockSpec(memory_space=pltpu.SMEM)


def dot(a, b):
    return jnp.dot(a, b, preferred_element_type=F32)


def head_at(h, width=HEAD_DIM):
    return slice(h * width, (h + 1) * width)


def lanes_at(j, h):
    return slice(j * HALF + h * HEAD_DIM, j * HALF + (h + 1) * HEAD_DIM)


def block_of(member, quad, core):
    return (member // 2) * 8 + ((quad * 2 + (member & 1) + core) & 7)


def run_copies(pairs, sems):
    copies = [
        pltpu.make_async_copy(source, to, sems.at[i]) for i, (source, to) in enumerate(pairs)
    ]
    for copy in copies:
        copy.start()
    for copy in copies:
        copy.wait()


def pack_kv_kernel(info, k, v, kp, vp, kv0, kv1, kv2, kv3, k_s, v_s, kp_s, vp_s, sems):
    mine = info[0]
    run_copies(((k, k_s), (v, v_s), (kp, kp_s), (vp, vp_s)), sems)
    for d, kv in enumerate((kv0, kv1, kv2, kv3)):
        at = pl.ds(pl.multiple_of((mine ^ d) * HEAD_DIM, HEAD_DIM), HEAD_DIM)
        kv[:ROWS, :HEAD_DIM] = k_s[:, at]
        kv[:ROWS, HEAD_DIM:] = v_s[:, at]
        kv[ROWS:, :HEAD_DIM] = kp_s[:, at]
        kv[ROWS:, HEAD_DIM:] = vp_s[:, at]


def pack_qd_kernel(info, q, do, qd0, qd1, qd2, qd3, q_s, do_s, sems):
    mine = info[0]
    run_copies(((q, q_s), (do, do_s)), sems)
    for d, qd in enumerate((qd0, qd1, qd2, qd3)):
        at = pl.ds(pl.multiple_of((mine ^ d) * HALF, HALF), HALF)
        qd[:, :HALF] = q_s[:, at]
        qd[:, HALF:] = do_s[:, at]


def rows_at(mine, d):
    return pl.ds(pl.multiple_of(CHUNK + (mine ^ d) // 2 * CHUNK + (d & 1) * ROWS, ROWS), ROWS)


def load_keys(mine, g, kvs, k_s, v_s):
    for d, kv in enumerate(kvs):
        k_s[g, rows_at(mine, d), :] = kv[:ROWS, :HEAD_DIM]
        v_s[g, rows_at(mine, d), :] = kv[:ROWS, HEAD_DIM:]
        k_s[g, head_at(d, PROWS), :] = kv[ROWS:, :HEAD_DIM]
        v_s[g, head_at(d, PROWS), :] = kv[ROWS:, HEAD_DIM:]


def query_rows(info, x):
    mine, quad, core = info[0], info[1], info[2]
    rows = []
    for j in range(2):
        start = block_of(x * 2 + ((mine & 1) ^ j), quad, core) * ROWS
        rows += [start + lax.broadcasted_iota(jnp.int32, (1, ROWS), 1)] * GROUP
    return jnp.concatenate(rows, axis=1)


def key_rows(info, x, quad):
    mine, core = info[0], info[2]
    rows = []
    for j in range(2):
        start = block_of(x * 2 + ((mine & 1) ^ j), quad, core) * ROWS
        rows.append(start + lax.broadcasted_iota(jnp.int32, (ROWS, 1), 0))
    return jnp.concatenate(rows, axis=0)


def fold(x, op):
    return op(x.reshape(x.shape[0] // 8, 8, LANES), axis=0)


def each(count, step, carry):
    return step(0, carry) if count == 1 else lax.fori_loop(0, count, step, carry)


def forward(info, quads, count, k_s, v_s, qt, before, score_s, probs, vt_s, shift, total, acc):
    def turn_values(g, carry):
        vt_s[g] = v_s[g].T
        return carry

    each(count, turn_values, 0)
    for x in range(2):
        place = query_rows(info, x)
        start, span = TILE_STARTS[x], TILE_SPANS[x]

        def score_step(g, running):
            for c in range(span // CHUNK):
                at = slice(c * CHUNK, (c + 1) * CHUNK)
                score = dot(k_s[g, at, :], qt[x])
                if c > 0:
                    score = jnp.where(key_rows(info, c - 1, quads(g)) <= place, score, NEG)
                score_s[g, at, :] = score
                running = jnp.maximum(running, fold(score, jnp.max))
            return running

        running = each(count, score_step, jnp.full((8, LANES), NEG, F32))
        now = jnp.max(running, axis=0, keepdims=True) * SCALE2
        if before is not None:
            now = jnp.maximum(now, before[0][x])
            factor = jnp.exp2(before[0][x] - now)
            acc[x] = before[2][x] * factor

        def prob_step(g, running):
            for c in range(span // CHUNK):
                prob = jnp.exp2(score_s[g, c * CHUNK : (c + 1) * CHUNK, :] * SCALE2 - now)
                running = running + fold(prob, jnp.sum)
                probs[g, start + c * CHUNK : start + (c + 1) * CHUNK, :] = prob.astype(BF16)
            part = dot(vt_s[g, :, :span], probs[g, start : start + span, :])
            if before is None:
                acc[x] = part
            else:
                acc[x] += part
            return running

        running = each(count, prob_step, jnp.zeros((8, LANES), F32))
        sums = jnp.sum(running, axis=0, keepdims=True)
        if before is not None:
            sums = sums + before[1][x] * factor
        shift[x], total[x] = now, sums


def chunk_at(c, start):
    if isinstance(c, int):
        return slice(start + c * CHUNK, start + (c + 1) * CHUNK)
    return pl.ds(pl.multiple_of(start + c * CHUNK, CHUNK), CHUNK)


def backward(count, looped, k_s, v_s, kt_s, q, uplt, upl, delta, probs, factors, grad_s, before, dqt):
    for x in range(2):
        dqt[x] = jnp.zeros((HEAD_DIM, LANES), F32) if before is None else before[x]

    def chunk(g, c, tiles):
        at = chunk_at(c, 0)
        dk, dv = None, None
        for x in tiles:
            here = chunk_at(c, TILE_STARTS[x])
            low = probs[g, here, :]
            if factors is not None:
                low = (low.astype(F32) * factors[x]).astype(BF16)
            prob_grad = dot(v_s[g, at, :], uplt[x])
            grad = (low.astype(F32) * (prob_grad - delta[x])).astype(BF16)
            grad_s[here, :] = grad
            dv_part = dot(low, upl[x])
            dk_part = dot(grad, q[x])
            dv = dv_part if dv is None else dv + dv_part
            dk = dk_part if dk is None else dk + dk_part
        k_s[g, at, :] = (dk * SCALE).astype(BF16)
        v_s[g, at, :] = dv.astype(BF16)

    def step(g, carry):
        kt_s[...] = k_s[g].T

        def two_tiles(c, carry):
            chunk(g, c, (0, 1))
            return carry

        if looped:
            lax.fori_loop(0, 2, two_tiles, 0)
        else:
            two_tiles(0, 0)
            two_tiles(1, 0)
        chunk(g, 2, (1,))
        for x in range(2):
            start, span = TILE_STARTS[x], TILE_SPANS[x]
            dqt[x] += dot(kt_s[:, :span], grad_s[start : start + span, :])
        return carry

    each(count, step, 0)


def store_grads(mine, g, k_s, v_s, outs):
    for d, out in enumerate(outs):
        out[:ROWS, :HEAD_DIM] = k_s[g, rows_at(mine, d), :]
        out[:ROWS, HEAD_DIM:] = v_s[g, rows_at(mine, d), :]
        out[ROWS:, :HEAD_DIM] = k_s[g, head_at(d, PROWS), :]
        out[ROWS:, HEAD_DIM:] = v_s[g, head_at(d, PROWS), :]


def pieces(*parts):
    return [part.at[d] for part in parts for d in range(part.shape[0])]


def first_kernel(
    info, weight, qd0, qd1, qd2, qd3, own_a, own_b,
    qt, q, upt, probs, shift, total, acc,
    k_s, v_s, vt_s, score_s,
):
    mine, quad, core, count = info[0], info[1], info[2], info[4]
    load_keys(mine, 0, pieces(own_a, own_b), k_s, v_s)
    for d, qd in enumerate((qd0, qd1, qd2, qd3)):
        x = (mine ^ d) // 2
        row = block_of(mine ^ d, quad, core) * ROWS
        row = row + lax.broadcasted_iota(jnp.int32, (1, ROWS), 1)
        row_weight = jnp.where(row < count, weight[0], 0.0)
        for h in range(GROUP):
            cols = lanes_at(d & 1, h)
            q_head = qd[:, head_at(h)]
            q[x, cols, :] = q_head
            qt[x, :, cols] = q_head.T
            grad = qd[:, HALF + h * HEAD_DIM : HALF + (h + 1) * HEAD_DIM]
            upt[x, :, cols] = (grad.T.astype(F32) * row_weight).astype(BF16)
    forward(
        info, lambda g: quad, 1, k_s, v_s, qt, None, score_s, probs, vt_s, shift, total, acc
    )


def side_kernel(
    info, qt, left_a, left_b, right_a, right_b, shift0, total0, acc0,
    probs, shift, total, acc,
    k_s, v_s, vt_s, score_s,
):
    mine, quad = info[0], info[1]
    load_keys(mine, 0, pieces(left_a, left_b), k_s, v_s)
    load_keys(mine, 1, pieces(right_a, right_b), k_s, v_s)
    forward(
        info, lambda g: (quad + 3 + 2 * g) & 3, 2, k_s, v_s, qt, (shift0, total0, acc0),
        score_s, probs, vt_s, shift, total, acc,
    )


def far_kernel(
    info, qt, q, upt, far_a, far_b, shift0, total0, acc0,
    shift, uplt, upl, delta, dqt, attn, out_a, out_b,
    k_s, v_s, vt_s, kt_s, score_s, probs, grad_s, acc, total,
):
    mine, quad, length = info[0], info[1], info[3]
    load_keys(mine, 0, pieces(far_a, far_b), k_s, v_s)
    forward(
        info, lambda g: (quad + 2) & 3, 1, k_s, v_s, qt, (shift0, total0, acc0),
        score_s, probs, vt_s, shift, total, acc,
    )
    for x in range(2):
        inverse = 1.0 / total[x]
        valid = jnp.where(query_rows(info, x) < length, 1.0, 0.0)
        out_t = (acc[x] * (inverse * valid)).astype(BF16)
        up_low = (upt[x].astype(F32) * inverse).astype(BF16)
        uplt[x] = up_low
        delta[x] = jnp.sum(up_low.astype(F32) * out_t.astype(F32), axis=0, keepdims=True)
        attn[x] = out_t
        for j in range(2):
            for h in range(GROUP):
                upl[x, lanes_at(j, h), :] = up_low[:, lanes_at(j, h)].T
    backward(
        1, False, k_s, v_s, kt_s, q, uplt, upl, delta, probs, None, grad_s, None, dqt
    )
    store_grads(mine, 0, k_s, v_s, pieces(out_a, out_b))


def back_side_kernel(
    info, q, uplt, upl, delta, shift_then, shift_last, probs,
    left_a, left_b, right_a, right_b, dqt0,
    dqt, out_l, out_r,
    k_s, v_s, kt_s, grad_s,
):
    mine = info[0]
    factors = [jnp.exp2(shift_then[x] - shift_last[x]) for x in range(2)]
    load_keys(mine, 0, pieces(left_a, left_b), k_s, v_s)
    load_keys(mine, 1, pieces(right_a, right_b), k_s, v_s)
    backward(
        2, False, k_s, v_s, kt_s, q, uplt, upl, delta, probs, factors, grad_s, dqt0, dqt
    )
    store_grads(mine, 0, k_s, v_s, pieces(out_l))
    store_grads(mine, 1, k_s, v_s, pieces(out_r))


def back_own_kernel(
    info, q, uplt, upl, delta, shift_then, shift_last, probs, own_a, own_b, dqt0, attn,
    out, od0, od1, od2, od3,
    k_s, v_s, kt_s, grad_s, dqt, dq_s,
):
    mine = info[0]
    factors = [jnp.exp2(shift_then[x] - shift_last[x]) for x in range(2)]
    load_keys(mine, 0, pieces(own_a, own_b), k_s, v_s)
    backward(
        1, True, k_s, v_s, kt_s, q, uplt, upl, delta, probs, factors, grad_s, dqt0, dqt
    )
    store_grads(mine, 0, k_s, v_s, pieces(out))
    for x in range(2):
        dq_s[x] = (dqt[x] * SCALE).astype(BF16)
    for d, od in enumerate((od0, od1, od2, od3)):
        x = (mine ^ d) // 2
        for h in range(GROUP):
            od[:, head_at(h)] = attn[x, :, lanes_at(d & 1, h)].T
            od[:, HALF + h * HEAD_DIM : HALF + (h + 1) * HEAD_DIM] = dq_s[
                x, :, lanes_at(d & 1, h)
            ].T


def unpack_kernel(info, od0, od1, od2, od3, attended, query_grad):
    mine = info[0]
    for d, od in enumerate((od0, od1, od2, od3)):
        at = pl.ds(pl.multiple_of((mine ^ d) * HALF, HALF), HALF)
        attended[:, at] = od[:, :HALF]
        query_grad[:, at] = od[:, HALF:]


def both(a, b):
    return (a.astype(F32) + b.astype(F32)).astype(BF16)


def add_kernel(side_l, side_r, far_a, far_b, out_l, out_r):
    out_r[:2] = both(side_r[:2], far_a[...])
    out_r[2:] = side_r[2:]
    out_l[:2] = side_l[:2]
    out_l[2:] = both(side_l[2:], far_b[...])


def sum_kernel(own, left, right, *outs):
    for d, out in enumerate(outs):
        total = own[d].astype(F32) + left[d].astype(F32) + right[d].astype(F32)
        out[...] = total.astype(BF16)


def share_kernel(info, g0, g1, g2, g3, keep, send):
    mine, first = info[0], info[2] == 0
    for d, g in enumerate((g0, g1, g2, g3)):
        at = pl.ds(pl.multiple_of((mine ^ d) * HEAD_DIM, HEAD_DIM), HEAD_DIM)
        keys, values = g[ROWS:, :HEAD_DIM], g[ROWS:, HEAD_DIM:]
        keep[:, at] = jnp.where(first, keys, values)
        send[:, at] = jnp.where(first, values, keys)


def finish_kernel(info, g0, g1, g2, g3, key_grad, value_grad):
    mine = info[0]
    for d, g in enumerate((g0, g1, g2, g3)):
        at = pl.ds(pl.multiple_of((mine ^ d) * HEAD_DIM, HEAD_DIM), HEAD_DIM)
        key_grad[:, at] = g[:ROWS, :HEAD_DIM]
        value_grad[:, at] = g[:ROWS, HEAD_DIM:]


def bf16(*shape):
    return jax.ShapeDtypeStruct(shape, BF16)


def f32(*shape):
    return jax.ShapeDtypeStruct(shape, F32)


def call(kernel, outs, scratch, scalars, *operands, copies=0, products=0):
    place = pl.BlockSpec(memory_space=pl.ANY) if copies else VMEM
    scratch = [pltpu.VMEM(shape, dtype) for shape, dtype in scratch]
    if copies:
        scratch.append(pltpu.SemaphoreType.DMA((copies,)))
    return pl.pallas_call(
        kernel,
        out_shape=tuple(outs),
        in_specs=[SMEM] * len(scalars) + [place] * len(operands),
        out_specs=(VMEM,) * len(outs),
        scratch_shapes=scratch,
        compiler_params=pltpu.CompilerParams(vmem_limit_bytes=(56 if copies else 32) * 2**20),
        cost_estimate=pl.CostEstimate(
            flops=products * PROBS * LANES * HEAD_DIM * 4,
            bytes_accessed=1_000_000,
            transcendentals=0,
        ),
    )(*scalars, *operands)


def swap(x, axis):
    return lax.ppermute(x, axis, [(0, 1), (1, 0)])


def turn(x, axis, step):
    size = lax.axis_size(axis)
    return lax.ppermute(x, axis, [(i, (i + step) % size) for i in range(size)])


def local_permute(x, place):
    pairs = []
    for i in range(32):
        xh, z, core = i // 16, i // 2 % 8, i % 2
        xh, z = place(xh, (z - core) % 8)
        pairs.append((i, (xh * 8 + (z + core) % 8) * 2 + core))
    return lax.ppermute(x, LOCAL, pairs)


def partner(x, d):
    return local_permute(x, lambda xh, z: (xh ^ (d // 2), z ^ (d & 1)))


def quad_turn(x, step):
    return local_permute(x, lambda xh, z: (xh, (z + 2 * step) % 8))


def rounded(x):
    return lax.optimization_barrier(x.astype(BF16))


def body(q_resp, k_resp, v_resp, k_prompt, v_prompt, d_out, lengths, counts):
    core = lax.axis_index("core")
    z = (lax.axis_index("z") - core) & 7
    mine = lax.axis_index("xh") * 2 + (z & 1)
    info = jnp.stack([mine, z // 2, core, lengths[0], counts[0]]).astype(jnp.int32)
    weight = (RESP_LEN / counts[0].astype(F32)).reshape(1)
    spot = mine.reshape(1).astype(jnp.int32)
    width = KV_HEADS * HEAD_DIM
    kv = list(
        call(
            pack_kv_kernel,
            (bf16(BOTH, WIDE),) * 4,
            [((ROWS, width), BF16)] * 2 + [((PROWS, width), BF16)] * 2,
            (spot,),
            k_resp[0], v_resp[0], k_prompt, v_prompt,
            copies=4,
        )
    )
    for d in (1, 2, 3):
        kv[d] = partner(kv[d], d)
    own_a = jnp.stack(kv[:2])
    own_a, spot = lax.optimization_barrier((own_a, spot))
    qd = list(
        call(
            pack_qd_kernel,
            (bf16(ROWS, LANES),) * 4,
            [((ROWS, HEADS * HEAD_DIM), BF16)] * 2,
            (spot,),
            q_resp[0], d_out[0],
            copies=2,
        )
    )
    left_a, right_a = quad_turn(own_a, 1), quad_turn(own_a, -1)
    for d in (1, 2, 3):
        qd[d] = partner(qd[d], d)
    own_b = jnp.stack(kv[2:])
    own_b, left_a, right_a = lax.optimization_barrier((own_b, left_a, right_a))
    left_b, right_b = quad_turn(own_b, 1), quad_turn(own_b, -1)
    far_a, far_b = quad_turn(left_a, 1), quad_turn(right_b, -1)

    tiles = (2, HEAD_DIM, LANES)
    line = f32(2, 1, LANES)

    def keys(count):
        return [((count, SPAN, HEAD_DIM), BF16)] * 2

    def forward_scratch(count):
        return keys(count) + [((count, HEAD_DIM, SPAN), BF16), ((count, SPAN, LANES), F32)]

    turned = ((HEAD_DIM, SPAN), BF16)
    grad_s = ((PROBS, LANES), BF16)
    whole, pair = bf16(4, BOTH, WIDE), bf16(2, BOTH, WIDE)
    qt, q, upt, probs1, shift1, total1, acc1 = call(
        first_kernel,
        (bf16(*tiles), bf16(2, LANES, HEAD_DIM), bf16(*tiles), bf16(1, PROBS, LANES), line, line, f32(*tiles)),
        forward_scratch(1),
        (info, weight),
        *qd, own_a, own_b,
        products=2,
    )
    probs2, shift2, total2, acc2 = call(
        side_kernel,
        (bf16(2, PROBS, LANES), line, line, f32(*tiles)),
        forward_scratch(2),
        (info,),
        qt, left_a, left_b, right_a, right_b, shift1, total1, acc1,
        products=4,
    )
    shift3, uplt, upl, delta, dqt, attn, far_ga, far_gb = call(
        far_kernel,
        (line, bf16(*tiles), bf16(2, LANES, HEAD_DIM), line, f32(*tiles), bf16(*tiles), pair, pair),
        keys(1) + [((1, HEAD_DIM, SPAN), BF16), turned, ((1, SPAN, LANES), F32)]
        + [((1, PROBS, LANES), BF16), grad_s, (tiles, F32), ((2, 1, LANES), F32)],
        (info,),
        qt, q, upt, far_a, far_b, shift2, total2, acc2,
        products=6,
    )
    far_ga, far_gb = quad_turn(far_ga, 1), quad_turn(far_gb, -1)
    dqt, left_g, right_g = call(
        back_side_kernel,
        (f32(*tiles), whole, whole),
        keys(2) + [turned, grad_s],
        (info,),
        q, uplt, upl, delta, shift2, shift3, probs2,
        left_a, left_b, right_a, right_b, dqt,
        products=8,
    )
    left_g, right_g = call(add_kernel, (whole, whole), (), (), left_g, right_g, far_ga, far_gb)
    left_g, right_g = quad_turn(left_g, -1), quad_turn(right_g, 1)
    own_g, *od = call(
        back_own_kernel,
        (whole,) + (bf16(ROWS, LANES),) * 4,
        keys(1) + [turned, grad_s, (tiles, F32), (tiles, BF16)],
        (info,),
        q, uplt, upl, delta, shift1, shift3, probs1, own_a, own_b, dqt, attn,
        products=4,
    )
    od[3], od[2] = partner(od[3], 3), partner(od[2], 2)
    left_g, right_g, od[1] = lax.optimization_barrier((left_g, right_g, od[1]))
    od[1] = partner(od[1], 1)
    grads = list(call(sum_kernel, (bf16(BOTH, WIDE),) * 4, (), (), own_g, left_g, right_g))
    for d in (3, 2, 1):
        grads[d] = partner(grads[d], d)
    tied = lax.optimization_barrier((*grads[::-1], *od[:0:-1]))
    grads, od[1:] = tied[3::-1], tied[:3:-1]
    rows = bf16(ROWS, HEADS * HEAD_DIM)
    keep, send = call(share_kernel, (bf16(PROWS, width),) * 2, (), (info,), *grads)
    share = rounded(keep.astype(F32) + swap(send, "core").astype(F32))
    share = rounded(share.astype(F32) + swap(share, "xl").astype(F32))
    key_grad, value_grad = call(
        finish_kernel, (bf16(ROWS, width),) * 2, (), (info,), *grads
    )
    attended, query_grad = call(unpack_kernel, (rows, rows), (), (info,), *od)
    share, key_grad, value_grad, attended, query_grad = lax.optimization_barrier(
        (share, key_grad, value_grad, attended, query_grad)
    )
    across = share.astype(F32) + turn(share, "y", 2).astype(F32)
    beside = turn(share, "y", 1).astype(F32) + turn(share, "y", 3).astype(F32)
    share = rounded(across + beside)
    other = swap(share, "core")
    key_share = jnp.where(core == 0, share, other)
    value_share = jnp.where(core == 0, other, share)
    return (
        attended[None],
        query_grad[None],
        key_grad[None],
        value_grad[None],
        key_share,
        value_share,
    )


def solution(mesh):
    split = Mesh(mesh.devices.reshape(2, 8, 4, 2, 2), CTX + RESP)
    rows = P(RESP, CTX, None)
    prompt = P(CTX, None)
    return jax.shard_map(
        body,
        mesh=split,
        in_specs=(rows, rows, rows, prompt, prompt, rows, P(RESP), P(RESP)),
        out_specs=(rows, rows, rows, rows, prompt, prompt),
        check_vma=False,
    )
```

```python
import math

import jax
import jax.numpy as jnp
from jax import lax
from jax.experimental import pallas as pl
from jax.experimental.pallas import tpu as pltpu
from jax.sharding import Mesh
from jax.sharding import PartitionSpec as P

HEADS = 16
KV_HEADS = 4
HEAD_DIM = 128
GROUP = HEADS // KV_HEADS
RESP_LEN = 2048
PROMPT_LEN = 1024
CTX = ("xh", "z")
LOCAL = ("xh", "z", "core")
RESP = ("y", "xl", "core")
ROWS = 128
PROWS = 64
BOTH = ROWS + PROWS
CHUNK = 256
SPAN = 3 * CHUNK
TILE_SPANS = (2 * CHUNK, 3 * CHUNK)
TILE_STARTS = (0, 2 * CHUNK)
PROBS = 5 * CHUNK
HALF = GROUP * ROWS
LANES = 2 * HALF
WIDE = 2 * HEAD_DIM
SCALE = HEAD_DIM**-0.5
SCALE2 = SCALE * math.log2(math.e)
NEG = -1e30
F32 = jnp.float32
BF16 = jnp.bfloat16
VMEM = pl.BlockSpec(memory_space=pltpu.VMEM)
SMEM = pl.BlockSpec(memory_space=pltpu.SMEM)


def dot(a, b):
    return jnp.dot(a, b, preferred_element_type=F32)


def head_at(h, width=HEAD_DIM):
    return slice(h * width, (h + 1) * width)


def lanes_at(j, h):
    return slice(j * HALF + h * HEAD_DIM, j * HALF + (h + 1) * HEAD_DIM)


def block_of(member, quad, core):
    return (member // 2) * 8 + ((quad * 2 + (member & 1) + core) & 7)


def run_copies(pairs, sems):
    copies = [
        pltpu.make_async_copy(source, to, sems.at[i]) for i, (source, to) in enumerate(pairs)
    ]
    for copy in copies:
        copy.start()
    for copy in copies:
        copy.wait()


def pack_kv_kernel(info, k, v, kp, vp, kv0, kv1, kv2, kv3, k_s, v_s, kp_s, vp_s, sems):
    mine = info[0]
    run_copies(((k, k_s), (v, v_s), (kp, kp_s), (vp, vp_s)), sems)
    for d, kv in enumerate((kv0, kv1, kv2, kv3)):
        at = pl.ds(pl.multiple_of((mine ^ d) * HEAD_DIM, HEAD_DIM), HEAD_DIM)
        kv[:ROWS, :HEAD_DIM] = k_s[:, at]
        kv[:ROWS, HEAD_DIM:] = v_s[:, at]
        kv[ROWS:, :HEAD_DIM] = kp_s[:, at]
        kv[ROWS:, HEAD_DIM:] = vp_s[:, at]


def pack_qd_kernel(info, q, do, qd0, qd1, qd2, qd3, q_s, do_s, sems):
    mine = info[0]
    run_copies(((q, q_s), (do, do_s)), sems)
    for d, qd in enumerate((qd0, qd1, qd2, qd3)):
        at = pl.ds(pl.multiple_of((mine ^ d) * HALF, HALF), HALF)
        qd[:, :HALF] = q_s[:, at]
        qd[:, HALF:] = do_s[:, at]


def rows_at(mine, d):
    return pl.ds(pl.multiple_of(CHUNK + (mine ^ d) // 2 * CHUNK + (d & 1) * ROWS, ROWS), ROWS)


def load_keys(mine, g, kvs, k_s, v_s):
    for d, kv in enumerate(kvs):
        k_s[g, rows_at(mine, d), :] = kv[:ROWS, :HEAD_DIM]
        v_s[g, rows_at(mine, d), :] = kv[:ROWS, HEAD_DIM:]
        k_s[g, head_at(d, PROWS), :] = kv[ROWS:, :HEAD_DIM]
        v_s[g, head_at(d, PROWS), :] = kv[ROWS:, HEAD_DIM:]


def query_rows(info, x):
    mine, quad, core = info[0], info[1], info[2]
    rows = []
    for j in range(2):
        start = block_of(x * 2 + ((mine & 1) ^ j), quad, core) * ROWS
        rows += [start + lax.broadcasted_iota(jnp.int32, (1, ROWS), 1)] * GROUP
    return jnp.concatenate(rows, axis=1)


def key_rows(info, x, quad):
    mine, core = info[0], info[2]
    rows = []
    for j in range(2):
        start = block_of(x * 2 + ((mine & 1) ^ j), quad, core) * ROWS
        rows.append(start + lax.broadcasted_iota(jnp.int32, (ROWS, 1), 0))
    return jnp.concatenate(rows, axis=0)


def fold(x, op):
    return op(x.reshape(x.shape[0] // 8, 8, LANES), axis=0)


def each(count, step, carry):
    return step(0, carry) if count == 1 else lax.fori_loop(0, count, step, carry)


def forward(info, quads, count, k_s, v_s, qt, before, score_s, probs, vt_s, shift, total, acc):
    def turn_values(g, carry):
        vt_s[g] = v_s[g].T
        return carry

    each(count, turn_values, 0)
    for x in range(2):
        place = query_rows(info, x)
        start, span = TILE_STARTS[x], TILE_SPANS[x]

        def score_step(g, running):
            for c in range(span // CHUNK):
                at = slice(c * CHUNK, (c + 1) * CHUNK)
                score = dot(k_s[g, at, :], qt[x])
                if c > 0:
                    score = jnp.where(key_rows(info, c - 1, quads(g)) <= place, score, NEG)
                score_s[g, at, :] = score
                running = jnp.maximum(running, fold(score, jnp.max))
            return running

        running = each(count, score_step, jnp.full((8, LANES), NEG, F32))
        now = jnp.max(running, axis=0, keepdims=True) * SCALE2
        if before is not None:
            now = jnp.maximum(now, before[0][x])
            factor = jnp.exp2(before[0][x] - now)
            acc[x] = before[2][x] * factor

        def prob_step(g, running):
            for c in range(span // CHUNK):
                prob = jnp.exp2(score_s[g, c * CHUNK : (c + 1) * CHUNK, :] * SCALE2 - now)
                running = running + fold(prob, jnp.sum)
                probs[g, start + c * CHUNK : start + (c + 1) * CHUNK, :] = prob.astype(BF16)
            part = dot(vt_s[g, :, :span], probs[g, start : start + span, :])
            if before is None:
                acc[x] = part
            else:
                acc[x] += part
            return running

        running = each(count, prob_step, jnp.zeros((8, LANES), F32))
        sums = jnp.sum(running, axis=0, keepdims=True)
        if before is not None:
            sums = sums + before[1][x] * factor
        shift[x], total[x] = now, sums


def chunk_at(c, start):
    if isinstance(c, int):
        return slice(start + c * CHUNK, start + (c + 1) * CHUNK)
    return pl.ds(pl.multiple_of(start + c * CHUNK, CHUNK), CHUNK)


def backward(count, looped, k_s, v_s, kt_s, q, uplt, upl, delta, probs, factors, grad_s, before, dqt):
    for x in range(2):
        dqt[x] = jnp.zeros((HEAD_DIM, LANES), F32) if before is None else before[x]

    def chunk(g, c, tiles):
        at = chunk_at(c, 0)
        dk, dv = None, None
        for x in tiles:
            here = chunk_at(c, TILE_STARTS[x])
            low = probs[g, here, :]
            if factors is not None:
                low = (low.astype(F32) * factors[x]).astype(BF16)
            prob_grad = dot(v_s[g, at, :], uplt[x])
            grad = (low.astype(F32) * (prob_grad - delta[x])).astype(BF16)
            grad_s[here, :] = grad
            dv_part = dot(low, upl[x])
            dk_part = dot(grad, q[x])
            dv = dv_part if dv is None else dv + dv_part
            dk = dk_part if dk is None else dk + dk_part
        k_s[g, at, :] = (dk * SCALE).astype(BF16)
        v_s[g, at, :] = dv.astype(BF16)

    def step(g, carry):
        kt_s[...] = k_s[g].T

        def two_tiles(c, carry):
            chunk(g, c, (0, 1))
            return carry

        if looped:
            lax.fori_loop(0, 2, two_tiles, 0)
        else:
            two_tiles(0, 0)
            two_tiles(1, 0)
        chunk(g, 2, (1,))
        for x in range(2):
            start, span = TILE_STARTS[x], TILE_SPANS[x]
            dqt[x] += dot(kt_s[:, :span], grad_s[start : start + span, :])
        return carry

    each(count, step, 0)


def store_grads(mine, g, k_s, v_s, outs):
    for d, out in enumerate(outs):
        out[:ROWS, :HEAD_DIM] = k_s[g, rows_at(mine, d), :]
        out[:ROWS, HEAD_DIM:] = v_s[g, rows_at(mine, d), :]
        out[ROWS:, :HEAD_DIM] = k_s[g, head_at(d, PROWS), :]
        out[ROWS:, HEAD_DIM:] = v_s[g, head_at(d, PROWS), :]


def pieces(*parts):
    return [part.at[d] for part in parts for d in range(part.shape[0])]


def first_kernel(
    info, weight, qd0, qd1, qd2, qd3, own_a, own_b,
    qt, q, upt, probs, shift, total, acc,
    k_s, v_s, vt_s, score_s,
):
    mine, quad, core, count = info[0], info[1], info[2], info[4]
    load_keys(mine, 0, pieces(own_a, own_b), k_s, v_s)
    for d, qd in enumerate((qd0, qd1, qd2, qd3)):
        x = (mine ^ d) // 2
        row = block_of(mine ^ d, quad, core) * ROWS
        row = row + lax.broadcasted_iota(jnp.int32, (1, ROWS), 1)
        row_weight = jnp.where(row < count, weight[0], 0.0)
        for h in range(GROUP):
            cols = lanes_at(d & 1, h)
            q_head = qd[:, head_at(h)]
            q[x, cols, :] = q_head
            qt[x, :, cols] = q_head.T
            grad = qd[:, HALF + h * HEAD_DIM : HALF + (h + 1) * HEAD_DIM]
            upt[x, :, cols] = (grad.T.astype(F32) * row_weight).astype(BF16)
    forward(
        info, lambda g: quad, 1, k_s, v_s, qt, None, score_s, probs, vt_s, shift, total, acc
    )


def side_kernel(
    info, qt, left_a, left_b, right_a, right_b, shift0, total0, acc0,
    probs, shift, total, acc,
    k_s, v_s, vt_s, score_s,
):
    mine, quad = info[0], info[1]
    load_keys(mine, 0, pieces(left_a, left_b), k_s, v_s)
    load_keys(mine, 1, pieces(right_a, right_b), k_s, v_s)
    forward(
        info, lambda g: (quad + 3 + 2 * g) & 3, 2, k_s, v_s, qt, (shift0, total0, acc0),
        score_s, probs, vt_s, shift, total, acc,
    )


def far_kernel(
    info, qt, q, upt, far_a, far_b, shift0, total0, acc0,
    shift, uplt, upl, delta, dqt, attn, out_a, out_b,
    k_s, v_s, vt_s, kt_s, score_s, probs, grad_s, acc, total,
):
    mine, quad, length = info[0], info[1], info[3]
    load_keys(mine, 0, pieces(far_a, far_b), k_s, v_s)
    forward(
        info, lambda g: (quad + 2) & 3, 1, k_s, v_s, qt, (shift0, total0, acc0),
        score_s, probs, vt_s, shift, total, acc,
    )
    for x in range(2):
        inverse = 1.0 / total[x]
        valid = jnp.where(query_rows(info, x) < length, 1.0, 0.0)
        out_t = (acc[x] * (inverse * valid)).astype(BF16)
        up_low = (upt[x].astype(F32) * inverse).astype(BF16)
        uplt[x] = up_low
        delta[x] = jnp.sum(up_low.astype(F32) * out_t.astype(F32), axis=0, keepdims=True)
        attn[x] = out_t
        for j in range(2):
            for h in range(GROUP):
                upl[x, lanes_at(j, h), :] = up_low[:, lanes_at(j, h)].T
    backward(
        1, False, k_s, v_s, kt_s, q, uplt, upl, delta, probs, None, grad_s, None, dqt
    )
    store_grads(mine, 0, k_s, v_s, pieces(out_a, out_b))


def back_side_kernel(
    info, q, uplt, upl, delta, shift_then, shift_last, probs,
    left_a, left_b, right_a, right_b, dqt0,
    dqt, out_l, out_r,
    k_s, v_s, kt_s, grad_s,
):
    mine = info[0]
    factors = [jnp.exp2(shift_then[x] - shift_last[x]) for x in range(2)]
    load_keys(mine, 0, pieces(left_a, left_b), k_s, v_s)
    load_keys(mine, 1, pieces(right_a, right_b), k_s, v_s)
    backward(
        2, False, k_s, v_s, kt_s, q, uplt, upl, delta, probs, factors, grad_s, dqt0, dqt
    )
    store_grads(mine, 0, k_s, v_s, pieces(out_l))
    store_grads(mine, 1, k_s, v_s, pieces(out_r))


def back_own_kernel(
    info, q, uplt, upl, delta, shift_then, shift_last, probs, own_a, own_b, dqt0, attn,
    out, od0, od1, od2, od3,
    k_s, v_s, kt_s, grad_s, dqt, dq_s,
):
    mine = info[0]
    factors = [jnp.exp2(shift_then[x] - shift_last[x]) for x in range(2)]
    load_keys(mine, 0, pieces(own_a, own_b), k_s, v_s)
    backward(
        1, True, k_s, v_s, kt_s, q, uplt, upl, delta, probs, factors, grad_s, dqt0, dqt
    )
    store_grads(mine, 0, k_s, v_s, pieces(out))
    for x in range(2):
        dq_s[x] = (dqt[x] * SCALE).astype(BF16)
    for d, od in enumerate((od0, od1, od2, od3)):
        x = (mine ^ d) // 2
        for h in range(GROUP):
            od[:, head_at(h)] = attn[x, :, lanes_at(d & 1, h)].T
            od[:, HALF + h * HEAD_DIM : HALF + (h + 1) * HEAD_DIM] = dq_s[
                x, :, lanes_at(d & 1, h)
            ].T


def unpack_kernel(info, od0, od1, od2, od3, attended, query_grad):
    mine = info[0]
    for d, od in enumerate((od0, od1, od2, od3)):
        at = pl.ds(pl.multiple_of((mine ^ d) * HALF, HALF), HALF)
        attended[:, at] = od[:, :HALF]
        query_grad[:, at] = od[:, HALF:]


def both(a, b):
    return (a.astype(F32) + b.astype(F32)).astype(BF16)


def add_kernel(side_l, side_r, far_a, far_b, out_l, out_r):
    out_r[:2] = both(side_r[:2], far_a[...])
    out_r[2:] = side_r[2:]
    out_l[:2] = side_l[:2]
    out_l[2:] = both(side_l[2:], far_b[...])


def sum_kernel(own, left, right, *outs):
    for d, out in enumerate(outs):
        total = own[d].astype(F32) + left[d].astype(F32) + right[d].astype(F32)
        out[...] = total.astype(BF16)


def share_kernel(info, g0, g1, g2, g3, keep, send):
    mine, first = info[0], info[2] == 0
    for d, g in enumerate((g0, g1, g2, g3)):
        at = pl.ds(pl.multiple_of((mine ^ d) * HEAD_DIM, HEAD_DIM), HEAD_DIM)
        keys, values = g[ROWS:, :HEAD_DIM], g[ROWS:, HEAD_DIM:]
        keep[:, at] = jnp.where(first, keys, values)
        send[:, at] = jnp.where(first, values, keys)


def finish_kernel(info, g0, g1, g2, g3, key_grad, value_grad):
    mine = info[0]
    for d, g in enumerate((g0, g1, g2, g3)):
        at = pl.ds(pl.multiple_of((mine ^ d) * HEAD_DIM, HEAD_DIM), HEAD_DIM)
        key_grad[:, at] = g[:ROWS, :HEAD_DIM]
        value_grad[:, at] = g[:ROWS, HEAD_DIM:]


def bf16(*shape):
    return jax.ShapeDtypeStruct(shape, BF16)


def f32(*shape):
    return jax.ShapeDtypeStruct(shape, F32)


def call(kernel, outs, scratch, scalars, *operands, copies=0, products=0):
    place = pl.BlockSpec(memory_space=pl.ANY) if copies else VMEM
    scratch = [pltpu.VMEM(shape, dtype) for shape, dtype in scratch]
    if copies:
        scratch.append(pltpu.SemaphoreType.DMA((copies,)))
    return pl.pallas_call(
        kernel,
        out_shape=tuple(outs),
        in_specs=[SMEM] * len(scalars) + [place] * len(operands),
        out_specs=(VMEM,) * len(outs),
        scratch_shapes=scratch,
        compiler_params=pltpu.CompilerParams(vmem_limit_bytes=(56 if copies else 32) * 2**20),
        cost_estimate=pl.CostEstimate(
            flops=products * PROBS * LANES * HEAD_DIM * 4,
            bytes_accessed=1_000_000,
            transcendentals=0,
        ),
    )(*scalars, *operands)


def swap(x, axis):
    return lax.ppermute(x, axis, [(0, 1), (1, 0)])


def turn(x, axis, step):
    size = lax.axis_size(axis)
    return lax.ppermute(x, axis, [(i, (i + step) % size) for i in range(size)])


def local_permute(x, place):
    pairs = []
    for i in range(32):
        xh, z, core = i // 16, i // 2 % 8, i % 2
        xh, z = place(xh, (z - core) % 8)
        pairs.append((i, (xh * 8 + (z + core) % 8) * 2 + core))
    return lax.ppermute(x, LOCAL, pairs)


def partner(x, d):
    return local_permute(x, lambda xh, z: (xh ^ (d // 2), z ^ (d & 1)))


def quad_turn(x, step):
    return local_permute(x, lambda xh, z: (xh, (z + 2 * step) % 8))


def rounded(x):
    return lax.optimization_barrier(x.astype(BF16))


def body(q_resp, k_resp, v_resp, k_prompt, v_prompt, d_out, lengths, counts):
    core = lax.axis_index("core")
    z = (lax.axis_index("z") - core) & 7
    mine = lax.axis_index("xh") * 2 + (z & 1)
    info = jnp.stack([mine, z // 2, core, lengths[0], counts[0]]).astype(jnp.int32)
    weight = (RESP_LEN / counts[0].astype(F32)).reshape(1)
    spot = mine.reshape(1).astype(jnp.int32)
    width = KV_HEADS * HEAD_DIM
    kv = list(
        call(
            pack_kv_kernel,
            (bf16(BOTH, WIDE),) * 4,
            [((ROWS, width), BF16)] * 2 + [((PROWS, width), BF16)] * 2,
            (spot,),
            k_resp[0], v_resp[0], k_prompt, v_prompt,
            copies=4,
        )
    )
    for d in (1, 2, 3):
        kv[d] = partner(kv[d], d)
    own_a = jnp.stack(kv[:2])
    own_a, spot = lax.optimization_barrier((own_a, spot))
    qd = list(
        call(
            pack_qd_kernel,
            (bf16(ROWS, LANES),) * 4,
            [((ROWS, HEADS * HEAD_DIM), BF16)] * 2,
            (spot,),
            q_resp[0], d_out[0],
            copies=2,
        )
    )
    left_a, right_a = quad_turn(own_a, 1), quad_turn(own_a, -1)
    for d in (1, 2, 3):
        qd[d] = partner(qd[d], d)
    own_b = jnp.stack(kv[2:])
    own_b, left_a, right_a = lax.optimization_barrier((own_b, left_a, right_a))
    left_b, right_b = quad_turn(own_b, 1), quad_turn(own_b, -1)
    right_b, qd[3] = lax.optimization_barrier((right_b, qd[3]))
    far_a, far_b = quad_turn(left_a, 1), quad_turn(right_b, -1)

    tiles = (2, HEAD_DIM, LANES)
    line = f32(2, 1, LANES)

    def keys(count):
        return [((count, SPAN, HEAD_DIM), BF16)] * 2

    def forward_scratch(count):
        return keys(count) + [((count, HEAD_DIM, SPAN), BF16), ((count, SPAN, LANES), F32)]

    turned = ((HEAD_DIM, SPAN), BF16)
    grad_s = ((PROBS, LANES), BF16)
    whole, pair = bf16(4, BOTH, WIDE), bf16(2, BOTH, WIDE)
    qt, q, upt, probs1, shift1, total1, acc1 = call(
        first_kernel,
        (bf16(*tiles), bf16(2, LANES, HEAD_DIM), bf16(*tiles), bf16(1, PROBS, LANES), line, line, f32(*tiles)),
        forward_scratch(1),
        (info, weight),
        *qd, own_a, own_b,
        products=2,
    )
    probs2, shift2, total2, acc2 = call(
        side_kernel,
        (bf16(2, PROBS, LANES), line, line, f32(*tiles)),
        forward_scratch(2),
        (info,),
        qt, left_a, left_b, right_a, right_b, shift1, total1, acc1,
        products=4,
    )
    shift3, uplt, upl, delta, dqt, attn, far_ga, far_gb = call(
        far_kernel,
        (line, bf16(*tiles), bf16(2, LANES, HEAD_DIM), line, f32(*tiles), bf16(*tiles), pair, pair),
        keys(1) + [((1, HEAD_DIM, SPAN), BF16), turned, ((1, SPAN, LANES), F32)]
        + [((1, PROBS, LANES), BF16), grad_s, (tiles, F32), ((2, 1, LANES), F32)],
        (info,),
        qt, q, upt, far_a, far_b, shift2, total2, acc2,
        products=6,
    )
    far_ga, far_gb = quad_turn(far_ga, 1), quad_turn(far_gb, -1)
    dqt, left_g, right_g = call(
        back_side_kernel,
        (f32(*tiles), whole, whole),
        keys(2) + [turned, grad_s],
        (info,),
        q, uplt, upl, delta, shift2, shift3, probs2,
        left_a, left_b, right_a, right_b, dqt,
        products=8,
    )
    left_g, right_g = call(add_kernel, (whole, whole), (), (), left_g, right_g, far_ga, far_gb)
    left_g, right_g = quad_turn(left_g, -1), quad_turn(right_g, 1)
    own_g, *od = call(
        back_own_kernel,
        (whole,) + (bf16(ROWS, LANES),) * 4,
        keys(1) + [turned, grad_s, (tiles, F32), (tiles, BF16)],
        (info,),
        q, uplt, upl, delta, shift1, shift3, probs1, own_a, own_b, dqt, attn,
        products=4,
    )
    od[3], od[2] = partner(od[3], 3), partner(od[2], 2)
    left_g, right_g, od[1] = lax.optimization_barrier((left_g, right_g, od[1]))
    od[1] = partner(od[1], 1)
    grads = list(call(sum_kernel, (bf16(BOTH, WIDE),) * 4, (), (), own_g, left_g, right_g))
    for d in (3, 2, 1):
        grads[d] = partner(grads[d], d)
    tied = lax.optimization_barrier((*grads[::-1], *od[:0:-1]))
    grads, od[1:] = tied[3::-1], tied[:3:-1]
    rows = bf16(ROWS, HEADS * HEAD_DIM)
    keep, send = call(share_kernel, (bf16(PROWS, width),) * 2, (), (info,), *grads)
    share = rounded(keep.astype(F32) + swap(send, "core").astype(F32))
    share = rounded(share.astype(F32) + swap(share, "xl").astype(F32))
    key_grad, value_grad = call(
        finish_kernel, (bf16(ROWS, width),) * 2, (), (info,), *grads
    )
    attended, query_grad = call(unpack_kernel, (rows, rows), (), (info,), *od)
    share, key_grad, value_grad, attended, query_grad = lax.optimization_barrier(
        (share, key_grad, value_grad, attended, query_grad)
    )
    across = share.astype(F32) + turn(share, "y", 2).astype(F32)
    beside = turn(share, "y", 1).astype(F32) + turn(share, "y", 3).astype(F32)
    share = rounded(across + beside)
    other = swap(share, "core")
    key_share = jnp.where(core == 0, share, other)
    value_share = jnp.where(core == 0, other, share)
    return (
        attended[None],
        query_grad[None],
        key_grad[None],
        value_grad[None],
        key_share,
        value_share,
    )


def solution(mesh):
    split = Mesh(mesh.devices.reshape(2, 8, 4, 2, 2), CTX + RESP)
    rows = P(RESP, CTX, None)
    prompt = P(CTX, None)
    return jax.shard_map(
        body,
        mesh=split,
        in_specs=(rows, rows, rows, prompt, prompt, rows, P(RESP), P(RESP)),
        out_specs=(rows, rows, rows, rows, prompt, prompt),
        check_vma=False,
    )
```

```python
import math

import jax
import jax.numpy as jnp
from jax import lax
from jax.experimental import pallas as pl
from jax.experimental.pallas import tpu as pltpu
from jax.sharding import Mesh
from jax.sharding import PartitionSpec as P

HEADS = 16
KV_HEADS = 4
HEAD_DIM = 128
GROUP = HEADS // KV_HEADS
RESP_LEN = 2048
PROMPT_LEN = 1024
CTX = ("xh", "z")
LOCAL = ("xh", "z", "core")
RESP = ("y", "xl", "core")
ROWS = 128
PROWS = 64
BOTH = ROWS + PROWS
CHUNK = 256
SPAN = 3 * CHUNK
TILE_SPANS = (2 * CHUNK, 3 * CHUNK)
TILE_STARTS = (0, 2 * CHUNK)
PROBS = 5 * CHUNK
HALF = GROUP * ROWS
LANES = 2 * HALF
WIDE = 2 * HEAD_DIM
SCALE = HEAD_DIM**-0.5
SCALE2 = SCALE * math.log2(math.e)
NEG = -1e30
F32 = jnp.float32
BF16 = jnp.bfloat16
VMEM = pl.BlockSpec(memory_space=pltpu.VMEM)
SMEM = pl.BlockSpec(memory_space=pltpu.SMEM)


def dot(a, b):
    return jnp.dot(a, b, preferred_element_type=F32)


def head_at(h, width=HEAD_DIM):
    return slice(h * width, (h + 1) * width)


def lanes_at(j, h):
    return slice(j * HALF + h * HEAD_DIM, j * HALF + (h + 1) * HEAD_DIM)


def block_of(member, quad, core):
    return (member // 2) * 8 + ((quad * 2 + (member & 1) + core) & 7)


def run_copies(pairs, sems):
    copies = [
        pltpu.make_async_copy(source, to, sems.at[i]) for i, (source, to) in enumerate(pairs)
    ]
    for copy in copies:
        copy.start()
    for copy in copies:
        copy.wait()


def pack_kv_kernel(info, k, v, kp, vp, kv0, kv1, kv2, kv3, k_s, v_s, kp_s, vp_s, sems):
    mine = info[0]
    run_copies(((k, k_s), (v, v_s), (kp, kp_s), (vp, vp_s)), sems)
    for d, kv in enumerate((kv0, kv1, kv2, kv3)):
        at = pl.ds(pl.multiple_of((mine ^ d) * HEAD_DIM, HEAD_DIM), HEAD_DIM)
        kv[:ROWS, :HEAD_DIM] = k_s[:, at]
        kv[:ROWS, HEAD_DIM:] = v_s[:, at]
        kv[ROWS:, :HEAD_DIM] = kp_s[:, at]
        kv[ROWS:, HEAD_DIM:] = vp_s[:, at]


def pack_qd_kernel(info, q, do, qd0, qd1, qd2, qd3, q_s, do_s, sems):
    mine = info[0]
    run_copies(((q, q_s), (do, do_s)), sems)
    for d, qd in enumerate((qd0, qd1, qd2, qd3)):
        at = pl.ds(pl.multiple_of((mine ^ d) * HALF, HALF), HALF)
        qd[:, :HALF] = q_s[:, at]
        qd[:, HALF:] = do_s[:, at]


def rows_at(mine, d):
    return pl.ds(pl.multiple_of(CHUNK + (mine ^ d) // 2 * CHUNK + (d & 1) * ROWS, ROWS), ROWS)


def load_keys(mine, g, kvs, k_s, v_s):
    for d, kv in enumerate(kvs):
        k_s[g, rows_at(mine, d), :] = kv[:ROWS, :HEAD_DIM]
        v_s[g, rows_at(mine, d), :] = kv[:ROWS, HEAD_DIM:]
        k_s[g, head_at(d, PROWS), :] = kv[ROWS:, :HEAD_DIM]
        v_s[g, head_at(d, PROWS), :] = kv[ROWS:, HEAD_DIM:]


def query_rows(info, x):
    mine, quad, core = info[0], info[1], info[2]
    rows = []
    for j in range(2):
        start = block_of(x * 2 + ((mine & 1) ^ j), quad, core) * ROWS
        rows += [start + lax.broadcasted_iota(jnp.int32, (1, ROWS), 1)] * GROUP
    return jnp.concatenate(rows, axis=1)


def key_rows(info, x, quad):
    mine, core = info[0], info[2]
    rows = []
    for j in range(2):
        start = block_of(x * 2 + ((mine & 1) ^ j), quad, core) * ROWS
        rows.append(start + lax.broadcasted_iota(jnp.int32, (ROWS, 1), 0))
    return jnp.concatenate(rows, axis=0)


def fold(x, op):
    return op(x.reshape(x.shape[0] // 8, 8, LANES), axis=0)


def each(count, step, carry):
    return step(0, carry) if count == 1 else lax.fori_loop(0, count, step, carry)


def forward(info, quads, count, k_s, v_s, qt, before, score_s, probs, vt_s, shift, total, acc):
    def turn_values(g, carry):
        vt_s[g] = v_s[g].T
        return carry

    each(count, turn_values, 0)
    for x in range(2):
        place = query_rows(info, x)
        start, span = TILE_STARTS[x], TILE_SPANS[x]

        def score_step(g, running):
            for c in range(span // CHUNK):
                at = slice(c * CHUNK, (c + 1) * CHUNK)
                score = dot(k_s[g, at, :], qt[x])
                if c > 0:
                    score = jnp.where(key_rows(info, c - 1, quads(g)) <= place, score, NEG)
                score_s[g, at, :] = score
                running = jnp.maximum(running, fold(score, jnp.max))
            return running

        running = each(count, score_step, jnp.full((8, LANES), NEG, F32))
        now = jnp.max(running, axis=0, keepdims=True) * SCALE2
        if before is not None:
            now = jnp.maximum(now, before[0][x])
            factor = jnp.exp2(before[0][x] - now)
            acc[x] = before[2][x] * factor

        def prob_step(g, running):
            for c in range(span // CHUNK):
                prob = jnp.exp2(score_s[g, c * CHUNK : (c + 1) * CHUNK, :] * SCALE2 - now)
                running = running + fold(prob, jnp.sum)
                probs[g, start + c * CHUNK : start + (c + 1) * CHUNK, :] = prob.astype(BF16)
            part = dot(vt_s[g, :, :span], probs[g, start : start + span, :])
            if before is None:
                acc[x] = part
            else:
                acc[x] += part
            return running

        running = each(count, prob_step, jnp.zeros((8, LANES), F32))
        sums = jnp.sum(running, axis=0, keepdims=True)
        if before is not None:
            sums = sums + before[1][x] * factor
        shift[x], total[x] = now, sums


def chunk_at(c, start):
    if isinstance(c, int):
        return slice(start + c * CHUNK, start + (c + 1) * CHUNK)
    return pl.ds(pl.multiple_of(start + c * CHUNK, CHUNK), CHUNK)


def backward(count, looped, k_s, v_s, kt_s, q, uplt, upl, delta, probs, factors, grad_s, before, dqt):
    for x in range(2):
        dqt[x] = jnp.zeros((HEAD_DIM, LANES), F32) if before is None else before[x]

    def chunk(g, c, tiles):
        at = chunk_at(c, 0)
        dk, dv = None, None
        for x in tiles:
            here = chunk_at(c, TILE_STARTS[x])
            low = probs[g, here, :]
            if factors is not None:
                low = (low.astype(F32) * factors[x]).astype(BF16)
            prob_grad = dot(v_s[g, at, :], uplt[x])
            grad = (low.astype(F32) * (prob_grad - delta[x])).astype(BF16)
            grad_s[here, :] = grad
            dv_part = dot(low, upl[x])
            dk_part = dot(grad, q[x])
            dv = dv_part if dv is None else dv + dv_part
            dk = dk_part if dk is None else dk + dk_part
        k_s[g, at, :] = (dk * SCALE).astype(BF16)
        v_s[g, at, :] = dv.astype(BF16)

    def step(g, carry):
        kt_s[...] = k_s[g].T

        def two_tiles(c, carry):
            chunk(g, c, (0, 1))
            return carry

        if looped:
            lax.fori_loop(0, 2, two_tiles, 0)
        else:
            two_tiles(0, 0)
            two_tiles(1, 0)
        chunk(g, 2, (1,))
        for x in range(2):
            start, span = TILE_STARTS[x], TILE_SPANS[x]
            dqt[x] += dot(kt_s[:, :span], grad_s[start : start + span, :])
        return carry

    each(count, step, 0)


def store_grads(mine, g, k_s, v_s, outs):
    for d, out in enumerate(outs):
        out[:ROWS, :HEAD_DIM] = k_s[g, rows_at(mine, d), :]
        out[:ROWS, HEAD_DIM:] = v_s[g, rows_at(mine, d), :]
        out[ROWS:, :HEAD_DIM] = k_s[g, head_at(d, PROWS), :]
        out[ROWS:, HEAD_DIM:] = v_s[g, head_at(d, PROWS), :]


def pieces(*parts):
    return [part.at[d] for part in parts for d in range(part.shape[0])]


def first_kernel(
    info, weight, qd0, qd1, qd2, qd3, own_a, own_b,
    qt, q, upt, probs, shift, total, acc,
    k_s, v_s, vt_s, score_s,
):
    mine, quad, core, count = info[0], info[1], info[2], info[4]
    load_keys(mine, 0, pieces(own_a, own_b), k_s, v_s)
    for d, qd in enumerate((qd0, qd1, qd2, qd3)):
        x = (mine ^ d) // 2
        row = block_of(mine ^ d, quad, core) * ROWS
        row = row + lax.broadcasted_iota(jnp.int32, (1, ROWS), 1)
        row_weight = jnp.where(row < count, weight[0], 0.0)
        for h in range(GROUP):
            cols = lanes_at(d & 1, h)
            q_head = qd[:, head_at(h)]
            q[x, cols, :] = q_head
            qt[x, :, cols] = q_head.T
            grad = qd[:, HALF + h * HEAD_DIM : HALF + (h + 1) * HEAD_DIM]
            upt[x, :, cols] = (grad.T.astype(F32) * row_weight).astype(BF16)
    forward(
        info, lambda g: quad, 1, k_s, v_s, qt, None, score_s, probs, vt_s, shift, total, acc
    )


def side_kernel(
    info, qt, left_a, left_b, right_a, right_b, shift0, total0, acc0,
    probs, shift, total, acc,
    k_s, v_s, vt_s, score_s,
):
    mine, quad = info[0], info[1]
    load_keys(mine, 0, pieces(left_a, left_b), k_s, v_s)
    load_keys(mine, 1, pieces(right_a, right_b), k_s, v_s)
    forward(
        info, lambda g: (quad + 3 + 2 * g) & 3, 2, k_s, v_s, qt, (shift0, total0, acc0),
        score_s, probs, vt_s, shift, total, acc,
    )


def far_kernel(
    info, qt, q, upt, far_a, far_b, shift0, total0, acc0,
    shift, uplt, upl, delta, dqt, attn, out_a, out_b,
    k_s, v_s, vt_s, kt_s, score_s, probs, grad_s, acc, total,
):
    mine, quad, length = info[0], info[1], info[3]
    load_keys(mine, 0, pieces(far_a, far_b), k_s, v_s)
    forward(
        info, lambda g: (quad + 2) & 3, 1, k_s, v_s, qt, (shift0, total0, acc0),
        score_s, probs, vt_s, shift, total, acc,
    )
    for x in range(2):
        inverse = 1.0 / total[x]
        valid = jnp.where(query_rows(info, x) < length, 1.0, 0.0)
        out_t = (acc[x] * (inverse * valid)).astype(BF16)
        up_low = (upt[x].astype(F32) * inverse).astype(BF16)
        uplt[x] = up_low
        delta[x] = jnp.sum(up_low.astype(F32) * out_t.astype(F32), axis=0, keepdims=True)
        attn[x] = out_t
        for j in range(2):
            for h in range(GROUP):
                upl[x, lanes_at(j, h), :] = up_low[:, lanes_at(j, h)].T
    backward(
        1, False, k_s, v_s, kt_s, q, uplt, upl, delta, probs, None, grad_s, None, dqt
    )
    store_grads(mine, 0, k_s, v_s, pieces(out_a, out_b))


def back_side_kernel(
    info, q, uplt, upl, delta, shift_then, shift_last, probs,
    left_a, left_b, right_a, right_b, dqt0,
    dqt, out_l, out_r,
    k_s, v_s, kt_s, grad_s,
):
    mine = info[0]
    factors = [jnp.exp2(shift_then[x] - shift_last[x]) for x in range(2)]
    load_keys(mine, 0, pieces(left_a, left_b), k_s, v_s)
    load_keys(mine, 1, pieces(right_a, right_b), k_s, v_s)
    backward(
        2, False, k_s, v_s, kt_s, q, uplt, upl, delta, probs, factors, grad_s, dqt0, dqt
    )
    store_grads(mine, 0, k_s, v_s, pieces(out_l))
    store_grads(mine, 1, k_s, v_s, pieces(out_r))


def back_own_kernel(
    info, q, uplt, upl, delta, shift_then, shift_last, probs, own_a, own_b, dqt0, attn,
    out, od0, od1, od2, od3,
    k_s, v_s, kt_s, grad_s, dqt, dq_s,
):
    mine = info[0]
    factors = [jnp.exp2(shift_then[x] - shift_last[x]) for x in range(2)]
    load_keys(mine, 0, pieces(own_a, own_b), k_s, v_s)
    backward(
        1, True, k_s, v_s, kt_s, q, uplt, upl, delta, probs, factors, grad_s, dqt0, dqt
    )
    store_grads(mine, 0, k_s, v_s, pieces(out))
    for x in range(2):
        dq_s[x] = (dqt[x] * SCALE).astype(BF16)
    for d, od in enumerate((od0, od1, od2, od3)):
        x = (mine ^ d) // 2
        for h in range(GROUP):
            od[:, head_at(h)] = attn[x, :, lanes_at(d & 1, h)].T
            od[:, HALF + h * HEAD_DIM : HALF + (h + 1) * HEAD_DIM] = dq_s[
                x, :, lanes_at(d & 1, h)
            ].T


def unpack_kernel(info, od0, od1, od2, od3, attended, query_grad):
    mine = info[0]
    for d, od in enumerate((od0, od1, od2, od3)):
        at = pl.ds(pl.multiple_of((mine ^ d) * HALF, HALF), HALF)
        attended[:, at] = od[:, :HALF]
        query_grad[:, at] = od[:, HALF:]


def both(a, b):
    return (a.astype(F32) + b.astype(F32)).astype(BF16)


def add_kernel(side_l, side_r, far_a, far_b, out_l, out_r):
    out_r[:2] = both(side_r[:2], far_a[...])
    out_r[2:] = side_r[2:]
    out_l[:2] = side_l[:2]
    out_l[2:] = both(side_l[2:], far_b[...])


def sum_kernel(own, left, right, *outs):
    for d, out in enumerate(outs):
        total = own[d].astype(F32) + left[d].astype(F32) + right[d].astype(F32)
        out[...] = total.astype(BF16)


def share_kernel(info, g0, g1, g2, g3, keep, send):
    mine, first = info[0], info[2] == 0
    for d, g in enumerate((g0, g1, g2, g3)):
        at = pl.ds(pl.multiple_of((mine ^ d) * HEAD_DIM, HEAD_DIM), HEAD_DIM)
        keys, values = g[ROWS:, :HEAD_DIM], g[ROWS:, HEAD_DIM:]
        keep[:, at] = jnp.where(first, keys, values)
        send[:, at] = jnp.where(first, values, keys)


def finish_kernel(info, g0, g1, g2, g3, key_grad, value_grad):
    mine = info[0]
    for d, g in enumerate((g0, g1, g2, g3)):
        at = pl.ds(pl.multiple_of((mine ^ d) * HEAD_DIM, HEAD_DIM), HEAD_DIM)
        key_grad[:, at] = g[:ROWS, :HEAD_DIM]
        value_grad[:, at] = g[:ROWS, HEAD_DIM:]


def bf16(*shape):
    return jax.ShapeDtypeStruct(shape, BF16)


def f32(*shape):
    return jax.ShapeDtypeStruct(shape, F32)


def call(kernel, outs, scratch, scalars, *operands, copies=0, products=0):
    place = pl.BlockSpec(memory_space=pl.ANY) if copies else VMEM
    scratch = [pltpu.VMEM(shape, dtype) for shape, dtype in scratch]
    if copies:
        scratch.append(pltpu.SemaphoreType.DMA((copies,)))
    return pl.pallas_call(
        kernel,
        out_shape=tuple(outs),
        in_specs=[SMEM] * len(scalars) + [place] * len(operands),
        out_specs=(VMEM,) * len(outs),
        scratch_shapes=scratch,
        compiler_params=pltpu.CompilerParams(vmem_limit_bytes=(56 if copies else 32) * 2**20),
        cost_estimate=pl.CostEstimate(
            flops=products * PROBS * LANES * HEAD_DIM * 4,
            bytes_accessed=1_000_000 * products,
            transcendentals=0,
        ),
    )(*scalars, *operands)


def swap(x, axis):
    return lax.ppermute(x, axis, [(0, 1), (1, 0)])


def turn(x, axis, step):
    size = lax.axis_size(axis)
    return lax.ppermute(x, axis, [(i, (i + step) % size) for i in range(size)])


def local_permute(x, place):
    pairs = []
    for i in range(32):
        xh, z, core = i // 16, i // 2 % 8, i % 2
        xh, z = place(xh, (z - core) % 8)
        pairs.append((i, (xh * 8 + (z + core) % 8) * 2 + core))
    return lax.ppermute(x, LOCAL, pairs)


def partner(x, d):
    return local_permute(x, lambda xh, z: (xh ^ (d // 2), z ^ (d & 1)))


def quad_turn(x, step):
    return local_permute(x, lambda xh, z: (xh, (z + 2 * step) % 8))


def rounded(x):
    return lax.optimization_barrier(x.astype(BF16))


def body(q_resp, k_resp, v_resp, k_prompt, v_prompt, d_out, lengths, counts):
    core = lax.axis_index("core")
    z = (lax.axis_index("z") - core) & 7
    mine = lax.axis_index("xh") * 2 + (z & 1)
    info = jnp.stack([mine, z // 2, core, lengths[0], counts[0]]).astype(jnp.int32)
    weight = (RESP_LEN / counts[0].astype(F32)).reshape(1)
    spot = mine.reshape(1).astype(jnp.int32)
    width = KV_HEADS * HEAD_DIM
    kv = list(
        call(
            pack_kv_kernel,
            (bf16(BOTH, WIDE),) * 4,
            [((ROWS, width), BF16)] * 2 + [((PROWS, width), BF16)] * 2,
            (spot,),
            k_resp[0], v_resp[0], k_prompt, v_prompt,
            copies=4,
        )
    )
    for d in (1, 2, 3):
        kv[d] = partner(kv[d], d)
    own_a = jnp.stack(kv[:2])
    own_a, spot = lax.optimization_barrier((own_a, spot))
    qd = list(
        call(
            pack_qd_kernel,
            (bf16(ROWS, LANES),) * 4,
            [((ROWS, HEADS * HEAD_DIM), BF16)] * 2,
            (spot,),
            q_resp[0], d_out[0],
            copies=2,
        )
    )
    left_a, right_a = quad_turn(own_a, 1), quad_turn(own_a, -1)
    for d in (1, 2, 3):
        qd[d] = partner(qd[d], d)
    own_b = jnp.stack(kv[2:])
    own_b, left_a, right_a = lax.optimization_barrier((own_b, left_a, right_a))
    left_b, right_b = quad_turn(own_b, 1), quad_turn(own_b, -1)
    right_b, qd[3] = lax.optimization_barrier((right_b, qd[3]))
    far_a, far_b = quad_turn(left_a, 1), quad_turn(right_b, -1)

    tiles = (2, HEAD_DIM, LANES)
    line = f32(2, 1, LANES)

    def keys(count):
        return [((count, SPAN, HEAD_DIM), BF16)] * 2

    def forward_scratch(count):
        return keys(count) + [((count, HEAD_DIM, SPAN), BF16), ((count, SPAN, LANES), F32)]

    turned = ((HEAD_DIM, SPAN), BF16)
    grad_s = ((PROBS, LANES), BF16)
    whole, pair = bf16(4, BOTH, WIDE), bf16(2, BOTH, WIDE)
    qt, q, upt, probs1, shift1, total1, acc1 = call(
        first_kernel,
        (bf16(*tiles), bf16(2, LANES, HEAD_DIM), bf16(*tiles), bf16(1, PROBS, LANES), line, line, f32(*tiles)),
        forward_scratch(1),
        (info, weight),
        *qd, own_a, own_b,
        products=2,
    )
    probs2, shift2, total2, acc2 = call(
        side_kernel,
        (bf16(2, PROBS, LANES), line, line, f32(*tiles)),
        forward_scratch(2),
        (info,),
        qt, left_a, left_b, right_a, right_b, shift1, total1, acc1,
    )
    shift3, uplt, upl, delta, dqt, attn, far_ga, far_gb = call(
        far_kernel,
        (line, bf16(*tiles), bf16(2, LANES, HEAD_DIM), line, f32(*tiles), bf16(*tiles), pair, pair),
        keys(1) + [((1, HEAD_DIM, SPAN), BF16), turned, ((1, SPAN, LANES), F32)]
        + [((1, PROBS, LANES), BF16), grad_s, (tiles, F32), ((2, 1, LANES), F32)],
        (info,),
        qt, q, upt, far_a, far_b, shift2, total2, acc2,
        products=6,
    )
    far_ga, far_gb = quad_turn(far_ga, 1), quad_turn(far_gb, -1)
    dqt, left_g, right_g = call(
        back_side_kernel,
        (f32(*tiles), whole, whole),
        keys(2) + [turned, grad_s],
        (info,),
        q, uplt, upl, delta, shift2, shift3, probs2,
        left_a, left_b, right_a, right_b, dqt,
        products=8,
    )
    left_g, right_g = call(add_kernel, (whole, whole), (), (), left_g, right_g, far_ga, far_gb)
    left_g, right_g = quad_turn(left_g, -1), quad_turn(right_g, 1)
    own_g, *od = call(
        back_own_kernel,
        (whole,) + (bf16(ROWS, LANES),) * 4,
        keys(1) + [turned, grad_s, (tiles, F32), (tiles, BF16)],
        (info,),
        q, uplt, upl, delta, shift1, shift3, probs1, own_a, own_b, dqt, attn,
        products=4,
    )
    od[3], od[2] = partner(od[3], 3), partner(od[2], 2)
    left_g, right_g, od[1] = lax.optimization_barrier((left_g, right_g, od[1]))
    od[1] = partner(od[1], 1)
    grads = list(call(sum_kernel, (bf16(BOTH, WIDE),) * 4, (), (), own_g, left_g, right_g))
    for d in (3, 2, 1):
        grads[d] = partner(grads[d], d)
    tied = lax.optimization_barrier((*grads[::-1], *od[:0:-1]))
    grads, od[1:] = tied[3::-1], tied[:3:-1]
    rows = bf16(ROWS, HEADS * HEAD_DIM)
    keep, send = call(share_kernel, (bf16(PROWS, width),) * 2, (), (info,), *grads)
    share = rounded(keep.astype(F32) + swap(send, "core").astype(F32))
    share = rounded(share.astype(F32) + swap(share, "xl").astype(F32))
    key_grad, value_grad = call(
        finish_kernel, (bf16(ROWS, width),) * 2, (), (info,), *grads
    )
    attended, query_grad = call(unpack_kernel, (rows, rows), (), (info,), *od)
    share, key_grad, value_grad, attended, query_grad = lax.optimization_barrier(
        (share, key_grad, value_grad, attended, query_grad)
    )
    across = share.astype(F32) + turn(share, "y", 2).astype(F32)
    beside = turn(share, "y", 1).astype(F32) + turn(share, "y", 3).astype(F32)
    share = rounded(across + beside)
    other = swap(share, "core")
    key_share = jnp.where(core == 0, share, other)
    value_share = jnp.where(core == 0, other, share)
    return (
        attended[None],
        query_grad[None],
        key_grad[None],
        value_grad[None],
        key_share,
        value_share,
    )


def solution(mesh):
    split = Mesh(mesh.devices.reshape(2, 8, 4, 2, 2), CTX + RESP)
    rows = P(RESP, CTX, None)
    prompt = P(CTX, None)
    return jax.shard_map(
        body,
        mesh=split,
        in_specs=(rows, rows, rows, prompt, prompt, rows, P(RESP), P(RESP)),
        out_specs=(rows, rows, rows, rows, prompt, prompt),
        check_vma=False,
    )
```
